32 devices in a mesh: grp: 2 (over y), sec: 16 (over z, x, core), op: 1.
Axes of the slice: x: 2, y: 2, z: 4, core: 2. Of those that a mesh axis runs over, the one named last changes fastest.
Arguments:
- psi: bfloat16 [256, 8, 64, 128], P(('grp', 'sec')), parts along dimension 0, may hold values from -6 to 6
- left_ops: bfloat16 [256, 64, 64], P(('grp', 'sec'), None, 'op'), parts along dimension 0, may hold values from -0.75 to 0.75
- right_ops: bfloat16 [512, 64, 64], P(('grp', 'sec'), None, 'op'), parts along dimension 0, may hold values from -0.75 to 0.75
- dims_left: int32 [256], P(('grp', 'sec')), parts along dimension 0, may hold values from 32 to 64
- dims_right: int32 [512], P(('grp', 'sec')), parts along dimension 0, may hold values from 32 to 64
- right_owner: int32 [256, 8], P(('grp', 'sec')), parts along dimension 0, may hold values from 0 to 15, all different within a row; in each aligned block of 8 rows (0 to 7, 8 to 15, ...) at most 8 rows name the same one
- right_slot: int32 [256, 8], P(('grp', 'sec')), parts along dimension 0, may hold values from 0 to 15
- term_active: int32 [256, 8, 1], P(('grp', 'sec'), None, 'op'), parts along dimension 0, may hold values 0 or 1
Outputs:
- sigma: bfloat16 [256, 8, 64, 128], P(('grp', 'sec'), None, None, 'op'), parts along dimension 0
The draws below stay inside these ranges and needn't reach their ends.
There are 2 independent parts, one for each index of `grp`. The reference program is written for one: setup_inputs(seed, part) draws one part's arguments, and reference() takes and returns one part's arrays. A program takes and returns all parts, laid end to end along the dimension named above; each array names one. Nothing has to cross between parts.
Inputs may be any that keep to these rules, and one draw needn't show every extreme that they name: `right_owner`: each row names 8 different sec indices; within the rows of one device (aligned blocks of 8 rows) no index is named more than 8 times, a bound that some block reaches.
All inputs are finite; a program needn't handle non-finite values. No bound on the sum of `term_active` on one device may be relied on, other than what follows from the above.
Results may differ from the reference program's by a relative error of at most 0.0056.
Values may be sent and summed in bfloat16 or wider, within the bound.
No kernel may reach another device: no remote copies, remote signals or barrier semaphores. Data moves between devices by JAX's collectives and lax.ppermute only.
A program may use at most 64 MiB of HBM per device.

```python
import math
import jax
import jax.numpy as jnp
import numpy as np
from jax import lax

TILE = 64
BLOCKS = 8
LSEC_DEV = 8
RSEC_DEV = 16
TERM_DEV = 1
VECS = 2
TERMS = 1
NLS = 128
NRS = 256
CAP = 8
N_SEC = 16
N_OP = 1


def touch_ends(array, stream_key, smallest, high):
    dims = array.shape
    index_at = [jax.random.randint(jax.random.fold_in(stream_key, axis), (), 0, dims[axis]) for axis in range(len(dims))]
    array = array.at[tuple(index_at)].set(smallest)
    longest = dims.index(max(dims))
    index_at[longest] = (index_at[longest] + 1) % dims[longest]
    return array.at[tuple(index_at)].set(high)


def level_of(own_key, dims, cuts, low, largest):
    def one(axis_at, parts):
        steps = jax.random.uniform(jax.random.fold_in(jax.random.fold_in(own_key, 6), axis_at), (parts,), jnp.float32, low / len(cuts), largest / len(cuts))
        return jnp.repeat(jnp.exp(steps), dims[axis_at] // parts).reshape((-1,) + (1,) * (len(dims) - axis_at - 1))

    loudness = one(*cuts[0])
    for cut in cuts[1:]:
        loudness = loudness * one(*cut)
    return loudness


def shared_out(own_key, own, number, rows, count, top, most, skew):
    sequence = jax.random.permutation(own_key, count)
    crowded, ordinary = shares(count, rows * top, most, skew, True), shares(count, rows * top, most, skew, False)
    places = jnp.arange(count)

    def named(sizes, offset_by):
        used = int((sizes > 0).sum())
        fixed = max(1, used // 4)
        passed = fixed + (places - fixed + offset_by * (used - fixed)) % max(1, count - fixed)
        return jnp.zeros((count,), jnp.int32).at[sequence[jnp.where(places < fixed, places, passed)]].set(jnp.asarray(sizes, jnp.int32))

    sizes = jnp.where(number % 4 == 0, named(crowded, number // 4), named(ordinary, number - number // 4 - 1))
    mixed = jax.random.permutation(jax.random.fold_in(own, 3), count)
    giver, receiver = mixed[0:count // 2 * 2:2], mixed[1:count // 2 * 2:2]
    slack = jnp.minimum(sizes[giver] - 1, most - sizes[receiver]) // 2
    slack = jnp.where((giver == sequence[0]) | (receiver == sequence[0]) | (sizes[receiver] == 0), 0, jnp.maximum(slack, 0))
    passed = jax.random.randint(jax.random.fold_in(own, 4), (count // 2,), 0, 1 << 20) % (slack + 1)
    sizes = sizes.at[giver].add(-passed).at[receiver].add(passed)
    members = jnp.searchsorted(jnp.cumsum(sizes), jnp.arange(rows * top), side="right").astype(jnp.int32)
    grid = members.reshape(top, rows).T
    grid = grid[jax.random.permutation(jax.random.fold_in(own, 1), rows)]
    offset_by = jax.random.randint(jax.random.fold_in(own, 2), (rows, 1), 0, top)
    return jnp.take_along_axis(grid, (jnp.arange(top)[None, :] + offset_by) % top, axis=1)


def shares(amount, total, limit, lean, full):
    weights = [(1 << 20) // math.isqrt(grade ** lean) + 1 for grade in range(1, amount + 1)]
    largest = limit if full else min(limit, max(-(-total // amount), total * weights[0] // sum(weights)))
    least = 1 if total - largest >= amount - 1 else 0
    given, spare = [largest] + [least] * (amount - 1), total - largest - least * (amount - 1)
    while spare > 0:
        free = [i for i in range(1, amount) if given[i] < largest] or [i for i in range(1, amount) if given[i] < limit]
        whole, left = sum([weights[i] for i in free]), spare
        for i in free:
            addition = min(limit - given[i], max(1, left * weights[i] // whole), spare)
            given[i] = given[i] + addition
            spare = spare - addition
    return np.array(given)


def noise(key, extent, width, bound, shards=(), held_as=jnp.bfloat16):
    entries = jax.random.normal(key, extent, jnp.float32) * width
    if len(shards) > 0:
        entries = level_of(key, extent, shards, -0.22, 0.18) * entries
    return jnp.clip(entries, min=-bound, max=bound).astype(held_as)


def setup_inputs(seed: int = 0, part: int = 0) -> dict:
    splits = jax.random.split(jax.random.key(seed), 9)
    part_splits = jax.random.split(jax.random.fold_in(splits[8], part), 9)
    psi = noise(part_splits[0], (NLS, BLOCKS, TILE, VECS * TILE), 1.0, 6.0, ((0, 16),))
    left_ops = noise(part_splits[1], (NLS, TILE, TERMS * TILE), TILE ** -0.5, 0.75, ((0, 16),))
    right_ops = noise(part_splits[2], (NRS, TILE, TERMS * TILE), (TILE * TERMS) ** -0.5, 0.75, ((0, 16),))
    dims_left = touch_ends(jax.random.randint(part_splits[3], (NLS,), TILE // 2, TILE + 1), jax.random.fold_in(part_splits[3], 1), TILE // 2, TILE).astype(jnp.int32)
    dims_right = touch_ends(jax.random.randint(part_splits[4], (NRS,), TILE // 2, TILE + 1), jax.random.fold_in(part_splits[4], 1), TILE // 2, TILE).astype(jnp.int32)
    right_owner_keys = jax.random.split(jax.random.fold_in(part_splits[5], 1), NLS // LSEC_DEV)
    right_owner_turns = jax.random.permutation(jax.random.fold_in(part_splits[5], 3), NLS // LSEC_DEV)
    right_owner = jax.vmap(lambda own, number: shared_out(jax.random.fold_in(part_splits[5], 2), own, number, LSEC_DEV, N_SEC, BLOCKS, CAP, 1))(right_owner_keys, right_owner_turns).reshape((NLS, BLOCKS))
    right_slot = touch_ends(jax.random.randint(part_splits[6], (NLS, BLOCKS), 0, RSEC_DEV), jax.random.fold_in(part_splits[6], 1), 0, RSEC_DEV - 1).astype(jnp.int32)
    term_active = touch_ends((jax.random.randint(part_splits[7], (NLS, BLOCKS, TERMS), 0, 4) < 3).astype(jnp.int32), jax.random.fold_in(part_splits[7], 1), 0, 1)
    return dict(psi=psi, left_ops=left_ops, right_ops=right_ops, dims_left=dims_left, dims_right=dims_right, right_owner=right_owner, right_slot=right_slot, term_active=term_active)


def sector_sigma(psi_a, lop_a, dim_a, owner_a, slot_a, active_a, right_ops, dims_right):
    right_index = owner_a * RSEC_DEV + slot_a
    right_tiles = jnp.take(right_ops, right_index, axis=0).astype(jnp.float32)
    right_dims = jnp.take(dims_right, right_index)
    lanes = lax.iota(jnp.int32, TILE)
    row_keep = (lanes < dim_a).astype(jnp.float32)
    col_keep = (lanes[None, :] < right_dims[:, None]).astype(jnp.float32)
    tiles = psi_a.astype(jnp.float32).reshape(BLOCKS, TILE, VECS, TILE) * row_keep[None, :, None, None]
    left_tiles = lop_a.astype(jnp.float32).reshape(TILE, TERMS, TILE)
    half = jnp.einsum('itl,klvj->kitvj', left_tiles, tiles)
    half = half * active_a.astype(jnp.float32)[:, None, :, None, None]
    half = lax.optimization_barrier(half.astype(jnp.bfloat16)).astype(jnp.float32)
    half_split = half.reshape(BLOCKS, TILE, N_OP, TERM_DEV, VECS, TILE)
    right_split = right_tiles.reshape(BLOCKS, TILE, N_OP, TERM_DEV, TILE) * col_keep[:, None, None, None, :]
    partial_sums = jnp.einsum('kiptvj,ksptj->kpivs', half_split, right_split)
    partial_sums = partial_sums * col_keep[:, None, None, None, :]
    partial_sums = lax.optimization_barrier(partial_sums.astype(jnp.bfloat16)).astype(jnp.float32)
    total = jnp.sum(partial_sums, axis=1) * row_keep[None, :, None, None]
    return total.reshape(BLOCKS, TILE, VECS * TILE).astype(jnp.bfloat16)


def reference(psi, left_ops, right_ops, dims_left, dims_right, right_owner, right_slot, term_active):
    def one_sector(pieces):
        psi_a, lop_a, dim_a, owner_a, slot_a, active_a = pieces
        return sector_sigma(psi_a, lop_a, dim_a, owner_a, slot_a, active_a, right_ops, dims_right)

    return lax.map(one_sector, (psi, left_ops, dims_left, right_owner, right_slot, term_active))
```

```python
import functools

import jax
import jax.numpy as jnp
from jax import lax
from jax.experimental import pallas as pl
from jax.experimental.pallas import tpu as pltpu
from jax.sharding import PartitionSpec as P

VMEM_LIMIT = 48 * 1024 * 1024


def left_kernel(dims_ref, active_ref, left_ref, psi_ref, half_ref):
    sectors, blocks, tile, width = psi_ref.shape
    rows = lax.broadcasted_iota(jnp.int32, (tile, tile), 0)
    cols = lax.broadcasted_iota(jnp.int32, (tile, tile), 1)

    def one(a, carry):
        dim = dims_ref[a]
        keep = (rows < dim) & (cols < dim)
        op = jnp.where(keep, left_ref[a].astype(jnp.float32), 0.0).astype(jnp.bfloat16)
        for k in range(blocks):
            part = jnp.dot(op, psi_ref[a, k], preferred_element_type=jnp.float32)
            part = part * active_ref[a, k].astype(jnp.float32)
            half_ref[a, k] = part.astype(jnp.bfloat16)
        return carry

    lax.fori_loop(0, sectors, one, 0)


def right_kernel(owner_ref, slot_ref, half_ref, pairs_ref, out_ref):
    sectors, blocks, tile, width = half_ref.shape
    per_owner = pairs_ref.shape[1]
    lanes = lax.broadcasted_iota(jnp.int32, (tile, width), 1)

    def one(a, carry):
        for k in range(blocks):
            slot = slot_ref[a, k]
            second = (slot >= per_owner).astype(jnp.int32)
            pair = pairs_ref[owner_ref[a, k], slot - second * per_owner].astype(jnp.float32)
            swapped = pltpu.roll(pair, tile, 1)
            first_half = lanes < tile
            both = jnp.where((lanes >= tile).astype(jnp.int32) == second, pair, swapped)
            top = jnp.where(first_half, both, 0.0)
            low = jnp.where(first_half, 0.0, both)
            diag = jnp.concatenate([top, low], axis=0).astype(jnp.bfloat16)
            part = lax.dot_general(
                half_ref[a, k], diag, (((1,), (1,)), ((), ())), preferred_element_type=jnp.float32
            )
            out_ref[a, k] = part.astype(jnp.bfloat16)
        return carry

    lax.fori_loop(0, sectors, one, 0)


def per_device(
    psi, left_ops, right_ops, dims_left, dims_right, right_owner, right_slot, term_active
):
    left_count, block_count, tile, width = psi.shape
    right_count = right_ops.shape[0]
    pair_count = right_count // 2
    flops = 2 * psi.size * tile

    lanes = lax.iota(jnp.int32, tile)
    keep = lanes[None, :] < dims_right[:, None]
    kept = jnp.where(keep[:, :, None] & keep[:, None, :], right_ops, jnp.zeros_like(right_ops))
    pairs = jnp.concatenate([kept[:pair_count], kept[pair_count:]], axis=2)
    pairs_all = lax.all_gather(pairs, "sec", axis=0, tiled=False)

    smem = pl.BlockSpec(memory_space=pltpu.SMEM)
    vmem = pl.BlockSpec(memory_space=pltpu.VMEM)
    params = pltpu.CompilerParams(vmem_limit_bytes=VMEM_LIMIT)
    half = pl.pallas_call(
        left_kernel,
        out_shape=jax.ShapeDtypeStruct(psi.shape, jnp.bfloat16),
        in_specs=[smem, smem, vmem, vmem],
        out_specs=vmem,
        compiler_params=params,
        cost_estimate=pl.CostEstimate(flops=flops, bytes_accessed=4 * psi.size, transcendentals=0),
    )(dims_left, term_active.reshape(left_count, block_count), left_ops, psi)
    sigma = pl.pallas_call(
        right_kernel,
        out_shape=jax.ShapeDtypeStruct(psi.shape, jnp.bfloat16),
        in_specs=[smem, smem, vmem, vmem],
        out_specs=vmem,
        compiler_params=params,
        cost_estimate=pl.CostEstimate(flops=flops, bytes_accessed=8 * psi.size, transcendentals=0),
    )(right_owner, right_slot, half, pairs_all)
    if lax.axis_size("op") > 1:
        sigma = lax.psum_scatter(sigma, "op", scatter_dimension=3, tiled=True)
    return sigma


def solution(mesh):
    placed = (
        P(("grp", "sec"), None, None, None),
        P(("grp", "sec"), None, "op"),
        P(("grp", "sec"), None, "op"),
        P(("grp", "sec")),
        P(("grp", "sec")),
        P(("grp", "sec"), None),
        P(("grp", "sec"), None),
        P(("grp", "sec"), None, "op"),
    )
    return jax.shard_map(
        per_device,
        mesh=mesh,
        in_specs=placed,
        out_specs=P(("grp", "sec"), None, None, "op"),
        check_vma=False,
    )
```

```python
import functools

import jax
import jax.numpy as jnp
from jax import lax
from jax.experimental import pallas as pl
from jax.experimental.pallas import tpu as pltpu
from jax.sharding import PartitionSpec as P

VMEM_LIMIT = 48 * 1024 * 1024


def left_kernel(dims_ref, active_ref, left_ref, psi_ref, half_ref):
    sectors, blocks, tile, width = psi_ref.shape
    rows = lax.broadcasted_iota(jnp.int32, (tile, tile), 0)
    cols = lax.broadcasted_iota(jnp.int32, (tile, tile), 1)

    def one(a, carry):
        dim = dims_ref[a]
        keep = (rows < dim) & (cols < dim)
        op = jnp.where(keep, left_ref[a].astype(jnp.float32), 0.0).astype(jnp.bfloat16)
        for k in range(blocks):
            part = jnp.dot(op, psi_ref[a, k], preferred_element_type=jnp.float32)
            part = part * active_ref[a, k].astype(jnp.float32)
            half_ref[a, k] = part.astype(jnp.bfloat16)
        return carry

    lax.fori_loop(0, sectors, one, 0)


def pack_kernel(dims_ref, right_ref, pairs_ref):
    count, tile, width = pairs_ref.shape
    rows = lax.broadcasted_iota(jnp.int32, (tile, tile), 0)
    cols = lax.broadcasted_iota(jnp.int32, (tile, tile), 1)
    most = jnp.maximum(rows, cols)

    def kept(b):
        return jnp.where(most < dims_ref[b], right_ref[b].astype(jnp.float32), 0.0)

    for p in range(count):
        both = jnp.concatenate([kept(p), kept(p + count)], axis=1)
        pairs_ref[p] = both.astype(jnp.bfloat16)


def right_kernel(code_ref, half_ref, *refs):
    piece_refs, out_ref, pairs_ref, sems = refs[:-3], refs[-3], refs[-2], refs[-1]
    sectors, blocks, tile, width = half_ref.shape
    step = pairs_ref.shape[0] // len(piece_refs)
    copies = [
        pltpu.make_async_copy(piece, pairs_ref.at[pl.ds(i * step, step)], sems.at[i])
        for i, piece in enumerate(piece_refs)
    ]
    for copy in copies:
        copy.start()
    for copy in copies:
        copy.wait()
    lanes = lax.broadcasted_iota(jnp.int32, (tile, width), 1)
    upper = (lanes >= tile).astype(jnp.int32)

    def one(a, carry):
        for k in range(blocks):
            code = code_ref[a, k]
            second = code & 1
            pair = pairs_ref[code >> 1].astype(jnp.float32)
            swapped = pltpu.roll(pair, tile, 1)
            both = jnp.where(upper == second, pair, swapped)
            top = jnp.where(upper == 0, both, 0.0)
            low = jnp.where(upper == 0, 0.0, both)
            diag = jnp.concatenate([top, low], axis=0).astype(jnp.bfloat16)
            part = lax.dot_general(
                half_ref[a, k], diag, (((1,), (1,)), ((), ())), preferred_element_type=jnp.float32
            )
            out_ref[a, k] = part.astype(jnp.bfloat16)
        return carry

    lax.fori_loop(0, sectors, one, 0)


def gather_pieces(pairs):
    count = lax.axis_size("sec")
    me = lax.axis_index("sec")
    if count % 4 or count > 32:
        return [lax.all_gather(pairs, "sec", axis=0, tiled=True)], lambda owner: owner
    lines = count // 4
    pieces = [pairs]
    for shift in range(1, lines):
        route = [(i, (i + 4 * shift) % count) for i in range(count)]
        pieces.append(lax.ppermute(pairs, "sec", route))
    for bit in (2, 1):
        route = [(i, i ^ bit) for i in range(count)]
        pieces = pieces + [lax.ppermute(piece, "sec", route) for piece in pieces]

    def order(owner):
        shift = (me // 4 - owner // 4 + lines) % lines
        flip = (me ^ owner) & 3
        return ((flip & 1) * 2 + (flip >> 1)) * lines + shift

    return pieces, order


def per_device(
    psi, left_ops, right_ops, dims_left, dims_right, right_owner, right_slot, term_active
):
    left_count, block_count, tile, width = psi.shape
    pair_count = right_ops.shape[0] // 2
    flops = 2 * psi.size * tile
    smem = pl.BlockSpec(memory_space=pltpu.SMEM)
    vmem = pl.BlockSpec(memory_space=pltpu.VMEM)
    params = pltpu.CompilerParams(vmem_limit_bytes=VMEM_LIMIT)

    pairs = pl.pallas_call(
        pack_kernel,
        out_shape=jax.ShapeDtypeStruct((pair_count, tile, 2 * tile), jnp.bfloat16),
        in_specs=[smem, vmem],
        out_specs=vmem,
        compiler_params=params,
        cost_estimate=pl.CostEstimate(flops=0, bytes_accessed=6 * right_ops.size, transcendentals=0),
    )(dims_right, right_ops)
    pieces, order = gather_pieces(pairs)
    code = order(right_owner) * pair_count + right_slot % pair_count
    code = code * 2 + right_slot // pair_count

    half = pl.pallas_call(
        left_kernel,
        out_shape=jax.ShapeDtypeStruct(psi.shape, jnp.bfloat16),
        in_specs=[smem, smem, vmem, vmem],
        out_specs=vmem,
        compiler_params=params,
        cost_estimate=pl.CostEstimate(flops=flops, bytes_accessed=4 * psi.size, transcendentals=0),
    )(dims_left, term_active.reshape(left_count, block_count), left_ops, psi)
    sigma = pl.pallas_call(
        right_kernel,
        out_shape=jax.ShapeDtypeStruct(psi.shape, jnp.bfloat16),
        in_specs=[smem, vmem] + [pl.BlockSpec(memory_space=pl.ANY)] * len(pieces),
        out_specs=vmem,
        scratch_shapes=[
            pltpu.VMEM((lax.axis_size("sec") * pair_count, tile, 2 * tile), jnp.bfloat16),
            pltpu.SemaphoreType.DMA((len(pieces),)),
        ],
        compiler_params=params,
        cost_estimate=pl.CostEstimate(flops=flops, bytes_accessed=8 * psi.size, transcendentals=0),
    )(code, half, *pieces)
    if lax.axis_size("op") > 1:
        sigma = lax.psum_scatter(sigma, "op", scatter_dimension=3, tiled=True)
    return sigma


def solution(mesh):
    placed = (
        P(("grp", "sec"), None, None, None),
        P(("grp", "sec"), None, "op"),
        P(("grp", "sec"), None, "op"),
        P(("grp", "sec")),
        P(("grp", "sec")),
        P(("grp", "sec"), None),
        P(("grp", "sec"), None),
        P(("grp", "sec"), None, "op"),
    )
    return jax.shard_map(
        per_device,
        mesh=mesh,
        in_specs=placed,
        out_specs=P(("grp", "sec"), None, None, "op"),
        check_vma=False,
    )
```

```python
import jax
import jax.numpy as jnp
from jax import lax
from jax.experimental import pallas as pl
from jax.experimental.pallas import tpu as pltpu
from jax.sharding import PartitionSpec as P

VMEM_LIMIT = 48 * 1024 * 1024
RING_MOST = 32


def pack_kernel(dims_hbm, right_hbm, pairs_ref, dims_ref, right_ref, sems):
    count, tile, width = pairs_ref.shape
    load_right = pltpu.make_async_copy(right_hbm, right_ref, sems.at[0])
    load_dims = pltpu.make_async_copy(dims_hbm, dims_ref, sems.at[1])
    load_right.start()
    load_dims.start()
    rows = lax.broadcasted_iota(jnp.int32, (tile, tile), 0)
    cols = lax.broadcasted_iota(jnp.int32, (tile, tile), 1)
    most = jnp.maximum(rows, cols)
    load_dims.wait()
    load_right.wait()

    def kept(b):
        return jnp.where(most < dims_ref[b], right_ref[b].astype(jnp.float32), 0.0)

    for p in range(count):
        both = jnp.concatenate([kept(p), kept(p + count)], axis=1)
        pairs_ref[p] = both.astype(jnp.bfloat16)


def left_kernel(dims_ref, active_ref, code_ref, left_ref, psi_ref, half_ref):
    sectors, blocks, tile, width = psi_ref.shape
    rows = lax.broadcasted_iota(jnp.int32, (tile, tile), 0)
    cols = lax.broadcasted_iota(jnp.int32, (tile, tile), 1)
    most = jnp.maximum(rows, cols)
    upper = (lax.broadcasted_iota(jnp.int32, (tile, width), 1) >= tile).astype(jnp.int32)

    def one(a, carry):
        op = jnp.where(most < dims_ref[a], left_ref[a].astype(jnp.float32), 0.0).astype(jnp.bfloat16)
        for k in range(blocks):
            part = jnp.dot(op, psi_ref[a, k], preferred_element_type=jnp.float32)
            part = part * active_ref[a, k].astype(jnp.float32)
            other = pltpu.roll(part, tile, 1)
            second = code_ref[a, k] & 1
            here = upper == second
            first = jnp.where(upper == 0, part, other)
            last = jnp.where(upper == 0, other, part)
            half_ref[a, k, :, :width] = jnp.where(here, first, 0.0).astype(jnp.bfloat16)
            half_ref[a, k, :, width:] = jnp.where(here, last, 0.0).astype(jnp.bfloat16)
        return carry

    lax.fori_loop(0, sectors, one, 0)


def right_kernel(code_ref, half_ref, *refs):
    piece_refs, (out_hbm, pairs_ref, out_ref, sems) = refs[:-4], refs[-4:]
    sectors, blocks, tile, width = out_ref.shape
    step = pairs_ref.shape[0] // len(piece_refs)
    for i, piece in enumerate(piece_refs):
        pairs_ref[i * step:(i + 1) * step] = piece[...]
    zero = jnp.zeros((tile, width), jnp.bfloat16)

    def store(a):
        return pltpu.make_async_copy(out_ref.at[a], out_hbm.at[a], sems.at[a])

    def one(a, carry):
        for k in range(blocks):
            pair = pairs_ref[code_ref[a, k] >> 1]
            top = jnp.concatenate([pair, zero], axis=1)
            low = jnp.concatenate([zero, pair], axis=1)
            diag = jnp.concatenate([top, low], axis=0)
            part = lax.dot_general(
                half_ref[a, k], diag, (((1,), (1,)), ((), ())), preferred_element_type=jnp.float32
            )
            out_ref[a, k] = part.astype(jnp.bfloat16)
        store(a).start()
        return carry

    lax.fori_loop(0, sectors, one, 0)
    for a in range(sectors):
        store(a).wait()


def gather_pieces(pairs):
    count = lax.axis_size("sec")
    if count % 4 or count > RING_MOST:
        return [lax.all_gather(pairs, "sec", axis=0, tiled=True)], lambda owner: owner
    lines, chips = count // 4, count // 2
    ring = [4 * z for z in range(lines)] + [4 * z + 2 for z in reversed(range(lines))]
    onward = [(ring[p], ring[(p + 1) % chips]) for p in range(chips)]
    onward += [(ring[p] + 1, ring[p - 1] + 1) for p in range(chips)]
    across = [(i, i ^ 1) for i in range(count)]

    def swap(piece):
        return lax.ppermute(piece, "sec", across)

    def send(piece):
        return lax.ppermute(piece, "sec", onward)

    mid = chips // 2
    own, partner = [pairs], [swap(pairs)]
    for hop in range(1, mid):
        own.append(send(own[-1]))
        partner.append(send(partner[-1]))
    own.append(send(own[-1]))
    pieces = []
    for hop in range(mid):
        pieces += [own[hop], partner[hop]]
    pieces += [own[mid], swap(own[mid])]
    for hop in reversed(range(1, mid)):
        pieces += [swap(partner[hop]), swap(own[hop])]

    def place(index):
        line, cross = index // 4, (index // 2) % 2
        return jnp.where(cross == 0, line, chips - 1 - line), index % 2

    def order(owner):
        me_at, me_core = place(lax.axis_index("sec"))
        at, core = place(owner)
        behind = jnp.where(me_core == 0, me_at - at, at - me_at)
        return ((behind + chips) % chips) * 2 + (core ^ me_core)

    return pieces, order


def per_device(
    psi, left_ops, right_ops, dims_left, dims_right, right_owner, right_slot, term_active
):
    left_count, block_count, tile, width = psi.shape
    pair_count = right_ops.shape[0] // 2
    flops = 2 * psi.size * tile
    smem = pl.BlockSpec(memory_space=pltpu.SMEM)
    vmem = pl.BlockSpec(memory_space=pltpu.VMEM)
    hbm = pl.BlockSpec(memory_space=pltpu.HBM)
    params = pltpu.CompilerParams(vmem_limit_bytes=VMEM_LIMIT)

    pairs = pl.pallas_call(
        pack_kernel,
        out_shape=jax.ShapeDtypeStruct((pair_count, tile, 2 * tile), jnp.bfloat16),
        in_specs=[hbm, hbm],
        out_specs=vmem,
        scratch_shapes=[
            pltpu.SMEM(dims_right.shape, jnp.int32),
            pltpu.VMEM(right_ops.shape, jnp.bfloat16),
            pltpu.SemaphoreType.DMA((2,)),
        ],
        compiler_params=params,
        cost_estimate=pl.CostEstimate(flops=0, bytes_accessed=6 * right_ops.size, transcendentals=0),
    )(dims_right, right_ops)
    pieces, order = gather_pieces(pairs)
    code = order(right_owner) * pair_count + right_slot % pair_count
    code = code * 2 + right_slot // pair_count

    half = pl.pallas_call(
        left_kernel,
        out_shape=jax.ShapeDtypeStruct((left_count, block_count, tile, 2 * width), jnp.bfloat16),
        in_specs=[smem, smem, smem, vmem, vmem],
        out_specs=vmem,
        compiler_params=params,
        cost_estimate=pl.CostEstimate(flops=flops, bytes_accessed=6 * psi.size, transcendentals=0),
    )(dims_left, term_active.reshape(left_count, block_count), code, left_ops, psi)
    sigma = pl.pallas_call(
        right_kernel,
        out_shape=jax.ShapeDtypeStruct(psi.shape, jnp.bfloat16),
        in_specs=[smem] + [vmem] * (1 + len(pieces)),
        out_specs=hbm,
        scratch_shapes=[
            pltpu.VMEM((lax.axis_size("sec") * pair_count, tile, 2 * tile), jnp.bfloat16),
            pltpu.VMEM(psi.shape, jnp.bfloat16),
            pltpu.SemaphoreType.DMA((left_count,)),
        ],
        compiler_params=params,
        cost_estimate=pl.CostEstimate(flops=flops, bytes_accessed=8 * psi.size, transcendentals=0),
    )(code, half, *pieces)
    if lax.axis_size("op") > 1:
        sigma = lax.psum_scatter(sigma, "op", scatter_dimension=3, tiled=True)
    return sigma


def solution(mesh):
    placed = (
        P(("grp", "sec"), None, None, None),
        P(("grp", "sec"), None, "op"),
        P(("grp", "sec"), None, "op"),
        P(("grp", "sec")),
        P(("grp", "sec")),
        P(("grp", "sec"), None),
        P(("grp", "sec"), None),
        P(("grp", "sec"), None, "op"),
    )
    return jax.shard_map(
        per_device,
        mesh=mesh,
        in_specs=placed,
        out_specs=P(("grp", "sec"), None, None, "op"),
        check_vma=False,
    )
```

```python
import jax
import jax.numpy as jnp
from jax import lax
from jax.experimental import pallas as pl
from jax.experimental.pallas import tpu as pltpu
from jax.sharding import PartitionSpec as P

VMEM_LIMIT = 48 * 1024 * 1024
GROUP = 4


def pack_kernel(dims_hbm, right_hbm, pairs_ref, dims_ref, right_ref, sems):
    count, tile, width = pairs_ref.shape
    load_right = pltpu.make_async_copy(right_hbm, right_ref, sems.at[0])
    load_dims = pltpu.make_async_copy(dims_hbm, dims_ref, sems.at[1])
    load_right.start()
    load_dims.start()
    rows = lax.broadcasted_iota(jnp.int32, (tile, tile), 0)
    cols = lax.broadcasted_iota(jnp.int32, (tile, tile), 1)
    most = jnp.maximum(rows, cols)
    load_dims.wait()
    load_right.wait()

    def kept(b):
        return jnp.where(most < dims_ref[b], right_ref[b].astype(jnp.float32), 0.0)

    for p in range(count):
        both = jnp.concatenate([kept(p), kept(p + count)], axis=1)
        pairs_ref[p] = both.astype(jnp.bfloat16)


def left_kernel(dims_ref, active_ref, code_ref, left_ref, psi_ref, half_ref):
    sectors, blocks, tile, width = psi_ref.shape
    rows = lax.broadcasted_iota(jnp.int32, (tile, tile), 0)
    cols = lax.broadcasted_iota(jnp.int32, (tile, tile), 1)
    most = jnp.maximum(rows, cols)
    upper = (lax.broadcasted_iota(jnp.int32, (tile, width), 1) >= tile).astype(jnp.int32)

    def one(a, carry):
        op = jnp.where(most < dims_ref[a], left_ref[a].astype(jnp.float32), 0.0).astype(jnp.bfloat16)
        for k in range(blocks):
            part = jnp.dot(op, psi_ref[a, k], preferred_element_type=jnp.float32)
            part = part * active_ref[a, k].astype(jnp.float32)
            other = pltpu.roll(part, tile, 1)
            second = code_ref[a * blocks + k] & 1
            here = upper == second
            first = jnp.where(upper == 0, part, other)
            last = jnp.where(upper == 0, other, part)
            half_ref[a, k, :, :width] = jnp.where(here, first, 0.0).astype(jnp.bfloat16)
            half_ref[a, k, :, width:] = jnp.where(here, last, 0.0).astype(jnp.bfloat16)
        return carry

    lax.fori_loop(0, sectors, one, 0, unroll=2)


def times_operator(half, pair):
    zero = jnp.zeros_like(pair)
    top = jnp.concatenate([pair, zero], axis=1)
    low = jnp.concatenate([zero, pair], axis=1)
    both = jnp.concatenate([top, low], axis=0)
    part = lax.dot_general(half, both, (((1,), (1,)), ((), ())), preferred_element_type=jnp.float32)
    return part.astype(jnp.bfloat16)


def merge(piece_refs, pairs_ref):
    step = pairs_ref.shape[0] // len(piece_refs)
    for i, piece in enumerate(piece_refs):
        pairs_ref[i * step:(i + 1) * step] = piece[...]


def early_kernel(code_ref, half_ref, *refs):
    piece_refs, (out_hbm, late_ref, pairs_ref, out_ref, sems) = refs[:-5], refs[-5:]
    sectors, blocks, tile, width = out_ref.shape
    count = pairs_ref.shape[0]
    merge(piece_refs, pairs_ref)

    def store(a):
        return pltpu.make_async_copy(out_ref.at[a], out_hbm.at[a], sems.at[a])

    def one(a, listed):
        for k in range(blocks):
            item = a * blocks + k
            at = code_ref[item] >> 1
            late = at >= count
            pair = pairs_ref[jnp.where(late, 0, at)]
            out_ref[a, k] = times_operator(half_ref[a, k], pair)
            late_ref[listed] = item
            listed = listed + late.astype(jnp.int32)
        store(a).start()
        return listed

    listed = lax.fori_loop(0, sectors, one, 0)
    late_ref[sectors * blocks] = listed
    for a in range(sectors):
        store(a).wait()


def late_kernel(code_ref, late_ref, early_hbm, half_ref, *refs):
    piece_refs, (out_hbm, pairs_ref, out_ref, sems) = refs[:-4], refs[-4:]
    sectors, blocks, tile, width = half_ref.shape
    items = sectors * blocks
    skipped = early_count(len(piece_refs)) * (pairs_ref.shape[0] // len(piece_refs))
    listed = late_ref[items]
    merge(piece_refs, pairs_ref)

    def store(slot, item):
        return pltpu.make_async_copy(out_ref.at[slot], out_hbm.at[item // blocks, item % blocks], sems.at[slot])

    def group(g, carry):
        for u in range(GROUP):
            slot = g * GROUP + u
            item = late_ref[jnp.minimum(slot, listed - 1)]
            pair = pairs_ref[(code_ref[item] >> 1) - skipped]
            out_ref[slot] = times_operator(half_ref[item // blocks, item % blocks], pair)
        for u in range(GROUP):
            slot = g * GROUP + u

            @pl.when(slot < listed)
            def _():
                store(slot, late_ref[slot]).start()
        return carry

    def drain(slot, carry):
        store(slot, 0).wait()
        return carry

    lax.fori_loop(0, (listed + GROUP - 1) // GROUP, group, 0)
    lax.fori_loop(0, listed, drain, 0)


def early_count(late_count):
    return 3 * late_count


def swap(piece, bit):
    count = lax.axis_size("sec")
    return lax.ppermute(piece, "sec", [(i, i ^ bit) for i in range(count)])


def exchange(pairs, half_of):
    pieces = {0: pairs}
    half = None
    bit = lax.axis_size("sec") // 2
    while bit:
        if half is None and len(pieces) > 1:
            top = max(pieces)
            pieces[top], half = lax.optimization_barrier((pieces[top], half_of()))
        for r in list(pieces):
            if bit > 1 or r < max(pieces):
                pieces[r | bit] = swap(pieces[r], bit)
        bit //= 2
    return pieces, half


def per_device(
    psi, left_ops, right_ops, dims_left, dims_right, right_owner, right_slot, term_active
):
    left_count, block_count, tile, width = psi.shape
    items = left_count * block_count
    pair_count = right_ops.shape[0] // 2
    count = lax.axis_size("sec")
    flops = 2 * psi.size * tile
    smem = pl.BlockSpec(memory_space=pltpu.SMEM)
    vmem = pl.BlockSpec(memory_space=pltpu.VMEM)
    hbm = pl.BlockSpec(memory_space=pltpu.HBM)
    params = pltpu.CompilerParams(vmem_limit_bytes=VMEM_LIMIT)

    pairs = pl.pallas_call(
        pack_kernel,
        out_shape=jax.ShapeDtypeStruct((pair_count, tile, 2 * tile), jnp.bfloat16),
        in_specs=[hbm, hbm],
        out_specs=vmem,
        scratch_shapes=[
            pltpu.SMEM(dims_right.shape, jnp.int32),
            pltpu.VMEM(right_ops.shape, jnp.bfloat16),
            pltpu.SemaphoreType.DMA((2,)),
        ],
        compiler_params=params,
        cost_estimate=pl.CostEstimate(flops=0, bytes_accessed=6 * right_ops.size, transcendentals=0),
    )(dims_right, right_ops)

    by_swaps = count in (8, 16, 32)
    if by_swaps:
        last = count - 4
        order = [r for r in range(count) if r < last and r != last - 1] + [last]
        order += [r for r in range(count) if r not in order]
        where = [order.index(r) for r in range(count)]
        place = lax.axis_index("sec") ^ right_owner
        at = jnp.zeros_like(place)
        for r in range(count):
            at = at + jnp.where(place == r, where[r], 0)
    else:
        at = right_owner
    code = at * pair_count + right_slot % pair_count
    code = (code * 2 + right_slot // pair_count).reshape(items)

    def half_of():
        return pl.pallas_call(
            left_kernel,
            out_shape=jax.ShapeDtypeStruct((left_count, block_count, tile, 2 * width), jnp.bfloat16),
            in_specs=[smem, smem, smem, vmem, vmem],
            out_specs=vmem,
            compiler_params=params,
            cost_estimate=pl.CostEstimate(flops=flops, bytes_accessed=6 * psi.size, transcendentals=0),
        )(dims_left, term_active.reshape(left_count, block_count), code, left_ops, psi)

    if by_swaps:
        pieces, half = exchange(pairs, half_of)
        split = early_count(count // 4)
        early = [pieces[r] for r in order[:split]]
    else:
        half = half_of()
        early = [lax.all_gather(pairs, "sec", axis=0, tiled=True)]

    sigma, listed = pl.pallas_call(
        early_kernel,
        out_shape=(
            jax.ShapeDtypeStruct(psi.shape, jnp.bfloat16),
            jax.ShapeDtypeStruct((items + 1,), jnp.int32),
        ),
        in_specs=[smem] + [vmem] * (1 + len(early)),
        out_specs=(hbm, smem),
        scratch_shapes=[
            pltpu.VMEM((sum(piece.shape[0] for piece in early), tile, 2 * tile), jnp.bfloat16),
            pltpu.VMEM(psi.shape, jnp.bfloat16),
            pltpu.SemaphoreType.DMA((left_count,)),
        ],
        compiler_params=params,
        cost_estimate=pl.CostEstimate(flops=flops, bytes_accessed=8 * psi.size, transcendentals=0),
    )(code, half, *early)
    if by_swaps:
        top = count - 2
        pieces[top], sigma = lax.optimization_barrier((pieces[top], sigma))
        pieces[top + 1] = swap(pieces[top], 1)
        late = [pieces[r] for r in order[split:]]
        sigma = pl.pallas_call(
            late_kernel,
            out_shape=jax.ShapeDtypeStruct(psi.shape, jnp.bfloat16),
            in_specs=[smem, smem, hbm] + [vmem] * (1 + len(late)),
            out_specs=hbm,
            scratch_shapes=[
                pltpu.VMEM((len(late) * pair_count, tile, 2 * tile), jnp.bfloat16),
                pltpu.VMEM((items + GROUP, tile, width), jnp.bfloat16),
                pltpu.SemaphoreType.DMA((items,)),
            ],
            input_output_aliases={2: 0},
            compiler_params=params,
            cost_estimate=pl.CostEstimate(flops=flops // 4, bytes_accessed=2 * psi.size, transcendentals=0),
        )(code, listed, sigma, half, *late)
    if lax.axis_size("op") > 1:
        sigma = lax.psum_scatter(sigma, "op", scatter_dimension=3, tiled=True)
    return sigma


def solution(mesh):
    placed = (
        P(("grp", "sec"), None, None, None),
        P(("grp", "sec"), None, "op"),
        P(("grp", "sec"), None, "op"),
        P(("grp", "sec")),
        P(("grp", "sec")),
        P(("grp", "sec"), None),
        P(("grp", "sec"), None),
        P(("grp", "sec"), None, "op"),
    )
    return jax.shard_map(
        per_device,
        mesh=mesh,
        in_specs=placed,
        out_specs=P(("grp", "sec"), None, None, "op"),
        check_vma=False,
    )
```

```python
import functools

import jax
import jax.numpy as jnp
from jax import lax
from jax.experimental import pallas as pl
from jax.experimental.pallas import tpu as pltpu
from jax.sharding import PartitionSpec as P

VMEM_LIMIT = 48 * 1024 * 1024
GROUP = 4
FAR, NEAR, CROSS, CORE = 8, 4, 2, 1
EARLY = (0, CORE, NEAR, NEAR | CORE, CROSS, CROSS | CORE, FAR, NEAR | CROSS, NEAR | CROSS | CORE, FAR | NEAR)
LATE = tuple(r for r in range(16) if r not in EARLY)
ORDER = EARLY + LATE


def load_all(*copies):
    copies = [pltpu.make_async_copy(*copy) for copy in copies]
    for copy in copies:
        copy.start()
    return copies


def pack_kernel(dims_hbm, right_hbm, pairs_ref, dims_ref, right_ref, sems):
    count, tile, width = pairs_ref.shape
    copies = load_all((dims_hbm, dims_ref, sems.at[0]), (right_hbm, right_ref, sems.at[1]))
    rows = lax.broadcasted_iota(jnp.int32, (tile, tile), 0)
    cols = lax.broadcasted_iota(jnp.int32, (tile, tile), 1)
    most = jnp.maximum(rows, cols)
    for copy in copies:
        copy.wait()

    def kept(b):
        return jnp.where(most < dims_ref[b], right_ref[b].astype(jnp.float32), 0.0)

    for p in range(count):
        both = jnp.concatenate([kept(p), kept(p + count)], axis=1)
        pairs_ref[p] = both.astype(jnp.bfloat16)


def left_kernel(
    pair_count, dims_hbm, active_hbm, slot_hbm, left_hbm, psi_hbm,
    half_ref, dims_ref, active_ref, slot_ref, left_ref, psi_ref, sems, psi_sems,
):
    sectors, blocks, tile, width = psi_ref.shape
    copies = load_all(
        (dims_hbm, dims_ref, sems.at[0]),
        (active_hbm, active_ref, sems.at[1]),
        (slot_hbm, slot_ref, sems.at[2]),
        (left_hbm, left_ref, sems.at[3]),
    )
    psi_copies = load_all(*[(psi_hbm.at[a], psi_ref.at[a], psi_sems.at[a]) for a in range(sectors)])
    rows = lax.broadcasted_iota(jnp.int32, (tile, tile), 0)
    cols = lax.broadcasted_iota(jnp.int32, (tile, tile), 1)
    most = jnp.maximum(rows, cols)
    upper = (lax.broadcasted_iota(jnp.int32, (tile, width), 1) >= tile).astype(jnp.int32)
    for copy in copies:
        copy.wait()
    for a in range(sectors):
        psi_copies[a].wait()
        op = jnp.where(most < dims_ref[a], left_ref[a].astype(jnp.float32), 0.0).astype(jnp.bfloat16)
        for k in range(blocks):
            part = jnp.dot(op, psi_ref[a, k], preferred_element_type=jnp.float32)
            part = part * active_ref[a, k].astype(jnp.float32)
            other = pltpu.roll(part, tile, 1)
            here = upper == (slot_ref[a, k] >= pair_count).astype(jnp.int32)
            first = jnp.where(upper == 0, part, other)
            last = jnp.where(upper == 0, other, part)
            half_ref[a, k, :, :width] = jnp.where(here, first, 0.0).astype(jnp.bfloat16)
            half_ref[a, k, :, width:] = jnp.where(here, last, 0.0).astype(jnp.bfloat16)


def times_operator(half, pair):
    zero = jnp.zeros_like(pair)
    top = jnp.concatenate([pair, zero], axis=1)
    low = jnp.concatenate([zero, pair], axis=1)
    both = jnp.concatenate([top, low], axis=0)
    part = lax.dot_general(half, both, (((1,), (1,)), ((), ())), preferred_element_type=jnp.float32)
    return part.astype(jnp.bfloat16)


def merge(piece_refs, pairs_ref):
    at = 0
    for piece in piece_refs:
        pairs_ref[at:at + piece.shape[0]] = piece[...]
        at += piece.shape[0]


def piece_at(r):
    low = sum(ORDER.index(i) << (4 * i) for i in range(7))
    high = sum(ORDER.index(i + 8) << (4 * i) for i in range(7))
    packed = jnp.where(r < 8, low, high) >> (4 * (r & 7))
    end = jnp.where(r < 8, ORDER.index(7), ORDER.index(15))
    return jnp.where(r & 7 == 7, end, packed & 15)


def early_kernel(pair_count, owner_hbm, slot_hbm, half_ref, *refs):
    piece_refs = refs[:-7]
    out_hbm, late_ref, pairs_ref, out_ref, owner_ref, slot_ref, sems = refs[-7:]
    sectors, blocks, tile, width = out_ref.shape
    items, held = sectors * blocks, pairs_ref.shape[0]
    copies = load_all((owner_hbm, owner_ref, sems.at[0]), (slot_hbm, slot_ref, sems.at[1]))
    merge(piece_refs, pairs_ref)
    me = lax.axis_index("sec")
    for copy in copies:
        copy.wait()

    def store(a):
        return pltpu.make_async_copy(out_ref.at[a], out_hbm.at[a], sems.at[a])

    def one(a, listed):
        for k in range(blocks):
            owner, slot = owner_ref[a, k], slot_ref[a, k]
            at = piece_at(owner ^ me) if len(piece_refs) > 1 else owner
            at = at * pair_count + jnp.where(slot >= pair_count, slot - pair_count, slot)
            late = at >= held
            pair = pairs_ref[jnp.where(late, 0, at)]
            out_ref[a, k] = times_operator(half_ref[a, k], pair)
            late_ref[listed] = (at - held) * items + a * blocks + k
            listed = listed + late.astype(jnp.int32)
        store(a).start()
        return listed

    listed = lax.fori_loop(0, sectors, one, 0, unroll=2)
    late_ref[items] = listed
    for a in range(sectors):
        store(a).wait()


def late_kernel(late_ref, early_hbm, half_ref, *refs):
    piece_refs, (out_hbm, pairs_ref, out_ref, sems) = refs[:-4], refs[-4:]
    sectors, blocks, tile, width = half_ref.shape
    items = sectors * blocks
    listed = late_ref[items]
    merge(piece_refs, pairs_ref)

    def store(slot, item):
        return pltpu.make_async_copy(out_ref.at[slot], out_hbm.at[item // blocks, item % blocks], sems.at[slot])

    def group(g, carry):
        for u in range(GROUP):
            slot = g * GROUP + u
            entry = late_ref[jnp.minimum(slot, listed - 1)]
            item = entry % items
            out_ref[slot] = times_operator(half_ref[item // blocks, item % blocks], pairs_ref[entry // items])
        for u in range(GROUP):
            slot = g * GROUP + u

            @pl.when(slot < listed)
            def _():
                store(slot, late_ref[slot] % items).start()
        return carry

    def drain(slot, carry):
        store(slot, 0).wait()
        return carry

    lax.fori_loop(0, (listed + GROUP - 1) // GROUP, group, 0)
    lax.fori_loop(0, listed, drain, 0)


def swap(piece, bit):
    count = lax.axis_size("sec")
    return lax.ppermute(piece, "sec", [(i, i ^ bit) for i in range(count)])


def per_device(
    psi, left_ops, right_ops, dims_left, dims_right, right_owner, right_slot, term_active
):
    left_count, block_count, tile, width = psi.shape
    items = left_count * block_count
    pair_count = right_ops.shape[0] // 2
    count = lax.axis_size("sec")
    by_swaps = count == len(ORDER)
    flops = 2 * psi.size * tile
    smem = pl.BlockSpec(memory_space=pltpu.SMEM)
    vmem = pl.BlockSpec(memory_space=pltpu.VMEM)
    hbm = pl.BlockSpec(memory_space=pltpu.HBM)
    params = pltpu.CompilerParams(vmem_limit_bytes=VMEM_LIMIT)

    def in_hbm(*arrays):
        return [pltpu.with_memory_space_constraint(array, pltpu.HBM) for array in arrays]

    pairs = pl.pallas_call(
        pack_kernel,
        out_shape=jax.ShapeDtypeStruct((pair_count, tile, 2 * tile), jnp.bfloat16),
        in_specs=[hbm, hbm],
        out_specs=vmem,
        scratch_shapes=[
            pltpu.SMEM(dims_right.shape, jnp.int32),
            pltpu.VMEM(right_ops.shape, jnp.bfloat16),
            pltpu.SemaphoreType.DMA((2,)),
        ],
        compiler_params=params,
        cost_estimate=pl.CostEstimate(flops=0, bytes_accessed=2 * right_ops.size, transcendentals=0),
    )(*in_hbm(dims_right, right_ops))

    def half_of(dims_left):
        active = term_active.reshape(left_count, block_count)
        return pl.pallas_call(
            functools.partial(left_kernel, pair_count),
            out_shape=jax.ShapeDtypeStruct((left_count, block_count, tile, 2 * width), jnp.bfloat16),
            in_specs=[hbm] * 5,
            out_specs=vmem,
            scratch_shapes=[
                pltpu.SMEM(dims_left.shape, jnp.int32),
                pltpu.SMEM(active.shape, jnp.int32),
                pltpu.SMEM(right_slot.shape, jnp.int32),
                pltpu.VMEM(left_ops.shape, jnp.bfloat16),
                pltpu.VMEM(psi.shape, jnp.bfloat16),
                pltpu.SemaphoreType.DMA((4,)),
                pltpu.SemaphoreType.DMA((left_count,)),
            ],
            compiler_params=params,
            cost_estimate=pl.CostEstimate(flops=flops, bytes_accessed=2 * psi.size, transcendentals=0),
        )(*in_hbm(dims_left, active, right_slot, left_ops, psi))

    if by_swaps:
        pieces = {0: pairs}
        def pass_on(*pairs_of):
            for r, bit in pairs_of:
                pieces[r | bit] = swap(pieces[r], bit)

        pass_on((0, FAR), (0, NEAR))
        half, pieces[0] = lax.optimization_barrier((half_of(dims_left), pairs))
        pass_on((0, CROSS), (0, CORE), (NEAR, CORE), (CROSS, CORE), (NEAR, CROSS))
        pass_on((FAR, NEAR), (FAR, CROSS), (FAR | NEAR, CROSS), (NEAR | CROSS, CORE), (FAR | NEAR, CORE))
        early = [pieces[r] for r in EARLY]
    else:
        half = half_of(dims_left)
        early = [lax.all_gather(pairs, "sec", axis=0, tiled=True)]

    sigma, listed = pl.pallas_call(
        functools.partial(early_kernel, pair_count),
        out_shape=(
            jax.ShapeDtypeStruct(psi.shape, jnp.bfloat16),
            jax.ShapeDtypeStruct((items + 1,), jnp.int32),
        ),
        in_specs=[hbm, hbm] + [vmem] * (1 + len(early)),
        out_specs=(hbm, smem),
        scratch_shapes=[
            pltpu.VMEM((sum(piece.shape[0] for piece in early), tile, 2 * tile), jnp.bfloat16),
            pltpu.VMEM(psi.shape, jnp.bfloat16),
            pltpu.SMEM(right_owner.shape, jnp.int32),
            pltpu.SMEM(right_slot.shape, jnp.int32),
            pltpu.SemaphoreType.DMA((max(left_count, 2),)),
        ],
        compiler_params=params,
        cost_estimate=pl.CostEstimate(flops=flops, bytes_accessed=2 * psi.size, transcendentals=0),
    )(*in_hbm(right_owner, right_slot), half, *early)
    if by_swaps:
        ends = (FAR, FAR | CROSS, FAR | NEAR | CROSS)
        held, sigma = lax.optimization_barrier(([pieces[r] for r in ends], sigma))
        for r, piece in zip(ends, held):
            pieces[r], pieces[r | CORE] = piece, swap(piece, CORE)
        late = [pieces[r] for r in LATE]
        sigma = pl.pallas_call(
            late_kernel,
            out_shape=jax.ShapeDtypeStruct(psi.shape, jnp.bfloat16),
            in_specs=[smem, hbm] + [vmem] * (1 + len(late)),
            out_specs=hbm,
            scratch_shapes=[
                pltpu.VMEM((len(late) * pair_count, tile, 2 * tile), jnp.bfloat16),
                pltpu.VMEM((items + GROUP, tile, width), jnp.bfloat16),
                pltpu.SemaphoreType.DMA((items,)),
            ],
            input_output_aliases={1: 0},
            compiler_params=params,
            cost_estimate=pl.CostEstimate(flops=flops // 4, bytes_accessed=psi.size, transcendentals=0),
        )(listed, sigma, half, *late)
    if lax.axis_size("op") > 1:
        sigma = lax.psum_scatter(sigma, "op", scatter_dimension=3, tiled=True)
    return sigma


def solution(mesh):
    placed = (
        P(("grp", "sec"), None, None, None),
        P(("grp", "sec"), None, "op"),
        P(("grp", "sec"), None, "op"),
        P(("grp", "sec")),
        P(("grp", "sec")),
        P(("grp", "sec"), None),
        P(("grp", "sec"), None),
        P(("grp", "sec"), None, "op"),
    )
    return jax.shard_map(
        per_device,
        mesh=mesh,
        in_specs=placed,
        out_specs=P(("grp", "sec"), None, None, "op"),
        check_vma=False,
    )
```

```python
import functools

import jax
import jax.numpy as jnp
from jax import lax
from jax.experimental import pallas as pl
from jax.experimental.pallas import tpu as pltpu
from jax.sharding import PartitionSpec as P

VMEM_LIMIT = 48 * 1024 * 1024
GROUP = 4
FAR, NEAR, CROSS, CORE = 8, 4, 2, 1
EARLY = (0, CORE, NEAR, NEAR | CORE, CROSS, CROSS | CORE, FAR, NEAR | CROSS, NEAR | CROSS | CORE, FAR | NEAR)
LATE = tuple(r for r in range(16) if r not in EARLY)
ORDER = EARLY + LATE


def load_all(*copies):
    copies = [pltpu.make_async_copy(*copy) for copy in copies]
    for copy in copies:
        copy.start()
    return copies


def pack_kernel(dims_hbm, right_hbm, pairs_ref, dims_ref, right_ref, sems):
    count, tile, width = pairs_ref.shape
    copies = load_all((dims_hbm, dims_ref, sems.at[0]), (right_hbm, right_ref, sems.at[1]))
    rows = lax.broadcasted_iota(jnp.int32, (tile, tile), 0)
    cols = lax.broadcasted_iota(jnp.int32, (tile, tile), 1)
    most = jnp.maximum(rows, cols)
    for copy in copies:
        copy.wait()

    def kept(b):
        return jnp.where(most < dims_ref[b], right_ref[b].astype(jnp.float32), 0.0)

    for p in range(count):
        both = jnp.concatenate([kept(p), kept(p + count)], axis=1)
        pairs_ref[p] = both.astype(jnp.bfloat16)


def left_kernel(
    pair_count, dims_hbm, active_hbm, slot_hbm, left_hbm, psi_hbm,
    half_ref, dims_ref, active_ref, slot_ref, left_ref, psi_ref, sems, psi_sems,
):
    sectors, blocks, tile, width = psi_ref.shape
    copies = load_all(
        (dims_hbm, dims_ref, sems.at[0]),
        (active_hbm, active_ref, sems.at[1]),
        (slot_hbm, slot_ref, sems.at[2]),
        (left_hbm, left_ref, sems.at[3]),
    )
    psi_copies = load_all(*[(psi_hbm.at[a], psi_ref.at[a], psi_sems.at[a]) for a in range(sectors)])
    rows = lax.broadcasted_iota(jnp.int32, (tile, tile), 0)
    cols = lax.broadcasted_iota(jnp.int32, (tile, tile), 1)
    most = jnp.maximum(rows, cols)
    upper = (lax.broadcasted_iota(jnp.int32, (tile, width), 1) >= tile).astype(jnp.int32)
    for copy in copies:
        copy.wait()
    for a in range(sectors):
        psi_copies[a].wait()
        op = jnp.where(most < dims_ref[a], left_ref[a].astype(jnp.float32), 0.0).astype(jnp.bfloat16)
        for k in range(blocks):
            part = jnp.dot(op, psi_ref[a, k], preferred_element_type=jnp.float32)
            part = part * active_ref[a, k].astype(jnp.float32)
            other = pltpu.roll(part, tile, 1)
            here = upper == (slot_ref[a, k] >= pair_count).astype(jnp.int32)
            first = jnp.where(upper == 0, part, other)
            last = jnp.where(upper == 0, other, part)
            half_ref[a, k, :, :width] = jnp.where(here, first, 0.0).astype(jnp.bfloat16)
            half_ref[a, k, :, width:] = jnp.where(here, last, 0.0).astype(jnp.bfloat16)


def times_operator(half, pair):
    zero = jnp.zeros_like(pair)
    top = jnp.concatenate([pair, zero], axis=1)
    low = jnp.concatenate([zero, pair], axis=1)
    both = jnp.concatenate([top, low], axis=0)
    part = lax.dot_general(half, both, (((1,), (1,)), ((), ())), preferred_element_type=jnp.float32)
    return part.astype(jnp.bfloat16)


def merge(piece_refs, pairs_ref):
    at = 0
    for piece in piece_refs:
        pairs_ref[at:at + piece.shape[0]] = piece[...]
        at += piece.shape[0]


def piece_at(r):
    low = sum(ORDER.index(i) << (4 * i) for i in range(7))
    high = sum(ORDER.index(i + 8) << (4 * i) for i in range(7))
    packed = jnp.where(r < 8, low, high) >> (4 * (r & 7))
    end = jnp.where(r < 8, ORDER.index(7), ORDER.index(15))
    return jnp.where(r & 7 == 7, end, packed & 15)


def early_kernel(pair_count, owner_hbm, slot_hbm, half_ref, *refs):
    piece_refs = refs[:-7]
    out_hbm, late_ref, pairs_ref, out_ref, owner_ref, slot_ref, sems = refs[-7:]
    sectors, blocks, tile, width = out_ref.shape
    items, held = sectors * blocks, pairs_ref.shape[0]
    copies = load_all((owner_hbm, owner_ref, sems.at[0]), (slot_hbm, slot_ref, sems.at[1]))
    merge(piece_refs, pairs_ref)
    me = lax.axis_index("sec")
    for copy in copies:
        copy.wait()

    def store(a):
        return pltpu.make_async_copy(out_ref.at[a], out_hbm.at[a], sems.at[a])

    def one(a, listed):
        for k in range(blocks):
            owner, slot = owner_ref[a, k], slot_ref[a, k]
            at = piece_at(owner ^ me) if len(piece_refs) > 1 else owner
            at = at * pair_count + jnp.where(slot >= pair_count, slot - pair_count, slot)
            late = at >= held
            pair = pairs_ref[jnp.where(late, 0, at)]
            out_ref[a, k] = times_operator(half_ref[a, k], pair)
            late_ref[listed] = (at - held) * items + a * blocks + k
            listed = listed + late.astype(jnp.int32)
        store(a).start()
        return listed

    listed = lax.fori_loop(0, sectors, one, 0, unroll=2)
    late_ref[items] = listed
    for a in range(sectors):
        store(a).wait()


def late_kernel(late_ref, early_hbm, half_ref, *refs):
    piece_refs, (out_hbm, pairs_ref, out_ref, sems) = refs[:-4], refs[-4:]
    sectors, blocks, tile, width = half_ref.shape
    items = sectors * blocks
    listed = late_ref[items]
    merge(piece_refs, pairs_ref)

    def store(slot, item):
        return pltpu.make_async_copy(out_ref.at[slot], out_hbm.at[item // blocks, item % blocks], sems.at[slot])

    def group(g, carry):
        for u in range(GROUP):
            slot = g * GROUP + u
            entry = late_ref[jnp.minimum(slot, listed - 1)]
            item = entry % items
            out_ref[slot] = times_operator(half_ref[item // blocks, item % blocks], pairs_ref[entry // items])
        for u in range(GROUP):
            slot = g * GROUP + u

            @pl.when(slot < listed)
            def _():
                store(slot, late_ref[slot] % items).start()
        return carry

    def drain(slot, carry):
        store(slot, 0).wait()
        return carry

    lax.fori_loop(0, (listed + GROUP - 1) // GROUP, group, 0)
    lax.fori_loop(0, listed, drain, 0)


def swap(piece, bit):
    count = lax.axis_size("sec")
    return lax.ppermute(piece, "sec", [(i, i ^ bit) for i in range(count)])


def per_device(
    psi, left_ops, right_ops, dims_left, dims_right, right_owner, right_slot, term_active
):
    left_count, block_count, tile, width = psi.shape
    items = left_count * block_count
    pair_count = right_ops.shape[0] // 2
    count = lax.axis_size("sec")
    by_swaps = count == len(ORDER)
    flops = 2 * psi.size * tile
    smem = pl.BlockSpec(memory_space=pltpu.SMEM)
    vmem = pl.BlockSpec(memory_space=pltpu.VMEM)
    hbm = pl.BlockSpec(memory_space=pltpu.HBM)
    params = pltpu.CompilerParams(vmem_limit_bytes=VMEM_LIMIT)

    def in_hbm(*arrays):
        return [pltpu.with_memory_space_constraint(array, pltpu.HBM) for array in arrays]

    pairs = pl.pallas_call(
        pack_kernel,
        out_shape=jax.ShapeDtypeStruct((pair_count, tile, 2 * tile), jnp.bfloat16),
        in_specs=[hbm, hbm],
        out_specs=vmem,
        scratch_shapes=[
            pltpu.SMEM(dims_right.shape, jnp.int32),
            pltpu.VMEM(right_ops.shape, jnp.bfloat16),
            pltpu.SemaphoreType.DMA((2,)),
        ],
        compiler_params=params,
        cost_estimate=pl.CostEstimate(flops=0, bytes_accessed=2 * right_ops.size, transcendentals=0),
    )(*in_hbm(dims_right, right_ops))

    def half_of(dims_left):
        active = term_active.reshape(left_count, block_count)
        return pl.pallas_call(
            functools.partial(left_kernel, pair_count),
            out_shape=jax.ShapeDtypeStruct((left_count, block_count, tile, 2 * width), jnp.bfloat16),
            in_specs=[hbm] * 5,
            out_specs=vmem,
            scratch_shapes=[
                pltpu.SMEM(dims_left.shape, jnp.int32),
                pltpu.SMEM(active.shape, jnp.int32),
                pltpu.SMEM(right_slot.shape, jnp.int32),
                pltpu.VMEM(left_ops.shape, jnp.bfloat16),
                pltpu.VMEM(psi.shape, jnp.bfloat16),
                pltpu.SemaphoreType.DMA((4,)),
                pltpu.SemaphoreType.DMA((left_count,)),
            ],
            compiler_params=params,
            cost_estimate=pl.CostEstimate(flops=flops, bytes_accessed=2 * psi.size, transcendentals=0),
        )(*in_hbm(dims_left, active, right_slot, left_ops, psi))

    if by_swaps:
        pieces = {0: pairs}
        def pass_on(*pairs_of):
            for r, bit in pairs_of:
                pieces[r | bit] = swap(pieces[r], bit)

        pass_on((0, FAR), (0, NEAR), (0, CROSS))
        half, pieces[0] = lax.optimization_barrier((half_of(dims_left), pairs))
        pass_on((0, CORE), (NEAR, CORE), (CROSS, CORE), (NEAR, CROSS))
        pass_on((FAR, NEAR), (FAR, CROSS), (FAR | NEAR, CROSS), (NEAR | CROSS, CORE), (FAR | NEAR, CORE))
        early = [pieces[r] for r in EARLY]
    else:
        half = half_of(dims_left)
        early = [lax.all_gather(pairs, "sec", axis=0, tiled=True)]

    sigma, listed = pl.pallas_call(
        functools.partial(early_kernel, pair_count),
        out_shape=(
            jax.ShapeDtypeStruct(psi.shape, jnp.bfloat16),
            jax.ShapeDtypeStruct((items + 1,), jnp.int32),
        ),
        in_specs=[hbm, hbm] + [vmem] * (1 + len(early)),
        out_specs=(hbm, smem),
        scratch_shapes=[
            pltpu.VMEM((sum(piece.shape[0] for piece in early), tile, 2 * tile), jnp.bfloat16),
            pltpu.VMEM(psi.shape, jnp.bfloat16),
            pltpu.SMEM(right_owner.shape, jnp.int32),
            pltpu.SMEM(right_slot.shape, jnp.int32),
            pltpu.SemaphoreType.DMA((max(left_count, 2),)),
        ],
        compiler_params=params,
        cost_estimate=pl.CostEstimate(flops=flops, bytes_accessed=2 * psi.size, transcendentals=0),
    )(*in_hbm(right_owner, right_slot), half, *early)
    if by_swaps:
        ends = (FAR, FAR | CROSS, FAR | NEAR | CROSS)
        held, sigma = lax.optimization_barrier(([pieces[r] for r in ends], sigma))
        for r, piece in zip(ends, held):
            pieces[r], pieces[r | CORE] = piece, swap(piece, CORE)
        late = [pieces[r] for r in LATE]
        sigma = pl.pallas_call(
            late_kernel,
            out_shape=jax.ShapeDtypeStruct(psi.shape, jnp.bfloat16),
            in_specs=[smem, hbm] + [vmem] * (1 + len(late)),
            out_specs=hbm,
            scratch_shapes=[
                pltpu.VMEM((len(late) * pair_count, tile, 2 * tile), jnp.bfloat16),
                pltpu.VMEM((items + GROUP, tile, width), jnp.bfloat16),
                pltpu.SemaphoreType.DMA((items,)),
            ],
            input_output_aliases={1: 0},
            compiler_params=params,
            cost_estimate=pl.CostEstimate(flops=flops // 4, bytes_accessed=psi.size, transcendentals=0),
        )(listed, sigma, half, *late)
    if lax.axis_size("op") > 1:
        sigma = lax.psum_scatter(sigma, "op", scatter_dimension=3, tiled=True)
    return sigma


def solution(mesh):
    placed = (
        P(("grp", "sec"), None, None, None),
        P(("grp", "sec"), None, "op"),
        P(("grp", "sec"), None, "op"),
        P(("grp", "sec")),
        P(("grp", "sec")),
        P(("grp", "sec"), None),
        P(("grp", "sec"), None),
        P(("grp", "sec"), None, "op"),
    )
    return jax.shard_map(
        per_device,
        mesh=mesh,
        in_specs=placed,
        out_specs=P(("grp", "sec"), None, None, "op"),
        check_vma=False,
    )
```

```python
import functools

import jax
import jax.numpy as jnp
from jax import lax
from jax.experimental import pallas as pl
from jax.experimental.pallas import tpu as pltpu
from jax.sharding import PartitionSpec as P

VMEM_LIMIT = 48 * 1024 * 1024
GROUP = 4
FAR, NEAR, CROSS, CORE = 8, 4, 2, 1
LATE = (FAR | CORE, FAR | NEAR | CORE, FAR | CROSS | CORE, FAR | NEAR | CROSS, FAR | NEAR | CROSS | CORE)
EARLY = tuple(r for r in range(16) if r not in LATE)
ORDER = EARLY + LATE


def load_all(*copies):
    copies = [pltpu.make_async_copy(*copy) for copy in copies]
    for copy in copies:
        copy.start()
    return copies


def pack_kernel(dims_hbm, right_hbm, pairs_ref, dims_ref, right_ref, sems):
    count, tile, width = pairs_ref.shape
    copies = load_all((dims_hbm, dims_ref, sems.at[0]), (right_hbm, right_ref, sems.at[1]))
    rows = lax.broadcasted_iota(jnp.int32, (tile, tile), 0)
    cols = lax.broadcasted_iota(jnp.int32, (tile, tile), 1)
    most = jnp.maximum(rows, cols)
    for copy in copies:
        copy.wait()

    def kept(b):
        return jnp.where(most < dims_ref[b], right_ref[b].astype(jnp.float32), 0.0)

    for p in range(count):
        both = jnp.concatenate([kept(p), kept(p + count)], axis=1)
        pairs_ref[p] = both.astype(jnp.bfloat16)


def left_kernel(
    pair_count, dims_hbm, active_hbm, slot_hbm, left_hbm, psi_hbm,
    half_ref, dims_ref, active_ref, slot_ref, left_ref, psi_ref, sems, psi_sems,
):
    sectors, blocks, tile, width = psi_ref.shape
    copies = load_all(
        (dims_hbm, dims_ref, sems.at[0]),
        (active_hbm, active_ref, sems.at[1]),
        (slot_hbm, slot_ref, sems.at[2]),
        (left_hbm, left_ref, sems.at[3]),
    )
    psi_copies = load_all(*[(psi_hbm.at[a], psi_ref.at[a], psi_sems.at[a]) for a in range(sectors)])
    rows = lax.broadcasted_iota(jnp.int32, (tile, tile), 0)
    cols = lax.broadcasted_iota(jnp.int32, (tile, tile), 1)
    most = jnp.maximum(rows, cols)
    upper = (lax.broadcasted_iota(jnp.int32, (tile, width), 1) >= tile).astype(jnp.int32)
    for copy in copies:
        copy.wait()
    for a in range(sectors):
        psi_copies[a].wait()
        op = jnp.where(most < dims_ref[a], left_ref[a].astype(jnp.float32), 0.0).astype(jnp.bfloat16)
        for k in range(blocks):
            part = jnp.dot(op, psi_ref[a, k], preferred_element_type=jnp.float32)
            part = part * active_ref[a, k].astype(jnp.float32)
            other = pltpu.roll(part, tile, 1)
            here = upper == (slot_ref[a, k] >= pair_count).astype(jnp.int32)
            first = jnp.where(upper == 0, part, other)
            last = jnp.where(upper == 0, other, part)
            half_ref[a, k, :, :width] = jnp.where(here, first, 0.0).astype(jnp.bfloat16)
            half_ref[a, k, :, width:] = jnp.where(here, last, 0.0).astype(jnp.bfloat16)


def times_operator(half, pair):
    zero = jnp.zeros_like(pair)
    top = jnp.concatenate([pair, zero], axis=1)
    low = jnp.concatenate([zero, pair], axis=1)
    both = jnp.concatenate([top, low], axis=0)
    part = lax.dot_general(half, both, (((1,), (1,)), ((), ())), preferred_element_type=jnp.float32)
    return part.astype(jnp.bfloat16)


def merge(piece_refs, pairs_ref):
    at = 0
    for piece in piece_refs:
        pairs_ref[at:at + piece.shape[0]] = piece[...]
        at += piece.shape[0]


def piece_at(r):
    low = sum(ORDER.index(i) << (4 * i) for i in range(7))
    high = sum(ORDER.index(i + 8) << (4 * i) for i in range(7))
    packed = jnp.where(r < 8, low, high) >> (4 * (r & 7))
    end = jnp.where(r < 8, ORDER.index(7), ORDER.index(15))
    return jnp.where(r & 7 == 7, end, packed & 15)


def early_kernel(pair_count, owner_hbm, slot_hbm, half_ref, *refs):
    piece_refs = refs[:-7]
    out_hbm, late_ref, pairs_ref, out_ref, owner_ref, slot_ref, sems = refs[-7:]
    sectors, blocks, tile, width = out_ref.shape
    items, held = sectors * blocks, pairs_ref.shape[0]
    copies = load_all((owner_hbm, owner_ref, sems.at[0]), (slot_hbm, slot_ref, sems.at[1]))
    merge(piece_refs, pairs_ref)
    me = lax.axis_index("sec")
    for copy in copies:
        copy.wait()

    def store(a):
        return pltpu.make_async_copy(out_ref.at[a], out_hbm.at[a], sems.at[a])

    def one(a, listed):
        for k in range(blocks):
            owner, slot = owner_ref[a, k], slot_ref[a, k]
            at = piece_at(owner ^ me) if len(piece_refs) > 1 else owner
            at = at * pair_count + jnp.where(slot >= pair_count, slot - pair_count, slot)
            late = at >= held
            pair = pairs_ref[jnp.where(late, 0, at)]
            out_ref[a, k] = times_operator(half_ref[a, k], pair)
            late_ref[listed] = (at - held) * items + a * blocks + k
            listed = listed + late.astype(jnp.int32)
        store(a).start()
        return listed

    listed = lax.fori_loop(0, sectors, one, 0, unroll=2)
    late_ref[items] = listed
    for a in range(sectors):
        store(a).wait()


def late_kernel(late_ref, early_hbm, half_ref, *refs):
    piece_refs, (out_hbm, pairs_ref, out_ref, sems) = refs[:-4], refs[-4:]
    sectors, blocks, tile, width = half_ref.shape
    items = sectors * blocks
    listed = late_ref[items]
    merge(piece_refs, pairs_ref)

    def store(slot, item):
        return pltpu.make_async_copy(out_ref.at[slot], out_hbm.at[item // blocks, item % blocks], sems.at[slot])

    def group(g, carry):
        for u in range(GROUP):
            slot = g * GROUP + u
            entry = late_ref[jnp.minimum(slot, listed - 1)]
            item = entry % items
            out_ref[slot] = times_operator(half_ref[item // blocks, item % blocks], pairs_ref[entry // items])
        for u in range(GROUP):
            slot = g * GROUP + u

            @pl.when(slot < listed)
            def _():
                store(slot, late_ref[slot] % items).start()
        return carry

    def drain(slot, carry):
        store(slot, 0).wait()
        return carry

    lax.fori_loop(0, (listed + GROUP - 1) // GROUP, group, 0)
    lax.fori_loop(0, listed, drain, 0)


def swap(piece, bit):
    count = lax.axis_size("sec")
    return lax.ppermute(piece, "sec", [(i, i ^ bit) for i in range(count)])


def per_device(
    psi, left_ops, right_ops, dims_left, dims_right, right_owner, right_slot, term_active
):
    left_count, block_count, tile, width = psi.shape
    items = left_count * block_count
    pair_count = right_ops.shape[0] // 2
    count = lax.axis_size("sec")
    by_swaps = count == len(ORDER)
    flops = 2 * psi.size * tile
    smem = pl.BlockSpec(memory_space=pltpu.SMEM)
    vmem = pl.BlockSpec(memory_space=pltpu.VMEM)
    hbm = pl.BlockSpec(memory_space=pltpu.HBM)
    params = pltpu.CompilerParams(vmem_limit_bytes=VMEM_LIMIT)

    def in_hbm(*arrays):
        return [pltpu.with_memory_space_constraint(array, pltpu.HBM) for array in arrays]

    pairs = pl.pallas_call(
        pack_kernel,
        out_shape=jax.ShapeDtypeStruct((pair_count, tile, 2 * tile), jnp.bfloat16),
        in_specs=[hbm, hbm],
        out_specs=vmem,
        scratch_shapes=[
            pltpu.SMEM(dims_right.shape, jnp.int32),
            pltpu.VMEM(right_ops.shape, jnp.bfloat16),
            pltpu.SemaphoreType.DMA((2,)),
        ],
        compiler_params=params,
        cost_estimate=pl.CostEstimate(flops=0, bytes_accessed=2 * right_ops.size, transcendentals=0),
    )(*in_hbm(dims_right, right_ops))

    def half_of(dims_left):
        active = term_active.reshape(left_count, block_count)
        return pl.pallas_call(
            functools.partial(left_kernel, pair_count),
            out_shape=jax.ShapeDtypeStruct((left_count, block_count, tile, 2 * width), jnp.bfloat16),
            in_specs=[hbm] * 5,
            out_specs=vmem,
            scratch_shapes=[
                pltpu.SMEM(dims_left.shape, jnp.int32),
                pltpu.SMEM(active.shape, jnp.int32),
                pltpu.SMEM(right_slot.shape, jnp.int32),
                pltpu.VMEM(left_ops.shape, jnp.bfloat16),
                pltpu.VMEM(psi.shape, jnp.bfloat16),
                pltpu.SemaphoreType.DMA((4,)),
                pltpu.SemaphoreType.DMA((left_count,)),
            ],
            compiler_params=params,
            cost_estimate=pl.CostEstimate(flops=flops, bytes_accessed=2 * psi.size, transcendentals=0),
        )(*in_hbm(dims_left, active, right_slot, left_ops, psi))

    if by_swaps:
        pieces = {0: pairs}
        def pass_on(*pairs_of):
            for r, bit in pairs_of:
                pieces[r | bit] = swap(pieces[r], bit)

        pass_on((0, FAR), (0, NEAR), (0, CROSS), (0, CORE), (NEAR, CROSS), (FAR, NEAR), (FAR, CROSS), (FAR | NEAR, CROSS))
        dims_left, pieces[FAR] = lax.optimization_barrier((dims_left, pieces[FAR]))
        half = half_of(dims_left)
        held = (NEAR, CROSS, NEAR | CROSS,)
        half, ends = lax.optimization_barrier((half, [pieces[r] for r in held]))
        pieces.update(zip(held, ends))
        pass_on((NEAR, CORE), (CROSS, CORE), (NEAR | CROSS, CORE), (FAR | NEAR, CORE))
        early = [pieces[r] for r in EARLY]
    else:
        half = half_of(dims_left)
        early = [lax.all_gather(pairs, "sec", axis=0, tiled=True)]

    sigma, listed = pl.pallas_call(
        functools.partial(early_kernel, pair_count),
        out_shape=(
            jax.ShapeDtypeStruct(psi.shape, jnp.bfloat16),
            jax.ShapeDtypeStruct((items + 1,), jnp.int32),
        ),
        in_specs=[hbm, hbm] + [vmem] * (1 + len(early)),
        out_specs=(hbm, smem),
        scratch_shapes=[
            pltpu.VMEM((sum(piece.shape[0] for piece in early), tile, 2 * tile), jnp.bfloat16),
            pltpu.VMEM(psi.shape, jnp.bfloat16),
            pltpu.SMEM(right_owner.shape, jnp.int32),
            pltpu.SMEM(right_slot.shape, jnp.int32),
            pltpu.SemaphoreType.DMA((max(left_count, 2),)),
        ],
        compiler_params=params,
        cost_estimate=pl.CostEstimate(flops=flops, bytes_accessed=2 * psi.size, transcendentals=0),
    )(*in_hbm(right_owner, right_slot), half, *early)
    if by_swaps:
        ends = (FAR, FAR | CROSS, FAR | NEAR | CROSS,)
        held, sigma = lax.optimization_barrier(([pieces[r] for r in ends], sigma))
        for r, piece in zip(ends, held):
            pieces[r], pieces[r | CORE] = piece, swap(piece, CORE)
        late = [pieces[r] for r in LATE]
        sigma = pl.pallas_call(
            late_kernel,
            out_shape=jax.ShapeDtypeStruct(psi.shape, jnp.bfloat16),
            in_specs=[smem, hbm] + [vmem] * (1 + len(late)),
            out_specs=hbm,
            scratch_shapes=[
                pltpu.VMEM((len(late) * pair_count, tile, 2 * tile), jnp.bfloat16),
                pltpu.VMEM((items + GROUP, tile, width), jnp.bfloat16),
                pltpu.SemaphoreType.DMA((items,)),
            ],
            input_output_aliases={1: 0},
            compiler_params=params,
            cost_estimate=pl.CostEstimate(flops=flops // 4, bytes_accessed=psi.size, transcendentals=0),
        )(listed, sigma, half, *late)
    if lax.axis_size("op") > 1:
        sigma = lax.psum_scatter(sigma, "op", scatter_dimension=3, tiled=True)
    return sigma


def solution(mesh):
    placed = (
        P(("grp", "sec"), None, None, None),
        P(("grp", "sec"), None, "op"),
        P(("grp", "sec"), None, "op"),
        P(("grp", "sec")),
        P(("grp", "sec")),
        P(("grp", "sec"), None),
        P(("grp", "sec"), None),
        P(("grp", "sec"), None, "op"),
    )
    return jax.shard_map(
        per_device,
        mesh=mesh,
        in_specs=placed,
        out_specs=P(("grp", "sec"), None, None, "op"),
        check_vma=False,
    )
```

```python
import functools

import jax
import jax.numpy as jnp
from jax import lax
from jax.experimental import pallas as pl
from jax.experimental.pallas import tpu as pltpu
from jax.sharding import PartitionSpec as P

VMEM_LIMIT = 48 * 1024 * 1024
GROUP = 8
FAR, NEAR, CROSS, CORE = 8, 4, 2, 1
LATE = (FAR | CORE, FAR | NEAR | CORE, FAR | CROSS | CORE, FAR | NEAR | CROSS, FAR | NEAR | CROSS | CORE)
EARLY = tuple(r for r in range(16) if r not in LATE)
ORDER = EARLY + LATE


def load_all(*copies):
    copies = [pltpu.make_async_copy(*copy) for copy in copies]
    for copy in copies:
        copy.start()
    return copies


def pack_kernel(dims_hbm, right_hbm, pairs_ref, dims_ref, right_ref, sems):
    count, tile, width = pairs_ref.shape
    copies = load_all((dims_hbm, dims_ref, sems.at[0]), (right_hbm, right_ref, sems.at[1]))
    rows = lax.broadcasted_iota(jnp.int32, (tile, tile), 0)
    cols = lax.broadcasted_iota(jnp.int32, (tile, tile), 1)
    most = jnp.maximum(rows, cols)
    for copy in copies:
        copy.wait()

    def kept(b):
        return jnp.where(most < dims_ref[b], right_ref[b].astype(jnp.float32), 0.0)

    for p in range(count):
        both = jnp.concatenate([kept(p), kept(p + count)], axis=1)
        pairs_ref[p] = both.astype(jnp.bfloat16)


def left_kernel(dims_hbm, active_hbm, left_hbm, psi_hbm, half_ref, dims_ref, active_ref, left_ref, psi_ref, sems, psi_sems):
    sectors, blocks, tile, width = psi_ref.shape
    copies = load_all(
        (dims_hbm, dims_ref, sems.at[0]),
        (active_hbm, active_ref, sems.at[1]),
        (left_hbm, left_ref, sems.at[2]),
    )
    psi_copies = load_all(*[(psi_hbm.at[a], psi_ref.at[a], psi_sems.at[a]) for a in range(sectors)])
    rows = lax.broadcasted_iota(jnp.int32, (tile, tile), 0)
    cols = lax.broadcasted_iota(jnp.int32, (tile, tile), 1)
    most = jnp.maximum(rows, cols)
    for copy in copies:
        copy.wait()
    for a in range(sectors):
        psi_copies[a].wait()
        op = jnp.where(most < dims_ref[a], left_ref[a].astype(jnp.float32), 0.0).astype(jnp.bfloat16)
        for k in range(0, blocks, 2):
            both = jnp.concatenate([psi_ref[a, k], psi_ref[a, k + 1]], axis=1)
            part = jnp.dot(op, both, preferred_element_type=jnp.float32)
            for u in range(2):
                active = active_ref[a, k + u].astype(jnp.float32)
                half_ref[a, k + u] = (part[:, u * width:(u + 1) * width] * active).astype(jnp.bfloat16)


def times_operator(half, pair, second):
    tile, width = pair.shape
    lower = (lax.broadcasted_iota(jnp.int32, pair.shape, 1) < tile).astype(jnp.bfloat16)
    other = pltpu.roll(pair, tile, 1)
    top = jnp.where(second, other, pair) * lower
    low = jnp.where(second, pair, other) * (1 - lower)
    both = jnp.concatenate([top, low], axis=0)
    part = lax.dot_general(half, both, (((1,), (1,)), ((), ())), preferred_element_type=jnp.float32)
    return part.astype(jnp.bfloat16)


def merge(piece_refs, pairs_ref):
    at = 0
    for piece in piece_refs:
        pairs_ref[at:at + piece.shape[0]] = piece[...]
        at += piece.shape[0]


def piece_at(r):
    low = sum(ORDER.index(i) << (4 * i) for i in range(7))
    high = sum(ORDER.index(i + 8) << (4 * i) for i in range(7))
    packed = jnp.where(r < 8, low, high) >> (4 * (r & 7))
    end = jnp.where(r < 8, ORDER.index(7), ORDER.index(15))
    return jnp.where(r & 7 == 7, end, packed & 15)


def early_kernel(pair_count, owner_hbm, slot_hbm, half_ref, *refs):
    piece_refs = refs[:-7]
    out_hbm, late_ref, pairs_ref, out_ref, owner_ref, slot_ref, sems = refs[-7:]
    sectors, blocks, tile, width = out_ref.shape
    items, held = sectors * blocks, pairs_ref.shape[0]
    copies = load_all((owner_hbm, owner_ref, sems.at[0]), (slot_hbm, slot_ref, sems.at[1]))
    merge(piece_refs, pairs_ref)
    me = lax.axis_index("sec")
    for copy in copies:
        copy.wait()

    def store(a):
        return pltpu.make_async_copy(out_ref.at[a], out_hbm.at[a], sems.at[a])

    def one(a, listed):
        for k in range(blocks):
            owner, slot = owner_ref[a, k], slot_ref[a, k]
            at = piece_at(owner ^ me) if len(piece_refs) > 1 else owner
            second = slot >= pair_count
            at = at * pair_count + jnp.where(second, slot - pair_count, slot)
            late = at >= held
            pair = pairs_ref[jnp.where(late, 0, at)]
            out_ref[a, k] = times_operator(half_ref[a, k], pair, second)
            late_ref[listed] = ((at - held) * 2 + second.astype(jnp.int32)) * items + a * blocks + k
            listed = listed + late.astype(jnp.int32)
        store(a).start()
        return listed

    listed = lax.fori_loop(0, sectors, one, 0, unroll=2)
    late_ref[items] = listed
    for a in range(sectors):
        store(a).wait()


def late_kernel(late_ref, early_hbm, half_ref, *refs):
    piece_refs, (out_hbm, pairs_ref, out_ref, sems) = refs[:-4], refs[-4:]
    sectors, blocks, tile, width = half_ref.shape
    items = sectors * blocks
    listed = late_ref[items]
    merge(piece_refs, pairs_ref)

    def store(slot, item):
        return pltpu.make_async_copy(out_ref.at[slot], out_hbm.at[item // blocks, item % blocks], sems.at[slot])

    def group(g, carry):
        for u in range(GROUP):
            slot = g * GROUP + u
            entry = late_ref[jnp.minimum(slot, listed - 1)]
            item = entry % items
            at = entry // items
            half = half_ref[item // blocks, item % blocks]
            out_ref[slot] = times_operator(half, pairs_ref[at // 2], at % 2 == 1)
        for u in range(GROUP):
            slot = g * GROUP + u

            @pl.when(slot < listed)
            def _():
                store(slot, late_ref[slot] % items).start()
        return carry

    def drain(slot, carry):
        store(slot, 0).wait()
        return carry

    lax.fori_loop(0, (listed + GROUP - 1) // GROUP, group, 0)
    lax.fori_loop(0, listed, drain, 0)


def swap(piece, bit):
    count = lax.axis_size("sec")
    return lax.ppermute(piece, "sec", [(i, i ^ bit) for i in range(count)])


def per_device(
    psi, left_ops, right_ops, dims_left, dims_right, right_owner, right_slot, term_active
):
    left_count, block_count, tile, width = psi.shape
    items = left_count * block_count
    pair_count = right_ops.shape[0] // 2
    count = lax.axis_size("sec")
    by_swaps = count == len(ORDER)
    flops = 2 * psi.size * tile
    smem = pl.BlockSpec(memory_space=pltpu.SMEM)
    vmem = pl.BlockSpec(memory_space=pltpu.VMEM)
    hbm = pl.BlockSpec(memory_space=pltpu.HBM)
    params = pltpu.CompilerParams(vmem_limit_bytes=VMEM_LIMIT)

    def in_hbm(*arrays):
        return [pltpu.with_memory_space_constraint(array, pltpu.HBM) for array in arrays]

    pairs = pl.pallas_call(
        pack_kernel,
        out_shape=jax.ShapeDtypeStruct((pair_count, tile, 2 * tile), jnp.bfloat16),
        in_specs=[hbm, hbm],
        out_specs=vmem,
        scratch_shapes=[
            pltpu.SMEM(dims_right.shape, jnp.int32),
            pltpu.VMEM(right_ops.shape, jnp.bfloat16),
            pltpu.SemaphoreType.DMA((2,)),
        ],
        compiler_params=params,
        cost_estimate=pl.CostEstimate(flops=0, bytes_accessed=2 * right_ops.size, transcendentals=0),
    )(*in_hbm(dims_right, right_ops))

    def half_of(dims_left):
        active = term_active.reshape(left_count, block_count)
        return pl.pallas_call(
            left_kernel,
            out_shape=jax.ShapeDtypeStruct(psi.shape, jnp.bfloat16),
            in_specs=[hbm] * 4,
            out_specs=vmem,
            scratch_shapes=[
                pltpu.SMEM(dims_left.shape, jnp.int32),
                pltpu.SMEM(active.shape, jnp.int32),
                pltpu.VMEM(left_ops.shape, jnp.bfloat16),
                pltpu.VMEM(psi.shape, jnp.bfloat16),
                pltpu.SemaphoreType.DMA((3,)),
                pltpu.SemaphoreType.DMA((left_count,)),
            ],
            compiler_params=params,
            cost_estimate=pl.CostEstimate(flops=flops, bytes_accessed=2 * psi.size, transcendentals=0),
        )(*in_hbm(dims_left, active, left_ops, psi))

    if by_swaps:
        pieces = {0: pairs}
        def pass_on(*pairs_of):
            for r, bit in pairs_of:
                pieces[r | bit] = swap(pieces[r], bit)

        pass_on((0, FAR), (0, NEAR), (0, CROSS), (0, CORE), (NEAR, CROSS), (FAR, NEAR), (FAR, CROSS), (FAR | NEAR, CROSS))
        dims_left, pieces[FAR] = lax.optimization_barrier((dims_left, pieces[FAR]))
        half = half_of(dims_left)
        held = (NEAR, CROSS, NEAR | CROSS,)
        half, ends = lax.optimization_barrier((half, [pieces[r] for r in held]))
        pieces.update(zip(held, ends))
        pass_on((NEAR, CORE), (CROSS, CORE), (NEAR | CROSS, CORE), (FAR | NEAR, CORE))
        early = [pieces[r] for r in EARLY]
    else:
        half = half_of(dims_left)
        early = [lax.all_gather(pairs, "sec", axis=0, tiled=True)]

    sigma, listed = pl.pallas_call(
        functools.partial(early_kernel, pair_count),
        out_shape=(
            jax.ShapeDtypeStruct(psi.shape, jnp.bfloat16),
            jax.ShapeDtypeStruct((items + 1,), jnp.int32),
        ),
        in_specs=[hbm, hbm] + [vmem] * (1 + len(early)),
        out_specs=(hbm, smem),
        scratch_shapes=[
            pltpu.VMEM((sum(piece.shape[0] for piece in early), tile, 2 * tile), jnp.bfloat16),
            pltpu.VMEM(psi.shape, jnp.bfloat16),
            pltpu.SMEM(right_owner.shape, jnp.int32),
            pltpu.SMEM(right_slot.shape, jnp.int32),
            pltpu.SemaphoreType.DMA((max(left_count, 2),)),
        ],
        compiler_params=params,
        cost_estimate=pl.CostEstimate(flops=flops, bytes_accessed=2 * psi.size, transcendentals=0),
    )(*in_hbm(right_owner, right_slot), half, *early)
    if by_swaps:
        ends = (FAR, FAR | CROSS, FAR | NEAR | CROSS,)
        held, sigma = lax.optimization_barrier(([pieces[r] for r in ends], sigma))
        for r, piece in zip(ends, held):
            pieces[r], pieces[r | CORE] = piece, swap(piece, CORE)
        late = [pieces[r] for r in LATE]
        sigma = pl.pallas_call(
            late_kernel,
            out_shape=jax.ShapeDtypeStruct(psi.shape, jnp.bfloat16),
            in_specs=[smem, hbm] + [vmem] * (1 + len(late)),
            out_specs=hbm,
            scratch_shapes=[
                pltpu.VMEM((len(late) * pair_count, tile, 2 * tile), jnp.bfloat16),
                pltpu.VMEM((items + GROUP, tile, width), jnp.bfloat16),
                pltpu.SemaphoreType.DMA((items,)),
            ],
            input_output_aliases={1: 0},
            compiler_params=params,
            cost_estimate=pl.CostEstimate(flops=flops // 4, bytes_accessed=psi.size, transcendentals=0),
        )(listed, sigma, half, *late)
    if lax.axis_size("op") > 1:
        sigma = lax.psum_scatter(sigma, "op", scatter_dimension=3, tiled=True)
    return sigma


def solution(mesh):
    placed = (
        P(("grp", "sec"), None, None, None),
        P(("grp", "sec"), None, "op"),
        P(("grp", "sec"), None, "op"),
        P(("grp", "sec")),
        P(("grp", "sec")),
        P(("grp", "sec"), None),
        P(("grp", "sec"), None),
        P(("grp", "sec"), None, "op"),
    )
    return jax.shard_map(
        per_device,
        mesh=mesh,
        in_specs=placed,
        out_specs=P(("grp", "sec"), None, None, "op"),
        check_vma=False,
    )
```

```python
import functools

import jax
import jax.numpy as jnp
from jax import lax
from jax.experimental import pallas as pl
from jax.experimental.pallas import tpu as pltpu
from jax.sharding import PartitionSpec as P

VMEM_LIMIT = 48 * 1024 * 1024
GROUP = 8
FAR, NEAR, CROSS, CORE = 8, 4, 2, 1
LATE = (FAR | CORE, FAR | NEAR | CORE, FAR | CROSS | CORE, FAR | NEAR | CROSS, FAR | NEAR | CROSS | CORE)
EARLY = tuple(r for r in range(16) if r not in LATE)
ORDER = EARLY + LATE


def load_all(*copies):
    copies = [pltpu.make_async_copy(*copy) for copy in copies]
    for copy in copies:
        copy.start()
    return copies


def pack_kernel(dims_hbm, right_hbm, pairs_ref, dims_ref, right_ref, sems):
    count, tile, width = pairs_ref.shape
    copies = load_all((dims_hbm, dims_ref, sems.at[0]), (right_hbm, right_ref, sems.at[1]))
    rows = lax.broadcasted_iota(jnp.int32, (tile, tile), 0)
    cols = lax.broadcasted_iota(jnp.int32, (tile, tile), 1)
    most = jnp.maximum(rows, cols)
    for copy in copies:
        copy.wait()

    def kept(b):
        return jnp.where(most < dims_ref[b], right_ref[b].astype(jnp.float32), 0.0)

    for p in range(count):
        both = jnp.concatenate([kept(p), kept(p + count)], axis=0)
        pairs_ref[p] = both.T.astype(jnp.bfloat16)


def left_kernel(dims_hbm, active_hbm, left_hbm, psi_hbm, half_ref, dims_ref, active_ref, left_ref, psi_ref, sems, psi_sems):
    sectors, blocks, tile, width = psi_ref.shape
    copies = load_all(
        (dims_hbm, dims_ref, sems.at[0]),
        (active_hbm, active_ref, sems.at[1]),
        (left_hbm, left_ref, sems.at[2]),
    )
    psi_copies = load_all(*[(psi_hbm.at[a], psi_ref.at[a], psi_sems.at[a]) for a in range(sectors)])
    rows = lax.broadcasted_iota(jnp.int32, (tile, tile), 0)
    cols = lax.broadcasted_iota(jnp.int32, (tile, tile), 1)
    most = jnp.maximum(rows, cols)
    for copy in copies:
        copy.wait()
    for a in range(sectors):
        psi_copies[a].wait()
        op = jnp.where(most < dims_ref[a], left_ref[a].astype(jnp.float32), 0.0).astype(jnp.bfloat16)
        for k in range(0, blocks, 2):
            both = jnp.concatenate([psi_ref[a, k], psi_ref[a, k + 1]], axis=1)
            part = jnp.dot(op, both, preferred_element_type=jnp.float32)
            for u in range(2):
                active = active_ref[a, k + u].astype(jnp.float32)
                half_ref[a, k + u] = (part[:, u * width:(u + 1) * width] * active).astype(jnp.bfloat16)


def block_form(pair, second):
    tile, width = pair.shape
    lower = (lax.broadcasted_iota(jnp.int32, pair.shape, 1) < tile).astype(jnp.bfloat16)
    other = pltpu.roll(pair, tile, 1)
    top = jnp.where(second, other, pair) * lower
    low = jnp.where(second, pair, other) * (1 - lower)
    return jnp.concatenate([top, low], axis=0)


def two_products(halves, forms):
    zero = jnp.zeros_like(forms[0])
    top = jnp.concatenate([forms[0], zero], axis=1)
    low = jnp.concatenate([zero, forms[1]], axis=1)
    both = jnp.concatenate([top, low], axis=0)
    part = jnp.dot(jnp.concatenate(halves, axis=1), both, preferred_element_type=jnp.float32)
    width = part.shape[1] // 2
    return part[:, :width].astype(jnp.bfloat16), part[:, width:].astype(jnp.bfloat16)


def merge(piece_refs, pairs_ref):
    at = 0
    for piece in piece_refs:
        pairs_ref[at:at + piece.shape[0]] = piece[...]
        at += piece.shape[0]


def piece_at(r):
    low = sum(ORDER.index(i) << (4 * i) for i in range(7))
    high = sum(ORDER.index(i + 8) << (4 * i) for i in range(7))
    packed = jnp.where(r < 8, low, high) >> (4 * (r & 7))
    end = jnp.where(r < 8, ORDER.index(7), ORDER.index(15))
    return jnp.where(r & 7 == 7, end, packed & 15)


def early_kernel(pair_count, owner_hbm, slot_hbm, half_ref, *refs):
    piece_refs = refs[:-7]
    out_hbm, late_ref, pairs_ref, out_ref, owner_ref, slot_ref, sems = refs[-7:]
    sectors, blocks, tile, width = out_ref.shape
    items, held = sectors * blocks, pairs_ref.shape[0]
    copies = load_all((owner_hbm, owner_ref, sems.at[0]), (slot_hbm, slot_ref, sems.at[1]))
    merge(piece_refs, pairs_ref)
    me = lax.axis_index("sec")
    for copy in copies:
        copy.wait()

    def store(a):
        return pltpu.make_async_copy(out_ref.at[a], out_hbm.at[a], sems.at[a])

    def one(a, listed):
        for k in range(0, blocks, 2):
            forms = []
            for u in range(2):
                owner, slot = owner_ref[a, k + u], slot_ref[a, k + u]
                at = piece_at(owner ^ me) if len(piece_refs) > 1 else owner
                second = slot >= pair_count
                at = at * pair_count + jnp.where(second, slot - pair_count, slot)
                late = at >= held
                forms.append(block_form(pairs_ref[jnp.where(late, 0, at)], second))
                late_ref[listed] = ((at - held) * 2 + second.astype(jnp.int32)) * items + a * blocks + k + u
                listed = listed + late.astype(jnp.int32)
            out_ref[a, k], out_ref[a, k + 1] = two_products([half_ref[a, k], half_ref[a, k + 1]], forms)
        store(a).start()
        return listed

    listed = lax.fori_loop(0, sectors, one, 0, unroll=2)
    late_ref[items] = listed
    for a in range(sectors):
        store(a).wait()


def late_kernel(late_ref, early_hbm, half_ref, *refs):
    piece_refs, (out_hbm, pairs_ref, out_ref, sems) = refs[:-4], refs[-4:]
    sectors, blocks, tile, width = half_ref.shape
    items = sectors * blocks
    listed = late_ref[items]
    merge(piece_refs, pairs_ref)

    def store(slot, item):
        return pltpu.make_async_copy(out_ref.at[slot], out_hbm.at[item // blocks, item % blocks], sems.at[slot])

    def group(g, carry):
        for u in range(0, GROUP, 2):
            slot = g * GROUP + u
            entries = [late_ref[jnp.minimum(slot + n, listed - 1)] for n in range(2)]
            halves, forms = [], []
            for entry in entries:
                item, at = entry % items, entry // items
                halves.append(half_ref[item // blocks, item % blocks])
                forms.append(block_form(pairs_ref[at // 2], at % 2 == 1))
            out_ref[slot], out_ref[slot + 1] = two_products(halves, forms)
        for u in range(GROUP):
            slot = g * GROUP + u

            @pl.when(slot < listed)
            def _():
                store(slot, late_ref[slot] % items).start()
        return carry

    def drain(slot, carry):
        store(slot, 0).wait()
        return carry

    lax.fori_loop(0, (listed + GROUP - 1) // GROUP, group, 0)
    lax.fori_loop(0, listed, drain, 0)


def swap(piece, bit):
    count = lax.axis_size("sec")
    return lax.ppermute(piece, "sec", [(i, i ^ bit) for i in range(count)])


def per_device(
    psi, left_ops, right_ops, dims_left, dims_right, right_owner, right_slot, term_active
):
    left_count, block_count, tile, width = psi.shape
    items = left_count * block_count
    pair_count = right_ops.shape[0] // 2
    count = lax.axis_size("sec")
    by_swaps = count == len(ORDER)
    flops = 2 * psi.size * tile
    smem = pl.BlockSpec(memory_space=pltpu.SMEM)
    vmem = pl.BlockSpec(memory_space=pltpu.VMEM)
    hbm = pl.BlockSpec(memory_space=pltpu.HBM)
    params = pltpu.CompilerParams(vmem_limit_bytes=VMEM_LIMIT)

    def in_hbm(*arrays):
        return [pltpu.with_memory_space_constraint(array, pltpu.HBM) for array in arrays]

    pairs = pl.pallas_call(
        pack_kernel,
        out_shape=jax.ShapeDtypeStruct((pair_count, tile, 2 * tile), jnp.bfloat16),
        in_specs=[hbm, hbm],
        out_specs=vmem,
        scratch_shapes=[
            pltpu.SMEM(dims_right.shape, jnp.int32),
            pltpu.VMEM(right_ops.shape, jnp.bfloat16),
            pltpu.SemaphoreType.DMA((2,)),
        ],
        compiler_params=params,
        cost_estimate=pl.CostEstimate(flops=0, bytes_accessed=2 * right_ops.size, transcendentals=0),
    )(*in_hbm(dims_right, right_ops))

    def half_of(dims_left):
        active = term_active.reshape(left_count, block_count)
        return pl.pallas_call(
            left_kernel,
            out_shape=jax.ShapeDtypeStruct(psi.shape, jnp.bfloat16),
            in_specs=[hbm] * 4,
            out_specs=vmem,
            scratch_shapes=[
                pltpu.SMEM(dims_left.shape, jnp.int32),
                pltpu.SMEM(active.shape, jnp.int32),
                pltpu.VMEM(left_ops.shape, jnp.bfloat16),
                pltpu.VMEM(psi.shape, jnp.bfloat16),
                pltpu.SemaphoreType.DMA((3,)),
                pltpu.SemaphoreType.DMA((left_count,)),
            ],
            compiler_params=params,
            cost_estimate=pl.CostEstimate(flops=flops, bytes_accessed=2 * psi.size, transcendentals=0),
        )(*in_hbm(dims_left, active, left_ops, psi))

    if by_swaps:
        pieces = {0: pairs}
        def pass_on(*pairs_of):
            for r, bit in pairs_of:
                pieces[r | bit] = swap(pieces[r], bit)

        pass_on((0, FAR), (0, NEAR), (0, CROSS), (0, CORE), (NEAR, CROSS), (FAR, NEAR), (FAR, CROSS), (FAR | NEAR, CROSS))
        held = (FAR,)
        dims_left, ends = lax.optimization_barrier((dims_left, [pieces[r] for r in held]))
        pieces.update(zip(held, ends))
        half = half_of(dims_left)
        held = (NEAR, CROSS, NEAR | CROSS,)
        half, ends = lax.optimization_barrier((half, [pieces[r] for r in held]))
        pieces.update(zip(held, ends))
        pass_on((NEAR, CORE), (CROSS, CORE), (NEAR | CROSS, CORE), (FAR | NEAR, CORE), (FAR, CORE), (FAR | CROSS, CORE))
        early = [pieces[r] for r in EARLY]
    else:
        half = half_of(dims_left)
        early = [lax.all_gather(pairs, "sec", axis=0, tiled=True)]

    sigma, listed = pl.pallas_call(
        functools.partial(early_kernel, pair_count),
        out_shape=(
            jax.ShapeDtypeStruct(psi.shape, jnp.bfloat16),
            jax.ShapeDtypeStruct((items + 1,), jnp.int32),
        ),
        in_specs=[hbm, hbm] + [vmem] * (1 + len(early)),
        out_specs=(hbm, smem),
        scratch_shapes=[
            pltpu.VMEM((sum(piece.shape[0] for piece in early), tile, 2 * tile), jnp.bfloat16),
            pltpu.VMEM(psi.shape, jnp.bfloat16),
            pltpu.SMEM(right_owner.shape, jnp.int32),
            pltpu.SMEM(right_slot.shape, jnp.int32),
            pltpu.SemaphoreType.DMA((max(left_count, 2),)),
        ],
        compiler_params=params,
        cost_estimate=pl.CostEstimate(flops=flops, bytes_accessed=2 * psi.size, transcendentals=0),
    )(*in_hbm(right_owner, right_slot), half, *early)
    if by_swaps:
        ends = (FAR | NEAR | CROSS,)
        held, sigma = lax.optimization_barrier(([pieces[r] for r in ends], sigma))
        for r, piece in zip(ends, held):
            pieces[r], pieces[r | CORE] = piece, swap(piece, CORE)
        late = [pieces[r] for r in LATE]
        sigma = pl.pallas_call(
            late_kernel,
            out_shape=jax.ShapeDtypeStruct(psi.shape, jnp.bfloat16),
            in_specs=[smem, hbm] + [vmem] * (1 + len(late)),
            out_specs=hbm,
            scratch_shapes=[
                pltpu.VMEM((len(late) * pair_count, tile, 2 * tile), jnp.bfloat16),
                pltpu.VMEM((items + GROUP, tile, width), jnp.bfloat16),
                pltpu.SemaphoreType.DMA((items,)),
            ],
            input_output_aliases={1: 0},
            compiler_params=params,
            cost_estimate=pl.CostEstimate(flops=flops // 4, bytes_accessed=psi.size, transcendentals=0),
        )(listed, sigma, half, *late)
    if lax.axis_size("op") > 1:
        sigma = lax.psum_scatter(sigma, "op", scatter_dimension=3, tiled=True)
    return sigma


def solution(mesh):
    placed = (
        P(("grp", "sec"), None, None, None),
        P(("grp", "sec"), None, "op"),
        P(("grp", "sec"), None, "op"),
        P(("grp", "sec")),
        P(("grp", "sec")),
        P(("grp", "sec"), None),
        P(("grp", "sec"), None),
        P(("grp", "sec"), None, "op"),
    )
    return jax.shard_map(
        per_device,
        mesh=mesh,
        in_specs=placed,
        out_specs=P(("grp", "sec"), None, None, "op"),
        check_vma=False,
    )
```

```python
import functools

import jax
import jax.numpy as jnp
from jax import lax
from jax.experimental import pallas as pl
from jax.experimental.pallas import tpu as pltpu
from jax.sharding import PartitionSpec as P

VMEM_LIMIT = 48 * 1024 * 1024
GROUP = 8
FAR, NEAR, CROSS, CORE = 8, 4, 2, 1
LATE = (FAR | CORE, FAR | NEAR | CORE, FAR | CROSS | CORE, FAR | NEAR | CROSS, FAR | NEAR | CROSS | CORE)
EARLY = tuple(r for r in range(16) if r not in LATE)
ORDER = EARLY + LATE


def load_all(*copies):
    copies = [pltpu.make_async_copy(*copy) for copy in copies]
    for copy in copies:
        copy.start()
    return copies


def pack_kernel(dims_hbm, right_hbm, pairs_ref, dims_ref, right_ref, sems):
    count, tile, width = pairs_ref.shape
    copies = load_all((dims_hbm, dims_ref, sems.at[0]), (right_hbm, right_ref, sems.at[1]))
    rows = lax.broadcasted_iota(jnp.int32, (tile, tile), 0)
    cols = lax.broadcasted_iota(jnp.int32, (tile, tile), 1)
    most = jnp.maximum(rows, cols)
    for copy in copies:
        copy.wait()

    def kept(b):
        return jnp.where(most < dims_ref[b], right_ref[b].astype(jnp.float32), 0.0)

    for p in range(count):
        both = jnp.concatenate([kept(p), kept(p + count)], axis=0)
        pairs_ref[p] = both.T.astype(jnp.bfloat16)


def left_kernel(dims_hbm, active_hbm, left_hbm, psi_hbm, half_ref, dims_ref, active_ref, left_ref, psi_ref, sems, psi_sems):
    sectors, blocks, tile, width = psi_ref.shape
    copies = load_all(
        (dims_hbm, dims_ref, sems.at[0]),
        (active_hbm, active_ref, sems.at[1]),
        (left_hbm, left_ref, sems.at[2]),
    )
    psi_copies = load_all(*[(psi_hbm.at[a], psi_ref.at[a], psi_sems.at[a]) for a in range(sectors)])
    rows = lax.broadcasted_iota(jnp.int32, (tile, tile), 0)
    cols = lax.broadcasted_iota(jnp.int32, (tile, tile), 1)
    most = jnp.maximum(rows, cols)
    for copy in copies:
        copy.wait()
    for a in range(sectors):
        psi_copies[a].wait()
        op = jnp.where(most < dims_ref[a], left_ref[a].astype(jnp.float32), 0.0).astype(jnp.bfloat16)
        for k in range(0, blocks, 2):
            both = jnp.concatenate([psi_ref[a, k], psi_ref[a, k + 1]], axis=1)
            part = jnp.dot(op, both, preferred_element_type=jnp.float32)
            for u in range(2):
                active = active_ref[a, k + u].astype(jnp.float32)
                half_ref[a, k + u] = (part[:, u * width:(u + 1) * width] * active).astype(jnp.bfloat16)


def block_form(pair, second):
    tile, width = pair.shape
    lower = (lax.broadcasted_iota(jnp.int32, pair.shape, 1) < tile).astype(jnp.bfloat16)
    other = pltpu.roll(pair, tile, 1)
    top = jnp.where(second, other, pair) * lower
    low = jnp.where(second, pair, other) * (1 - lower)
    return jnp.concatenate([top, low], axis=0)


def two_products(halves, forms):
    zero = jnp.zeros_like(forms[0])
    top = jnp.concatenate([forms[0], zero], axis=1)
    low = jnp.concatenate([zero, forms[1]], axis=1)
    both = jnp.concatenate([top, low], axis=0)
    part = jnp.dot(jnp.concatenate(halves, axis=1), both, preferred_element_type=jnp.float32)
    width = part.shape[1] // 2
    return part[:, :width].astype(jnp.bfloat16), part[:, width:].astype(jnp.bfloat16)


def merge(piece_refs, pairs_ref):
    at = 0
    for piece in piece_refs:
        pairs_ref[at:at + piece.shape[0]] = piece[...]
        at += piece.shape[0]


def piece_at(r):
    low = sum(ORDER.index(i) << (4 * i) for i in range(7))
    high = sum(ORDER.index(i + 8) << (4 * i) for i in range(7))
    packed = jnp.where(r < 8, low, high) >> (4 * (r & 7))
    end = jnp.where(r < 8, ORDER.index(7), ORDER.index(15))
    return jnp.where(r & 7 == 7, end, packed & 15)


def early_kernel(pair_count, owner_hbm, slot_hbm, half_ref, *refs):
    piece_refs = refs[:-6]
    out_ref, late_ref, pairs_ref, owner_ref, slot_ref, sems = refs[-6:]
    sectors, blocks, tile, width = out_ref.shape
    items, held = sectors * blocks, pairs_ref.shape[0]
    copies = load_all((owner_hbm, owner_ref, sems.at[0]), (slot_hbm, slot_ref, sems.at[1]))
    merge(piece_refs, pairs_ref)
    me = lax.axis_index("sec")
    for copy in copies:
        copy.wait()

    def one(a, listed):
        for k in range(0, blocks, 2):
            forms = []
            for u in range(2):
                owner, slot = owner_ref[a, k + u], slot_ref[a, k + u]
                at = piece_at(owner ^ me) if len(piece_refs) > 1 else owner
                second = slot >= pair_count
                at = at * pair_count + jnp.where(second, slot - pair_count, slot)
                late = at >= held
                forms.append(block_form(pairs_ref[jnp.where(late, 0, at)], second))
                late_ref[listed] = ((at - held) * 2 + second.astype(jnp.int32)) * items + a * blocks + k + u
                listed = listed + late.astype(jnp.int32)
            out_ref[a, k], out_ref[a, k + 1] = two_products([half_ref[a, k], half_ref[a, k + 1]], forms)
        return listed

    listed = lax.fori_loop(0, sectors, one, 0, unroll=2)
    late_ref[items] = listed


def late_kernel(late_ref, early_ref, half_ref, *refs):
    piece_refs, (out_hbm, pairs_ref, out_ref, sems, early_sems) = refs[:-5], refs[-5:]
    sectors, blocks, tile, width = half_ref.shape
    items = sectors * blocks
    early_stores = load_all(*[(early_ref.at[a], out_hbm.at[a], early_sems.at[a]) for a in range(sectors)])
    listed = late_ref[items]
    merge(piece_refs, pairs_ref)

    def store(slot, item):
        return pltpu.make_async_copy(out_ref.at[slot], out_hbm.at[item // blocks, item % blocks], sems.at[slot])

    def group(g, carry):
        for u in range(0, GROUP, 2):
            slot = g * GROUP + u
            entries = [late_ref[jnp.minimum(slot + n, listed - 1)] for n in range(2)]
            halves, forms = [], []
            for entry in entries:
                item, at = entry % items, entry // items
                halves.append(half_ref[item // blocks, item % blocks])
                forms.append(block_form(pairs_ref[at // 2], at % 2 == 1))
            out_ref[slot], out_ref[slot + 1] = two_products(halves, forms)
        return carry

    def place(slot, carry):
        store(slot, late_ref[slot] % items).start()
        return carry

    def drain(slot, carry):
        store(slot, 0).wait()
        return carry

    lax.fori_loop(0, (listed + GROUP - 1) // GROUP, group, 0)
    for early_store in early_stores:
        early_store.wait()
    lax.fori_loop(0, listed, place, 0)
    lax.fori_loop(0, listed, drain, 0)


def swap(piece, bit):
    count = lax.axis_size("sec")
    return lax.ppermute(piece, "sec", [(i, i ^ bit) for i in range(count)])


def per_device(
    psi, left_ops, right_ops, dims_left, dims_right, right_owner, right_slot, term_active
):
    left_count, block_count, tile, width = psi.shape
    items = left_count * block_count
    pair_count = right_ops.shape[0] // 2
    count = lax.axis_size("sec")
    by_swaps = count == len(ORDER)
    flops = 2 * psi.size * tile
    smem = pl.BlockSpec(memory_space=pltpu.SMEM)
    vmem = pl.BlockSpec(memory_space=pltpu.VMEM)
    hbm = pl.BlockSpec(memory_space=pltpu.HBM)
    params = pltpu.CompilerParams(vmem_limit_bytes=VMEM_LIMIT)

    def in_hbm(*arrays):
        return [pltpu.with_memory_space_constraint(array, pltpu.HBM) for array in arrays]

    pairs = pl.pallas_call(
        pack_kernel,
        out_shape=jax.ShapeDtypeStruct((pair_count, tile, 2 * tile), jnp.bfloat16),
        in_specs=[hbm, hbm],
        out_specs=vmem,
        scratch_shapes=[
            pltpu.SMEM(dims_right.shape, jnp.int32),
            pltpu.VMEM(right_ops.shape, jnp.bfloat16),
            pltpu.SemaphoreType.DMA((2,)),
        ],
        compiler_params=params,
        cost_estimate=pl.CostEstimate(flops=0, bytes_accessed=2 * right_ops.size, transcendentals=0),
    )(*in_hbm(dims_right, right_ops))

    def half_of(dims_left):
        active = term_active.reshape(left_count, block_count)
        return pl.pallas_call(
            left_kernel,
            out_shape=jax.ShapeDtypeStruct(psi.shape, jnp.bfloat16),
            in_specs=[hbm] * 4,
            out_specs=vmem,
            scratch_shapes=[
                pltpu.SMEM(dims_left.shape, jnp.int32),
                pltpu.SMEM(active.shape, jnp.int32),
                pltpu.VMEM(left_ops.shape, jnp.bfloat16),
                pltpu.VMEM(psi.shape, jnp.bfloat16),
                pltpu.SemaphoreType.DMA((3,)),
                pltpu.SemaphoreType.DMA((left_count,)),
            ],
            compiler_params=params,
            cost_estimate=pl.CostEstimate(flops=flops, bytes_accessed=2 * psi.size, transcendentals=0),
        )(*in_hbm(dims_left, active, left_ops, psi))

    if by_swaps:
        pieces = {0: pairs}
        def pass_on(*pairs_of):
            for r, bit in pairs_of:
                pieces[r | bit] = swap(pieces[r], bit)

        pass_on((0, FAR), (0, NEAR), (0, CROSS), (0, CORE), (NEAR, CROSS), (FAR, NEAR), (FAR, CROSS), (FAR | NEAR, CROSS))
        held = (FAR,)
        dims_left, ends = lax.optimization_barrier((dims_left, [pieces[r] for r in held]))
        pieces.update(zip(held, ends))
        half = half_of(dims_left)
        held = (NEAR, CROSS, NEAR | CROSS,)
        half, ends = lax.optimization_barrier((half, [pieces[r] for r in held]))
        pieces.update(zip(held, ends))
        pass_on((NEAR, CORE), (CROSS, CORE), (NEAR | CROSS, CORE), (FAR | NEAR, CORE), (FAR, CORE), (FAR | CROSS, CORE))
        early = [pieces[r] for r in EARLY]
    else:
        half = half_of(dims_left)
        early = [lax.all_gather(pairs, "sec", axis=0, tiled=True)]

    sigma, listed = pl.pallas_call(
        functools.partial(early_kernel, pair_count),
        out_shape=(
            jax.ShapeDtypeStruct(psi.shape, jnp.bfloat16),
            jax.ShapeDtypeStruct((items + 1,), jnp.int32),
        ),
        in_specs=[hbm, hbm] + [vmem] * (1 + len(early)),
        out_specs=(vmem, smem),
        scratch_shapes=[
            pltpu.VMEM((sum(piece.shape[0] for piece in early), tile, 2 * tile), jnp.bfloat16),
            pltpu.SMEM(right_owner.shape, jnp.int32),
            pltpu.SMEM(right_slot.shape, jnp.int32),
            pltpu.SemaphoreType.DMA((2,)),
        ],
        compiler_params=params,
        cost_estimate=pl.CostEstimate(flops=flops, bytes_accessed=2 * psi.size, transcendentals=0),
    )(*in_hbm(right_owner, right_slot), half, *early)
    if by_swaps:
        ends = (FAR | NEAR | CROSS,)
        held, sigma = lax.optimization_barrier(([pieces[r] for r in ends], sigma))
        for r, piece in zip(ends, held):
            pieces[r], pieces[r | CORE] = piece, swap(piece, CORE)
        late = [pieces[r] for r in LATE]
        sigma = pl.pallas_call(
            late_kernel,
            out_shape=jax.ShapeDtypeStruct(psi.shape, jnp.bfloat16),
            in_specs=[smem] + [vmem] * (2 + len(late)),
            out_specs=hbm,
            scratch_shapes=[
                pltpu.VMEM((len(late) * pair_count, tile, 2 * tile), jnp.bfloat16),
                pltpu.VMEM((items + GROUP, tile, width), jnp.bfloat16),
                pltpu.SemaphoreType.DMA((items,)),
                pltpu.SemaphoreType.DMA((left_count,)),
            ],
            compiler_params=params,
            cost_estimate=pl.CostEstimate(flops=flops // 4, bytes_accessed=psi.size, transcendentals=0),
        )(listed, sigma, half, *late)
    if lax.axis_size("op") > 1:
        sigma = lax.psum_scatter(sigma, "op", scatter_dimension=3, tiled=True)
    return sigma


def solution(mesh):
    placed = (
        P(("grp", "sec"), None, None, None),
        P(("grp", "sec"), None, "op"),
        P(("grp", "sec"), None, "op"),
        P(("grp", "sec")),
        P(("grp", "sec")),
        P(("grp", "sec"), None),
        P(("grp", "sec"), None),
        P(("grp", "sec"), None, "op"),
    )
    return jax.shard_map(
        per_device,
        mesh=mesh,
        in_specs=placed,
        out_specs=P(("grp", "sec"), None, None, "op"),
        check_vma=False,
    )
```

```python
import functools

import jax
import jax.numpy as jnp
from jax import lax
from jax.experimental import pallas as pl
from jax.experimental.pallas import tpu as pltpu
from jax.sharding import PartitionSpec as P

VMEM_LIMIT = 48 * 1024 * 1024
GROUP = 8
FAR, NEAR, CROSS, CORE = 8, 4, 2, 1
LATE = (FAR | CORE, FAR | CROSS | CORE, FAR | NEAR | CROSS, FAR | NEAR | CROSS | CORE)
EARLY = tuple(r for r in range(16) if r not in LATE)
ORDER = EARLY + LATE


def load_all(*copies):
    copies = [pltpu.make_async_copy(*copy) for copy in copies]
    for copy in copies:
        copy.start()
    return copies


def pack_kernel(dims_hbm, right_hbm, pairs_ref, dims_ref, right_ref, sems):
    count, tile, width = pairs_ref.shape
    copies = load_all((dims_hbm, dims_ref, sems.at[0]), (right_hbm, right_ref, sems.at[1]))
    rows = lax.broadcasted_iota(jnp.int32, (tile, tile), 0)
    cols = lax.broadcasted_iota(jnp.int32, (tile, tile), 1)
    most = jnp.maximum(rows, cols)
    for copy in copies:
        copy.wait()

    def kept(b):
        return jnp.where(most < dims_ref[b], right_ref[b].astype(jnp.float32), 0.0)

    for p in range(count):
        both = jnp.concatenate([kept(p), kept(p + count)], axis=0)
        pairs_ref[p] = both.T.astype(jnp.bfloat16)


def left_kernel(dims_hbm, active_hbm, left_hbm, psi_hbm, half_ref, dims_ref, active_ref, left_ref, psi_ref, sems, psi_sems):
    sectors, blocks, tile, width = psi_ref.shape
    copies = load_all(
        (dims_hbm, dims_ref, sems.at[0]),
        (active_hbm, active_ref, sems.at[1]),
        (left_hbm, left_ref, sems.at[2]),
    )
    psi_copies = load_all(*[(psi_hbm.at[a], psi_ref.at[a], psi_sems.at[a]) for a in range(sectors)])
    rows = lax.broadcasted_iota(jnp.int32, (tile, tile), 0)
    cols = lax.broadcasted_iota(jnp.int32, (tile, tile), 1)
    most = jnp.maximum(rows, cols)
    for copy in copies:
        copy.wait()
    for a in range(sectors):
        psi_copies[a].wait()
        op = jnp.where(most < dims_ref[a], left_ref[a].astype(jnp.float32), 0.0).astype(jnp.bfloat16)
        for k in range(0, blocks, 2):
            both = jnp.concatenate([psi_ref[a, k], psi_ref[a, k + 1]], axis=1)
            part = jnp.dot(op, both, preferred_element_type=jnp.float32)
            for u in range(2):
                active = active_ref[a, k + u].astype(jnp.float32)
                half_ref[a, k + u] = (part[:, u * width:(u + 1) * width] * active).astype(jnp.bfloat16)


def block_form(pair, second):
    tile, width = pair.shape
    lower = (lax.broadcasted_iota(jnp.int32, pair.shape, 1) < tile).astype(jnp.bfloat16)
    other = pltpu.roll(pair, tile, 1)
    top = jnp.where(second, other, pair) * lower
    low = jnp.where(second, pair, other) * (1 - lower)
    return jnp.concatenate([top, low], axis=0)


def two_products(halves, forms):
    zero = jnp.zeros_like(forms[0])
    top = jnp.concatenate([forms[0], zero], axis=1)
    low = jnp.concatenate([zero, forms[1]], axis=1)
    both = jnp.concatenate([top, low], axis=0)
    part = jnp.dot(jnp.concatenate(halves, axis=1), both, preferred_element_type=jnp.float32)
    width = part.shape[1] // 2
    return part[:, :width].astype(jnp.bfloat16), part[:, width:].astype(jnp.bfloat16)


def merge(piece_refs, pairs_ref):
    at = 0
    for piece in piece_refs:
        pairs_ref[at:at + piece.shape[0]] = piece[...]
        at += piece.shape[0]


def piece_at(r):
    low = sum(ORDER.index(i) << (4 * i) for i in range(7))
    high = sum(ORDER.index(i + 8) << (4 * i) for i in range(7))
    packed = jnp.where(r < 8, low, high) >> (4 * (r & 7))
    end = jnp.where(r < 8, ORDER.index(7), ORDER.index(15))
    return jnp.where(r & 7 == 7, end, packed & 15)


def early_kernel(pair_count, owner_hbm, slot_hbm, half_ref, *refs):
    piece_refs = refs[:-6]
    out_ref, late_ref, pairs_ref, owner_ref, slot_ref, sems = refs[-6:]
    sectors, blocks, tile, width = out_ref.shape
    items, held = sectors * blocks, pairs_ref.shape[0]
    copies = load_all((owner_hbm, owner_ref, sems.at[0]), (slot_hbm, slot_ref, sems.at[1]))
    merge(piece_refs, pairs_ref)
    me = lax.axis_index("sec")
    for copy in copies:
        copy.wait()

    def one(a, listed):
        for k in range(0, blocks, 2):
            forms = []
            for u in range(2):
                owner, slot = owner_ref[a, k + u], slot_ref[a, k + u]
                at = piece_at(owner ^ me) if len(piece_refs) > 1 else owner
                second = slot >= pair_count
                at = at * pair_count + jnp.where(second, slot - pair_count, slot)
                late = at >= held
                forms.append(block_form(pairs_ref[jnp.where(late, 0, at)], second))
                late_ref[listed] = ((at - held) * 2 + second.astype(jnp.int32)) * items + a * blocks + k + u
                listed = listed + late.astype(jnp.int32)
            out_ref[a, k], out_ref[a, k + 1] = two_products([half_ref[a, k], half_ref[a, k + 1]], forms)
        return listed

    listed = lax.fori_loop(0, sectors, one, 0, unroll=2)
    late_ref[items] = listed


def late_kernel(late_ref, early_ref, half_ref, *refs):
    piece_refs, (out_hbm, pairs_ref, out_ref, sems, early_sems) = refs[:-5], refs[-5:]
    sectors, blocks, tile, width = half_ref.shape
    items = sectors * blocks
    early_stores = load_all(*[(early_ref.at[a], out_hbm.at[a], early_sems.at[a]) for a in range(sectors)])
    listed = late_ref[items]
    merge(piece_refs, pairs_ref)

    def store(slot, item):
        return pltpu.make_async_copy(out_ref.at[slot], out_hbm.at[item // blocks, item % blocks], sems.at[slot])

    def group(g, carry):
        for u in range(0, GROUP, 2):
            slot = g * GROUP + u
            entries = [late_ref[jnp.minimum(slot + n, listed - 1)] for n in range(2)]
            halves, forms = [], []
            for entry in entries:
                item, at = entry % items, entry // items
                halves.append(half_ref[item // blocks, item % blocks])
                forms.append(block_form(pairs_ref[at // 2], at % 2 == 1))
            out_ref[slot], out_ref[slot + 1] = two_products(halves, forms)
        return carry

    def place(slot, carry):
        store(slot, late_ref[slot] % items).start()
        return carry

    def drain(slot, carry):
        store(slot, 0).wait()
        return carry

    lax.fori_loop(0, (listed + GROUP - 1) // GROUP, group, 0)
    for early_store in early_stores:
        early_store.wait()
    lax.fori_loop(0, listed, place, 0)
    lax.fori_loop(0, listed, drain, 0)


def swap(piece, bit):
    count = lax.axis_size("sec")
    return lax.ppermute(piece, "sec", [(i, i ^ bit) for i in range(count)])


def per_device(
    psi, left_ops, right_ops, dims_left, dims_right, right_owner, right_slot, term_active
):
    left_count, block_count, tile, width = psi.shape
    items = left_count * block_count
    pair_count = right_ops.shape[0] // 2
    count = lax.axis_size("sec")
    by_swaps = count == len(ORDER)
    flops = 2 * psi.size * tile
    smem = pl.BlockSpec(memory_space=pltpu.SMEM)
    vmem = pl.BlockSpec(memory_space=pltpu.VMEM)
    hbm = pl.BlockSpec(memory_space=pltpu.HBM)
    params = pltpu.CompilerParams(vmem_limit_bytes=VMEM_LIMIT)

    def in_hbm(*arrays):
        return [pltpu.with_memory_space_constraint(array, pltpu.HBM) for array in arrays]

    pairs = pl.pallas_call(
        pack_kernel,
        out_shape=jax.ShapeDtypeStruct((pair_count, tile, 2 * tile), jnp.bfloat16),
        in_specs=[hbm, hbm],
        out_specs=vmem,
        scratch_shapes=[
            pltpu.SMEM(dims_right.shape, jnp.int32),
            pltpu.VMEM(right_ops.shape, jnp.bfloat16),
            pltpu.SemaphoreType.DMA((2,)),
        ],
        compiler_params=params,
        cost_estimate=pl.CostEstimate(flops=0, bytes_accessed=2 * right_ops.size, transcendentals=0),
    )(*in_hbm(dims_right, right_ops))

    def half_of(dims_left):
        active = term_active.reshape(left_count, block_count)
        return pl.pallas_call(
            left_kernel,
            out_shape=jax.ShapeDtypeStruct(psi.shape, jnp.bfloat16),
            in_specs=[hbm] * 4,
            out_specs=vmem,
            scratch_shapes=[
                pltpu.SMEM(dims_left.shape, jnp.int32),
                pltpu.SMEM(active.shape, jnp.int32),
                pltpu.VMEM(left_ops.shape, jnp.bfloat16),
                pltpu.VMEM(psi.shape, jnp.bfloat16),
                pltpu.SemaphoreType.DMA((3,)),
                pltpu.SemaphoreType.DMA((left_count,)),
            ],
            compiler_params=params,
            cost_estimate=pl.CostEstimate(flops=flops, bytes_accessed=2 * psi.size, transcendentals=0),
        )(*in_hbm(dims_left, active, left_ops, psi))

    if by_swaps:
        pieces = {0: pairs}
        def pass_on(*pairs_of):
            for r, bit in pairs_of:
                pieces[r | bit] = swap(pieces[r], bit)

        pass_on((0, FAR), (0, NEAR), (0, CROSS))
        half = half_of(dims_left)
        held = (0, NEAR,)
        half, ends = lax.optimization_barrier((half, [pieces[r] for r in held]))
        pieces.update(zip(held, ends))
        pass_on((NEAR, CROSS), (FAR, NEAR), (FAR, CROSS), (FAR | NEAR, CROSS))
        pass_on((0, CORE), (NEAR, CORE), (CROSS, CORE), (NEAR | CROSS, CORE), (FAR | NEAR, CORE), (FAR, CORE), (FAR | CROSS, CORE))
        early = [pieces[r] for r in EARLY]
    else:
        half = half_of(dims_left)
        early = [lax.all_gather(pairs, "sec", axis=0, tiled=True)]

    sigma, listed = pl.pallas_call(
        functools.partial(early_kernel, pair_count),
        out_shape=(
            jax.ShapeDtypeStruct(psi.shape, jnp.bfloat16),
            pltpu.SMEM((items + 1,), jnp.int32),
        ),
        in_specs=[hbm, hbm] + [vmem] * (1 + len(early)),
        out_specs=(vmem, smem),
        scratch_shapes=[
            pltpu.VMEM((sum(piece.shape[0] for piece in early), tile, 2 * tile), jnp.bfloat16),
            pltpu.SMEM(right_owner.shape, jnp.int32),
            pltpu.SMEM(right_slot.shape, jnp.int32),
            pltpu.SemaphoreType.DMA((2,)),
        ],
        compiler_params=params,
        cost_estimate=pl.CostEstimate(flops=flops, bytes_accessed=2 * psi.size, transcendentals=0),
    )(*in_hbm(right_owner, right_slot), half, *early)
    if by_swaps:
        ends = (FAR | NEAR | CROSS,)
        held, sigma = lax.optimization_barrier(([pieces[r] for r in ends], sigma))
        for r, piece in zip(ends, held):
            pieces[r], pieces[r | CORE] = piece, swap(piece, CORE)
        late = [pieces[r] for r in LATE]
        sigma = pl.pallas_call(
            late_kernel,
            out_shape=jax.ShapeDtypeStruct(psi.shape, jnp.bfloat16),
            in_specs=[smem] + [vmem] * (2 + len(late)),
            out_specs=hbm,
            scratch_shapes=[
                pltpu.VMEM((len(late) * pair_count, tile, 2 * tile), jnp.bfloat16),
                pltpu.VMEM((items + GROUP, tile, width), jnp.bfloat16),
                pltpu.SemaphoreType.DMA((items,)),
                pltpu.SemaphoreType.DMA((left_count,)),
            ],
            compiler_params=params,
            cost_estimate=pl.CostEstimate(flops=flops // 4, bytes_accessed=psi.size, transcendentals=0),
        )(pltpu.with_memory_space_constraint(listed, pltpu.SMEM), sigma, half, *late)
    if lax.axis_size("op") > 1:
        sigma = lax.psum_scatter(sigma, "op", scatter_dimension=3, tiled=True)
    return sigma


def solution(mesh):
    placed = (
        P(("grp", "sec"), None, None, None),
        P(("grp", "sec"), None, "op"),
        P(("grp", "sec"), None, "op"),
        P(("grp", "sec")),
        P(("grp", "sec")),
        P(("grp", "sec"), None),
        P(("grp", "sec"), None),
        P(("grp", "sec"), None, "op"),
    )
    return jax.shard_map(
        per_device,
        mesh=mesh,
        in_specs=placed,
        out_specs=P(("grp", "sec"), None, None, "op"),
        check_vma=False,
    )
```

```python
import functools

import jax
import jax.numpy as jnp
from jax import lax
from jax.experimental import pallas as pl
from jax.experimental.pallas import tpu as pltpu
from jax.sharding import PartitionSpec as P

VMEM_LIMIT = 48 * 1024 * 1024
GROUP = 8
FAR, NEAR, CROSS, CORE = 8, 4, 2, 1
LATE = (NEAR | CROSS | CORE, FAR | CORE, FAR | CROSS | CORE, FAR | NEAR | CROSS, FAR | NEAR | CROSS | CORE)
EARLY = tuple(r for r in range(16) if r not in LATE)
ORDER = EARLY + LATE


def load_all(*copies):
    copies = [pltpu.make_async_copy(*copy) for copy in copies]
    for copy in copies:
        copy.start()
    return copies


def pack_kernel(dims_hbm, right_hbm, pairs_ref, dims_ref, right_ref, sems):
    count, tile, width = pairs_ref.shape
    copies = load_all((dims_hbm, dims_ref, sems.at[0]), (right_hbm, right_ref, sems.at[1]))
    rows = lax.broadcasted_iota(jnp.int32, (tile, tile), 0)
    cols = lax.broadcasted_iota(jnp.int32, (tile, tile), 1)
    most = jnp.maximum(rows, cols)
    for copy in copies:
        copy.wait()

    def kept(b):
        return jnp.where(most < dims_ref[b], right_ref[b].astype(jnp.float32), 0.0)

    for p in range(count):
        both = jnp.concatenate([kept(p), kept(p + count)], axis=0)
        pairs_ref[p] = both.T.astype(jnp.bfloat16)


def left_kernel(dims_hbm, active_hbm, left_hbm, psi_hbm, half_ref, dims_ref, active_ref, left_ref, psi_ref, sems, psi_sems):
    sectors, blocks, tile, width = psi_ref.shape
    copies = load_all(
        (dims_hbm, dims_ref, sems.at[0]),
        (active_hbm, active_ref, sems.at[1]),
        (left_hbm, left_ref, sems.at[2]),
    )
    psi_copies = load_all(*[(psi_hbm.at[a], psi_ref.at[a], psi_sems.at[a]) for a in range(sectors)])
    rows = lax.broadcasted_iota(jnp.int32, (tile, tile), 0)
    cols = lax.broadcasted_iota(jnp.int32, (tile, tile), 1)
    most = jnp.maximum(rows, cols)
    for copy in copies:
        copy.wait()
    for a in range(sectors):
        psi_copies[a].wait()
        op = jnp.where(most < dims_ref[a], left_ref[a].astype(jnp.float32), 0.0).astype(jnp.bfloat16)
        for k in range(0, blocks, 2):
            both = jnp.concatenate([psi_ref[a, k], psi_ref[a, k + 1]], axis=1)
            part = jnp.dot(op, both, preferred_element_type=jnp.float32)
            for u in range(2):
                active = active_ref[a, k + u].astype(jnp.float32)
                half_ref[a, k + u] = (part[:, u * width:(u + 1) * width] * active).astype(jnp.bfloat16)


def block_form(pair, second):
    tile, width = pair.shape
    lower = (lax.broadcasted_iota(jnp.int32, pair.shape, 1) < tile).astype(jnp.bfloat16)
    other = pltpu.roll(pair, tile, 1)
    top = jnp.where(second, other, pair) * lower
    low = jnp.where(second, pair, other) * (1 - lower)
    return jnp.concatenate([top, low], axis=0)


def two_products(halves, forms):
    zero = jnp.zeros_like(forms[0])
    top = jnp.concatenate([forms[0], zero], axis=1)
    low = jnp.concatenate([zero, forms[1]], axis=1)
    both = jnp.concatenate([top, low], axis=0)
    part = jnp.dot(jnp.concatenate(halves, axis=1), both, preferred_element_type=jnp.float32)
    width = part.shape[1] // 2
    return part[:, :width].astype(jnp.bfloat16), part[:, width:].astype(jnp.bfloat16)


def merge(piece_refs, pairs_ref):
    at = 0
    for piece in piece_refs:
        pairs_ref[at:at + piece.shape[0]] = piece[...]
        at += piece.shape[0]


def piece_at(r):
    low = sum(ORDER.index(i) << (4 * i) for i in range(7))
    high = sum(ORDER.index(i + 8) << (4 * i) for i in range(7))
    packed = jnp.where(r < 8, low, high) >> (4 * (r & 7))
    end = jnp.where(r < 8, ORDER.index(7), ORDER.index(15))
    return jnp.where(r & 7 == 7, end, packed & 15)


def early_kernel(pair_count, owner_hbm, slot_hbm, half_ref, *refs):
    piece_refs = refs[:-6]
    out_ref, late_ref, pairs_ref, owner_ref, slot_ref, sems = refs[-6:]
    sectors, blocks, tile, width = out_ref.shape
    items, held = sectors * blocks, pairs_ref.shape[0]
    copies = load_all((owner_hbm, owner_ref, sems.at[0]), (slot_hbm, slot_ref, sems.at[1]))
    merge(piece_refs, pairs_ref)
    me = lax.axis_index("sec")
    for copy in copies:
        copy.wait()

    def one(a, listed):
        for k in range(0, blocks, 2):
            forms = []
            for u in range(2):
                owner, slot = owner_ref[a, k + u], slot_ref[a, k + u]
                at = piece_at(owner ^ me) if len(piece_refs) > 1 else owner
                second = slot >= pair_count
                at = at * pair_count + jnp.where(second, slot - pair_count, slot)
                late = at >= held
                forms.append(block_form(pairs_ref[jnp.where(late, 0, at)], second))
                late_ref[listed] = ((at - held) * 2 + second.astype(jnp.int32)) * items + a * blocks + k + u
                listed = listed + late.astype(jnp.int32)
            out_ref[a, k], out_ref[a, k + 1] = two_products([half_ref[a, k], half_ref[a, k + 1]], forms)
        return listed

    listed = lax.fori_loop(0, sectors, one, 0, unroll=2)
    late_ref[items] = listed


def late_kernel(late_ref, early_ref, half_ref, *refs):
    piece_refs, (out_hbm, pairs_ref, out_ref, sems, early_sems) = refs[:-5], refs[-5:]
    sectors, blocks, tile, width = half_ref.shape
    items = sectors * blocks
    early_stores = load_all(*[(early_ref.at[a], out_hbm.at[a], early_sems.at[a]) for a in range(sectors)])
    listed = late_ref[items]
    merge(piece_refs, pairs_ref)

    def store(slot, item):
        return pltpu.make_async_copy(out_ref.at[slot], out_hbm.at[item // blocks, item % blocks], sems.at[slot])

    def group(g, carry):
        for u in range(0, GROUP, 2):
            slot = g * GROUP + u
            entries = [late_ref[jnp.minimum(slot + n, listed - 1)] for n in range(2)]
            halves, forms = [], []
            for entry in entries:
                item, at = entry % items, entry // items
                halves.append(half_ref[item // blocks, item % blocks])
                forms.append(block_form(pairs_ref[at // 2], at % 2 == 1))
            out_ref[slot], out_ref[slot + 1] = two_products(halves, forms)
        return carry

    def place(slot, carry):
        store(slot, late_ref[slot] % items).start()
        return carry

    def drain(slot, carry):
        store(slot, 0).wait()
        return carry

    lax.fori_loop(0, (listed + GROUP - 1) // GROUP, group, 0)
    for early_store in early_stores:
        early_store.wait()
    lax.fori_loop(0, listed, place, 0)
    lax.fori_loop(0, listed, drain, 0)


def swap(piece, bit):
    count = lax.axis_size("sec")
    return lax.ppermute(piece, "sec", [(i, i ^ bit) for i in range(count)])


def per_device(
    psi, left_ops, right_ops, dims_left, dims_right, right_owner, right_slot, term_active
):
    left_count, block_count, tile, width = psi.shape
    items = left_count * block_count
    pair_count = right_ops.shape[0] // 2
    count = lax.axis_size("sec")
    by_swaps = count == len(ORDER)
    flops = 2 * psi.size * tile
    smem = pl.BlockSpec(memory_space=pltpu.SMEM)
    vmem = pl.BlockSpec(memory_space=pltpu.VMEM)
    hbm = pl.BlockSpec(memory_space=pltpu.HBM)
    params = pltpu.CompilerParams(vmem_limit_bytes=VMEM_LIMIT)

    def in_hbm(*arrays):
        return [pltpu.with_memory_space_constraint(array, pltpu.HBM) for array in arrays]

    pairs = pl.pallas_call(
        pack_kernel,
        out_shape=jax.ShapeDtypeStruct((pair_count, tile, 2 * tile), jnp.bfloat16),
        in_specs=[hbm, hbm],
        out_specs=vmem,
        scratch_shapes=[
            pltpu.SMEM(dims_right.shape, jnp.int32),
            pltpu.VMEM(right_ops.shape, jnp.bfloat16),
            pltpu.SemaphoreType.DMA((2,)),
        ],
        compiler_params=params,
        cost_estimate=pl.CostEstimate(flops=0, bytes_accessed=2 * right_ops.size, transcendentals=0),
    )(*in_hbm(dims_right, right_ops))

    def half_of(dims_left):
        active = term_active.reshape(left_count, block_count)
        return pl.pallas_call(
            left_kernel,
            out_shape=jax.ShapeDtypeStruct(psi.shape, jnp.bfloat16),
            in_specs=[hbm] * 4,
            out_specs=vmem,
            scratch_shapes=[
                pltpu.SMEM(dims_left.shape, jnp.int32),
                pltpu.SMEM(active.shape, jnp.int32),
                pltpu.VMEM(left_ops.shape, jnp.bfloat16),
                pltpu.VMEM(psi.shape, jnp.bfloat16),
                pltpu.SemaphoreType.DMA((3,)),
                pltpu.SemaphoreType.DMA((left_count,)),
            ],
            compiler_params=params,
            cost_estimate=pl.CostEstimate(flops=flops, bytes_accessed=2 * psi.size, transcendentals=0),
        )(*in_hbm(dims_left, active, left_ops, psi))

    if by_swaps:
        pieces = {0: pairs}
        def pass_on(*pairs_of):
            for r, bit in pairs_of:
                pieces[r | bit] = swap(pieces[r], bit)

        pass_on((0, FAR), (0, CORE), (0, CROSS))
        held = (CORE,)
        pieces[0], ends = lax.optimization_barrier((pieces[0], [pieces[r] for r in held]))
        pieces.update(zip(held, ends))
        pieces[NEAR] = swap(pieces[0], NEAR)
        half = half_of(dims_left)
        held = (FAR, NEAR,)
        half, ends = lax.optimization_barrier((half, [pieces[r] for r in held]))
        pieces.update(zip(held, ends))
        pass_on((NEAR, CROSS), (FAR, NEAR), (FAR, CROSS), (FAR | NEAR, CROSS))
        pass_on((NEAR, CORE), (CROSS, CORE), (NEAR | CROSS, CORE), (FAR | NEAR, CORE), (FAR, CORE), (FAR | CROSS, CORE))
        early = [pieces[r] for r in EARLY]
    else:
        half = half_of(dims_left)
        early = [lax.all_gather(pairs, "sec", axis=0, tiled=True)]

    sigma, listed = pl.pallas_call(
        functools.partial(early_kernel, pair_count),
        out_shape=(
            jax.ShapeDtypeStruct(psi.shape, jnp.bfloat16),
            pltpu.SMEM((items + 1,), jnp.int32),
        ),
        in_specs=[hbm, hbm] + [vmem] * (1 + len(early)),
        out_specs=(vmem, smem),
        scratch_shapes=[
            pltpu.VMEM((sum(piece.shape[0] for piece in early), tile, 2 * tile), jnp.bfloat16),
            pltpu.SMEM(right_owner.shape, jnp.int32),
            pltpu.SMEM(right_slot.shape, jnp.int32),
            pltpu.SemaphoreType.DMA((2,)),
        ],
        compiler_params=params,
        cost_estimate=pl.CostEstimate(flops=flops, bytes_accessed=2 * psi.size, transcendentals=0),
    )(*in_hbm(right_owner, right_slot), half, *early)
    if by_swaps:
        ends = (FAR | NEAR | CROSS,)
        held, sigma = lax.optimization_barrier(([pieces[r] for r in ends], sigma))
        for r, piece in zip(ends, held):
            pieces[r], pieces[r | CORE] = piece, swap(piece, CORE)
        late = [pieces[r] for r in LATE]
        sigma = pl.pallas_call(
            late_kernel,
            out_shape=jax.ShapeDtypeStruct(psi.shape, jnp.bfloat16),
            in_specs=[smem] + [vmem] * (2 + len(late)),
            out_specs=hbm,
            scratch_shapes=[
                pltpu.VMEM((len(late) * pair_count, tile, 2 * tile), jnp.bfloat16),
                pltpu.VMEM((items + GROUP, tile, width), jnp.bfloat16),
                pltpu.SemaphoreType.DMA((items,)),
                pltpu.SemaphoreType.DMA((left_count,)),
            ],
            compiler_params=params,
            cost_estimate=pl.CostEstimate(flops=flops // 4, bytes_accessed=psi.size, transcendentals=0),
        )(pltpu.with_memory_space_constraint(listed, pltpu.SMEM), sigma, half, *late)
    if lax.axis_size("op") > 1:
        sigma = lax.psum_scatter(sigma, "op", scatter_dimension=3, tiled=True)
    return sigma


def solution(mesh):
    placed = (
        P(("grp", "sec"), None, None, None),
        P(("grp", "sec"), None, "op"),
        P(("grp", "sec"), None, "op"),
        P(("grp", "sec")),
        P(("grp", "sec")),
        P(("grp", "sec"), None),
        P(("grp", "sec"), None),
        P(("grp", "sec"), None, "op"),
    )
    return jax.shard_map(
        per_device,
        mesh=mesh,
        in_specs=placed,
        out_specs=P(("grp", "sec"), None, None, "op"),
        check_vma=False,
    )
```

```python
import functools

import jax
import jax.numpy as jnp
from jax import lax
from jax.experimental import pallas as pl
from jax.experimental.pallas import tpu as pltpu
from jax.sharding import PartitionSpec as P

VMEM_LIMIT = 48 * 1024 * 1024
GROUP = 8
FAR, NEAR, CROSS, CORE = 8, 4, 2, 1
OWN, SIDE = (0, 0), (CROSS, CROSS)
FIRST, SECOND = (FAR, NEAR), (NEAR, FAR)
THIRD, FOURTH, FIFTH = (FAR | NEAR, NEAR | CROSS), (NEAR | CROSS, FAR | CROSS), (FAR | CROSS, FAR | NEAR)
LAST = (FAR | NEAR | CROSS, FAR | NEAR | CROSS)


def partner(name):
    return name[1] | CORE, name[0] | CORE


LATE = (partner(SIDE), partner(THIRD), partner(FOURTH), partner(FIFTH), LAST, partner(LAST))
EARLY = tuple(name for name in (
    OWN, SIDE, FIRST, SECOND, THIRD, FOURTH, FIFTH,
    partner(OWN), partner(SIDE), partner(FIRST), partner(SECOND), partner(THIRD), partner(FOURTH), partner(FIFTH),
) if name not in LATE)
ORDER = EARLY + LATE


def load_all(*copies):
    copies = [pltpu.make_async_copy(*copy) for copy in copies]
    for copy in copies:
        copy.start()
    return copies


def pack_kernel(dims_hbm, right_hbm, pairs_ref, dims_ref, right_ref, sems):
    count, tile, width = pairs_ref.shape
    copies = load_all((dims_hbm, dims_ref, sems.at[0]), (right_hbm, right_ref, sems.at[1]))
    rows = lax.broadcasted_iota(jnp.int32, (tile, tile), 0)
    cols = lax.broadcasted_iota(jnp.int32, (tile, tile), 1)
    most = jnp.maximum(rows, cols)
    for copy in copies:
        copy.wait()

    def kept(b):
        return jnp.where(most < dims_ref[b], right_ref[b].astype(jnp.float32), 0.0)

    for p in range(count):
        both = jnp.concatenate([kept(p), kept(p + count)], axis=0)
        pairs_ref[p] = both.T.astype(jnp.bfloat16)


def left_kernel(dims_hbm, active_hbm, left_hbm, psi_hbm, half_ref, dims_ref, active_ref, left_ref, psi_ref, sems, psi_sems):
    sectors, blocks, tile, width = psi_ref.shape
    copies = load_all(
        (dims_hbm, dims_ref, sems.at[0]),
        (active_hbm, active_ref, sems.at[1]),
        (left_hbm, left_ref, sems.at[2]),
    )
    psi_copies = load_all(*[(psi_hbm.at[a], psi_ref.at[a], psi_sems.at[a]) for a in range(sectors)])
    rows = lax.broadcasted_iota(jnp.int32, (tile, tile), 0)
    cols = lax.broadcasted_iota(jnp.int32, (tile, tile), 1)
    most = jnp.maximum(rows, cols)
    for copy in copies:
        copy.wait()
    for a in range(sectors):
        psi_copies[a].wait()
        op = jnp.where(most < dims_ref[a], left_ref[a].astype(jnp.float32), 0.0).astype(jnp.bfloat16)
        for k in range(0, blocks, 2):
            both = jnp.concatenate([psi_ref[a, k], psi_ref[a, k + 1]], axis=1)
            part = jnp.dot(op, both, preferred_element_type=jnp.float32)
            for u in range(2):
                active = active_ref[a, k + u].astype(jnp.float32)
                half_ref[a, k + u] = (part[:, u * width:(u + 1) * width] * active).astype(jnp.bfloat16)


def block_form(pair, second):
    tile, width = pair.shape
    lower = (lax.broadcasted_iota(jnp.int32, pair.shape, 1) < tile).astype(jnp.bfloat16)
    other = pltpu.roll(pair, tile, 1)
    top = jnp.where(second, other, pair) * lower
    low = jnp.where(second, pair, other) * (1 - lower)
    return jnp.concatenate([top, low], axis=0)


def two_products(halves, forms):
    zero = jnp.zeros_like(forms[0])
    top = jnp.concatenate([forms[0], zero], axis=1)
    low = jnp.concatenate([zero, forms[1]], axis=1)
    both = jnp.concatenate([top, low], axis=0)
    part = jnp.dot(jnp.concatenate(halves, axis=1), both, preferred_element_type=jnp.float32)
    width = part.shape[1] // 2
    return part[:, :width].astype(jnp.bfloat16), part[:, width:].astype(jnp.bfloat16)


def merge(piece_refs, pairs_ref):
    at = 0
    for piece in piece_refs:
        pairs_ref[at:at + piece.shape[0]] = piece[...]
        at += piece.shape[0]


def piece_at(r, me):
    places = [[0] * len(ORDER), [0] * len(ORDER)]
    for at, name in enumerate(ORDER):
        places[0][name[0]], places[1][name[1]] = at, at
    at = jnp.int32(0)
    for parity in range(2):
        for half in range(2):
            packed = sum(place << (4 * i) for i, place in enumerate(places[parity][8 * half:8 * half + 7]))
            mine = jnp.where(r & 7 == 7, places[parity][8 * half + 7], (packed >> (4 * (r & 7))) & 15)
            at = jnp.where((me & 1 == parity) & (r >> 3 == half), mine, at)
    return at


def early_kernel(pair_count, owner_hbm, slot_hbm, half_ref, *refs):
    piece_refs = refs[:-6]
    out_ref, late_ref, pairs_ref, owner_ref, slot_ref, sems = refs[-6:]
    sectors, blocks, tile, width = out_ref.shape
    items, held = sectors * blocks, pairs_ref.shape[0]
    copies = load_all((owner_hbm, owner_ref, sems.at[0]), (slot_hbm, slot_ref, sems.at[1]))
    merge(piece_refs, pairs_ref)
    me = lax.axis_index("sec")
    for copy in copies:
        copy.wait()

    def one(a, listed):
        for k in range(0, blocks, 2):
            forms = []
            for u in range(2):
                owner, slot = owner_ref[a, k + u], slot_ref[a, k + u]
                at = piece_at(owner ^ me, me) if len(piece_refs) > 1 else owner
                second = slot >= pair_count
                at = at * pair_count + jnp.where(second, slot - pair_count, slot)
                late = at >= held
                forms.append(block_form(pairs_ref[jnp.where(late, 0, at)], second))
                late_ref[listed] = ((at - held) * 2 + second.astype(jnp.int32)) * items + a * blocks + k + u
                listed = listed + late.astype(jnp.int32)
            out_ref[a, k], out_ref[a, k + 1] = two_products([half_ref[a, k], half_ref[a, k + 1]], forms)
        return listed

    listed = lax.fori_loop(0, sectors, one, 0, unroll=2)
    late_ref[items] = listed


def late_kernel(late_ref, early_ref, half_ref, *refs):
    piece_refs, (out_hbm, pairs_ref, out_ref, sems, early_sems) = refs[:-5], refs[-5:]
    sectors, blocks, tile, width = half_ref.shape
    items = sectors * blocks
    early_stores = load_all(*[(early_ref.at[a], out_hbm.at[a], early_sems.at[a]) for a in range(sectors)])
    listed = late_ref[items]
    merge(piece_refs, pairs_ref)

    def store(slot, item):
        return pltpu.make_async_copy(out_ref.at[slot], out_hbm.at[item // blocks, item % blocks], sems.at[slot])

    def group(g, carry):
        for u in range(0, GROUP, 2):
            slot = g * GROUP + u
            entries = [late_ref[jnp.minimum(slot + n, listed - 1)] for n in range(2)]
            halves, forms = [], []
            for entry in entries:
                item, at = entry % items, entry // items
                halves.append(half_ref[item // blocks, item % blocks])
                forms.append(block_form(pairs_ref[at // 2], at % 2 == 1))
            out_ref[slot], out_ref[slot + 1] = two_products(halves, forms)
        return carry

    def place(slot, carry):
        store(slot, late_ref[slot] % items).start()
        return carry

    def drain(slot, carry):
        store(slot, 0).wait()
        return carry

    lax.fori_loop(0, (listed + GROUP - 1) // GROUP, group, 0)
    for early_store in early_stores:
        early_store.wait()
    lax.fori_loop(0, listed, place, 0)
    lax.fori_loop(0, listed, drain, 0)


def swap(piece, even_bit, odd_bit):
    count = lax.axis_size("sec")
    return lax.ppermute(piece, "sec", [(i, i ^ (odd_bit if i & CORE else even_bit)) for i in range(count)])


def per_device(
    psi, left_ops, right_ops, dims_left, dims_right, right_owner, right_slot, term_active
):
    left_count, block_count, tile, width = psi.shape
    items = left_count * block_count
    pair_count = right_ops.shape[0] // 2
    count = lax.axis_size("sec")
    by_swaps = count == len(ORDER)
    flops = 2 * psi.size * tile
    smem = pl.BlockSpec(memory_space=pltpu.SMEM)
    vmem = pl.BlockSpec(memory_space=pltpu.VMEM)
    hbm = pl.BlockSpec(memory_space=pltpu.HBM)
    params = pltpu.CompilerParams(vmem_limit_bytes=VMEM_LIMIT)

    def in_hbm(*arrays):
        return [pltpu.with_memory_space_constraint(array, pltpu.HBM) for array in arrays]

    pairs = pl.pallas_call(
        pack_kernel,
        out_shape=jax.ShapeDtypeStruct((pair_count, tile, 2 * tile), jnp.bfloat16),
        in_specs=[hbm, hbm],
        out_specs=vmem,
        scratch_shapes=[
            pltpu.SMEM(dims_right.shape, jnp.int32),
            pltpu.VMEM(right_ops.shape, jnp.bfloat16),
            pltpu.SemaphoreType.DMA((2,)),
        ],
        compiler_params=params,
        cost_estimate=pl.CostEstimate(flops=0, bytes_accessed=2 * right_ops.size, transcendentals=0),
    )(*in_hbm(dims_right, right_ops))

    def half_of(dims_left):
        active = term_active.reshape(left_count, block_count)
        return pl.pallas_call(
            left_kernel,
            out_shape=jax.ShapeDtypeStruct(psi.shape, jnp.bfloat16),
            in_specs=[hbm] * 4,
            out_specs=vmem,
            scratch_shapes=[
                pltpu.SMEM(dims_left.shape, jnp.int32),
                pltpu.SMEM(active.shape, jnp.int32),
                pltpu.VMEM(left_ops.shape, jnp.bfloat16),
                pltpu.VMEM(psi.shape, jnp.bfloat16),
                pltpu.SemaphoreType.DMA((3,)),
                pltpu.SemaphoreType.DMA((left_count,)),
            ],
            compiler_params=params,
            cost_estimate=pl.CostEstimate(flops=flops, bytes_accessed=2 * psi.size, transcendentals=0),
        )(*in_hbm(dims_left, active, left_ops, psi))

    if by_swaps:
        pieces = {OWN: pairs}

        def pass_on(*routes):
            for name, target in routes:
                pieces[target] = swap(pieces[name], name[0] ^ target[0], name[1] ^ target[1])

        def share(*names):
            for name in names:
                pieces[partner(name)] = swap(pieces[name], CORE, CORE)

        pass_on((OWN, FIRST), (OWN, SECOND), (OWN, SIDE))
        half = half_of(dims_left)
        held = (SECOND,)
        half, ends = lax.optimization_barrier((half, [pieces[r] for r in held]))
        pieces.update(zip(held, ends))
        pass_on((FIRST, THIRD), (SECOND, FOURTH), (FIRST, FIFTH), (THIRD, LAST))
        share(OWN, SIDE, FIRST, SECOND, THIRD, FOURTH, FIFTH)
        early = [pieces[name] for name in EARLY]
    else:
        half = half_of(dims_left)
        early = [lax.all_gather(pairs, "sec", axis=0, tiled=True)]

    sigma, listed = pl.pallas_call(
        functools.partial(early_kernel, pair_count),
        out_shape=(
            jax.ShapeDtypeStruct(psi.shape, jnp.bfloat16),
            pltpu.SMEM((items + 1,), jnp.int32),
        ),
        in_specs=[hbm, hbm] + [vmem] * (1 + len(early)),
        out_specs=(vmem, smem),
        scratch_shapes=[
            pltpu.VMEM((sum(piece.shape[0] for piece in early), tile, 2 * tile), jnp.bfloat16),
            pltpu.SMEM(right_owner.shape, jnp.int32),
            pltpu.SMEM(right_slot.shape, jnp.int32),
            pltpu.SemaphoreType.DMA((2,)),
        ],
        compiler_params=params,
        cost_estimate=pl.CostEstimate(flops=flops, bytes_accessed=2 * psi.size, transcendentals=0),
    )(*in_hbm(right_owner, right_slot), half, *early)
    if by_swaps:
        ends = (LAST,)
        held, sigma = lax.optimization_barrier(([pieces[name] for name in ends], sigma))
        pieces.update(zip(ends, held))
        share(*ends)
        late = [pieces[name] for name in LATE]
        sigma = pl.pallas_call(
            late_kernel,
            out_shape=jax.ShapeDtypeStruct(psi.shape, jnp.bfloat16),
            in_specs=[smem] + [vmem] * (2 + len(late)),
            out_specs=hbm,
            scratch_shapes=[
                pltpu.VMEM((len(late) * pair_count, tile, 2 * tile), jnp.bfloat16),
                pltpu.VMEM((items + GROUP, tile, width), jnp.bfloat16),
                pltpu.SemaphoreType.DMA((items,)),
                pltpu.SemaphoreType.DMA((left_count,)),
            ],
            compiler_params=params,
            cost_estimate=pl.CostEstimate(flops=flops // 4, bytes_accessed=psi.size, transcendentals=0),
        )(pltpu.with_memory_space_constraint(listed, pltpu.SMEM), sigma, half, *late)
    if lax.axis_size("op") > 1:
        sigma = lax.psum_scatter(sigma, "op", scatter_dimension=3, tiled=True)
    return sigma


def solution(mesh):
    placed = (
        P(("grp", "sec"), None, None, None),
        P(("grp", "sec"), None, "op"),
        P(("grp", "sec"), None, "op"),
        P(("grp", "sec")),
        P(("grp", "sec")),
        P(("grp", "sec"), None),
        P(("grp", "sec"), None),
        P(("grp", "sec"), None, "op"),
    )
    return jax.shard_map(
        per_device,
        mesh=mesh,
        in_specs=placed,
        out_specs=P(("grp", "sec"), None, None, "op"),
        check_vma=False,
    )
```

```python
import functools

import jax
import jax.numpy as jnp
from jax import lax
from jax.experimental import pallas as pl
from jax.experimental.pallas import tpu as pltpu
from jax.sharding import PartitionSpec as P

VMEM_LIMIT = 48 * 1024 * 1024
GROUP = 8
FAR, NEAR, CROSS, CORE = 8, 4, 2, 1
OWN, SIDE = (0, 0), (CROSS, CROSS)
FIRST, SECOND = (FAR, NEAR), (NEAR, FAR)
THIRD, FOURTH, FIFTH = (FAR | NEAR, NEAR | CROSS), (NEAR | CROSS, FAR | CROSS), (FAR | CROSS, FAR | NEAR)
LAST = (FAR | NEAR | CROSS, FAR | NEAR | CROSS)


def partner(name):
    return name[1] | CORE, name[0] | CORE


LATE = (partner(SECOND), partner(THIRD), partner(FOURTH), partner(FIFTH), LAST, partner(LAST))
EARLY = tuple(name for name in (
    OWN, SIDE, FIRST, SECOND, THIRD, FOURTH, FIFTH,
    partner(OWN), partner(SIDE), partner(FIRST), partner(SECOND), partner(THIRD), partner(FOURTH), partner(FIFTH),
) if name not in LATE)
ORDER = EARLY + LATE


def load_all(*copies):
    copies = [pltpu.make_async_copy(*copy) for copy in copies]
    for copy in copies:
        copy.start()
    return copies


def pack_kernel(dims_hbm, right_hbm, pairs_ref, dims_ref, right_ref, sems):
    count, tile, width = pairs_ref.shape
    copies = load_all((dims_hbm, dims_ref, sems.at[0]), (right_hbm, right_ref, sems.at[1]))
    rows = lax.broadcasted_iota(jnp.int32, (tile, tile), 0)
    cols = lax.broadcasted_iota(jnp.int32, (tile, tile), 1)
    most = jnp.maximum(rows, cols)
    for copy in copies:
        copy.wait()

    def kept(b):
        return jnp.where(most < dims_ref[b], right_ref[b].astype(jnp.float32), 0.0)

    for p in range(count):
        both = jnp.concatenate([kept(p), kept(p + count)], axis=0)
        pairs_ref[p] = both.T.astype(jnp.bfloat16)


def left_kernel(dims_hbm, active_hbm, left_hbm, psi_hbm, half_ref, dims_ref, active_ref, left_ref, psi_ref, sems, psi_sems):
    sectors, blocks, tile, width = psi_ref.shape
    copies = load_all(
        (dims_hbm, dims_ref, sems.at[0]),
        (active_hbm, active_ref, sems.at[1]),
        (left_hbm, left_ref, sems.at[2]),
    )
    psi_copies = load_all(*[(psi_hbm.at[a], psi_ref.at[a], psi_sems.at[a]) for a in range(sectors)])
    rows = lax.broadcasted_iota(jnp.int32, (tile, tile), 0)
    cols = lax.broadcasted_iota(jnp.int32, (tile, tile), 1)
    most = jnp.maximum(rows, cols)
    for copy in copies:
        copy.wait()
    for a in range(sectors):
        psi_copies[a].wait()
        op = jnp.where(most < dims_ref[a], left_ref[a].astype(jnp.float32), 0.0).astype(jnp.bfloat16)
        for k in range(0, blocks, 2):
            both = jnp.concatenate([psi_ref[a, k], psi_ref[a, k + 1]], axis=1)
            part = jnp.dot(op, both, preferred_element_type=jnp.float32)
            for u in range(2):
                active = active_ref[a, k + u].astype(jnp.float32)
                half_ref[a, k + u] = (part[:, u * width:(u + 1) * width] * active).astype(jnp.bfloat16)


def block_form(pair, second):
    tile, width = pair.shape
    lower = (lax.broadcasted_iota(jnp.int32, pair.shape, 1) < tile).astype(jnp.bfloat16)
    other = pltpu.roll(pair, tile, 1)
    top = jnp.where(second, other, pair) * lower
    low = jnp.where(second, pair, other) * (1 - lower)
    return jnp.concatenate([top, low], axis=0)


def two_products(halves, forms):
    zero = jnp.zeros_like(forms[0])
    top = jnp.concatenate([forms[0], zero], axis=1)
    low = jnp.concatenate([zero, forms[1]], axis=1)
    both = jnp.concatenate([top, low], axis=0)
    part = jnp.dot(jnp.concatenate(halves, axis=1), both, preferred_element_type=jnp.float32)
    width = part.shape[1] // 2
    return part[:, :width].astype(jnp.bfloat16), part[:, width:].astype(jnp.bfloat16)


def merge(piece_refs, pairs_ref):
    at = 0
    for piece in piece_refs:
        pairs_ref[at:at + piece.shape[0]] = piece[...]
        at += piece.shape[0]


def piece_at(r, me):
    places = [[0] * len(ORDER), [0] * len(ORDER)]
    for at, name in enumerate(ORDER):
        places[0][name[0]], places[1][name[1]] = at, at
    at = jnp.int32(0)
    for parity in range(2):
        for half in range(2):
            packed = sum(place << (4 * i) for i, place in enumerate(places[parity][8 * half:8 * half + 7]))
            mine = jnp.where(r & 7 == 7, places[parity][8 * half + 7], (packed >> (4 * (r & 7))) & 15)
            at = jnp.where((me & 1 == parity) & (r >> 3 == half), mine, at)
    return at


def early_kernel(pair_count, owner_hbm, slot_hbm, half_ref, *refs):
    piece_refs = refs[:-6]
    out_ref, late_ref, pairs_ref, owner_ref, slot_ref, sems = refs[-6:]
    sectors, blocks, tile, width = out_ref.shape
    items, held = sectors * blocks, pairs_ref.shape[0]
    copies = load_all((owner_hbm, owner_ref, sems.at[0]), (slot_hbm, slot_ref, sems.at[1]))
    merge(piece_refs, pairs_ref)
    me = lax.axis_index("sec")
    for copy in copies:
        copy.wait()

    def one(a, listed):
        for k in range(0, blocks, 2):
            forms = []
            for u in range(2):
                owner, slot = owner_ref[a, k + u], slot_ref[a, k + u]
                at = piece_at(owner ^ me, me) if len(piece_refs) > 1 else owner
                second = slot >= pair_count
                at = at * pair_count + jnp.where(second, slot - pair_count, slot)
                late = at >= held
                forms.append(block_form(pairs_ref[jnp.where(late, 0, at)], second))
                late_ref[listed] = ((at - held) * 2 + second.astype(jnp.int32)) * items + a * blocks + k + u
                listed = listed + late.astype(jnp.int32)
            out_ref[a, k], out_ref[a, k + 1] = two_products([half_ref[a, k], half_ref[a, k + 1]], forms)
        return listed

    listed = lax.fori_loop(0, sectors, one, 0, unroll=2)
    late_ref[items] = listed


def late_kernel(late_ref, early_ref, half_ref, *refs):
    piece_refs, (out_hbm, pairs_ref, out_ref, sems, early_sems) = refs[:-5], refs[-5:]
    sectors, blocks, tile, width = half_ref.shape
    items = sectors * blocks
    early_stores = load_all(*[(early_ref.at[a], out_hbm.at[a], early_sems.at[a]) for a in range(sectors)])
    listed = late_ref[items]
    merge(piece_refs, pairs_ref)

    def store(slot, item):
        return pltpu.make_async_copy(out_ref.at[slot], out_hbm.at[item // blocks, item % blocks], sems.at[slot])

    def group(g, carry):
        for u in range(0, GROUP, 2):
            slot = g * GROUP + u
            entries = [late_ref[jnp.minimum(slot + n, listed - 1)] for n in range(2)]
            halves, forms = [], []
            for entry in entries:
                item, at = entry % items, entry // items
                halves.append(half_ref[item // blocks, item % blocks])
                forms.append(block_form(pairs_ref[at // 2], at % 2 == 1))
            out_ref[slot], out_ref[slot + 1] = two_products(halves, forms)
        return carry

    def place(slot, carry):
        store(slot, late_ref[slot] % items).start()
        return carry

    def drain(slot, carry):
        store(slot, 0).wait()
        return carry

    lax.fori_loop(0, (listed + GROUP - 1) // GROUP, group, 0)
    for early_store in early_stores:
        early_store.wait()
    lax.fori_loop(0, listed, place, 0)
    lax.fori_loop(0, listed, drain, 0)


def swap(piece, even_bit, odd_bit):
    count = lax.axis_size("sec")
    return lax.ppermute(piece, "sec", [(i, i ^ (odd_bit if i & CORE else even_bit)) for i in range(count)])


def per_device(
    psi, left_ops, right_ops, dims_left, dims_right, right_owner, right_slot, term_active
):
    left_count, block_count, tile, width = psi.shape
    items = left_count * block_count
    pair_count = right_ops.shape[0] // 2
    count = lax.axis_size("sec")
    by_swaps = count == len(ORDER)
    flops = 2 * psi.size * tile
    smem = pl.BlockSpec(memory_space=pltpu.SMEM)
    vmem = pl.BlockSpec(memory_space=pltpu.VMEM)
    hbm = pl.BlockSpec(memory_space=pltpu.HBM)
    params = pltpu.CompilerParams(vmem_limit_bytes=VMEM_LIMIT)

    def in_hbm(*arrays):
        return [pltpu.with_memory_space_constraint(array, pltpu.HBM) for array in arrays]

    pairs = pl.pallas_call(
        pack_kernel,
        out_shape=jax.ShapeDtypeStruct((pair_count, tile, 2 * tile), jnp.bfloat16),
        in_specs=[hbm, hbm],
        out_specs=vmem,
        scratch_shapes=[
            pltpu.SMEM(dims_right.shape, jnp.int32),
            pltpu.VMEM(right_ops.shape, jnp.bfloat16),
            pltpu.SemaphoreType.DMA((2,)),
        ],
        compiler_params=params,
        cost_estimate=pl.CostEstimate(flops=0, bytes_accessed=2 * right_ops.size, transcendentals=0),
    )(*in_hbm(dims_right, right_ops))

    def half_of(dims_left):
        active = term_active.reshape(left_count, block_count)
        return pl.pallas_call(
            left_kernel,
            out_shape=jax.ShapeDtypeStruct(psi.shape, jnp.bfloat16),
            in_specs=[hbm] * 4,
            out_specs=vmem,
            scratch_shapes=[
                pltpu.SMEM(dims_left.shape, jnp.int32),
                pltpu.SMEM(active.shape, jnp.int32),
                pltpu.VMEM(left_ops.shape, jnp.bfloat16),
                pltpu.VMEM(psi.shape, jnp.bfloat16),
                pltpu.SemaphoreType.DMA((3,)),
                pltpu.SemaphoreType.DMA((left_count,)),
            ],
            compiler_params=params,
            cost_estimate=pl.CostEstimate(flops=flops, bytes_accessed=2 * psi.size, transcendentals=0),
        )(*in_hbm(dims_left, active, left_ops, psi))

    if by_swaps:
        pieces = {OWN: pairs}

        def pass_on(*routes):
            for name, target in routes:
                pieces[target] = swap(pieces[name], name[0] ^ target[0], name[1] ^ target[1])

        def share(*names):
            for name in names:
                pieces[partner(name)] = swap(pieces[name], CORE, CORE)

        pass_on((OWN, FIRST), (OWN, SECOND), (OWN, SIDE))
        half = half_of(dims_left)
        held = (FIRST,)
        half, ends = lax.optimization_barrier((half, [pieces[r] for r in held]))
        pieces.update(zip(held, ends))
        pass_on((FIRST, THIRD), (SECOND, FOURTH), (FIRST, FIFTH), (THIRD, LAST))
        share(OWN, SIDE, FIRST, SECOND, THIRD, FOURTH, FIFTH)
        early = [pieces[name] for name in EARLY]
    else:
        half = half_of(dims_left)
        early = [lax.all_gather(pairs, "sec", axis=0, tiled=True)]

    sigma, listed = pl.pallas_call(
        functools.partial(early_kernel, pair_count),
        out_shape=(
            jax.ShapeDtypeStruct(psi.shape, jnp.bfloat16),
            pltpu.SMEM((items + 1,), jnp.int32),
        ),
        in_specs=[hbm, hbm] + [vmem] * (1 + len(early)),
        out_specs=(vmem, smem),
        scratch_shapes=[
            pltpu.VMEM((sum(piece.shape[0] for piece in early), tile, 2 * tile), jnp.bfloat16),
            pltpu.SMEM(right_owner.shape, jnp.int32),
            pltpu.SMEM(right_slot.shape, jnp.int32),
            pltpu.SemaphoreType.DMA((2,)),
        ],
        compiler_params=params,
        cost_estimate=pl.CostEstimate(flops=flops, bytes_accessed=2 * psi.size, transcendentals=0),
    )(*in_hbm(right_owner, right_slot), half, *early)
    if by_swaps:
        ends = (LAST,)
        held, sigma = lax.optimization_barrier(([pieces[name] for name in ends], sigma))
        pieces.update(zip(ends, held))
        share(*ends)
        late = [pieces[name] for name in LATE]
        sigma = pl.pallas_call(
            late_kernel,
            out_shape=jax.ShapeDtypeStruct(psi.shape, jnp.bfloat16),
            in_specs=[smem] + [vmem] * (2 + len(late)),
            out_specs=hbm,
            scratch_shapes=[
                pltpu.VMEM((len(late) * pair_count, tile, 2 * tile), jnp.bfloat16),
                pltpu.VMEM((items + GROUP, tile, width), jnp.bfloat16),
                pltpu.SemaphoreType.DMA((items,)),
                pltpu.SemaphoreType.DMA((left_count,)),
            ],
            compiler_params=params,
            cost_estimate=pl.CostEstimate(flops=flops // 4, bytes_accessed=psi.size, transcendentals=0),
        )(pltpu.with_memory_space_constraint(listed, pltpu.SMEM), sigma, half, *late)
    if lax.axis_size("op") > 1:
        sigma = lax.psum_scatter(sigma, "op", scatter_dimension=3, tiled=True)
    return sigma


def solution(mesh):
    placed = (
        P(("grp", "sec"), None, None, None),
        P(("grp", "sec"), None, "op"),
        P(("grp", "sec"), None, "op"),
        P(("grp", "sec")),
        P(("grp", "sec")),
        P(("grp", "sec"), None),
        P(("grp", "sec"), None),
        P(("grp", "sec"), None, "op"),
    )
    return jax.shard_map(
        per_device,
        mesh=mesh,
        in_specs=placed,
        out_specs=P(("grp", "sec"), None, None, "op"),
        check_vma=False,
    )
```

```python
import functools

import jax
import jax.numpy as jnp
from jax import lax
from jax.experimental import pallas as pl
from jax.experimental.pallas import tpu as pltpu
from jax.sharding import PartitionSpec as P

VMEM_LIMIT = 48 * 1024 * 1024
FAR, NEAR, CROSS, CORE = 8, 4, 2, 1
MIDDLE = (FAR | CORE, FAR | NEAR | CORE, FAR | CROSS | CORE, FAR | NEAR | CROSS)
LAST = (FAR | NEAR | CROSS | CORE,)
EARLY = tuple(r for r in range(16) if r not in MIDDLE + LAST)
ORDER = EARLY + MIDDLE + LAST


def load_all(*copies):
    copies = [pltpu.make_async_copy(*copy) for copy in copies]
    for copy in copies:
        copy.start()
    return copies


def pack_kernel(dims_hbm, right_hbm, pairs_ref, dims_ref, right_ref, sems):
    count, tile, width = pairs_ref.shape
    copies = load_all((dims_hbm, dims_ref, sems.at[0]), (right_hbm, right_ref, sems.at[1]))
    rows = lax.broadcasted_iota(jnp.int32, (tile, tile), 0)
    cols = lax.broadcasted_iota(jnp.int32, (tile, tile), 1)
    most = jnp.maximum(rows, cols)
    for copy in copies:
        copy.wait()

    def kept(b):
        return jnp.where(most < dims_ref[b], right_ref[b].astype(jnp.float32), 0.0)

    for p in range(count):
        both = jnp.concatenate([kept(p), kept(p + count)], axis=0)
        pairs_ref[p] = both.T.astype(jnp.bfloat16)


def left_kernel(dims_hbm, active_hbm, left_hbm, psi_hbm, half_ref, dims_ref, active_ref, left_ref, psi_ref, sems, psi_sems):
    sectors, blocks, tile, width = psi_ref.shape
    copies = load_all(
        (dims_hbm, dims_ref, sems.at[0]),
        (active_hbm, active_ref, sems.at[1]),
        (left_hbm, left_ref, sems.at[2]),
    )
    psi_copies = load_all(*[(psi_hbm.at[a], psi_ref.at[a], psi_sems.at[a]) for a in range(sectors)])
    rows = lax.broadcasted_iota(jnp.int32, (tile, tile), 0)
    cols = lax.broadcasted_iota(jnp.int32, (tile, tile), 1)
    most = jnp.maximum(rows, cols)
    for copy in copies:
        copy.wait()
    for a in range(sectors):
        psi_copies[a].wait()
        op = jnp.where(most < dims_ref[a], left_ref[a].astype(jnp.float32), 0.0).astype(jnp.bfloat16)
        for k in range(0, blocks, 2):
            both = jnp.concatenate([psi_ref[a, k], psi_ref[a, k + 1]], axis=1)
            part = jnp.dot(op, both, preferred_element_type=jnp.float32)
            for u in range(2):
                active = active_ref[a, k + u].astype(jnp.float32)
                half_ref[a, k + u] = (part[:, u * width:(u + 1) * width] * active).astype(jnp.bfloat16)


def block_form(pair, second):
    tile, width = pair.shape
    lower = (lax.broadcasted_iota(jnp.int32, pair.shape, 1) < tile).astype(jnp.bfloat16)
    other = pltpu.roll(pair, tile, 1)
    top = jnp.where(second, other, pair) * lower
    low = jnp.where(second, pair, other) * (1 - lower)
    return jnp.concatenate([top, low], axis=0)


def two_products(halves, forms):
    zero = jnp.zeros_like(forms[0])
    top = jnp.concatenate([forms[0], zero], axis=1)
    low = jnp.concatenate([zero, forms[1]], axis=1)
    both = jnp.concatenate([top, low], axis=0)
    part = jnp.dot(jnp.concatenate(halves, axis=1), both, preferred_element_type=jnp.float32)
    width = part.shape[1] // 2
    return part[:, :width].astype(jnp.bfloat16), part[:, width:].astype(jnp.bfloat16)


def merge(piece_refs, pairs_ref):
    at = 0
    for piece in piece_refs:
        pairs_ref[at:at + piece.shape[0]] = piece[...]
        at += piece.shape[0]


def piece_at(r):
    low = sum(ORDER.index(i) << (4 * i) for i in range(7))
    high = sum(ORDER.index(i + 8) << (4 * i) for i in range(7))
    packed = jnp.where(r < 8, low, high) >> (4 * (r & 7))
    end = jnp.where(r < 8, ORDER.index(7), ORDER.index(15))
    return jnp.where(r & 7 == 7, end, packed & 15)


def early_kernel(pair_count, owner_hbm, slot_hbm, half_ref, *refs):
    piece_refs = refs[:-7]
    out_hbm, list_ref, pairs_ref, out_ref, owner_ref, slot_ref, sems = refs[-7:]
    sectors, blocks, tile, width = out_ref.shape
    items, held = sectors * blocks, pairs_ref.shape[0]
    last = held + len(MIDDLE) * pair_count
    copies = load_all((owner_hbm, owner_ref, sems.at[0]), (slot_hbm, slot_ref, sems.at[1]))
    merge(piece_refs, pairs_ref)
    me = lax.axis_index("sec")
    for copy in copies:
        copy.wait()

    def store(a):
        return pltpu.make_async_copy(out_ref.at[a], out_hbm.at[a], sems.at[a])

    def one(a, listed):
        for k in range(0, blocks, 2):
            forms = []
            for u in range(2):
                owner, slot = owner_ref[a, k + u], slot_ref[a, k + u]
                at = piece_at(owner ^ me) if len(piece_refs) > 1 else owner
                second = slot >= pair_count
                at = at * pair_count + jnp.where(second, slot - pair_count, slot)
                forms.append(block_form(pairs_ref[jnp.where(at >= held, 0, at)], second))
                in_last = at >= last
                entry = (at - jnp.where(in_last, last, held)) * 2 + second.astype(jnp.int32)
                entry = entry * items + a * blocks + k + u
                list_ref[jnp.where(in_last, items + 1 + listed[1], listed[0])] = entry
                in_middle = (at >= held) & (at < last)
                listed = listed[0] + in_middle.astype(jnp.int32), listed[1] + in_last.astype(jnp.int32)
            out_ref[a, k], out_ref[a, k + 1] = two_products([half_ref[a, k], half_ref[a, k + 1]], forms)
        store(a).start()
        return listed

    listed = lax.fori_loop(0, sectors, one, (0, 0), unroll=2)
    list_ref[items] = listed[0]
    list_ref[2 * items + 1] = listed[1]
    for a in range(sectors):
        store(a).wait()


def late_kernel(group_size, first, list_ref, early_hbm, half_ref, *refs):
    piece_refs, (out_hbm, pairs_ref, out_ref, sems) = refs[:-4], refs[-4:]
    sectors, blocks, tile, width = half_ref.shape
    items = sectors * blocks
    listed = list_ref[first + items]
    merge(piece_refs, pairs_ref)

    def store(slot, item):
        return pltpu.make_async_copy(out_ref.at[slot], out_hbm.at[item // blocks, item % blocks], sems.at[slot])

    def group(g, carry):
        for u in range(0, group_size, 2):
            slot = g * group_size + u
            entries = [list_ref[first + jnp.minimum(slot + n, listed - 1)] for n in range(2)]
            halves, forms = [], []
            for entry in entries:
                item, at = entry % items, entry // items
                halves.append(half_ref[item // blocks, item % blocks])
                forms.append(block_form(pairs_ref[at // 2], at % 2 == 1))
            out_ref[slot], out_ref[slot + 1] = two_products(halves, forms)
        for u in range(group_size):
            slot = g * group_size + u

            @pl.when(slot < listed)
            def _():
                store(slot, list_ref[first + slot] % items).start()
        return carry

    def drain(slot, carry):
        store(slot, 0).wait()
        return carry

    lax.fori_loop(0, (listed + group_size - 1) // group_size, group, 0)
    lax.fori_loop(0, listed, drain, 0)


def swap(piece, bit):
    count = lax.axis_size("sec")
    return lax.ppermute(piece, "sec", [(i, i ^ bit) for i in range(count)])


def per_device(
    psi, left_ops, right_ops, dims_left, dims_right, right_owner, right_slot, term_active
):
    left_count, block_count, tile, width = psi.shape
    items = left_count * block_count
    pair_count = right_ops.shape[0] // 2
    count = lax.axis_size("sec")
    by_swaps = count == len(ORDER)
    flops = 2 * psi.size * tile
    smem = pl.BlockSpec(memory_space=pltpu.SMEM)
    vmem = pl.BlockSpec(memory_space=pltpu.VMEM)
    hbm = pl.BlockSpec(memory_space=pltpu.HBM)
    params = pltpu.CompilerParams(vmem_limit_bytes=VMEM_LIMIT)

    def in_hbm(*arrays):
        return [pltpu.with_memory_space_constraint(array, pltpu.HBM) for array in arrays]

    pairs = pl.pallas_call(
        pack_kernel,
        out_shape=jax.ShapeDtypeStruct((pair_count, tile, 2 * tile), jnp.bfloat16),
        in_specs=[hbm, hbm],
        out_specs=vmem,
        scratch_shapes=[
            pltpu.SMEM(dims_right.shape, jnp.int32),
            pltpu.VMEM(right_ops.shape, jnp.bfloat16),
            pltpu.SemaphoreType.DMA((2,)),
        ],
        compiler_params=params,
        cost_estimate=pl.CostEstimate(flops=0, bytes_accessed=2 * right_ops.size, transcendentals=0),
    )(*in_hbm(dims_right, right_ops))

    def half_of(dims_left):
        active = term_active.reshape(left_count, block_count)
        return pl.pallas_call(
            left_kernel,
            out_shape=jax.ShapeDtypeStruct(psi.shape, jnp.bfloat16),
            in_specs=[hbm] * 4,
            out_specs=vmem,
            scratch_shapes=[
                pltpu.SMEM(dims_left.shape, jnp.int32),
                pltpu.SMEM(active.shape, jnp.int32),
                pltpu.VMEM(left_ops.shape, jnp.bfloat16),
                pltpu.VMEM(psi.shape, jnp.bfloat16),
                pltpu.SemaphoreType.DMA((3,)),
                pltpu.SemaphoreType.DMA((left_count,)),
            ],
            compiler_params=params,
            cost_estimate=pl.CostEstimate(flops=flops, bytes_accessed=2 * psi.size, transcendentals=0),
        )(*in_hbm(dims_left, active, left_ops, psi))

    if by_swaps:
        pieces = {0: pairs}
        def pass_on(*pairs_of):
            for r, bit in pairs_of:
                pieces[r | bit] = swap(pieces[r], bit)

        pass_on((0, FAR), (0, NEAR), (0, CROSS))
        half = half_of(dims_left)
        held = (0, NEAR,)
        half, ends = lax.optimization_barrier((half, [pieces[r] for r in held]))
        pieces.update(zip(held, ends))
        pass_on((NEAR, CROSS), (FAR, NEAR), (FAR, CROSS), (FAR | NEAR, CROSS))
        pass_on((0, CORE), (NEAR, CORE), (CROSS, CORE), (NEAR | CROSS, CORE), (FAR | NEAR, CORE), (FAR, CORE), (FAR | CROSS, CORE))
        early = [pieces[r] for r in EARLY]
    else:
        half = half_of(dims_left)
        early = [lax.all_gather(pairs, "sec", axis=0, tiled=True)]

    sigma, listed = pl.pallas_call(
        functools.partial(early_kernel, pair_count),
        out_shape=(
            jax.ShapeDtypeStruct(psi.shape, jnp.bfloat16),
            pltpu.SMEM((2 * items + 2,), jnp.int32),
        ),
        in_specs=[hbm, hbm] + [vmem] * (1 + len(early)),
        out_specs=(hbm, smem),
        scratch_shapes=[
            pltpu.VMEM((sum(piece.shape[0] for piece in early), tile, 2 * tile), jnp.bfloat16),
            pltpu.VMEM(psi.shape, jnp.bfloat16),
            pltpu.SMEM(right_owner.shape, jnp.int32),
            pltpu.SMEM(right_slot.shape, jnp.int32),
            pltpu.SemaphoreType.DMA((max(left_count, 2),)),
        ],
        compiler_params=params,
        cost_estimate=pl.CostEstimate(flops=flops, bytes_accessed=2 * psi.size, transcendentals=0),
    )(*in_hbm(right_owner, right_slot), half, *early)

    def late(group_size, first, sigma, names):
        return pl.pallas_call(
            functools.partial(late_kernel, group_size, first),
            out_shape=jax.ShapeDtypeStruct(psi.shape, jnp.bfloat16),
            in_specs=[smem, hbm] + [vmem] * (1 + len(names)),
            out_specs=hbm,
            scratch_shapes=[
                pltpu.VMEM((len(names) * pair_count, tile, 2 * tile), jnp.bfloat16),
                pltpu.VMEM((items + group_size, tile, width), jnp.bfloat16),
                pltpu.SemaphoreType.DMA((items,)),
            ],
            input_output_aliases={1: 0},
            compiler_params=params,
            cost_estimate=pl.CostEstimate(flops=flops // 4, bytes_accessed=psi.size // 2, transcendentals=0),
        )(pltpu.with_memory_space_constraint(listed, pltpu.SMEM), sigma, half, *[pieces[r] for r in names])

    if by_swaps:
        top = FAR | NEAR | CROSS
        pieces[top], sigma = lax.optimization_barrier((pieces[top], sigma))
        pieces[top | CORE] = swap(pieces[top], CORE)
        sigma = late(8, 0, sigma, MIDDLE)
        sigma = late(4, items + 1, sigma, LAST)
    if lax.axis_size("op") > 1:
        sigma = lax.psum_scatter(sigma, "op", scatter_dimension=3, tiled=True)
    return sigma


def solution(mesh):
    placed = (
        P(("grp", "sec"), None, None, None),
        P(("grp", "sec"), None, "op"),
        P(("grp", "sec"), None, "op"),
        P(("grp", "sec")),
        P(("grp", "sec")),
        P(("grp", "sec"), None),
        P(("grp", "sec"), None),
        P(("grp", "sec"), None, "op"),
    )
    return jax.shard_map(
        per_device,
        mesh=mesh,
        in_specs=placed,
        out_specs=P(("grp", "sec"), None, None, "op"),
        check_vma=False,
    )
```

```python
import functools

import jax
import jax.numpy as jnp
from jax import lax
from jax.experimental import pallas as pl
from jax.experimental.pallas import tpu as pltpu
from jax.sharding import PartitionSpec as P

VMEM_LIMIT = 48 * 1024 * 1024
FAR, NEAR, CROSS, CORE = 8, 4, 2, 1
MIDDLE = (FAR | CORE, FAR | NEAR | CORE, FAR | CROSS | CORE, FAR | NEAR | CROSS)
LAST = (FAR | NEAR | CROSS | CORE,)
EARLY = tuple(r for r in range(16) if r not in MIDDLE + LAST)
ORDER = EARLY + MIDDLE + LAST


def load_all(*copies):
    copies = [pltpu.make_async_copy(*copy) for copy in copies]
    for copy in copies:
        copy.start()
    return copies


def pack_kernel(dims_hbm, right_hbm, pairs_ref, dims_ref, right_ref, sems):
    count, tile, width = pairs_ref.shape
    copies = load_all((dims_hbm, dims_ref, sems.at[0]), (right_hbm, right_ref, sems.at[1]))
    rows = lax.broadcasted_iota(jnp.int32, (tile, tile), 0)
    cols = lax.broadcasted_iota(jnp.int32, (tile, tile), 1)
    most = jnp.maximum(rows, cols)
    for copy in copies:
        copy.wait()

    def kept(b):
        return jnp.where(most < dims_ref[b], right_ref[b].astype(jnp.float32), 0.0)

    for p in range(count):
        both = jnp.concatenate([kept(p), kept(p + count)], axis=0)
        pairs_ref[p] = both.T.astype(jnp.bfloat16)


def left_kernel(dims_hbm, active_hbm, left_hbm, psi_hbm, half_ref, dims_ref, active_ref, left_ref, psi_ref, sems, psi_sems):
    sectors, blocks, tile, width = psi_ref.shape
    copies = load_all(
        (dims_hbm, dims_ref, sems.at[0]),
        (active_hbm, active_ref, sems.at[1]),
        (left_hbm, left_ref, sems.at[2]),
    )
    psi_copies = load_all(*[(psi_hbm.at[a], psi_ref.at[a], psi_sems.at[a]) for a in range(sectors)])
    rows = lax.broadcasted_iota(jnp.int32, (tile, tile), 0)
    cols = lax.broadcasted_iota(jnp.int32, (tile, tile), 1)
    most = jnp.maximum(rows, cols)
    for copy in copies:
        copy.wait()
    for a in range(sectors):
        psi_copies[a].wait()
        op = jnp.where(most < dims_ref[a], left_ref[a].astype(jnp.float32), 0.0).astype(jnp.bfloat16)
        for k in range(0, blocks, 2):
            both = jnp.concatenate([psi_ref[a, k], psi_ref[a, k + 1]], axis=1)
            part = jnp.dot(op, both, preferred_element_type=jnp.float32)
            for u in range(2):
                active = active_ref[a, k + u].astype(jnp.float32)
                half_ref[a, k + u] = (part[:, u * width:(u + 1) * width] * active).astype(jnp.bfloat16)


def block_form(pair, second):
    tile, width = pair.shape
    lower = (lax.broadcasted_iota(jnp.int32, pair.shape, 1) < tile).astype(jnp.bfloat16)
    other = pltpu.roll(pair, tile, 1)
    top = jnp.where(second, other, pair) * lower
    low = jnp.where(second, pair, other) * (1 - lower)
    return jnp.concatenate([top, low], axis=0)


def two_products(halves, forms):
    zero = jnp.zeros_like(forms[0])
    top = jnp.concatenate([forms[0], zero], axis=1)
    low = jnp.concatenate([zero, forms[1]], axis=1)
    both = jnp.concatenate([top, low], axis=0)
    part = jnp.dot(jnp.concatenate(halves, axis=1), both, preferred_element_type=jnp.float32)
    width = part.shape[1] // 2
    return part[:, :width].astype(jnp.bfloat16), part[:, width:].astype(jnp.bfloat16)


def merge(piece_refs, pairs_ref):
    at = 0
    for piece in piece_refs:
        pairs_ref[at:at + piece.shape[0]] = piece[...]
        at += piece.shape[0]


def piece_at(r):
    low = sum(ORDER.index(i) << (4 * i) for i in range(7))
    high = sum(ORDER.index(i + 8) << (4 * i) for i in range(7))
    packed = jnp.where(r < 8, low, high) >> (4 * (r & 7))
    end = jnp.where(r < 8, ORDER.index(7), ORDER.index(15))
    return jnp.where(r & 7 == 7, end, packed & 15)


def early_kernel(pair_count, owner_hbm, slot_hbm, half_ref, *refs):
    piece_refs = refs[:-6]
    out_ref, list_ref, pairs_ref, owner_ref, slot_ref, sems = refs[-6:]
    sectors, blocks, tile, width = out_ref.shape
    items, held = sectors * blocks, pairs_ref.shape[0]
    last = held + len(MIDDLE) * pair_count
    copies = load_all((owner_hbm, owner_ref, sems.at[0]), (slot_hbm, slot_ref, sems.at[1]))
    merge(piece_refs, pairs_ref)
    me = lax.axis_index("sec")
    for copy in copies:
        copy.wait()

    def one(a, listed):
        before = listed[1]
        for k in range(0, blocks, 2):
            forms = []
            for u in range(2):
                owner, slot = owner_ref[a, k + u], slot_ref[a, k + u]
                at = piece_at(owner ^ me) if len(piece_refs) > 1 else owner
                second = slot >= pair_count
                at = at * pair_count + jnp.where(second, slot - pair_count, slot)
                forms.append(block_form(pairs_ref[jnp.where(at >= held, 0, at)], second))
                in_last = at >= last
                entry = (at - jnp.where(in_last, last, held)) * 2 + second.astype(jnp.int32)
                entry = entry * items + a * blocks + k + u
                list_ref[jnp.where(in_last, items + 1 + listed[1], listed[0])] = entry
                in_middle = (at >= held) & (at < last)
                listed = listed[0] + in_middle.astype(jnp.int32), listed[1] + in_last.astype(jnp.int32)
            out_ref[a, k], out_ref[a, k + 1] = two_products([half_ref[a, k], half_ref[a, k + 1]], forms)
        list_ref[2 * items + 2 + a] = listed[1] - before
        return listed

    listed = lax.fori_loop(0, sectors, one, (0, 0), unroll=2)
    list_ref[items] = listed[0]
    list_ref[2 * items + 1] = listed[1]


def listed_products(group_size, first, list_ref, half_ref, pairs_ref, out_ref):
    sectors, blocks, tile, width = half_ref.shape
    items = sectors * blocks
    listed = list_ref[first + items]

    def group(g, carry):
        for u in range(0, group_size, 2):
            entries = [list_ref[first + jnp.minimum(g * group_size + u + n, listed - 1)] for n in range(2)]
            places, halves, forms = [], [], []
            for entry in entries:
                item, at = entry % items, entry // items
                places.append((item // blocks, item % blocks))
                halves.append(half_ref[places[-1]])
                forms.append(block_form(pairs_ref[at // 2], at % 2 == 1))
            out_ref[places[0]], out_ref[places[1]] = two_products(halves, forms)
        return carry

    lax.fori_loop(0, (listed + group_size - 1) // group_size, group, 0)


def middle_kernel(list_ref, early_ref, half_ref, *refs):
    piece_refs, (out_ref, pairs_ref) = refs[:-2], refs[-2:]
    out_ref[...] = early_ref[...]
    merge(piece_refs, pairs_ref)
    listed_products(8, 0, list_ref, half_ref, pairs_ref, out_ref)


def last_kernel(list_ref, middle_ref, half_ref, pairs_ref, out_hbm, out_ref, sems):
    sectors, blocks, tile, width = half_ref.shape
    items = sectors * blocks

    def store(a, ref):
        return pltpu.make_async_copy(ref.at[a], out_hbm.at[a], sems.at[a])

    for a in range(sectors):
        changed = list_ref[2 * items + 2 + a] > 0

        @pl.when(changed)
        def _():
            out_ref[a] = middle_ref[a]

        @pl.when(jnp.logical_not(changed))
        def _():
            store(a, middle_ref).start()

    listed_products(4, items + 1, list_ref, half_ref, pairs_ref, out_ref)
    for a in range(sectors):

        @pl.when(list_ref[2 * items + 2 + a] > 0)
        def _():
            store(a, out_ref).start()

    for a in range(sectors):
        store(a, out_ref).wait()


def swap(piece, bit):
    count = lax.axis_size("sec")
    return lax.ppermute(piece, "sec", [(i, i ^ bit) for i in range(count)])


def per_device(
    psi, left_ops, right_ops, dims_left, dims_right, right_owner, right_slot, term_active
):
    left_count, block_count, tile, width = psi.shape
    items = left_count * block_count
    pair_count = right_ops.shape[0] // 2
    count = lax.axis_size("sec")
    by_swaps = count == len(ORDER)
    flops = 2 * psi.size * tile
    smem = pl.BlockSpec(memory_space=pltpu.SMEM)
    vmem = pl.BlockSpec(memory_space=pltpu.VMEM)
    hbm = pl.BlockSpec(memory_space=pltpu.HBM)
    params = pltpu.CompilerParams(vmem_limit_bytes=VMEM_LIMIT)

    def in_hbm(*arrays):
        return [pltpu.with_memory_space_constraint(array, pltpu.HBM) for array in arrays]

    pairs = pl.pallas_call(
        pack_kernel,
        out_shape=jax.ShapeDtypeStruct((pair_count, tile, 2 * tile), jnp.bfloat16),
        in_specs=[hbm, hbm],
        out_specs=vmem,
        scratch_shapes=[
            pltpu.SMEM(dims_right.shape, jnp.int32),
            pltpu.VMEM(right_ops.shape, jnp.bfloat16),
            pltpu.SemaphoreType.DMA((2,)),
        ],
        compiler_params=params,
        cost_estimate=pl.CostEstimate(flops=0, bytes_accessed=2 * right_ops.size, transcendentals=0),
    )(*in_hbm(dims_right, right_ops))

    def half_of(dims_left):
        active = term_active.reshape(left_count, block_count)
        return pl.pallas_call(
            left_kernel,
            out_shape=jax.ShapeDtypeStruct(psi.shape, jnp.bfloat16),
            in_specs=[hbm] * 4,
            out_specs=vmem,
            scratch_shapes=[
                pltpu.SMEM(dims_left.shape, jnp.int32),
                pltpu.SMEM(active.shape, jnp.int32),
                pltpu.VMEM(left_ops.shape, jnp.bfloat16),
                pltpu.VMEM(psi.shape, jnp.bfloat16),
                pltpu.SemaphoreType.DMA((3,)),
                pltpu.SemaphoreType.DMA((left_count,)),
            ],
            compiler_params=params,
            cost_estimate=pl.CostEstimate(flops=flops, bytes_accessed=2 * psi.size, transcendentals=0),
        )(*in_hbm(dims_left, active, left_ops, psi))

    if by_swaps:
        pieces = {0: pairs}
        def pass_on(*pairs_of):
            for r, bit in pairs_of:
                pieces[r | bit] = swap(pieces[r], bit)

        pass_on((0, FAR), (0, NEAR), (0, CROSS))
        half = half_of(dims_left)
        held = (0, NEAR,)
        half, ends = lax.optimization_barrier((half, [pieces[r] for r in held]))
        pieces.update(zip(held, ends))
        pass_on((NEAR, CROSS), (FAR, NEAR), (FAR, CROSS), (FAR | NEAR, CROSS))
        pass_on((0, CORE), (NEAR, CORE), (CROSS, CORE), (NEAR | CROSS, CORE), (FAR | NEAR, CORE), (FAR, CORE), (FAR | CROSS, CORE))
        early = [pieces[r] for r in EARLY]
    else:
        half = half_of(dims_left)
        early = [lax.all_gather(pairs, "sec", axis=0, tiled=True)]

    sigma, listed = pl.pallas_call(
        functools.partial(early_kernel, pair_count),
        out_shape=(
            jax.ShapeDtypeStruct(psi.shape, jnp.bfloat16),
            pltpu.SMEM((2 * items + 2 + left_count,), jnp.int32),
        ),
        in_specs=[hbm, hbm] + [vmem] * (1 + len(early)),
        out_specs=(vmem, smem),
        scratch_shapes=[
            pltpu.VMEM((sum(piece.shape[0] for piece in early), tile, 2 * tile), jnp.bfloat16),
            pltpu.SMEM(right_owner.shape, jnp.int32),
            pltpu.SMEM(right_slot.shape, jnp.int32),
            pltpu.SemaphoreType.DMA((2,)),
        ],
        compiler_params=params,
        cost_estimate=pl.CostEstimate(flops=flops, bytes_accessed=2 * psi.size, transcendentals=0),
    )(*in_hbm(right_owner, right_slot), half, *early)

    if by_swaps:
        top = FAR | NEAR | CROSS
        pieces[top], sigma = lax.optimization_barrier((pieces[top], sigma))
        pieces[top | CORE] = swap(pieces[top], CORE)
        listed = pltpu.with_memory_space_constraint(listed, pltpu.SMEM)
        sigma = pl.pallas_call(
            middle_kernel,
            out_shape=jax.ShapeDtypeStruct(psi.shape, jnp.bfloat16),
            in_specs=[smem] + [vmem] * (2 + len(MIDDLE)),
            out_specs=vmem,
            scratch_shapes=[pltpu.VMEM((len(MIDDLE) * pair_count, tile, 2 * tile), jnp.bfloat16)],
            compiler_params=params,
            cost_estimate=pl.CostEstimate(flops=flops // 4, bytes_accessed=psi.size // 2, transcendentals=0),
        )(listed, sigma, half, *[pieces[r] for r in MIDDLE])
        sigma = pl.pallas_call(
            last_kernel,
            out_shape=jax.ShapeDtypeStruct(psi.shape, jnp.bfloat16),
            in_specs=[smem] + [vmem] * 3,
            out_specs=hbm,
            scratch_shapes=[pltpu.VMEM(psi.shape, jnp.bfloat16), pltpu.SemaphoreType.DMA((left_count,))],
            compiler_params=params,
            cost_estimate=pl.CostEstimate(flops=flops // 16, bytes_accessed=2 * psi.size, transcendentals=0),
        )(listed, sigma, half, pieces[LAST[0]])
    if lax.axis_size("op") > 1:
        sigma = lax.psum_scatter(sigma, "op", scatter_dimension=3, tiled=True)
    return sigma


def solution(mesh):
    placed = (
        P(("grp", "sec"), None, None, None),
        P(("grp", "sec"), None, "op"),
        P(("grp", "sec"), None, "op"),
        P(("grp", "sec")),
        P(("grp", "sec")),
        P(("grp", "sec"), None),
        P(("grp", "sec"), None),
        P(("grp", "sec"), None, "op"),
    )
    return jax.shard_map(
        per_device,
        mesh=mesh,
        in_specs=placed,
        out_specs=P(("grp", "sec"), None, None, "op"),
        check_vma=False,
    )
```

```python
import functools

import jax
import jax.numpy as jnp
from jax import lax
from jax.experimental import pallas as pl
from jax.experimental.pallas import tpu as pltpu
from jax.sharding import PartitionSpec as P

VMEM_LIMIT = 48 * 1024 * 1024
FAR, NEAR, CROSS, CORE = 8, 4, 2, 1
MIDDLE = (FAR | CORE, FAR | NEAR | CORE, FAR | CROSS | CORE, FAR | NEAR | CROSS)
LAST = (FAR | NEAR | CROSS | CORE,)
EARLY = tuple(r for r in range(16) if r not in MIDDLE + LAST)
ORDER = EARLY + MIDDLE + LAST


def load_all(*copies):
    copies = [pltpu.make_async_copy(*copy) for copy in copies]
    for copy in copies:
        copy.start()
    return copies


def pack_kernel(dims_hbm, right_hbm, pairs_ref, dims_ref, right_ref, sems):
    count, tile, width = pairs_ref.shape
    copies = load_all((dims_hbm, dims_ref, sems.at[0]), (right_hbm, right_ref, sems.at[1]))
    rows = lax.broadcasted_iota(jnp.int32, (tile, tile), 0)
    cols = lax.broadcasted_iota(jnp.int32, (tile, tile), 1)
    most = jnp.maximum(rows, cols)
    for copy in copies:
        copy.wait()

    def kept(b):
        return jnp.where(most < dims_ref[b], right_ref[b].astype(jnp.float32), 0.0)

    for p in range(count):
        both = jnp.concatenate([kept(p), kept(p + count)], axis=0)
        pairs_ref[p] = both.T.astype(jnp.bfloat16)


def left_kernel(
    pair_count, held, dims_hbm, active_hbm, owner_hbm, slot_hbm, left_hbm, psi_hbm,
    half_ref, list_ref, dims_ref, active_ref, owner_ref, slot_ref, left_ref, psi_ref, sems, psi_sems,
):
    sectors, blocks, tile, width = psi_ref.shape
    items = sectors * blocks
    last = held + len(MIDDLE) * pair_count
    copies = load_all(
        (dims_hbm, dims_ref, sems.at[0]),
        (active_hbm, active_ref, sems.at[1]),
        (owner_hbm, owner_ref, sems.at[2]),
        (slot_hbm, slot_ref, sems.at[3]),
        (left_hbm, left_ref, sems.at[4]),
    )
    psi_copies = load_all(*[(psi_hbm.at[a], psi_ref.at[a], psi_sems.at[a]) for a in range(sectors)])
    rows = lax.broadcasted_iota(jnp.int32, (tile, tile), 0)
    cols = lax.broadcasted_iota(jnp.int32, (tile, tile), 1)
    most = jnp.maximum(rows, cols)
    me = lax.axis_index("sec")
    by_swaps = lax.axis_size("sec") == len(ORDER)
    for copy in copies:
        copy.wait()
    in_middle, in_last = jnp.int32(0), jnp.int32(0)
    for a in range(sectors):
        psi_copies[a].wait()
        op = jnp.where(most < dims_ref[a], left_ref[a].astype(jnp.float32), 0.0).astype(jnp.bfloat16)
        before = in_last
        for k in range(0, blocks, 2):
            both = jnp.concatenate([psi_ref[a, k], psi_ref[a, k + 1]], axis=1)
            part = jnp.dot(op, both, preferred_element_type=jnp.float32)
            for u in range(2):
                active = active_ref[a, k + u].astype(jnp.float32)
                half_ref[a, k + u] = (part[:, u * width:(u + 1) * width] * active).astype(jnp.bfloat16)
                item = a * blocks + k + u
                owner, slot = owner_ref[a, k + u], slot_ref[a, k + u]
                at = piece_at(owner ^ me) if by_swaps else owner
                second = slot >= pair_count
                at = at * pair_count + jnp.where(second, slot - pair_count, slot)
                is_early, is_last = at < held, at >= last
                at = (at - jnp.where(is_last, last, jnp.where(is_early, 0, held))) * 2 + second.astype(jnp.int32)
                list_ref[jnp.where(is_last, items + 1 + in_last, in_middle)] = at * items + item
                list_ref[2 * items + 2 + sectors + item] = jnp.where(is_early, at, 0)
                in_last = in_last + is_last.astype(jnp.int32)
                in_middle = in_middle + jnp.logical_not(is_early | is_last).astype(jnp.int32)
        list_ref[2 * items + 2 + a] = in_last - before
    list_ref[items] = in_middle
    list_ref[2 * items + 1] = in_last


def block_form(pair, second):
    tile, width = pair.shape
    lower = (lax.broadcasted_iota(jnp.int32, pair.shape, 1) < tile).astype(jnp.bfloat16)
    other = pltpu.roll(pair, tile, 1)
    top = jnp.where(second, other, pair) * lower
    low = jnp.where(second, pair, other) * (1 - lower)
    return jnp.concatenate([top, low], axis=0)


def two_products(halves, forms):
    zero = jnp.zeros_like(forms[0])
    top = jnp.concatenate([forms[0], zero], axis=1)
    low = jnp.concatenate([zero, forms[1]], axis=1)
    both = jnp.concatenate([top, low], axis=0)
    part = jnp.dot(jnp.concatenate(halves, axis=1), both, preferred_element_type=jnp.float32)
    width = part.shape[1] // 2
    return part[:, :width].astype(jnp.bfloat16), part[:, width:].astype(jnp.bfloat16)


def merge(piece_refs, pairs_ref):
    at = 0
    for piece in piece_refs:
        pairs_ref[at:at + piece.shape[0]] = piece[...]
        at += piece.shape[0]


def piece_at(r):
    low = sum(ORDER.index(i) << (4 * i) for i in range(7))
    high = sum(ORDER.index(i + 8) << (4 * i) for i in range(7))
    packed = jnp.where(r < 8, low, high) >> (4 * (r & 7))
    end = jnp.where(r < 8, ORDER.index(7), ORDER.index(15))
    return jnp.where(r & 7 == 7, end, packed & 15)


def early_kernel(list_ref, half_ref, *refs):
    piece_refs, (out_ref, pairs_ref) = refs[:-2], refs[-2:]
    sectors, blocks, tile, width = out_ref.shape
    first = 2 * sectors * blocks + 2 + sectors
    merge(piece_refs, pairs_ref)

    def one(a, carry):
        for k in range(0, blocks, 2):
            ats = [list_ref[first + a * blocks + k + u] for u in range(2)]
            forms = [block_form(pairs_ref[at // 2], at % 2 == 1) for at in ats]
            out_ref[a, k], out_ref[a, k + 1] = two_products([half_ref[a, k], half_ref[a, k + 1]], forms)
        return carry

    lax.fori_loop(0, sectors, one, 0, unroll=2)


def listed_products(group_size, first, list_ref, half_ref, pairs_ref, out_ref):
    sectors, blocks, tile, width = half_ref.shape
    items = sectors * blocks
    listed = list_ref[first + items]

    def group(g, carry):
        for u in range(0, group_size, 2):
            entries = [list_ref[first + jnp.minimum(g * group_size + u + n, listed - 1)] for n in range(2)]
            places, halves, forms = [], [], []
            for entry in entries:
                item, at = entry % items, entry // items
                places.append((item // blocks, item % blocks))
                halves.append(half_ref[places[-1]])
                forms.append(block_form(pairs_ref[at // 2], at % 2 == 1))
            out_ref[places[0]], out_ref[places[1]] = two_products(halves, forms)
        return carry

    lax.fori_loop(0, (listed + group_size - 1) // group_size, group, 0)


def middle_kernel(list_ref, early_ref, half_ref, *refs):
    piece_refs, (out_ref, pairs_ref) = refs[:-2], refs[-2:]
    out_ref[...] = early_ref[...]
    merge(piece_refs, pairs_ref)
    listed_products(8, 0, list_ref, half_ref, pairs_ref, out_ref)


def last_kernel(list_ref, middle_ref, half_ref, pairs_ref, out_hbm, out_ref, sems):
    sectors, blocks, tile, width = half_ref.shape
    items = sectors * blocks

    def store(a, ref):
        return pltpu.make_async_copy(ref.at[a], out_hbm.at[a], sems.at[a])

    for a in range(sectors):
        changed = list_ref[2 * items + 2 + a] > 0

        @pl.when(changed)
        def _():
            out_ref[a] = middle_ref[a]

        @pl.when(jnp.logical_not(changed))
        def _():
            store(a, middle_ref).start()

    listed_products(4, items + 1, list_ref, half_ref, pairs_ref, out_ref)
    for a in range(sectors):

        @pl.when(list_ref[2 * items + 2 + a] > 0)
        def _():
            store(a, out_ref).start()

    for a in range(sectors):
        store(a, out_ref).wait()


def swap(piece, bit):
    count = lax.axis_size("sec")
    return lax.ppermute(piece, "sec", [(i, i ^ bit) for i in range(count)])


def per_device(
    psi, left_ops, right_ops, dims_left, dims_right, right_owner, right_slot, term_active
):
    left_count, block_count, tile, width = psi.shape
    items = left_count * block_count
    pair_count = right_ops.shape[0] // 2
    count = lax.axis_size("sec")
    by_swaps = count == len(ORDER)
    flops = 2 * psi.size * tile
    smem = pl.BlockSpec(memory_space=pltpu.SMEM)
    vmem = pl.BlockSpec(memory_space=pltpu.VMEM)
    hbm = pl.BlockSpec(memory_space=pltpu.HBM)
    params = pltpu.CompilerParams(vmem_limit_bytes=VMEM_LIMIT)

    def in_hbm(*arrays):
        return [pltpu.with_memory_space_constraint(array, pltpu.HBM) for array in arrays]

    pairs = pl.pallas_call(
        pack_kernel,
        out_shape=jax.ShapeDtypeStruct((pair_count, tile, 2 * tile), jnp.bfloat16),
        in_specs=[hbm, hbm],
        out_specs=vmem,
        scratch_shapes=[
            pltpu.SMEM(dims_right.shape, jnp.int32),
            pltpu.VMEM(right_ops.shape, jnp.bfloat16),
            pltpu.SemaphoreType.DMA((2,)),
        ],
        compiler_params=params,
        cost_estimate=pl.CostEstimate(flops=0, bytes_accessed=2 * right_ops.size, transcendentals=0),
    )(*in_hbm(dims_right, right_ops))

    active = term_active.reshape(left_count, block_count)
    half, listed = pl.pallas_call(
        functools.partial(left_kernel, pair_count, len(EARLY if by_swaps else range(count)) * pair_count),
        out_shape=(
            jax.ShapeDtypeStruct(psi.shape, jnp.bfloat16),
            pltpu.SMEM((3 * items + 2 + left_count,), jnp.int32),
        ),
        in_specs=[hbm] * 6,
        out_specs=(vmem, smem),
        scratch_shapes=[
            pltpu.SMEM(dims_left.shape, jnp.int32),
            pltpu.SMEM(active.shape, jnp.int32),
            pltpu.SMEM(right_owner.shape, jnp.int32),
            pltpu.SMEM(right_slot.shape, jnp.int32),
            pltpu.VMEM(left_ops.shape, jnp.bfloat16),
            pltpu.VMEM(psi.shape, jnp.bfloat16),
            pltpu.SemaphoreType.DMA((5,)),
            pltpu.SemaphoreType.DMA((left_count,)),
        ],
        compiler_params=params,
        cost_estimate=pl.CostEstimate(flops=flops, bytes_accessed=2 * psi.size, transcendentals=0),
    )(*in_hbm(dims_left, active, right_owner, right_slot, left_ops, psi))
    listed = pltpu.with_memory_space_constraint(listed, pltpu.SMEM)

    if by_swaps:
        pieces = {0: pairs}
        def pass_on(*pairs_of):
            for r, bit in pairs_of:
                pieces[r | bit] = swap(pieces[r], bit)

        pass_on((0, FAR), (0, NEAR), (0, CROSS))
        held = (0, NEAR,)
        half, ends = lax.optimization_barrier((half, [pieces[r] for r in held]))
        pieces.update(zip(held, ends))
        pass_on((NEAR, CROSS), (FAR, NEAR), (FAR, CROSS), (FAR | NEAR, CROSS))
        pass_on((0, CORE), (NEAR, CORE), (CROSS, CORE), (NEAR | CROSS, CORE), (FAR | NEAR, CORE), (FAR, CORE), (FAR | CROSS, CORE))
        early = [pieces[r] for r in EARLY]
    else:
        early = [lax.all_gather(pairs, "sec", axis=0, tiled=True)]

    sigma = pl.pallas_call(
        early_kernel,
        out_shape=jax.ShapeDtypeStruct(psi.shape, jnp.bfloat16),
        in_specs=[smem] + [vmem] * (1 + len(early)),
        out_specs=vmem,
        scratch_shapes=[pltpu.VMEM((sum(piece.shape[0] for piece in early), tile, 2 * tile), jnp.bfloat16)],
        compiler_params=params,
        cost_estimate=pl.CostEstimate(flops=flops, bytes_accessed=2 * psi.size, transcendentals=0),
    )(listed, half, *early)
    if by_swaps:
        top = FAR | NEAR | CROSS
        pieces[top], sigma = lax.optimization_barrier((pieces[top], sigma))
        pieces[top | CORE] = swap(pieces[top], CORE)
        sigma = pl.pallas_call(
            middle_kernel,
            out_shape=jax.ShapeDtypeStruct(psi.shape, jnp.bfloat16),
            in_specs=[smem] + [vmem] * (2 + len(MIDDLE)),
            out_specs=vmem,
            scratch_shapes=[pltpu.VMEM((len(MIDDLE) * pair_count, tile, 2 * tile), jnp.bfloat16)],
            compiler_params=params,
            cost_estimate=pl.CostEstimate(flops=flops // 4, bytes_accessed=psi.size // 2, transcendentals=0),
        )(listed, sigma, half, *[pieces[r] for r in MIDDLE])
        sigma = pl.pallas_call(
            last_kernel,
            out_shape=jax.ShapeDtypeStruct(psi.shape, jnp.bfloat16),
            in_specs=[smem] + [vmem] * 3,
            out_specs=hbm,
            scratch_shapes=[pltpu.VMEM(psi.shape, jnp.bfloat16), pltpu.SemaphoreType.DMA((left_count,))],
            compiler_params=params,
            cost_estimate=pl.CostEstimate(flops=flops // 16, bytes_accessed=2 * psi.size, transcendentals=0),
        )(listed, sigma, half, pieces[LAST[0]])
    if lax.axis_size("op") > 1:
        sigma = lax.psum_scatter(sigma, "op", scatter_dimension=3, tiled=True)
    return sigma


def solution(mesh):
    placed = (
        P(("grp", "sec"), None, None, None),
        P(("grp", "sec"), None, "op"),
        P(("grp", "sec"), None, "op"),
        P(("grp", "sec")),
        P(("grp", "sec")),
        P(("grp", "sec"), None),
        P(("grp", "sec"), None),
        P(("grp", "sec"), None, "op"),
    )
    return jax.shard_map(
        per_device,
        mesh=mesh,
        in_specs=placed,
        out_specs=P(("grp", "sec"), None, None, "op"),
        check_vma=False,
    )
```

```python
import functools

import jax
import jax.numpy as jnp
from jax import lax
from jax.experimental import pallas as pl
from jax.experimental.pallas import tpu as pltpu
from jax.sharding import PartitionSpec as P

VMEM_LIMIT = 48 * 1024 * 1024
FAR, NEAR, CROSS, CORE = 8, 4, 2, 1
OWN, SIDE = (0, 0), (CROSS, CROSS)
FIRST, SECOND = (FAR, NEAR), (NEAR, FAR)
THIRD, FOURTH = (FAR | NEAR, NEAR | CROSS), (NEAR | CROSS, FAR | NEAR)
FAR_SIDE, END = (FAR | CROSS, FAR | CROSS), (FAR | NEAR | CROSS, FAR | NEAR | CROSS)


def partner(name):
    return name[1] | CORE, name[0] | CORE


EARLY = (OWN, SIDE, FIRST, SECOND, THIRD, FOURTH, FAR_SIDE, partner(OWN), partner(SIDE), partner(FIRST), partner(SECOND))
MIDDLE = (partner(THIRD), partner(FOURTH), partner(FAR_SIDE), END)
LAST = (partner(END),)
ORDER = EARLY + MIDDLE + LAST


def load_all(*copies):
    copies = [pltpu.make_async_copy(*copy) for copy in copies]
    for copy in copies:
        copy.start()
    return copies


def pack_kernel(dims_hbm, right_hbm, pairs_ref, dims_ref, right_ref, sems):
    count, tile, width = pairs_ref.shape
    copies = load_all((dims_hbm, dims_ref, sems.at[0]), (right_hbm, right_ref, sems.at[1]))
    rows = lax.broadcasted_iota(jnp.int32, (tile, tile), 0)
    cols = lax.broadcasted_iota(jnp.int32, (tile, tile), 1)
    most = jnp.maximum(rows, cols)
    for copy in copies:
        copy.wait()

    def kept(b):
        return jnp.where(most < dims_ref[b], right_ref[b].astype(jnp.float32), 0.0)

    for p in range(count):
        both = jnp.concatenate([kept(p), kept(p + count)], axis=0)
        pairs_ref[p] = both.T.astype(jnp.bfloat16)


def left_kernel(
    pair_count, held, dims_hbm, active_hbm, owner_hbm, slot_hbm, left_hbm, psi_hbm,
    half_ref, list_ref, dims_ref, active_ref, owner_ref, slot_ref, left_ref, psi_ref, sems, psi_sems,
):
    sectors, blocks, tile, width = psi_ref.shape
    items = sectors * blocks
    last = held + len(MIDDLE) * pair_count
    copies = load_all(
        (dims_hbm, dims_ref, sems.at[0]),
        (active_hbm, active_ref, sems.at[1]),
        (owner_hbm, owner_ref, sems.at[2]),
        (slot_hbm, slot_ref, sems.at[3]),
        (left_hbm, left_ref, sems.at[4]),
    )
    psi_copies = load_all(*[(psi_hbm.at[a], psi_ref.at[a], psi_sems.at[a]) for a in range(sectors)])
    rows = lax.broadcasted_iota(jnp.int32, (tile, tile), 0)
    cols = lax.broadcasted_iota(jnp.int32, (tile, tile), 1)
    most = jnp.maximum(rows, cols)
    me = lax.axis_index("sec")
    by_swaps = lax.axis_size("sec") == len(ORDER)
    for copy in copies:
        copy.wait()
    in_middle, in_last = jnp.int32(0), jnp.int32(0)
    for a in range(sectors):
        psi_copies[a].wait()
        op = jnp.where(most < dims_ref[a], left_ref[a].astype(jnp.float32), 0.0).astype(jnp.bfloat16)
        before = in_last
        for k in range(0, blocks, 2):
            both = jnp.concatenate([psi_ref[a, k], psi_ref[a, k + 1]], axis=1)
            part = jnp.dot(op, both, preferred_element_type=jnp.float32)
            for u in range(2):
                active = active_ref[a, k + u].astype(jnp.float32)
                half_ref[a, k + u] = (part[:, u * width:(u + 1) * width] * active).astype(jnp.bfloat16)
                item = a * blocks + k + u
                owner, slot = owner_ref[a, k + u], slot_ref[a, k + u]
                at = piece_at(owner ^ me, me) if by_swaps else owner
                second = slot >= pair_count
                at = at * pair_count + jnp.where(second, slot - pair_count, slot)
                is_early, is_last = at < held, at >= last
                at = (at - jnp.where(is_last, last, jnp.where(is_early, 0, held))) * 2 + second.astype(jnp.int32)
                list_ref[jnp.where(is_last, items + 1 + in_last, in_middle)] = at * items + item
                list_ref[2 * items + 2 + sectors + item] = jnp.where(is_early, at, 0)
                in_last = in_last + is_last.astype(jnp.int32)
                in_middle = in_middle + jnp.logical_not(is_early | is_last).astype(jnp.int32)
        list_ref[2 * items + 2 + a] = in_last - before
    list_ref[items] = in_middle
    list_ref[2 * items + 1] = in_last


def block_form(pair, second):
    tile, width = pair.shape
    lower = (lax.broadcasted_iota(jnp.int32, pair.shape, 1) < tile).astype(jnp.bfloat16)
    other = pltpu.roll(pair, tile, 1)
    top = jnp.where(second, other, pair) * lower
    low = jnp.where(second, pair, other) * (1 - lower)
    return jnp.concatenate([top, low], axis=0)


def two_products(halves, forms):
    zero = jnp.zeros_like(forms[0])
    top = jnp.concatenate([forms[0], zero], axis=1)
    low = jnp.concatenate([zero, forms[1]], axis=1)
    both = jnp.concatenate([top, low], axis=0)
    part = jnp.dot(jnp.concatenate(halves, axis=1), both, preferred_element_type=jnp.float32)
    width = part.shape[1] // 2
    return part[:, :width].astype(jnp.bfloat16), part[:, width:].astype(jnp.bfloat16)


def merge(piece_refs, pairs_ref):
    at = 0
    for piece in piece_refs:
        pairs_ref[at:at + piece.shape[0]] = piece[...]
        at += piece.shape[0]


def piece_at(r, me):
    at = jnp.int32(0)
    for parity in range(2):
        places = [ORDER.index(next(name for name in ORDER if name[parity] == i)) for i in range(len(ORDER))]
        for half in range(2):
            packed = sum(place << (4 * i) for i, place in enumerate(places[8 * half:8 * half + 7]))
            mine = jnp.where(r & 7 == 7, places[8 * half + 7], (packed >> (4 * (r & 7))) & 15)
            at = jnp.where((me & 1 == parity) & (r >> 3 == half), mine, at)
    return at


def early_kernel(list_ref, half_ref, *refs):
    piece_refs, (out_ref, pairs_ref) = refs[:-2], refs[-2:]
    sectors, blocks, tile, width = out_ref.shape
    first = 2 * sectors * blocks + 2 + sectors
    merge(piece_refs, pairs_ref)

    def one(a, carry):
        for k in range(0, blocks, 2):
            ats = [list_ref[first + a * blocks + k + u] for u in range(2)]
            forms = [block_form(pairs_ref[at // 2], at % 2 == 1) for at in ats]
            out_ref[a, k], out_ref[a, k + 1] = two_products([half_ref[a, k], half_ref[a, k + 1]], forms)
        return carry

    lax.fori_loop(0, sectors, one, 0, unroll=2)


def listed_products(group_size, first, list_ref, half_ref, pairs_ref, out_ref):
    sectors, blocks, tile, width = half_ref.shape
    items = sectors * blocks
    listed = list_ref[first + items]

    def group(g, carry):
        for u in range(0, group_size, 2):
            entries = [list_ref[first + jnp.minimum(g * group_size + u + n, listed - 1)] for n in range(2)]
            places, halves, forms = [], [], []
            for entry in entries:
                item, at = entry % items, entry // items
                places.append((item // blocks, item % blocks))
                halves.append(half_ref[places[-1]])
                forms.append(block_form(pairs_ref[at // 2], at % 2 == 1))
            out_ref[places[0]], out_ref[places[1]] = two_products(halves, forms)
        return carry

    lax.fori_loop(0, (listed + group_size - 1) // group_size, group, 0)


def middle_kernel(list_ref, early_ref, half_ref, *refs):
    piece_refs, (out_ref, pairs_ref) = refs[:-2], refs[-2:]
    out_ref[...] = early_ref[...]
    merge(piece_refs, pairs_ref)
    listed_products(8, 0, list_ref, half_ref, pairs_ref, out_ref)


def last_kernel(list_ref, middle_ref, half_ref, pairs_ref, out_hbm, out_ref, sems):
    sectors, blocks, tile, width = half_ref.shape
    items = sectors * blocks

    def store(a, ref):
        return pltpu.make_async_copy(ref.at[a], out_hbm.at[a], sems.at[a])

    for a in range(sectors):
        changed = list_ref[2 * items + 2 + a] > 0

        @pl.when(changed)
        def _():
            out_ref[a] = middle_ref[a]

        @pl.when(jnp.logical_not(changed))
        def _():
            store(a, middle_ref).start()

    listed_products(4, items + 1, list_ref, half_ref, pairs_ref, out_ref)
    for a in range(sectors):

        @pl.when(list_ref[2 * items + 2 + a] > 0)
        def _():
            store(a, out_ref).start()

    for a in range(sectors):
        store(a, out_ref).wait()


def swap(piece, even_bit, odd_bit):
    count = lax.axis_size("sec")
    return lax.ppermute(piece, "sec", [(i, i ^ (odd_bit if i & CORE else even_bit)) for i in range(count)])


def per_device(
    psi, left_ops, right_ops, dims_left, dims_right, right_owner, right_slot, term_active
):
    left_count, block_count, tile, width = psi.shape
    items = left_count * block_count
    pair_count = right_ops.shape[0] // 2
    count = lax.axis_size("sec")
    by_swaps = count == len(ORDER)
    flops = 2 * psi.size * tile
    smem = pl.BlockSpec(memory_space=pltpu.SMEM)
    vmem = pl.BlockSpec(memory_space=pltpu.VMEM)
    hbm = pl.BlockSpec(memory_space=pltpu.HBM)
    params = pltpu.CompilerParams(vmem_limit_bytes=VMEM_LIMIT)

    def in_hbm(*arrays):
        return [pltpu.with_memory_space_constraint(array, pltpu.HBM) for array in arrays]

    pairs = pl.pallas_call(
        pack_kernel,
        out_shape=jax.ShapeDtypeStruct((pair_count, tile, 2 * tile), jnp.bfloat16),
        in_specs=[hbm, hbm],
        out_specs=vmem,
        scratch_shapes=[
            pltpu.SMEM(dims_right.shape, jnp.int32),
            pltpu.VMEM(right_ops.shape, jnp.bfloat16),
            pltpu.SemaphoreType.DMA((2,)),
        ],
        compiler_params=params,
        cost_estimate=pl.CostEstimate(flops=0, bytes_accessed=2 * right_ops.size, transcendentals=0),
    )(*in_hbm(dims_right, right_ops))

    active = term_active.reshape(left_count, block_count)
    half, listed = pl.pallas_call(
        functools.partial(left_kernel, pair_count, len(EARLY if by_swaps else range(count)) * pair_count),
        out_shape=(
            jax.ShapeDtypeStruct(psi.shape, jnp.bfloat16),
            pltpu.SMEM((3 * items + 2 + left_count,), jnp.int32),
        ),
        in_specs=[hbm] * 6,
        out_specs=(vmem, smem),
        scratch_shapes=[
            pltpu.SMEM(dims_left.shape, jnp.int32),
            pltpu.SMEM(active.shape, jnp.int32),
            pltpu.SMEM(right_owner.shape, jnp.int32),
            pltpu.SMEM(right_slot.shape, jnp.int32),
            pltpu.VMEM(left_ops.shape, jnp.bfloat16),
            pltpu.VMEM(psi.shape, jnp.bfloat16),
            pltpu.SemaphoreType.DMA((5,)),
            pltpu.SemaphoreType.DMA((left_count,)),
        ],
        compiler_params=params,
        cost_estimate=pl.CostEstimate(flops=flops, bytes_accessed=2 * psi.size, transcendentals=0),
    )(*in_hbm(dims_left, active, right_owner, right_slot, left_ops, psi))
    listed = pltpu.with_memory_space_constraint(listed, pltpu.SMEM)

    if by_swaps:
        pieces = {OWN: pairs}
        odd = lax.axis_index("sec") & CORE == 1

        def pass_on(*routes):
            for name, target in routes:
                pieces[target] = swap(pieces[name], name[0] ^ target[0], name[1] ^ target[1])

        def share(*names):
            for name in names:
                pieces[partner(name)] = swap(pieces[name], CORE, CORE)

        def cross(even_name, odd_name, target):
            pieces[target] = swap(jnp.where(odd, pieces[odd_name], pieces[even_name]), CROSS, CROSS)

        pass_on((OWN, FIRST), (OWN, SIDE))
        share(OWN)
        held = (partner(OWN),)
        pieces[OWN], ends = lax.optimization_barrier((pieces[OWN], [pieces[r] for r in held]))
        pieces.update(zip(held, ends))
        pass_on((OWN, SECOND), )
        held = (FIRST,)
        half, ends = lax.optimization_barrier((half, [pieces[r] for r in held]))
        pieces.update(zip(held, ends))
        pass_on((FIRST, THIRD), (SECOND, FOURTH))
        cross(FIRST, SECOND, FAR_SIDE)
        cross(THIRD, FOURTH, END)
        share(SIDE, FIRST, SECOND, THIRD, FOURTH, FAR_SIDE)
        early = [pieces[name] for name in EARLY]
    else:
        early = [lax.all_gather(pairs, "sec", axis=0, tiled=True)]

    sigma = pl.pallas_call(
        early_kernel,
        out_shape=jax.ShapeDtypeStruct(psi.shape, jnp.bfloat16),
        in_specs=[smem] + [vmem] * (1 + len(early)),
        out_specs=vmem,
        scratch_shapes=[pltpu.VMEM((sum(piece.shape[0] for piece in early), tile, 2 * tile), jnp.bfloat16)],
        compiler_params=params,
        cost_estimate=pl.CostEstimate(flops=flops, bytes_accessed=2 * psi.size, transcendentals=0),
    )(listed, half, *early)
    if by_swaps:
        pieces[END], sigma = lax.optimization_barrier((pieces[END], sigma))
        share(END)
        sigma = pl.pallas_call(
            middle_kernel,
            out_shape=jax.ShapeDtypeStruct(psi.shape, jnp.bfloat16),
            in_specs=[smem] + [vmem] * (2 + len(MIDDLE)),
            out_specs=vmem,
            scratch_shapes=[pltpu.VMEM((len(MIDDLE) * pair_count, tile, 2 * tile), jnp.bfloat16)],
            compiler_params=params,
            cost_estimate=pl.CostEstimate(flops=flops // 4, bytes_accessed=psi.size // 2, transcendentals=0),
        )(listed, sigma, half, *[pieces[name] for name in MIDDLE])
        sigma = pl.pallas_call(
            last_kernel,
            out_shape=jax.ShapeDtypeStruct(psi.shape, jnp.bfloat16),
            in_specs=[smem] + [vmem] * 3,
            out_specs=hbm,
            scratch_shapes=[pltpu.VMEM(psi.shape, jnp.bfloat16), pltpu.SemaphoreType.DMA((left_count,))],
            compiler_params=params,
            cost_estimate=pl.CostEstimate(flops=flops // 16, bytes_accessed=2 * psi.size, transcendentals=0),
        )(listed, sigma, half, pieces[LAST[0]])
    if lax.axis_size("op") > 1:
        sigma = lax.psum_scatter(sigma, "op", scatter_dimension=3, tiled=True)
    return sigma


def solution(mesh):
    placed = (
        P(("grp", "sec"), None, None, None),
        P(("grp", "sec"), None, "op"),
        P(("grp", "sec"), None, "op"),
        P(("grp", "sec")),
        P(("grp", "sec")),
        P(("grp", "sec"), None),
        P(("grp", "sec"), None),
        P(("grp", "sec"), None, "op"),
    )
    return jax.shard_map(
        per_device,
        mesh=mesh,
        in_specs=placed,
        out_specs=P(("grp", "sec"), None, None, "op"),
        check_vma=False,
    )
```

```python
import functools

import jax
import jax.numpy as jnp
from jax import lax
from jax.experimental import pallas as pl
from jax.experimental.pallas import tpu as pltpu
from jax.sharding import PartitionSpec as P

VMEM_LIMIT = 48 * 1024 * 1024
FAR, NEAR, CROSS, CORE = 8, 4, 2, 1
OWN, SIDE, BESIDE, BEYOND, CORNER = (0, 0), (CROSS, CROSS), (NEAR, NEAR), (FAR, FAR), (NEAR | CROSS, NEAR | CROSS)
FIRST, SECOND = (FAR | NEAR, FAR | CROSS), (FAR | CROSS, FAR | NEAR)
END = (FAR | NEAR | CROSS, FAR | NEAR | CROSS)


def partner(name):
    return name[1] | CORE, name[0] | CORE


EARLY = (OWN, SIDE, BESIDE, BEYOND, CORNER, FIRST, SECOND, partner(OWN), partner(SIDE), partner(BESIDE), partner(CORNER))
MIDDLE = (partner(BEYOND), partner(FIRST), partner(SECOND), END)
LAST = (partner(END),)
ORDER = EARLY + MIDDLE + LAST


def load_all(*copies):
    copies = [pltpu.make_async_copy(*copy) for copy in copies]
    for copy in copies:
        copy.start()
    return copies


def pack_kernel(dims_hbm, right_hbm, pairs_ref, dims_ref, right_ref, sems):
    count, tile, width = pairs_ref.shape
    copies = load_all((dims_hbm, dims_ref, sems.at[0]), (right_hbm, right_ref, sems.at[1]))
    rows = lax.broadcasted_iota(jnp.int32, (tile, tile), 0)
    cols = lax.broadcasted_iota(jnp.int32, (tile, tile), 1)
    most = jnp.maximum(rows, cols)
    for copy in copies:
        copy.wait()

    def kept(b):
        return jnp.where(most < dims_ref[b], right_ref[b].astype(jnp.float32), 0.0)

    for p in range(count):
        both = jnp.concatenate([kept(p), kept(p + count)], axis=0)
        pairs_ref[p] = both.T.astype(jnp.bfloat16)


def left_kernel(
    pair_count, held, dims_hbm, active_hbm, owner_hbm, slot_hbm, left_hbm, psi_hbm,
    half_ref, list_ref, dims_ref, active_ref, owner_ref, slot_ref, left_ref, psi_ref, sems, psi_sems,
):
    sectors, blocks, tile, width = psi_ref.shape
    items = sectors * blocks
    last = held + len(MIDDLE) * pair_count
    copies = load_all(
        (dims_hbm, dims_ref, sems.at[0]),
        (active_hbm, active_ref, sems.at[1]),
        (owner_hbm, owner_ref, sems.at[2]),
        (slot_hbm, slot_ref, sems.at[3]),
        (left_hbm, left_ref, sems.at[4]),
    )
    psi_copies = load_all(*[(psi_hbm.at[a], psi_ref.at[a], psi_sems.at[a]) for a in range(sectors)])
    rows = lax.broadcasted_iota(jnp.int32, (tile, tile), 0)
    cols = lax.broadcasted_iota(jnp.int32, (tile, tile), 1)
    most = jnp.maximum(rows, cols)
    me = lax.axis_index("sec")
    by_swaps = lax.axis_size("sec") == len(ORDER)
    for copy in copies:
        copy.wait()
    in_middle, in_last = jnp.int32(0), jnp.int32(0)
    for a in range(sectors):
        psi_copies[a].wait()
        op = jnp.where(most < dims_ref[a], left_ref[a].astype(jnp.float32), 0.0).astype(jnp.bfloat16)
        before = in_last
        for k in range(0, blocks, 2):
            both = jnp.concatenate([psi_ref[a, k], psi_ref[a, k + 1]], axis=1)
            part = jnp.dot(op, both, preferred_element_type=jnp.float32)
            for u in range(2):
                active = active_ref[a, k + u].astype(jnp.float32)
                half_ref[a, k + u] = (part[:, u * width:(u + 1) * width] * active).astype(jnp.bfloat16)
                item = a * blocks + k + u
                owner, slot = owner_ref[a, k + u], slot_ref[a, k + u]
                at = piece_at(owner ^ me, me) if by_swaps else owner
                second = slot >= pair_count
                at = at * pair_count + jnp.where(second, slot - pair_count, slot)
                is_early, is_last = at < held, at >= last
                at = (at - jnp.where(is_last, last, jnp.where(is_early, 0, held))) * 2 + second.astype(jnp.int32)
                list_ref[jnp.where(is_last, items + 1 + in_last, in_middle)] = at * items + item
                list_ref[2 * items + 2 + sectors + item] = jnp.where(is_early, at, 0)
                in_last = in_last + is_last.astype(jnp.int32)
                in_middle = in_middle + jnp.logical_not(is_early | is_last).astype(jnp.int32)
        list_ref[2 * items + 2 + a] = in_last - before
    list_ref[items] = in_middle
    list_ref[2 * items + 1] = in_last


def block_form(pair, second):
    tile, width = pair.shape
    lower = (lax.broadcasted_iota(jnp.int32, pair.shape, 1) < tile).astype(jnp.bfloat16)
    other = pltpu.roll(pair, tile, 1)
    top = jnp.where(second, other, pair) * lower
    low = jnp.where(second, pair, other) * (1 - lower)
    return jnp.concatenate([top, low], axis=0)


def two_products(halves, forms):
    zero = jnp.zeros_like(forms[0])
    top = jnp.concatenate([forms[0], zero], axis=1)
    low = jnp.concatenate([zero, forms[1]], axis=1)
    both = jnp.concatenate([top, low], axis=0)
    part = jnp.dot(jnp.concatenate(halves, axis=1), both, preferred_element_type=jnp.float32)
    width = part.shape[1] // 2
    return part[:, :width].astype(jnp.bfloat16), part[:, width:].astype(jnp.bfloat16)


def merge(piece_refs, pairs_ref):
    at = 0
    for piece in piece_refs:
        pairs_ref[at:at + piece.shape[0]] = piece[...]
        at += piece.shape[0]


def piece_at(r, me):
    at = jnp.int32(0)
    for parity in range(2):
        places = [ORDER.index(next(name for name in ORDER if name[parity] == i)) for i in range(len(ORDER))]
        for half in range(2):
            packed = sum(place << (4 * i) for i, place in enumerate(places[8 * half:8 * half + 7]))
            mine = jnp.where(r & 7 == 7, places[8 * half + 7], (packed >> (4 * (r & 7))) & 15)
            at = jnp.where((me & 1 == parity) & (r >> 3 == half), mine, at)
    return at


def early_kernel(list_ref, half_ref, *refs):
    piece_refs, (out_ref, pairs_ref) = refs[:-2], refs[-2:]
    sectors, blocks, tile, width = out_ref.shape
    first = 2 * sectors * blocks + 2 + sectors
    merge(piece_refs, pairs_ref)

    def one(a, carry):
        for k in range(0, blocks, 2):
            ats = [list_ref[first + a * blocks + k + u] for u in range(2)]
            forms = [block_form(pairs_ref[at // 2], at % 2 == 1) for at in ats]
            out_ref[a, k], out_ref[a, k + 1] = two_products([half_ref[a, k], half_ref[a, k + 1]], forms)
        return carry

    lax.fori_loop(0, sectors, one, 0, unroll=2)


def listed_products(group_size, first, list_ref, half_ref, pairs_ref, out_ref):
    sectors, blocks, tile, width = half_ref.shape
    items = sectors * blocks
    listed = list_ref[first + items]

    def group(g, carry):
        for u in range(0, group_size, 2):
            entries = [list_ref[first + jnp.minimum(g * group_size + u + n, listed - 1)] for n in range(2)]
            places, halves, forms = [], [], []
            for entry in entries:
                item, at = entry % items, entry // items
                places.append((item // blocks, item % blocks))
                halves.append(half_ref[places[-1]])
                forms.append(block_form(pairs_ref[at // 2], at % 2 == 1))
            out_ref[places[0]], out_ref[places[1]] = two_products(halves, forms)
        return carry

    lax.fori_loop(0, (listed + group_size - 1) // group_size, group, 0)


def middle_kernel(list_ref, early_ref, half_ref, *refs):
    piece_refs, (out_ref, pairs_ref) = refs[:-2], refs[-2:]
    out_ref[...] = early_ref[...]
    merge(piece_refs, pairs_ref)
    listed_products(8, 0, list_ref, half_ref, pairs_ref, out_ref)


def last_kernel(list_ref, middle_ref, half_ref, pairs_ref, out_hbm, out_ref, sems):
    sectors, blocks, tile, width = half_ref.shape
    items = sectors * blocks

    def store(a, ref):
        return pltpu.make_async_copy(ref.at[a], out_hbm.at[a], sems.at[a])

    for a in range(sectors):
        changed = list_ref[2 * items + 2 + a] > 0

        @pl.when(changed)
        def _():
            out_ref[a] = middle_ref[a]

        @pl.when(jnp.logical_not(changed))
        def _():
            store(a, middle_ref).start()

    listed_products(4, items + 1, list_ref, half_ref, pairs_ref, out_ref)
    for a in range(sectors):

        @pl.when(list_ref[2 * items + 2 + a] > 0)
        def _():
            store(a, out_ref).start()

    for a in range(sectors):
        store(a, out_ref).wait()


def swap(piece, even_bit, odd_bit):
    count = lax.axis_size("sec")
    return lax.ppermute(piece, "sec", [(i, i ^ (odd_bit if i & CORE else even_bit)) for i in range(count)])


def per_device(
    psi, left_ops, right_ops, dims_left, dims_right, right_owner, right_slot, term_active
):
    left_count, block_count, tile, width = psi.shape
    items = left_count * block_count
    pair_count = right_ops.shape[0] // 2
    count = lax.axis_size("sec")
    by_swaps = count == len(ORDER)
    flops = 2 * psi.size * tile
    smem = pl.BlockSpec(memory_space=pltpu.SMEM)
    vmem = pl.BlockSpec(memory_space=pltpu.VMEM)
    hbm = pl.BlockSpec(memory_space=pltpu.HBM)
    params = pltpu.CompilerParams(vmem_limit_bytes=VMEM_LIMIT)

    def in_hbm(*arrays):
        return [pltpu.with_memory_space_constraint(array, pltpu.HBM) for array in arrays]

    pairs = pl.pallas_call(
        pack_kernel,
        out_shape=jax.ShapeDtypeStruct((pair_count, tile, 2 * tile), jnp.bfloat16),
        in_specs=[hbm, hbm],
        out_specs=vmem,
        scratch_shapes=[
            pltpu.SMEM(dims_right.shape, jnp.int32),
            pltpu.VMEM(right_ops.shape, jnp.bfloat16),
            pltpu.SemaphoreType.DMA((2,)),
        ],
        compiler_params=params,
        cost_estimate=pl.CostEstimate(flops=0, bytes_accessed=2 * right_ops.size, transcendentals=0),
    )(*in_hbm(dims_right, right_ops))

    active = term_active.reshape(left_count, block_count)
    half, listed = pl.pallas_call(
        functools.partial(left_kernel, pair_count, len(EARLY if by_swaps else range(count)) * pair_count),
        out_shape=(
            jax.ShapeDtypeStruct(psi.shape, jnp.bfloat16),
            pltpu.SMEM((3 * items + 2 + left_count,), jnp.int32),
        ),
        in_specs=[hbm] * 6,
        out_specs=(vmem, smem),
        scratch_shapes=[
            pltpu.SMEM(dims_left.shape, jnp.int32),
            pltpu.SMEM(active.shape, jnp.int32),
            pltpu.SMEM(right_owner.shape, jnp.int32),
            pltpu.SMEM(right_slot.shape, jnp.int32),
            pltpu.VMEM(left_ops.shape, jnp.bfloat16),
            pltpu.VMEM(psi.shape, jnp.bfloat16),
            pltpu.SemaphoreType.DMA((5,)),
            pltpu.SemaphoreType.DMA((left_count,)),
        ],
        compiler_params=params,
        cost_estimate=pl.CostEstimate(flops=flops, bytes_accessed=2 * psi.size, transcendentals=0),
    )(*in_hbm(dims_left, active, right_owner, right_slot, left_ops, psi))
    listed = pltpu.with_memory_space_constraint(listed, pltpu.SMEM)

    if by_swaps:
        pieces = {OWN: pairs}

        def pass_on(*routes):
            for name, target in routes:
                pieces[target] = swap(pieces[name], name[0] ^ target[0], name[1] ^ target[1])

        def share(*names):
            for name in names:
                pieces[partner(name)] = swap(pieces[name], CORE, CORE)

        pass_on((OWN, BEYOND), (OWN, BESIDE), (OWN, SIDE))
        held = (OWN, BESIDE,)
        half, ends = lax.optimization_barrier((half, [pieces[name] for name in held]))
        pieces.update(zip(held, ends))
        pass_on((BESIDE, CORNER), (BEYOND, FIRST), (BEYOND, SECOND), (FIRST, END))
        share(OWN, BESIDE, SIDE, CORNER, BEYOND, FIRST, SECOND)
        early = [pieces[name] for name in EARLY]
    else:
        early = [lax.all_gather(pairs, "sec", axis=0, tiled=True)]

    sigma = pl.pallas_call(
        early_kernel,
        out_shape=jax.ShapeDtypeStruct(psi.shape, jnp.bfloat16),
        in_specs=[smem] + [vmem] * (1 + len(early)),
        out_specs=vmem,
        scratch_shapes=[pltpu.VMEM((sum(piece.shape[0] for piece in early), tile, 2 * tile), jnp.bfloat16)],
        compiler_params=params,
        cost_estimate=pl.CostEstimate(flops=flops, bytes_accessed=2 * psi.size, transcendentals=0),
    )(listed, half, *early)
    if by_swaps:
        pieces[END], sigma = lax.optimization_barrier((pieces[END], sigma))
        share(END)
        sigma = pl.pallas_call(
            middle_kernel,
            out_shape=jax.ShapeDtypeStruct(psi.shape, jnp.bfloat16),
            in_specs=[smem] + [vmem] * (2 + len(MIDDLE)),
            out_specs=vmem,
            scratch_shapes=[pltpu.VMEM((len(MIDDLE) * pair_count, tile, 2 * tile), jnp.bfloat16)],
            compiler_params=params,
            cost_estimate=pl.CostEstimate(flops=flops // 4, bytes_accessed=psi.size // 2, transcendentals=0),
        )(listed, sigma, half, *[pieces[name] for name in MIDDLE])
        sigma = pl.pallas_call(
            last_kernel,
            out_shape=jax.ShapeDtypeStruct(psi.shape, jnp.bfloat16),
            in_specs=[smem] + [vmem] * 3,
            out_specs=hbm,
            scratch_shapes=[pltpu.VMEM(psi.shape, jnp.bfloat16), pltpu.SemaphoreType.DMA((left_count,))],
            compiler_params=params,
            cost_estimate=pl.CostEstimate(flops=flops // 16, bytes_accessed=2 * psi.size, transcendentals=0),
        )(listed, sigma, half, pieces[LAST[0]])
    if lax.axis_size("op") > 1:
        sigma = lax.psum_scatter(sigma, "op", scatter_dimension=3, tiled=True)
    return sigma


def solution(mesh):
    placed = (
        P(("grp", "sec"), None, None, None),
        P(("grp", "sec"), None, "op"),
        P(("grp", "sec"), None, "op"),
        P(("grp", "sec")),
        P(("grp", "sec")),
        P(("grp", "sec"), None),
        P(("grp", "sec"), None),
        P(("grp", "sec"), None, "op"),
    )
    return jax.shard_map(
        per_device,
        mesh=mesh,
        in_specs=placed,
        out_specs=P(("grp", "sec"), None, None, "op"),
        check_vma=False,
    )
```

```python
import functools

import jax
import jax.numpy as jnp
from jax import lax
from jax.experimental import pallas as pl
from jax.experimental.pallas import tpu as pltpu
from jax.sharding import PartitionSpec as P

VMEM_LIMIT = 48 * 1024 * 1024
FAR, NEAR, CROSS, CORE = 8, 4, 2, 1
OWN, SIDE, BESIDE, BEYOND, CORNER = (0, 0), (CROSS, NEAR), (NEAR, CROSS), (FAR, FAR), (NEAR | CROSS, NEAR | CROSS)
FIRST, SECOND = (FAR | NEAR, FAR | CROSS), (FAR | CROSS, FAR | NEAR)
END = (FAR | NEAR | CROSS, FAR | NEAR | CROSS)


def partner(name):
    return name[1] | CORE, name[0] | CORE


EARLY = (OWN, SIDE, BESIDE, BEYOND, CORNER, FIRST, SECOND, partner(OWN), partner(SIDE), partner(BESIDE), partner(CORNER))
MIDDLE = (partner(BEYOND), partner(FIRST), partner(SECOND), END)
LAST = (partner(END),)
ORDER = EARLY + MIDDLE + LAST


def load_all(*copies):
    copies = [pltpu.make_async_copy(*copy) for copy in copies]
    for copy in copies:
        copy.start()
    return copies


def pack_kernel(dims_hbm, right_hbm, pairs_ref, dims_ref, right_ref, sems):
    count, tile, width = pairs_ref.shape
    copies = load_all((dims_hbm, dims_ref, sems.at[0]), (right_hbm, right_ref, sems.at[1]))
    rows = lax.broadcasted_iota(jnp.int32, (tile, tile), 0)
    cols = lax.broadcasted_iota(jnp.int32, (tile, tile), 1)
    most = jnp.maximum(rows, cols)
    for copy in copies:
        copy.wait()

    def kept(b):
        return jnp.where(most < dims_ref[b], right_ref[b].astype(jnp.float32), 0.0)

    for p in range(count):
        both = jnp.concatenate([kept(p), kept(p + count)], axis=0)
        pairs_ref[p] = both.T.astype(jnp.bfloat16)


def left_kernel(
    pair_count, held, dims_hbm, active_hbm, owner_hbm, slot_hbm, left_hbm, psi_hbm,
    half_ref, list_ref, dims_ref, active_ref, owner_ref, slot_ref, left_ref, psi_ref, sems, psi_sems,
):
    sectors, blocks, tile, width = psi_ref.shape
    items = sectors * blocks
    last = held + len(MIDDLE) * pair_count
    copies = load_all(
        (dims_hbm, dims_ref, sems.at[0]),
        (active_hbm, active_ref, sems.at[1]),
        (owner_hbm, owner_ref, sems.at[2]),
        (slot_hbm, slot_ref, sems.at[3]),
        (left_hbm, left_ref, sems.at[4]),
    )
    psi_copies = load_all(*[(psi_hbm.at[a], psi_ref.at[a], psi_sems.at[a]) for a in range(sectors)])
    rows = lax.broadcasted_iota(jnp.int32, (tile, tile), 0)
    cols = lax.broadcasted_iota(jnp.int32, (tile, tile), 1)
    most = jnp.maximum(rows, cols)
    me = lax.axis_index("sec")
    by_swaps = lax.axis_size("sec") == len(ORDER)
    for copy in copies:
        copy.wait()
    in_middle, in_last = jnp.int32(0), jnp.int32(0)
    for a in range(sectors):
        psi_copies[a].wait()
        op = jnp.where(most < dims_ref[a], left_ref[a].astype(jnp.float32), 0.0).astype(jnp.bfloat16)
        before = in_last
        for k in range(0, blocks, 2):
            both = jnp.concatenate([psi_ref[a, k], psi_ref[a, k + 1]], axis=1)
            part = jnp.dot(op, both, preferred_element_type=jnp.float32)
            for u in range(2):
                active = active_ref[a, k + u].astype(jnp.float32)
                half_ref[a, k + u] = (part[:, u * width:(u + 1) * width] * active).astype(jnp.bfloat16)
                item = a * blocks + k + u
                owner, slot = owner_ref[a, k + u], slot_ref[a, k + u]
                at = piece_at(owner ^ me, me) if by_swaps else owner
                second = slot >= pair_count
                at = at * pair_count + jnp.where(second, slot - pair_count, slot)
                is_early, is_last = at < held, at >= last
                at = (at - jnp.where(is_last, last, jnp.where(is_early, 0, held))) * 2 + second.astype(jnp.int32)
                list_ref[jnp.where(is_last, items + 1 + in_last, in_middle)] = at * items + item
                list_ref[2 * items + 2 + sectors + item] = jnp.where(is_early, at, 0)
                in_last = in_last + is_last.astype(jnp.int32)
                in_middle = in_middle + jnp.logical_not(is_early | is_last).astype(jnp.int32)
        list_ref[2 * items + 2 + a] = in_last - before
    list_ref[items] = in_middle
    list_ref[2 * items + 1] = in_last


def block_form(pair, second):
    tile, width = pair.shape
    lower = (lax.broadcasted_iota(jnp.int32, pair.shape, 1) < tile).astype(jnp.bfloat16)
    other = pltpu.roll(pair, tile, 1)
    top = jnp.where(second, other, pair) * lower
    low = jnp.where(second, pair, other) * (1 - lower)
    return jnp.concatenate([top, low], axis=0)


def two_products(halves, forms):
    zero = jnp.zeros_like(forms[0])
    top = jnp.concatenate([forms[0], zero], axis=1)
    low = jnp.concatenate([zero, forms[1]], axis=1)
    both = jnp.concatenate([top, low], axis=0)
    part = jnp.dot(jnp.concatenate(halves, axis=1), both, preferred_element_type=jnp.float32)
    width = part.shape[1] // 2
    return part[:, :width].astype(jnp.bfloat16), part[:, width:].astype(jnp.bfloat16)


def merge(piece_refs, pairs_ref):
    at = 0
    for piece in piece_refs:
        pairs_ref[at:at + piece.shape[0]] = piece[...]
        at += piece.shape[0]


def piece_at(r, me):
    at = jnp.int32(0)
    for parity in range(2):
        places = [ORDER.index(next(name for name in ORDER if name[parity] == i)) for i in range(len(ORDER))]
        for half in range(2):
            packed = sum(place << (4 * i) for i, place in enumerate(places[8 * half:8 * half + 7]))
            mine = jnp.where(r & 7 == 7, places[8 * half + 7], (packed >> (4 * (r & 7))) & 15)
            at = jnp.where((me & 1 == parity) & (r >> 3 == half), mine, at)
    return at


def early_kernel(list_ref, half_ref, *refs):
    piece_refs, (out_ref, pairs_ref) = refs[:-2], refs[-2:]
    sectors, blocks, tile, width = out_ref.shape
    first = 2 * sectors * blocks + 2 + sectors
    merge(piece_refs, pairs_ref)

    def one(a, carry):
        for k in range(0, blocks, 2):
            ats = [list_ref[first + a * blocks + k + u] for u in range(2)]
            forms = [block_form(pairs_ref[at // 2], at % 2 == 1) for at in ats]
            out_ref[a, k], out_ref[a, k + 1] = two_products([half_ref[a, k], half_ref[a, k + 1]], forms)
        return carry

    lax.fori_loop(0, sectors, one, 0, unroll=2)


def listed_products(group_size, first, list_ref, half_ref, pairs_ref, out_ref):
    sectors, blocks, tile, width = half_ref.shape
    items = sectors * blocks
    listed = list_ref[first + items]

    def group(g, carry):
        for u in range(0, group_size, 2):
            entries = [list_ref[first + jnp.minimum(g * group_size + u + n, listed - 1)] for n in range(2)]
            places, halves, forms = [], [], []
            for entry in entries:
                item, at = entry % items, entry // items
                places.append((item // blocks, item % blocks))
                halves.append(half_ref[places[-1]])
                forms.append(block_form(pairs_ref[at // 2], at % 2 == 1))
            out_ref[places[0]], out_ref[places[1]] = two_products(halves, forms)
        return carry

    lax.fori_loop(0, (listed + group_size - 1) // group_size, group, 0)


def middle_kernel(list_ref, early_ref, half_ref, *refs):
    piece_refs, (out_ref, pairs_ref) = refs[:-2], refs[-2:]
    out_ref[...] = early_ref[...]
    merge(piece_refs, pairs_ref)
    listed_products(8, 0, list_ref, half_ref, pairs_ref, out_ref)


def last_kernel(list_ref, middle_ref, half_ref, pairs_ref, out_hbm, out_ref, sems):
    sectors, blocks, tile, width = half_ref.shape
    items = sectors * blocks

    def store(a, ref):
        return pltpu.make_async_copy(ref.at[a], out_hbm.at[a], sems.at[a])

    for a in range(sectors):
        changed = list_ref[2 * items + 2 + a] > 0

        @pl.when(changed)
        def _():
            out_ref[a] = middle_ref[a]

        @pl.when(jnp.logical_not(changed))
        def _():
            store(a, middle_ref).start()

    listed_products(4, items + 1, list_ref, half_ref, pairs_ref, out_ref)
    for a in range(sectors):

        @pl.when(list_ref[2 * items + 2 + a] > 0)
        def _():
            store(a, out_ref).start()

    for a in range(sectors):
        store(a, out_ref).wait()


def swap(piece, even_bit, odd_bit):
    count = lax.axis_size("sec")
    return lax.ppermute(piece, "sec", [(i, i ^ (odd_bit if i & CORE else even_bit)) for i in range(count)])


def per_device(
    psi, left_ops, right_ops, dims_left, dims_right, right_owner, right_slot, term_active
):
    left_count, block_count, tile, width = psi.shape
    items = left_count * block_count
    pair_count = right_ops.shape[0] // 2
    count = lax.axis_size("sec")
    by_swaps = count == len(ORDER)
    flops = 2 * psi.size * tile
    smem = pl.BlockSpec(memory_space=pltpu.SMEM)
    vmem = pl.BlockSpec(memory_space=pltpu.VMEM)
    hbm = pl.BlockSpec(memory_space=pltpu.HBM)
    params = pltpu.CompilerParams(vmem_limit_bytes=VMEM_LIMIT)

    def in_hbm(*arrays):
        return [pltpu.with_memory_space_constraint(array, pltpu.HBM) for array in arrays]

    pairs = pl.pallas_call(
        pack_kernel,
        out_shape=jax.ShapeDtypeStruct((pair_count, tile, 2 * tile), jnp.bfloat16),
        in_specs=[hbm, hbm],
        out_specs=vmem,
        scratch_shapes=[
            pltpu.SMEM(dims_right.shape, jnp.int32),
            pltpu.VMEM(right_ops.shape, jnp.bfloat16),
            pltpu.SemaphoreType.DMA((2,)),
        ],
        compiler_params=params,
        cost_estimate=pl.CostEstimate(flops=0, bytes_accessed=2 * right_ops.size, transcendentals=0),
    )(*in_hbm(dims_right, right_ops))

    active = term_active.reshape(left_count, block_count)
    half, listed = pl.pallas_call(
        functools.partial(left_kernel, pair_count, len(EARLY if by_swaps else range(count)) * pair_count),
        out_shape=(
            jax.ShapeDtypeStruct(psi.shape, jnp.bfloat16),
            pltpu.SMEM((3 * items + 2 + left_count,), jnp.int32),
        ),
        in_specs=[hbm] * 6,
        out_specs=(vmem, smem),
        scratch_shapes=[
            pltpu.SMEM(dims_left.shape, jnp.int32),
            pltpu.SMEM(active.shape, jnp.int32),
            pltpu.SMEM(right_owner.shape, jnp.int32),
            pltpu.SMEM(right_slot.shape, jnp.int32),
            pltpu.VMEM(left_ops.shape, jnp.bfloat16),
            pltpu.VMEM(psi.shape, jnp.bfloat16),
            pltpu.SemaphoreType.DMA((5,)),
            pltpu.SemaphoreType.DMA((left_count,)),
        ],
        compiler_params=params,
        cost_estimate=pl.CostEstimate(flops=flops, bytes_accessed=2 * psi.size, transcendentals=0),
    )(*in_hbm(dims_left, active, right_owner, right_slot, left_ops, psi))
    listed = pltpu.with_memory_space_constraint(listed, pltpu.SMEM)

    if by_swaps:
        pieces = {OWN: pairs}

        def pass_on(*routes):
            for name, target in routes:
                pieces[target] = swap(pieces[name], name[0] ^ target[0], name[1] ^ target[1])

        def share(*names):
            for name in names:
                pieces[partner(name)] = swap(pieces[name], CORE, CORE)

        pass_on((OWN, BEYOND), (OWN, BESIDE), (OWN, SIDE))
        held = (OWN, BESIDE,)
        half, ends = lax.optimization_barrier((half, [pieces[name] for name in held]))
        pieces.update(zip(held, ends))
        pass_on((BESIDE, CORNER), (BEYOND, FIRST), (BEYOND, SECOND), (FIRST, END))
        share(OWN, BESIDE, SIDE, CORNER, BEYOND, FIRST, SECOND)
        early = [pieces[name] for name in EARLY]
    else:
        early = [lax.all_gather(pairs, "sec", axis=0, tiled=True)]

    sigma = pl.pallas_call(
        early_kernel,
        out_shape=jax.ShapeDtypeStruct(psi.shape, jnp.bfloat16),
        in_specs=[smem] + [vmem] * (1 + len(early)),
        out_specs=vmem,
        scratch_shapes=[pltpu.VMEM((sum(piece.shape[0] for piece in early), tile, 2 * tile), jnp.bfloat16)],
        compiler_params=params,
        cost_estimate=pl.CostEstimate(flops=flops, bytes_accessed=2 * psi.size, transcendentals=0),
    )(listed, half, *early)
    if by_swaps:
        pieces[END], sigma = lax.optimization_barrier((pieces[END], sigma))
        share(END)
        sigma = pl.pallas_call(
            middle_kernel,
            out_shape=jax.ShapeDtypeStruct(psi.shape, jnp.bfloat16),
            in_specs=[smem] + [vmem] * (2 + len(MIDDLE)),
            out_specs=vmem,
            scratch_shapes=[pltpu.VMEM((len(MIDDLE) * pair_count, tile, 2 * tile), jnp.bfloat16)],
            compiler_params=params,
            cost_estimate=pl.CostEstimate(flops=flops // 4, bytes_accessed=psi.size // 2, transcendentals=0),
        )(listed, sigma, half, *[pieces[name] for name in MIDDLE])
        sigma = pl.pallas_call(
            last_kernel,
            out_shape=jax.ShapeDtypeStruct(psi.shape, jnp.bfloat16),
            in_specs=[smem] + [vmem] * 3,
            out_specs=hbm,
            scratch_shapes=[pltpu.VMEM(psi.shape, jnp.bfloat16), pltpu.SemaphoreType.DMA((left_count,))],
            compiler_params=params,
            cost_estimate=pl.CostEstimate(flops=flops // 16, bytes_accessed=2 * psi.size, transcendentals=0),
        )(listed, sigma, half, pieces[LAST[0]])
    if lax.axis_size("op") > 1:
        sigma = lax.psum_scatter(sigma, "op", scatter_dimension=3, tiled=True)
    return sigma


def solution(mesh):
    placed = (
        P(("grp", "sec"), None, None, None),
        P(("grp", "sec"), None, "op"),
        P(("grp", "sec"), None, "op"),
        P(("grp", "sec")),
        P(("grp", "sec")),
        P(("grp", "sec"), None),
        P(("grp", "sec"), None),
        P(("grp", "sec"), None, "op"),
    )
    return jax.shard_map(
        per_device,
        mesh=mesh,
        in_specs=placed,
        out_specs=P(("grp", "sec"), None, None, "op"),
        check_vma=False,
    )
```

```python
import functools

import jax
import jax.numpy as jnp
from jax import lax
from jax.experimental import pallas as pl
from jax.experimental.pallas import tpu as pltpu
from jax.sharding import PartitionSpec as P

VMEM_LIMIT = 48 * 1024 * 1024
FAR, NEAR, CROSS, CORE = 8, 4, 2, 1
MIDDLE = (NEAR | CROSS | CORE, FAR | CORE, FAR | NEAR | CORE, FAR | CROSS | CORE, FAR | NEAR | CROSS)
LAST = (FAR | NEAR | CROSS | CORE,)
EARLY = tuple(r for r in range(16) if r not in MIDDLE + LAST)
ORDER = EARLY + MIDDLE + LAST


def load_all(*copies):
    copies = [pltpu.make_async_copy(*copy) for copy in copies]
    for copy in copies:
        copy.start()
    return copies


def pack_kernel(dims_hbm, right_hbm, pairs_ref, dims_ref, right_ref, sems):
    count, tile, width = pairs_ref.shape
    copies = load_all((dims_hbm, dims_ref, sems.at[0]), (right_hbm, right_ref, sems.at[1]))
    rows = lax.broadcasted_iota(jnp.int32, (tile, tile), 0)
    cols = lax.broadcasted_iota(jnp.int32, (tile, tile), 1)
    most = jnp.maximum(rows, cols)
    for copy in copies:
        copy.wait()

    def kept(b):
        return jnp.where(most < dims_ref[b], right_ref[b].astype(jnp.float32), 0.0)

    for p in range(count):
        both = jnp.concatenate([kept(p), kept(p + count)], axis=0)
        pairs_ref[p] = both.T.astype(jnp.bfloat16)


def left_kernel(
    pair_count, held, dims_hbm, active_hbm, owner_hbm, slot_hbm, left_hbm, psi_hbm,
    half_ref, list_ref, dims_ref, active_ref, owner_ref, slot_ref, left_ref, psi_ref, sems, psi_sems,
):
    sectors, blocks, tile, width = psi_ref.shape
    items = sectors * blocks
    last = held + len(MIDDLE) * pair_count
    copies = load_all(
        (dims_hbm, dims_ref, sems.at[0]),
        (active_hbm, active_ref, sems.at[1]),
        (owner_hbm, owner_ref, sems.at[2]),
        (slot_hbm, slot_ref, sems.at[3]),
        (left_hbm, left_ref, sems.at[4]),
    )
    psi_copies = load_all(*[(psi_hbm.at[a], psi_ref.at[a], psi_sems.at[a]) for a in range(sectors)])
    rows = lax.broadcasted_iota(jnp.int32, (tile, tile), 0)
    cols = lax.broadcasted_iota(jnp.int32, (tile, tile), 1)
    most = jnp.maximum(rows, cols)
    me = lax.axis_index("sec")
    by_swaps = lax.axis_size("sec") == len(ORDER)
    for copy in copies:
        copy.wait()
    in_middle, in_last = jnp.int32(0), jnp.int32(0)
    for a in range(sectors):
        psi_copies[a].wait()
        op = jnp.where(most < dims_ref[a], left_ref[a].astype(jnp.float32), 0.0).astype(jnp.bfloat16)
        before = in_last
        for k in range(0, blocks, 2):
            both = jnp.concatenate([psi_ref[a, k], psi_ref[a, k + 1]], axis=1)
            part = jnp.dot(op, both, preferred_element_type=jnp.float32)
            for u in range(2):
                active = active_ref[a, k + u].astype(jnp.float32)
                half_ref[a, k + u] = (part[:, u * width:(u + 1) * width] * active).astype(jnp.bfloat16)
                item = a * blocks + k + u
                owner, slot = owner_ref[a, k + u], slot_ref[a, k + u]
                at = piece_at(owner ^ me) if by_swaps else owner
                second = slot >= pair_count
                at = at * pair_count + jnp.where(second, slot - pair_count, slot)
                is_early, is_last = at < held, at >= last
                at = (at - jnp.where(is_last, last, jnp.where(is_early, 0, held))) * 2 + second.astype(jnp.int32)
                list_ref[jnp.where(is_last, items + 1 + in_last, in_middle)] = at * items + item
                list_ref[2 * items + 2 + sectors + item] = jnp.where(is_early, at, 0)
                in_last = in_last + is_last.astype(jnp.int32)
                in_middle = in_middle + jnp.logical_not(is_early | is_last).astype(jnp.int32)
        list_ref[2 * items + 2 + a] = in_last - before
    list_ref[items] = in_middle
    list_ref[2 * items + 1] = in_last


def block_form(pair, second):
    tile, width = pair.shape
    lower = (lax.broadcasted_iota(jnp.int32, pair.shape, 1) < tile).astype(jnp.bfloat16)
    other = pltpu.roll(pair, tile, 1)
    top = jnp.where(second, other, pair) * lower
    low = jnp.where(second, pair, other) * (1 - lower)
    return jnp.concatenate([top, low], axis=0)


def two_products(halves, forms):
    zero = jnp.zeros_like(forms[0])
    top = jnp.concatenate([forms[0], zero], axis=1)
    low = jnp.concatenate([zero, forms[1]], axis=1)
    both = jnp.concatenate([top, low], axis=0)
    part = jnp.dot(jnp.concatenate(halves, axis=1), both, preferred_element_type=jnp.float32)
    width = part.shape[1] // 2
    return part[:, :width].astype(jnp.bfloat16), part[:, width:].astype(jnp.bfloat16)


def merge(piece_refs, pairs_ref):
    at = 0
    for piece in piece_refs:
        pairs_ref[at:at + piece.shape[0]] = piece[...]
        at += piece.shape[0]


def piece_at(r):
    low = sum(ORDER.index(i) << (4 * i) for i in range(7))
    high = sum(ORDER.index(i + 8) << (4 * i) for i in range(7))
    packed = jnp.where(r < 8, low, high) >> (4 * (r & 7))
    end = jnp.where(r < 8, ORDER.index(7), ORDER.index(15))
    return jnp.where(r & 7 == 7, end, packed & 15)


def early_kernel(list_ref, half_ref, *refs):
    piece_refs, (out_ref, pairs_ref) = refs[:-2], refs[-2:]
    sectors, blocks, tile, width = out_ref.shape
    first = 2 * sectors * blocks + 2 + sectors
    merge(piece_refs, pairs_ref)

    def one(a, carry):
        for k in range(0, blocks, 2):
            ats = [list_ref[first + a * blocks + k + u] for u in range(2)]
            forms = [block_form(pairs_ref[at // 2], at % 2 == 1) for at in ats]
            out_ref[a, k], out_ref[a, k + 1] = two_products([half_ref[a, k], half_ref[a, k + 1]], forms)
        return carry

    lax.fori_loop(0, sectors, one, 0, unroll=2)


def listed_products(group_size, first, list_ref, half_ref, pairs_ref, out_ref):
    sectors, blocks, tile, width = half_ref.shape
    items = sectors * blocks
    listed = list_ref[first + items]

    def group(g, carry):
        for u in range(0, group_size, 2):
            entries = [list_ref[first + jnp.minimum(g * group_size + u + n, listed - 1)] for n in range(2)]
            places, halves, forms = [], [], []
            for entry in entries:
                item, at = entry % items, entry // items
                places.append((item // blocks, item % blocks))
                halves.append(half_ref[places[-1]])
                forms.append(block_form(pairs_ref[at // 2], at % 2 == 1))
            out_ref[places[0]], out_ref[places[1]] = two_products(halves, forms)
        return carry

    lax.fori_loop(0, (listed + group_size - 1) // group_size, group, 0)


def middle_kernel(list_ref, early_ref, half_ref, *refs):
    piece_refs, (out_ref, pairs_ref) = refs[:-2], refs[-2:]
    out_ref[...] = early_ref[...]
    merge(piece_refs, pairs_ref)
    listed_products(8, 0, list_ref, half_ref, pairs_ref, out_ref)


def last_kernel(list_ref, middle_ref, half_ref, pairs_ref, out_hbm, out_ref, sems):
    sectors, blocks, tile, width = half_ref.shape
    items = sectors * blocks

    def store(a, ref):
        return pltpu.make_async_copy(ref.at[a], out_hbm.at[a], sems.at[a])

    for a in range(sectors):
        changed = list_ref[2 * items + 2 + a] > 0

        @pl.when(changed)
        def _():
            out_ref[a] = middle_ref[a]

        @pl.when(jnp.logical_not(changed))
        def _():
            store(a, middle_ref).start()

    listed_products(4, items + 1, list_ref, half_ref, pairs_ref, out_ref)
    for a in range(sectors):

        @pl.when(list_ref[2 * items + 2 + a] > 0)
        def _():
            store(a, out_ref).start()

    for a in range(sectors):
        store(a, out_ref).wait()


def swap(piece, bit):
    count = lax.axis_size("sec")
    return lax.ppermute(piece, "sec", [(i, i ^ bit) for i in range(count)])


def per_device(
    psi, left_ops, right_ops, dims_left, dims_right, right_owner, right_slot, term_active
):
    left_count, block_count, tile, width = psi.shape
    items = left_count * block_count
    pair_count = right_ops.shape[0] // 2
    count = lax.axis_size("sec")
    by_swaps = count == len(ORDER)
    flops = 2 * psi.size * tile
    smem = pl.BlockSpec(memory_space=pltpu.SMEM)
    vmem = pl.BlockSpec(memory_space=pltpu.VMEM)
    hbm = pl.BlockSpec(memory_space=pltpu.HBM)
    params = pltpu.CompilerParams(vmem_limit_bytes=VMEM_LIMIT)

    def in_hbm(*arrays):
        return [pltpu.with_memory_space_constraint(array, pltpu.HBM) for array in arrays]

    pairs = pl.pallas_call(
        pack_kernel,
        out_shape=jax.ShapeDtypeStruct((pair_count, tile, 2 * tile), jnp.bfloat16),
        in_specs=[hbm, hbm],
        out_specs=vmem,
        scratch_shapes=[
            pltpu.SMEM(dims_right.shape, jnp.int32),
            pltpu.VMEM(right_ops.shape, jnp.bfloat16),
            pltpu.SemaphoreType.DMA((2,)),
        ],
        compiler_params=params,
        cost_estimate=pl.CostEstimate(flops=0, bytes_accessed=2 * right_ops.size, transcendentals=0),
    )(*in_hbm(dims_right, right_ops))

    active = term_active.reshape(left_count, block_count)
    half, listed = pl.pallas_call(
        functools.partial(left_kernel, pair_count, len(EARLY if by_swaps else range(count)) * pair_count),
        out_shape=(
            jax.ShapeDtypeStruct(psi.shape, jnp.bfloat16),
            pltpu.SMEM((3 * items + 2 + left_count,), jnp.int32),
        ),
        in_specs=[hbm] * 6,
        out_specs=(vmem, smem),
        scratch_shapes=[
            pltpu.SMEM(dims_left.shape, jnp.int32),
            pltpu.SMEM(active.shape, jnp.int32),
            pltpu.SMEM(right_owner.shape, jnp.int32),
            pltpu.SMEM(right_slot.shape, jnp.int32),
            pltpu.VMEM(left_ops.shape, jnp.bfloat16),
            pltpu.VMEM(psi.shape, jnp.bfloat16),
            pltpu.SemaphoreType.DMA((5,)),
            pltpu.SemaphoreType.DMA((left_count,)),
        ],
        compiler_params=params,
        cost_estimate=pl.CostEstimate(flops=flops, bytes_accessed=2 * psi.size, transcendentals=0),
    )(*in_hbm(dims_left, active, right_owner, right_slot, left_ops, psi))
    listed = pltpu.with_memory_space_constraint(listed, pltpu.SMEM)

    if by_swaps:
        pieces = {0: pairs}
        def pass_on(*routes):
            for r, bit in routes:
                pieces[r | bit] = swap(pieces[r], bit)

        pass_on((0, FAR), (0, NEAR), (0, CROSS), (0, CORE))
        held = (FAR,)
        half, ends = lax.optimization_barrier((half, [pieces[r] for r in held]))
        pieces.update(zip(held, ends))
        pass_on((FAR, NEAR), (NEAR, CROSS), (FAR, CROSS), (FAR | NEAR, CROSS))
        pass_on((NEAR, CORE), (CROSS, CORE), (NEAR | CROSS, CORE), (FAR | NEAR, CORE), (FAR, CORE), (FAR | CROSS, CORE))
        early = [pieces[r] for r in EARLY]
    else:
        early = [lax.all_gather(pairs, "sec", axis=0, tiled=True)]

    sigma = pl.pallas_call(
        early_kernel,
        out_shape=jax.ShapeDtypeStruct(psi.shape, jnp.bfloat16),
        in_specs=[smem] + [vmem] * (1 + len(early)),
        out_specs=vmem,
        scratch_shapes=[pltpu.VMEM((sum(piece.shape[0] for piece in early), tile, 2 * tile), jnp.bfloat16)],
        compiler_params=params,
        cost_estimate=pl.CostEstimate(flops=flops, bytes_accessed=2 * psi.size, transcendentals=0),
    )(listed, half, *early)
    if by_swaps:
        top = FAR | NEAR | CROSS
        pieces[top], sigma = lax.optimization_barrier((pieces[top], sigma))
        pieces[top | CORE] = swap(pieces[top], CORE)
        sigma = pl.pallas_call(
            middle_kernel,
            out_shape=jax.ShapeDtypeStruct(psi.shape, jnp.bfloat16),
            in_specs=[smem] + [vmem] * (2 + len(MIDDLE)),
            out_specs=vmem,
            scratch_shapes=[pltpu.VMEM((len(MIDDLE) * pair_count, tile, 2 * tile), jnp.bfloat16)],
            compiler_params=params,
            cost_estimate=pl.CostEstimate(flops=flops // 4, bytes_accessed=psi.size // 2, transcendentals=0),
        )(listed, sigma, half, *[pieces[r] for r in MIDDLE])
        sigma = pl.pallas_call(
            last_kernel,
            out_shape=jax.ShapeDtypeStruct(psi.shape, jnp.bfloat16),
            in_specs=[smem] + [vmem] * 3,
            out_specs=hbm,
            scratch_shapes=[pltpu.VMEM(psi.shape, jnp.bfloat16), pltpu.SemaphoreType.DMA((left_count,))],
            compiler_params=params,
            cost_estimate=pl.CostEstimate(flops=flops // 16, bytes_accessed=2 * psi.size, transcendentals=0),
        )(listed, sigma, half, pieces[LAST[0]])
    if lax.axis_size("op") > 1:
        sigma = lax.psum_scatter(sigma, "op", scatter_dimension=3, tiled=True)
    return sigma


def solution(mesh):
    placed = (
        P(("grp", "sec"), None, None, None),
        P(("grp", "sec"), None, "op"),
        P(("grp", "sec"), None, "op"),
        P(("grp", "sec")),
        P(("grp", "sec")),
        P(("grp", "sec"), None),
        P(("grp", "sec"), None),
        P(("grp", "sec"), None, "op"),
    )
    return jax.shard_map(
        per_device,
        mesh=mesh,
        in_specs=placed,
        out_specs=P(("grp", "sec"), None, None, "op"),
        check_vma=False,
    )
```

```python
import functools

import jax
import jax.numpy as jnp
from jax import lax
from jax.experimental import pallas as pl
from jax.experimental.pallas import tpu as pltpu
from jax.sharding import PartitionSpec as P

VMEM_LIMIT = 48 * 1024 * 1024
FAR, NEAR, CROSS, CORE = 8, 4, 2, 1
OWN, SIDE, BESIDE, BEYOND, CORNER = (0, 0), (CROSS, CROSS), (NEAR, NEAR), (FAR, FAR), (NEAR | CROSS, NEAR | CROSS)
FIRST, SECOND = (FAR | NEAR, FAR | CROSS), (FAR | CROSS, FAR | NEAR)
END = (FAR | NEAR | CROSS, FAR | NEAR | CROSS)


def partner(name):
    return name[1] | CORE, name[0] | CORE


MIDDLE = (CORNER, partner(CORNER), partner(BEYOND), partner(FIRST), partner(SECOND), END)
LAST = (partner(END),)
EARLY = tuple(name for name in (
    OWN, SIDE, BESIDE, BEYOND, CORNER, FIRST, SECOND,
    partner(OWN), partner(SIDE), partner(BESIDE), partner(BEYOND), partner(CORNER), partner(FIRST), partner(SECOND),
) if name not in MIDDLE)
ORDER = EARLY + MIDDLE + LAST


def load_all(*copies):
    copies = [pltpu.make_async_copy(*copy) for copy in copies]
    for copy in copies:
        copy.start()
    return copies


def pack_kernel(dims_hbm, right_hbm, pairs_ref, dims_ref, right_ref, sems):
    count, tile, width = pairs_ref.shape
    copies = load_all((dims_hbm, dims_ref, sems.at[0]), (right_hbm, right_ref, sems.at[1]))
    rows = lax.broadcasted_iota(jnp.int32, (tile, tile), 0)
    cols = lax.broadcasted_iota(jnp.int32, (tile, tile), 1)
    most = jnp.maximum(rows, cols)
    for copy in copies:
        copy.wait()

    def kept(b):
        return jnp.where(most < dims_ref[b], right_ref[b].astype(jnp.float32), 0.0)

    for p in range(count):
        both = jnp.concatenate([kept(p), kept(p + count)], axis=0)
        pairs_ref[p] = both.T.astype(jnp.bfloat16)


def left_kernel(
    pair_count, held, dims_hbm, active_hbm, owner_hbm, slot_hbm, left_hbm, psi_hbm,
    half_ref, list_ref, dims_ref, active_ref, owner_ref, slot_ref, left_ref, psi_ref, sems, psi_sems,
):
    sectors, blocks, tile, width = psi_ref.shape
    items = sectors * blocks
    last = held + len(MIDDLE) * pair_count
    copies = load_all(
        (dims_hbm, dims_ref, sems.at[0]),
        (active_hbm, active_ref, sems.at[1]),
        (owner_hbm, owner_ref, sems.at[2]),
        (slot_hbm, slot_ref, sems.at[3]),
        (left_hbm, left_ref, sems.at[4]),
    )
    psi_copies = load_all(*[(psi_hbm.at[a], psi_ref.at[a], psi_sems.at[a]) for a in range(sectors)])
    rows = lax.broadcasted_iota(jnp.int32, (tile, tile), 0)
    cols = lax.broadcasted_iota(jnp.int32, (tile, tile), 1)
    most = jnp.maximum(rows, cols)
    me = lax.axis_index("sec")
    by_swaps = lax.axis_size("sec") == len(ORDER)
    for copy in copies:
        copy.wait()
    in_middle, in_last = jnp.int32(0), jnp.int32(0)
    for a in range(sectors):
        psi_copies[a].wait()
        op = jnp.where(most < dims_ref[a], left_ref[a].astype(jnp.float32), 0.0).astype(jnp.bfloat16)
        before = in_last
        for k in range(0, blocks, 2):
            both = jnp.concatenate([psi_ref[a, k], psi_ref[a, k + 1]], axis=1)
            part = jnp.dot(op, both, preferred_element_type=jnp.float32)
            for u in range(2):
                active = active_ref[a, k + u].astype(jnp.float32)
                half_ref[a, k + u] = (part[:, u * width:(u + 1) * width] * active).astype(jnp.bfloat16)
                item = a * blocks + k + u
                owner, slot = owner_ref[a, k + u], slot_ref[a, k + u]
                at = piece_at(owner ^ me, me) if by_swaps else owner
                second = slot >= pair_count
                at = at * pair_count + jnp.where(second, slot - pair_count, slot)
                is_early, is_last = at < held, at >= last
                at = (at - jnp.where(is_last, last, jnp.where(is_early, 0, held))) * 2 + second.astype(jnp.int32)
                list_ref[jnp.where(is_last, items + 1 + in_last, in_middle)] = at * items + item
                list_ref[2 * items + 2 + sectors + item] = jnp.where(is_early, at, 0)
                in_last = in_last + is_last.astype(jnp.int32)
                in_middle = in_middle + jnp.logical_not(is_early | is_last).astype(jnp.int32)
        list_ref[2 * items + 2 + a] = in_last - before
    list_ref[items] = in_middle
    list_ref[2 * items + 1] = in_last


def block_form(pair, second):
    tile, width = pair.shape
    lower = (lax.broadcasted_iota(jnp.int32, pair.shape, 1) < tile).astype(jnp.bfloat16)
    other = pltpu.roll(pair, tile, 1)
    top = jnp.where(second, other, pair) * lower
    low = jnp.where(second, pair, other) * (1 - lower)
    return jnp.concatenate([top, low], axis=0)


def two_products(halves, forms):
    zero = jnp.zeros_like(forms[0])
    top = jnp.concatenate([forms[0], zero], axis=1)
    low = jnp.concatenate([zero, forms[1]], axis=1)
    both = jnp.concatenate([top, low], axis=0)
    part = jnp.dot(jnp.concatenate(halves, axis=1), both, preferred_element_type=jnp.float32)
    width = part.shape[1] // 2
    return part[:, :width].astype(jnp.bfloat16), part[:, width:].astype(jnp.bfloat16)


def merge(piece_refs, pairs_ref):
    at = 0
    for piece in piece_refs:
        pairs_ref[at:at + piece.shape[0]] = piece[...]
        at += piece.shape[0]


def piece_at(r, me):
    at = jnp.int32(0)
    for parity in range(2):
        places = [ORDER.index(next(name for name in ORDER if name[parity] == i)) for i in range(len(ORDER))]
        for half in range(2):
            packed = sum(place << (4 * i) for i, place in enumerate(places[8 * half:8 * half + 7]))
            mine = jnp.where(r & 7 == 7, places[8 * half + 7], (packed >> (4 * (r & 7))) & 15)
            at = jnp.where((me & 1 == parity) & (r >> 3 == half), mine, at)
    return at


def early_kernel(list_ref, half_ref, *refs):
    piece_refs, (out_ref, pairs_ref) = refs[:-2], refs[-2:]
    sectors, blocks, tile, width = out_ref.shape
    first = 2 * sectors * blocks + 2 + sectors
    merge(piece_refs, pairs_ref)

    def one(a, carry):
        for k in range(0, blocks, 2):
            ats = [list_ref[first + a * blocks + k + u] for u in range(2)]
            forms = [block_form(pairs_ref[at // 2], at % 2 == 1) for at in ats]
            out_ref[a, k], out_ref[a, k + 1] = two_products([half_ref[a, k], half_ref[a, k + 1]], forms)
        return carry

    lax.fori_loop(0, sectors, one, 0, unroll=2)


def listed_products(group_size, first, list_ref, half_ref, pairs_ref, out_ref):
    sectors, blocks, tile, width = half_ref.shape
    items = sectors * blocks
    listed = list_ref[first + items]

    def group(g, carry):
        for u in range(0, group_size, 2):
            entries = [list_ref[first + jnp.minimum(g * group_size + u + n, listed - 1)] for n in range(2)]
            places, halves, forms = [], [], []
            for entry in entries:
                item, at = entry % items, entry // items
                places.append((item // blocks, item % blocks))
                halves.append(half_ref[places[-1]])
                forms.append(block_form(pairs_ref[at // 2], at % 2 == 1))
            out_ref[places[0]], out_ref[places[1]] = two_products(halves, forms)
        return carry

    lax.fori_loop(0, (listed + group_size - 1) // group_size, group, 0)


def middle_kernel(list_ref, early_ref, half_ref, *refs):
    piece_refs, (out_ref, pairs_ref) = refs[:-2], refs[-2:]
    out_ref[...] = early_ref[...]
    merge(piece_refs, pairs_ref)
    listed_products(8, 0, list_ref, half_ref, pairs_ref, out_ref)


def last_kernel(list_ref, middle_ref, half_ref, pairs_ref, out_hbm, out_ref, sems):
    sectors, blocks, tile, width = half_ref.shape
    items = sectors * blocks

    def store(a, ref):
        return pltpu.make_async_copy(ref.at[a], out_hbm.at[a], sems.at[a])

    for a in range(sectors):
        changed = list_ref[2 * items + 2 + a] > 0

        @pl.when(changed)
        def _():
            out_ref[a] = middle_ref[a]

        @pl.when(jnp.logical_not(changed))
        def _():
            store(a, middle_ref).start()

    listed_products(4, items + 1, list_ref, half_ref, pairs_ref, out_ref)
    for a in range(sectors):

        @pl.when(list_ref[2 * items + 2 + a] > 0)
        def _():
            store(a, out_ref).start()

    for a in range(sectors):
        store(a, out_ref).wait()


def swap(piece, even_bit, odd_bit):
    count = lax.axis_size("sec")
    return lax.ppermute(piece, "sec", [(i, i ^ (odd_bit if i & CORE else even_bit)) for i in range(count)])


def per_device(
    psi, left_ops, right_ops, dims_left, dims_right, right_owner, right_slot, term_active
):
    left_count, block_count, tile, width = psi.shape
    items = left_count * block_count
    pair_count = right_ops.shape[0] // 2
    count = lax.axis_size("sec")
    by_swaps = count == len(ORDER)
    flops = 2 * psi.size * tile
    smem = pl.BlockSpec(memory_space=pltpu.SMEM)
    vmem = pl.BlockSpec(memory_space=pltpu.VMEM)
    hbm = pl.BlockSpec(memory_space=pltpu.HBM)
    params = pltpu.CompilerParams(vmem_limit_bytes=VMEM_LIMIT)

    def in_hbm(*arrays):
        return [pltpu.with_memory_space_constraint(array, pltpu.HBM) for array in arrays]

    pairs = pl.pallas_call(
        pack_kernel,
        out_shape=jax.ShapeDtypeStruct((pair_count, tile, 2 * tile), jnp.bfloat16),
        in_specs=[hbm, hbm],
        out_specs=vmem,
        scratch_shapes=[
            pltpu.SMEM(dims_right.shape, jnp.int32),
            pltpu.VMEM(right_ops.shape, jnp.bfloat16),
            pltpu.SemaphoreType.DMA((2,)),
        ],
        compiler_params=params,
        cost_estimate=pl.CostEstimate(flops=0, bytes_accessed=2 * right_ops.size, transcendentals=0),
    )(*in_hbm(dims_right, right_ops))

    active = term_active.reshape(left_count, block_count)
    half, listed = pl.pallas_call(
        functools.partial(left_kernel, pair_count, len(EARLY if by_swaps else range(count)) * pair_count),
        out_shape=(
            jax.ShapeDtypeStruct(psi.shape, jnp.bfloat16),
            pltpu.SMEM((3 * items + 2 + left_count,), jnp.int32),
        ),
        in_specs=[hbm] * 6,
        out_specs=(vmem, smem),
        scratch_shapes=[
            pltpu.SMEM(dims_left.shape, jnp.int32),
            pltpu.SMEM(active.shape, jnp.int32),
            pltpu.SMEM(right_owner.shape, jnp.int32),
            pltpu.SMEM(right_slot.shape, jnp.int32),
            pltpu.VMEM(left_ops.shape, jnp.bfloat16),
            pltpu.VMEM(psi.shape, jnp.bfloat16),
            pltpu.SemaphoreType.DMA((5,)),
            pltpu.SemaphoreType.DMA((left_count,)),
        ],
        compiler_params=params,
        cost_estimate=pl.CostEstimate(flops=flops, bytes_accessed=2 * psi.size, transcendentals=0),
    )(*in_hbm(dims_left, active, right_owner, right_slot, left_ops, psi))
    listed = pltpu.with_memory_space_constraint(listed, pltpu.SMEM)

    if by_swaps:
        pieces = {OWN: pairs}

        def pass_on(*routes):
            for name, target in routes:
                pieces[target] = swap(pieces[name], name[0] ^ target[0], name[1] ^ target[1])

        def share(*names):
            for name in names:
                pieces[partner(name)] = swap(pieces[name], CORE, CORE)

        pass_on((OWN, BEYOND), (OWN, BESIDE), (OWN, SIDE))
        share(OWN)
        held = (BEYOND,)
        half, ends = lax.optimization_barrier((half, [pieces[name] for name in held]))
        pieces.update(zip(held, ends))
        pass_on((BEYOND, FIRST), (BESIDE, CORNER), (BEYOND, SECOND), (FIRST, END))
        share(BESIDE, SIDE, CORNER, FIRST, BEYOND, SECOND)
        early = [pieces[name] for name in EARLY]
    else:
        early = [lax.all_gather(pairs, "sec", axis=0, tiled=True)]

    sigma = pl.pallas_call(
        early_kernel,
        out_shape=jax.ShapeDtypeStruct(psi.shape, jnp.bfloat16),
        in_specs=[smem] + [vmem] * (1 + len(early)),
        out_specs=vmem,
        scratch_shapes=[pltpu.VMEM((sum(piece.shape[0] for piece in early), tile, 2 * tile), jnp.bfloat16)],
        compiler_params=params,
        cost_estimate=pl.CostEstimate(flops=flops, bytes_accessed=2 * psi.size, transcendentals=0),
    )(listed, half, *early)
    if by_swaps:
        pieces[END], sigma = lax.optimization_barrier((pieces[END], sigma))
        share(END)
        sigma = pl.pallas_call(
            middle_kernel,
            out_shape=jax.ShapeDtypeStruct(psi.shape, jnp.bfloat16),
            in_specs=[smem] + [vmem] * (2 + len(MIDDLE)),
            out_specs=vmem,
            scratch_shapes=[pltpu.VMEM((len(MIDDLE) * pair_count, tile, 2 * tile), jnp.bfloat16)],
            compiler_params=params,
            cost_estimate=pl.CostEstimate(flops=flops // 4, bytes_accessed=psi.size // 2, transcendentals=0),
        )(listed, sigma, half, *[pieces[name] for name in MIDDLE])
        sigma = pl.pallas_call(
            last_kernel,
            out_shape=jax.ShapeDtypeStruct(psi.shape, jnp.bfloat16),
            in_specs=[smem] + [vmem] * 3,
            out_specs=hbm,
            scratch_shapes=[pltpu.VMEM(psi.shape, jnp.bfloat16), pltpu.SemaphoreType.DMA((left_count,))],
            compiler_params=params,
            cost_estimate=pl.CostEstimate(flops=flops // 16, bytes_accessed=2 * psi.size, transcendentals=0),
        )(listed, sigma, half, pieces[LAST[0]])
    if lax.axis_size("op") > 1:
        sigma = lax.psum_scatter(sigma, "op", scatter_dimension=3, tiled=True)
    return sigma


def solution(mesh):
    placed = (
        P(("grp", "sec"), None, None, None),
        P(("grp", "sec"), None, "op"),
        P(("grp", "sec"), None, "op"),
        P(("grp", "sec")),
        P(("grp", "sec")),
        P(("grp", "sec"), None),
        P(("grp", "sec"), None),
        P(("grp", "sec"), None, "op"),
    )
    return jax.shard_map(
        per_device,
        mesh=mesh,
        in_specs=placed,
        out_specs=P(("grp", "sec"), None, None, "op"),
        check_vma=False,
    )
```

```python
import functools

import jax
import jax.numpy as jnp
from jax import lax
from jax.experimental import pallas as pl
from jax.experimental.pallas import tpu as pltpu
from jax.sharding import PartitionSpec as P

VMEM_LIMIT = 48 * 1024 * 1024
FAR, NEAR, CROSS, CORE = 8, 4, 2, 1
OWN, SIDE, BESIDE, BEYOND, CORNER = (0, 0), (CROSS, CROSS), (NEAR, NEAR), (FAR, FAR), (NEAR | CROSS, NEAR | CROSS)
FIRST, SECOND = (FAR | NEAR, FAR | CROSS), (FAR | CROSS, FAR | NEAR)
END = (FAR | NEAR | CROSS, FAR | NEAR | CROSS)


def partner(name):
    return name[1] | CORE, name[0] | CORE


MIDDLE = (partner(CORNER), partner(BEYOND), partner(FIRST), partner(SECOND), END)
LAST = (partner(END),)
EARLY = tuple(name for name in (
    OWN, SIDE, BESIDE, BEYOND, CORNER, FIRST, SECOND,
    partner(OWN), partner(SIDE), partner(BESIDE), partner(BEYOND), partner(CORNER), partner(FIRST), partner(SECOND),
) if name not in MIDDLE)
ORDER = EARLY + MIDDLE + LAST


def load_all(*copies):
    copies = [pltpu.make_async_copy(*copy) for copy in copies]
    for copy in copies:
        copy.start()
    return copies


def pack_kernel(dims_hbm, right_hbm, pairs_ref, dims_ref, right_ref, sems):
    count, tile, width = pairs_ref.shape
    copies = load_all((dims_hbm, dims_ref, sems.at[0]), (right_hbm, right_ref, sems.at[1]))
    rows = lax.broadcasted_iota(jnp.int32, (tile, tile), 0)
    cols = lax.broadcasted_iota(jnp.int32, (tile, tile), 1)
    most = jnp.maximum(rows, cols)
    for copy in copies:
        copy.wait()

    def kept(b):
        return jnp.where(most < dims_ref[b], right_ref[b].astype(jnp.float32), 0.0)

    for p in range(count):
        both = jnp.concatenate([kept(p), kept(p + count)], axis=0)
        pairs_ref[p] = both.T.astype(jnp.bfloat16)


def left_kernel(
    pair_count, held, dims_hbm, active_hbm, owner_hbm, slot_hbm, left_hbm, psi_hbm,
    half_ref, list_ref, dims_ref, active_ref, owner_ref, slot_ref, left_ref, psi_ref, sems, psi_sems,
):
    sectors, blocks, tile, width = psi_ref.shape
    items = sectors * blocks
    last = held + len(MIDDLE) * pair_count
    copies = load_all(
        (dims_hbm, dims_ref, sems.at[0]),
        (active_hbm, active_ref, sems.at[1]),
        (owner_hbm, owner_ref, sems.at[2]),
        (slot_hbm, slot_ref, sems.at[3]),
        (left_hbm, left_ref, sems.at[4]),
    )
    psi_copies = load_all(*[(psi_hbm.at[a], psi_ref.at[a], psi_sems.at[a]) for a in range(sectors)])
    rows = lax.broadcasted_iota(jnp.int32, (tile, tile), 0)
    cols = lax.broadcasted_iota(jnp.int32, (tile, tile), 1)
    most = jnp.maximum(rows, cols)
    me = lax.axis_index("sec")
    by_swaps = lax.axis_size("sec") == len(ORDER)
    for copy in copies:
        copy.wait()
    in_middle, in_last = jnp.int32(0), jnp.int32(0)
    for a in range(sectors):
        psi_copies[a].wait()
        op = jnp.where(most < dims_ref[a], left_ref[a].astype(jnp.float32), 0.0).astype(jnp.bfloat16)
        before = in_last
        for k in range(0, blocks, 2):
            both = jnp.concatenate([psi_ref[a, k], psi_ref[a, k + 1]], axis=1)
            part = jnp.dot(op, both, preferred_element_type=jnp.float32)
            for u in range(2):
                active = active_ref[a, k + u].astype(jnp.float32)
                half_ref[a, k + u] = (part[:, u * width:(u + 1) * width] * active).astype(jnp.bfloat16)
                item = a * blocks + k + u
                owner, slot = owner_ref[a, k + u], slot_ref[a, k + u]
                at = piece_at(owner ^ me, me) if by_swaps else owner
                second = slot >= pair_count
                at = at * pair_count + jnp.where(second, slot - pair_count, slot)
                is_early, is_last = at < held, at >= last
                at = (at - jnp.where(is_last, last, jnp.where(is_early, 0, held))) * 2 + second.astype(jnp.int32)
                list_ref[jnp.where(is_last, items + 1 + in_last, in_middle)] = at * items + item
                list_ref[2 * items + 2 + sectors + item] = jnp.where(is_early, at, 0)
                in_last = in_last + is_last.astype(jnp.int32)
                in_middle = in_middle + jnp.logical_not(is_early | is_last).astype(jnp.int32)
        list_ref[2 * items + 2 + a] = in_last - before
    list_ref[items] = in_middle
    list_ref[2 * items + 1] = in_last


def block_form(pair, second):
    tile, width = pair.shape
    lower = (lax.broadcasted_iota(jnp.int32, pair.shape, 1) < tile).astype(jnp.bfloat16)
    other = pltpu.roll(pair, tile, 1)
    top = jnp.where(second, other, pair) * lower
    low = jnp.where(second, pair, other) * (1 - lower)
    return jnp.concatenate([top, low], axis=0)


def two_products(halves, forms):
    zero = jnp.zeros_like(forms[0])
    top = jnp.concatenate([forms[0], zero], axis=1)
    low = jnp.concatenate([zero, forms[1]], axis=1)
    both = jnp.concatenate([top, low], axis=0)
    part = jnp.dot(jnp.concatenate(halves, axis=1), both, preferred_element_type=jnp.float32)
    width = part.shape[1] // 2
    return part[:, :width].astype(jnp.bfloat16), part[:, width:].astype(jnp.bfloat16)


def merge(piece_refs, pairs_ref):
    at = 0
    for piece in piece_refs:
        pairs_ref[at:at + piece.shape[0]] = piece[...]
        at += piece.shape[0]


def piece_at(r, me):
    at = jnp.int32(0)
    for parity in range(2):
        places = [ORDER.index(next(name for name in ORDER if name[parity] == i)) for i in range(len(ORDER))]
        for half in range(2):
            packed = sum(place << (4 * i) for i, place in enumerate(places[8 * half:8 * half + 7]))
            mine = jnp.where(r & 7 == 7, places[8 * half + 7], (packed >> (4 * (r & 7))) & 15)
            at = jnp.where((me & 1 == parity) & (r >> 3 == half), mine, at)
    return at


def early_kernel(list_ref, half_ref, *refs):
    piece_refs, (out_ref, pairs_ref) = refs[:-2], refs[-2:]
    sectors, blocks, tile, width = out_ref.shape
    first = 2 * sectors * blocks + 2 + sectors
    merge(piece_refs, pairs_ref)

    def one(a, carry):
        for k in range(0, blocks, 2):
            ats = [list_ref[first + a * blocks + k + u] for u in range(2)]
            forms = [block_form(pairs_ref[at // 2], at % 2 == 1) for at in ats]
            out_ref[a, k], out_ref[a, k + 1] = two_products([half_ref[a, k], half_ref[a, k + 1]], forms)
        return carry

    lax.fori_loop(0, sectors, one, 0, unroll=2)


def listed_products(group_size, first, list_ref, half_ref, pairs_ref, out_ref):
    sectors, blocks, tile, width = half_ref.shape
    items = sectors * blocks
    listed = list_ref[first + items]

    def group(g, carry):
        for u in range(0, group_size, 2):
            entries = [list_ref[first + jnp.minimum(g * group_size + u + n, listed - 1)] for n in range(2)]
            places, halves, forms = [], [], []
            for entry in entries:
                item, at = entry % items, entry // items
                places.append((item // blocks, item % blocks))
                halves.append(half_ref[places[-1]])
                forms.append(block_form(pairs_ref[at // 2], at % 2 == 1))
            out_ref[places[0]], out_ref[places[1]] = two_products(halves, forms)
        return carry

    lax.fori_loop(0, (listed + group_size - 1) // group_size, group, 0)


def middle_kernel(list_ref, early_ref, half_ref, *refs):
    piece_refs, (out_ref, pairs_ref) = refs[:-2], refs[-2:]
    out_ref[...] = early_ref[...]
    merge(piece_refs, pairs_ref)
    listed_products(16, 0, list_ref, half_ref, pairs_ref, out_ref)


def last_kernel(list_ref, middle_ref, half_ref, pairs_ref, out_hbm, out_ref, sems):
    sectors, blocks, tile, width = half_ref.shape
    items = sectors * blocks

    def store(a, ref):
        return pltpu.make_async_copy(ref.at[a], out_hbm.at[a], sems.at[a])

    for a in range(sectors):
        changed = list_ref[2 * items + 2 + a] > 0

        @pl.when(changed)
        def _():
            out_ref[a] = middle_ref[a]

        @pl.when(jnp.logical_not(changed))
        def _():
            store(a, middle_ref).start()

    listed_products(8, items + 1, list_ref, half_ref, pairs_ref, out_ref)
    for a in range(sectors):

        @pl.when(list_ref[2 * items + 2 + a] > 0)
        def _():
            store(a, out_ref).start()

    for a in range(sectors):
        store(a, out_ref).wait()


def swap(piece, even_bit, odd_bit):
    count = lax.axis_size("sec")
    return lax.ppermute(piece, "sec", [(i, i ^ (odd_bit if i & CORE else even_bit)) for i in range(count)])


def per_device(
    psi, left_ops, right_ops, dims_left, dims_right, right_owner, right_slot, term_active
):
    left_count, block_count, tile, width = psi.shape
    items = left_count * block_count
    pair_count = right_ops.shape[0] // 2
    count = lax.axis_size("sec")
    by_swaps = count == len(ORDER)
    flops = 2 * psi.size * tile
    smem = pl.BlockSpec(memory_space=pltpu.SMEM)
    vmem = pl.BlockSpec(memory_space=pltpu.VMEM)
    hbm = pl.BlockSpec(memory_space=pltpu.HBM)
    params = pltpu.CompilerParams(vmem_limit_bytes=VMEM_LIMIT)

    def in_hbm(*arrays):
        return [pltpu.with_memory_space_constraint(array, pltpu.HBM) for array in arrays]

    pairs = pl.pallas_call(
        pack_kernel,
        out_shape=jax.ShapeDtypeStruct((pair_count, tile, 2 * tile), jnp.bfloat16),
        in_specs=[hbm, hbm],
        out_specs=vmem,
        scratch_shapes=[
            pltpu.SMEM(dims_right.shape, jnp.int32),
            pltpu.VMEM(right_ops.shape, jnp.bfloat16),
            pltpu.SemaphoreType.DMA((2,)),
        ],
        compiler_params=params,
        cost_estimate=pl.CostEstimate(flops=0, bytes_accessed=2 * right_ops.size, transcendentals=0),
    )(*in_hbm(dims_right, right_ops))

    active = term_active.reshape(left_count, block_count)
    half, listed = pl.pallas_call(
        functools.partial(left_kernel, pair_count, len(EARLY if by_swaps else range(count)) * pair_count),
        out_shape=(
            jax.ShapeDtypeStruct(psi.shape, jnp.bfloat16),
            pltpu.SMEM((3 * items + 2 + left_count,), jnp.int32),
        ),
        in_specs=[hbm] * 6,
        out_specs=(vmem, smem),
        scratch_shapes=[
            pltpu.SMEM(dims_left.shape, jnp.int32),
            pltpu.SMEM(active.shape, jnp.int32),
            pltpu.SMEM(right_owner.shape, jnp.int32),
            pltpu.SMEM(right_slot.shape, jnp.int32),
            pltpu.VMEM(left_ops.shape, jnp.bfloat16),
            pltpu.VMEM(psi.shape, jnp.bfloat16),
            pltpu.SemaphoreType.DMA((5,)),
            pltpu.SemaphoreType.DMA((left_count,)),
        ],
        compiler_params=params,
        cost_estimate=pl.CostEstimate(flops=flops, bytes_accessed=2 * psi.size, transcendentals=0),
    )(*in_hbm(dims_left, active, right_owner, right_slot, left_ops, psi))
    listed = pltpu.with_memory_space_constraint(listed, pltpu.SMEM)

    if by_swaps:
        pieces = {OWN: pairs}

        def pass_on(*routes):
            for name, target in routes:
                pieces[target] = swap(pieces[name], name[0] ^ target[0], name[1] ^ target[1])

        def share(*names):
            for name in names:
                pieces[partner(name)] = swap(pieces[name], CORE, CORE)

        pass_on((OWN, BEYOND), (OWN, BESIDE), (OWN, SIDE))
        share(OWN)
        held = (BEYOND,)
        half, ends = lax.optimization_barrier((half, [pieces[name] for name in held]))
        pieces.update(zip(held, ends))
        pass_on((BEYOND, FIRST), (BESIDE, CORNER), (BEYOND, SECOND), (FIRST, END))
        share(BESIDE, SIDE, CORNER, FIRST, BEYOND, SECOND)
        early = [pieces[name] for name in EARLY]
    else:
        early = [lax.all_gather(pairs, "sec", axis=0, tiled=True)]

    sigma = pl.pallas_call(
        early_kernel,
        out_shape=jax.ShapeDtypeStruct(psi.shape, jnp.bfloat16),
        in_specs=[smem] + [vmem] * (1 + len(early)),
        out_specs=vmem,
        scratch_shapes=[pltpu.VMEM((sum(piece.shape[0] for piece in early), tile, 2 * tile), jnp.bfloat16)],
        compiler_params=params,
        cost_estimate=pl.CostEstimate(flops=flops, bytes_accessed=2 * psi.size, transcendentals=0),
    )(listed, half, *early)
    if by_swaps:
        pieces[END], sigma = lax.optimization_barrier((pieces[END], sigma))
        share(END)
        sigma = pl.pallas_call(
            middle_kernel,
            out_shape=jax.ShapeDtypeStruct(psi.shape, jnp.bfloat16),
            in_specs=[smem] + [vmem] * (2 + len(MIDDLE)),
            out_specs=vmem,
            scratch_shapes=[pltpu.VMEM((len(MIDDLE) * pair_count, tile, 2 * tile), jnp.bfloat16)],
            compiler_params=params,
            cost_estimate=pl.CostEstimate(flops=flops // 4, bytes_accessed=psi.size // 2, transcendentals=0),
        )(listed, sigma, half, *[pieces[name] for name in MIDDLE])
        sigma = pl.pallas_call(
            last_kernel,
            out_shape=jax.ShapeDtypeStruct(psi.shape, jnp.bfloat16),
            in_specs=[smem] + [vmem] * 3,
            out_specs=hbm,
            scratch_shapes=[pltpu.VMEM(psi.shape, jnp.bfloat16), pltpu.SemaphoreType.DMA((left_count,))],
            compiler_params=params,
            cost_estimate=pl.CostEstimate(flops=flops // 16, bytes_accessed=2 * psi.size, transcendentals=0),
        )(listed, sigma, half, pieces[LAST[0]])
    if lax.axis_size("op") > 1:
        sigma = lax.psum_scatter(sigma, "op", scatter_dimension=3, tiled=True)
    return sigma


def solution(mesh):
    placed = (
        P(("grp", "sec"), None, None, None),
        P(("grp", "sec"), None, "op"),
        P(("grp", "sec"), None, "op"),
        P(("grp", "sec")),
        P(("grp", "sec")),
        P(("grp", "sec"), None),
        P(("grp", "sec"), None),
        P(("grp", "sec"), None, "op"),
    )
    return jax.shard_map(
        per_device,
        mesh=mesh,
        in_specs=placed,
        out_specs=P(("grp", "sec"), None, None, "op"),
        check_vma=False,
    )
```

```python
import functools

import jax
import jax.numpy as jnp
from jax import lax
from jax.experimental import pallas as pl
from jax.experimental.pallas import tpu as pltpu
from jax.sharding import PartitionSpec as P

VMEM_LIMIT = 48 * 1024 * 1024
FAR, NEAR, CROSS, CORE = 8, 4, 2, 1
OWN, SIDE, BESIDE, BEYOND, CORNER = (0, 0), (CROSS, CROSS), (NEAR, NEAR), (FAR, FAR), (NEAR | CROSS, NEAR | CROSS)
FIRST, SECOND = (FAR | NEAR, FAR | CROSS), (FAR | CROSS, FAR | NEAR)
END = (FAR | NEAR | CROSS, FAR | NEAR | CROSS)


def partner(name):
    return name[1] | CORE, name[0] | CORE


MIDDLE = (CORNER, SECOND, partner(CORNER), partner(BEYOND), partner(FIRST), partner(SECOND), END)
LAST = (partner(END),)
EARLY = tuple(name for name in (
    OWN, SIDE, BESIDE, BEYOND, CORNER, FIRST, SECOND,
    partner(OWN), partner(SIDE), partner(BESIDE), partner(BEYOND), partner(CORNER), partner(FIRST), partner(SECOND),
) if name not in MIDDLE)
ORDER = EARLY + MIDDLE + LAST


def load_all(*copies):
    copies = [pltpu.make_async_copy(*copy) for copy in copies]
    for copy in copies:
        copy.start()
    return copies


def pack_kernel(dims_hbm, right_hbm, pairs_ref, dims_ref, right_ref, sems):
    count, tile, width = pairs_ref.shape
    copies = load_all((dims_hbm, dims_ref, sems.at[0]), (right_hbm, right_ref, sems.at[1]))
    rows = lax.broadcasted_iota(jnp.int32, (tile, tile), 0)
    cols = lax.broadcasted_iota(jnp.int32, (tile, tile), 1)
    most = jnp.maximum(rows, cols)
    for copy in copies:
        copy.wait()

    def kept(b):
        return jnp.where(most < dims_ref[b], right_ref[b].astype(jnp.float32), 0.0)

    for p in range(count):
        both = jnp.concatenate([kept(p), kept(p + count)], axis=0)
        pairs_ref[p] = both.T.astype(jnp.bfloat16)


def left_kernel(
    pair_count, held, dims_hbm, active_hbm, owner_hbm, slot_hbm, left_hbm, psi_hbm,
    half_ref, list_ref, dims_ref, active_ref, owner_ref, slot_ref, left_ref, psi_ref, sems, psi_sems,
):
    sectors, blocks, tile, width = psi_ref.shape
    items = sectors * blocks
    last = held + len(MIDDLE) * pair_count
    copies = load_all(
        (dims_hbm, dims_ref, sems.at[0]),
        (active_hbm, active_ref, sems.at[1]),
        (owner_hbm, owner_ref, sems.at[2]),
        (slot_hbm, slot_ref, sems.at[3]),
        (left_hbm, left_ref, sems.at[4]),
    )
    psi_copies = load_all(*[(psi_hbm.at[a], psi_ref.at[a], psi_sems.at[a]) for a in range(sectors)])
    rows = lax.broadcasted_iota(jnp.int32, (tile, tile), 0)
    cols = lax.broadcasted_iota(jnp.int32, (tile, tile), 1)
    most = jnp.maximum(rows, cols)
    me = lax.axis_index("sec")
    by_swaps = lax.axis_size("sec") == len(ORDER)
    for copy in copies:
        copy.wait()
    in_middle, in_last = jnp.int32(0), jnp.int32(0)
    for a in range(sectors):
        psi_copies[a].wait()
        op = jnp.where(most < dims_ref[a], left_ref[a].astype(jnp.float32), 0.0).astype(jnp.bfloat16)
        before = in_last
        for k in range(0, blocks, 2):
            both = jnp.concatenate([psi_ref[a, k], psi_ref[a, k + 1]], axis=1)
            part = jnp.dot(op, both, preferred_element_type=jnp.float32)
            for u in range(2):
                active = active_ref[a, k + u].astype(jnp.float32)
                half_ref[a, k + u] = (part[:, u * width:(u + 1) * width] * active).astype(jnp.bfloat16)
                item = a * blocks + k + u
                owner, slot = owner_ref[a, k + u], slot_ref[a, k + u]
                at = piece_at(owner ^ me, me) if by_swaps else owner
                second = slot >= pair_count
                at = at * pair_count + jnp.where(second, slot - pair_count, slot)
                is_early, is_last = at < held, at >= last
                at = (at - jnp.where(is_last, last, jnp.where(is_early, 0, held))) * 2 + second.astype(jnp.int32)
                list_ref[jnp.where(is_last, items + 1 + in_last, in_middle)] = at * items + item
                list_ref[2 * items + 2 + sectors + item] = jnp.where(is_early, at, 0)
                in_last = in_last + is_last.astype(jnp.int32)
                in_middle = in_middle + jnp.logical_not(is_early | is_last).astype(jnp.int32)
        list_ref[2 * items + 2 + a] = in_last - before
    list_ref[items] = in_middle
    list_ref[2 * items + 1] = in_last


def block_form(pair, second):
    tile, width = pair.shape
    lower = (lax.broadcasted_iota(jnp.int32, pair.shape, 1) < tile).astype(jnp.bfloat16)
    other = pltpu.roll(pair, tile, 1)
    top = jnp.where(second, other, pair) * lower
    low = jnp.where(second, pair, other) * (1 - lower)
    return jnp.concatenate([top, low], axis=0)


def two_products(halves, forms):
    zero = jnp.zeros_like(forms[0])
    top = jnp.concatenate([forms[0], zero], axis=1)
    low = jnp.concatenate([zero, forms[1]], axis=1)
    both = jnp.concatenate([top, low], axis=0)
    part = jnp.dot(jnp.concatenate(halves, axis=1), both, preferred_element_type=jnp.float32)
    width = part.shape[1] // 2
    return part[:, :width].astype(jnp.bfloat16), part[:, width:].astype(jnp.bfloat16)


def merge(piece_refs, pairs_ref):
    at = 0
    for piece in piece_refs:
        pairs_ref[at:at + piece.shape[0]] = piece[...]
        at += piece.shape[0]


def piece_at(r, me):
    at = jnp.int32(0)
    for parity in range(2):
        places = [ORDER.index(next(name for name in ORDER if name[parity] == i)) for i in range(len(ORDER))]
        for half in range(2):
            packed = sum(place << (4 * i) for i, place in enumerate(places[8 * half:8 * half + 7]))
            mine = jnp.where(r & 7 == 7, places[8 * half + 7], (packed >> (4 * (r & 7))) & 15)
            at = jnp.where((me & 1 == parity) & (r >> 3 == half), mine, at)
    return at


def early_kernel(list_ref, half_ref, *refs):
    piece_refs, (out_ref, pairs_ref) = refs[:-2], refs[-2:]
    sectors, blocks, tile, width = out_ref.shape
    first = 2 * sectors * blocks + 2 + sectors
    merge(piece_refs, pairs_ref)

    def one(a, carry):
        for k in range(0, blocks, 2):
            ats = [list_ref[first + a * blocks + k + u] for u in range(2)]
            forms = [block_form(pairs_ref[at // 2], at % 2 == 1) for at in ats]
            out_ref[a, k], out_ref[a, k + 1] = two_products([half_ref[a, k], half_ref[a, k + 1]], forms)
        return carry

    lax.fori_loop(0, sectors, one, 0, unroll=2)


def listed_products(group_size, first, list_ref, half_ref, pairs_ref, out_ref):
    sectors, blocks, tile, width = half_ref.shape
    items = sectors * blocks
    listed = list_ref[first + items]

    def group(g, carry):
        for u in range(0, group_size, 2):
            entries = [list_ref[first + jnp.minimum(g * group_size + u + n, listed - 1)] for n in range(2)]
            places, halves, forms = [], [], []
            for entry in entries:
                item, at = entry % items, entry // items
                places.append((item // blocks, item % blocks))
                halves.append(half_ref[places[-1]])
                forms.append(block_form(pairs_ref[at // 2], at % 2 == 1))
            out_ref[places[0]], out_ref[places[1]] = two_products(halves, forms)
        return carry

    lax.fori_loop(0, (listed + group_size - 1) // group_size, group, 0)


def middle_kernel(list_ref, early_ref, half_ref, *refs):
    piece_refs, (out_ref, pairs_ref) = refs[:-2], refs[-2:]
    out_ref[...] = early_ref[...]
    merge(piece_refs, pairs_ref)
    listed_products(16, 0, list_ref, half_ref, pairs_ref, out_ref)


def last_kernel(list_ref, middle_ref, half_ref, pairs_ref, out_hbm, out_ref, sems):
    sectors, blocks, tile, width = half_ref.shape
    items = sectors * blocks

    def store(a, ref):
        return pltpu.make_async_copy(ref.at[a], out_hbm.at[a], sems.at[a])

    for a in range(sectors):
        changed = list_ref[2 * items + 2 + a] > 0

        @pl.when(changed)
        def _():
            out_ref[a] = middle_ref[a]

        @pl.when(jnp.logical_not(changed))
        def _():
            store(a, middle_ref).start()

    listed_products(8, items + 1, list_ref, half_ref, pairs_ref, out_ref)
    for a in range(sectors):

        @pl.when(list_ref[2 * items + 2 + a] > 0)
        def _():
            store(a, out_ref).start()

    for a in range(sectors):
        store(a, out_ref).wait()


def swap(piece, even_bit, odd_bit):
    count = lax.axis_size("sec")
    return lax.ppermute(piece, "sec", [(i, i ^ (odd_bit if i & CORE else even_bit)) for i in range(count)])


def per_device(
    psi, left_ops, right_ops, dims_left, dims_right, right_owner, right_slot, term_active
):
    left_count, block_count, tile, width = psi.shape
    items = left_count * block_count
    pair_count = right_ops.shape[0] // 2
    count = lax.axis_size("sec")
    by_swaps = count == len(ORDER)
    flops = 2 * psi.size * tile
    smem = pl.BlockSpec(memory_space=pltpu.SMEM)
    vmem = pl.BlockSpec(memory_space=pltpu.VMEM)
    hbm = pl.BlockSpec(memory_space=pltpu.HBM)
    params = pltpu.CompilerParams(vmem_limit_bytes=VMEM_LIMIT)

    def in_hbm(*arrays):
        return [pltpu.with_memory_space_constraint(array, pltpu.HBM) for array in arrays]

    pairs = pl.pallas_call(
        pack_kernel,
        out_shape=jax.ShapeDtypeStruct((pair_count, tile, 2 * tile), jnp.bfloat16),
        in_specs=[hbm, hbm],
        out_specs=vmem,
        scratch_shapes=[
            pltpu.SMEM(dims_right.shape, jnp.int32),
            pltpu.VMEM(right_ops.shape, jnp.bfloat16),
            pltpu.SemaphoreType.DMA((2,)),
        ],
        compiler_params=params,
        cost_estimate=pl.CostEstimate(flops=0, bytes_accessed=2 * right_ops.size, transcendentals=0),
    )(*in_hbm(dims_right, right_ops))

    active = term_active.reshape(left_count, block_count)
    half, listed = pl.pallas_call(
        functools.partial(left_kernel, pair_count, len(EARLY if by_swaps else range(count)) * pair_count),
        out_shape=(
            jax.ShapeDtypeStruct(psi.shape, jnp.bfloat16),
            pltpu.SMEM((3 * items + 2 + left_count,), jnp.int32),
        ),
        in_specs=[hbm] * 6,
        out_specs=(vmem, smem),
        scratch_shapes=[
            pltpu.SMEM(dims_left.shape, jnp.int32),
            pltpu.SMEM(active.shape, jnp.int32),
            pltpu.SMEM(right_owner.shape, jnp.int32),
            pltpu.SMEM(right_slot.shape, jnp.int32),
            pltpu.VMEM(left_ops.shape, jnp.bfloat16),
            pltpu.VMEM(psi.shape, jnp.bfloat16),
            pltpu.SemaphoreType.DMA((5,)),
            pltpu.SemaphoreType.DMA((left_count,)),
        ],
        compiler_params=params,
        cost_estimate=pl.CostEstimate(flops=flops, bytes_accessed=2 * psi.size, transcendentals=0),
    )(*in_hbm(dims_left, active, right_owner, right_slot, left_ops, psi))
    listed = pltpu.with_memory_space_constraint(listed, pltpu.SMEM)

    if by_swaps:
        pieces = {OWN: pairs}

        def pass_on(*routes):
            for name, target in routes:
                pieces[target] = swap(pieces[name], name[0] ^ target[0], name[1] ^ target[1])

        def share(*names):
            for name in names:
                pieces[partner(name)] = swap(pieces[name], CORE, CORE)

        pass_on((OWN, BEYOND), (OWN, BESIDE), (OWN, SIDE))
        share(OWN)
        held = (BEYOND,)
        half, ends = lax.optimization_barrier((half, [pieces[name] for name in held]))
        pieces.update(zip(held, ends))
        pass_on((BEYOND, FIRST), (BESIDE, CORNER), (BEYOND, SECOND), (FIRST, END))
        share(BESIDE, SIDE, CORNER, FIRST, BEYOND)
        early = [pieces[name] for name in EARLY]
    else:
        early = [lax.all_gather(pairs, "sec", axis=0, tiled=True)]

    sigma = pl.pallas_call(
        early_kernel,
        out_shape=jax.ShapeDtypeStruct(psi.shape, jnp.bfloat16),
        in_specs=[smem] + [vmem] * (1 + len(early)),
        out_specs=vmem,
        scratch_shapes=[pltpu.VMEM((sum(piece.shape[0] for piece in early), tile, 2 * tile), jnp.bfloat16)],
        compiler_params=params,
        cost_estimate=pl.CostEstimate(flops=flops, bytes_accessed=2 * psi.size, transcendentals=0),
    )(listed, half, *early)
    if by_swaps:
        pieces[END], pieces[SECOND], sigma = lax.optimization_barrier((pieces[END], pieces[SECOND], sigma))
        share(END, SECOND)
        sigma = pl.pallas_call(
            middle_kernel,
            out_shape=jax.ShapeDtypeStruct(psi.shape, jnp.bfloat16),
            in_specs=[smem] + [vmem] * (2 + len(MIDDLE)),
            out_specs=vmem,
            scratch_shapes=[pltpu.VMEM((len(MIDDLE) * pair_count, tile, 2 * tile), jnp.bfloat16)],
            compiler_params=params,
            cost_estimate=pl.CostEstimate(flops=flops // 4, bytes_accessed=psi.size // 2, transcendentals=0),
        )(listed, sigma, half, *[pieces[name] for name in MIDDLE])
        sigma = pl.pallas_call(
            last_kernel,
            out_shape=jax.ShapeDtypeStruct(psi.shape, jnp.bfloat16),
            in_specs=[smem] + [vmem] * 3,
            out_specs=hbm,
            scratch_shapes=[pltpu.VMEM(psi.shape, jnp.bfloat16), pltpu.SemaphoreType.DMA((left_count,))],
            compiler_params=params,
            cost_estimate=pl.CostEstimate(flops=flops // 16, bytes_accessed=2 * psi.size, transcendentals=0),
        )(listed, sigma, half, pieces[LAST[0]])
    if lax.axis_size("op") > 1:
        sigma = lax.psum_scatter(sigma, "op", scatter_dimension=3, tiled=True)
    return sigma


def solution(mesh):
    placed = (
        P(("grp", "sec"), None, None, None),
        P(("grp", "sec"), None, "op"),
        P(("grp", "sec"), None, "op"),
        P(("grp", "sec")),
        P(("grp", "sec")),
        P(("grp", "sec"), None),
        P(("grp", "sec"), None),
        P(("grp", "sec"), None, "op"),
    )
    return jax.shard_map(
        per_device,
        mesh=mesh,
        in_specs=placed,
        out_specs=P(("grp", "sec"), None, None, "op"),
        check_vma=False,
    )
```

```python
import functools

import jax
import jax.numpy as jnp
from jax import lax
from jax.experimental import pallas as pl
from jax.experimental.pallas import tpu as pltpu
from jax.sharding import PartitionSpec as P

VMEM_LIMIT = 48 * 1024 * 1024
FAR, NEAR, CROSS, CORE = 8, 4, 2, 1
OWN, SIDE, BESIDE, BEYOND, CORNER = (0, 0), (CROSS, CROSS), (NEAR, NEAR), (FAR, FAR), (NEAR | CROSS, NEAR | CROSS)
FIRST, SECOND = (FAR | NEAR, FAR | CROSS), (FAR | CROSS, FAR | NEAR)
END = (FAR | NEAR | CROSS, FAR | NEAR | CROSS)


def partner(name):
    return name[1] | CORE, name[0] | CORE


MIDDLE = (SECOND, partner(CORNER), partner(BEYOND), partner(FIRST), partner(SECOND), END)
LAST = (partner(END),)
EARLY = tuple(name for name in (
    OWN, SIDE, BESIDE, BEYOND, CORNER, FIRST, SECOND,
    partner(OWN), partner(SIDE), partner(BESIDE), partner(BEYOND), partner(CORNER), partner(FIRST), partner(SECOND),
) if name not in MIDDLE)
ORDER = EARLY + MIDDLE + LAST


def load_all(*copies):
    copies = [pltpu.make_async_copy(*copy) for copy in copies]
    for copy in copies:
        copy.start()
    return copies


def pack_kernel(dims_hbm, right_hbm, pairs_ref, dims_ref, right_ref, sems):
    count, tile, width = pairs_ref.shape
    copies = load_all((dims_hbm, dims_ref, sems.at[0]), (right_hbm, right_ref, sems.at[1]))
    rows = lax.broadcasted_iota(jnp.int32, (tile, tile), 0)
    cols = lax.broadcasted_iota(jnp.int32, (tile, tile), 1)
    most = jnp.maximum(rows, cols)
    for copy in copies:
        copy.wait()

    def kept(b):
        return jnp.where(most < dims_ref[b], right_ref[b].astype(jnp.float32), 0.0)

    for p in range(count):
        both = jnp.concatenate([kept(p), kept(p + count)], axis=0)
        pairs_ref[p] = both.T.astype(jnp.bfloat16)


def left_kernel(
    pair_count, held, dims_hbm, active_hbm, owner_hbm, slot_hbm, left_hbm, psi_hbm,
    half_ref, list_ref, dims_ref, active_ref, owner_ref, slot_ref, left_ref, psi_ref, sems, psi_sems,
):
    sectors, blocks, tile, width = psi_ref.shape
    items = sectors * blocks
    last = held + len(MIDDLE) * pair_count
    copies = load_all(
        (dims_hbm, dims_ref, sems.at[0]),
        (active_hbm, active_ref, sems.at[1]),
        (owner_hbm, owner_ref, sems.at[2]),
        (slot_hbm, slot_ref, sems.at[3]),
        (left_hbm, left_ref, sems.at[4]),
    )
    psi_copies = load_all(*[(psi_hbm.at[a], psi_ref.at[a], psi_sems.at[a]) for a in range(sectors)])
    rows = lax.broadcasted_iota(jnp.int32, (tile, tile), 0)
    cols = lax.broadcasted_iota(jnp.int32, (tile, tile), 1)
    most = jnp.maximum(rows, cols)
    me = lax.axis_index("sec")
    by_swaps = lax.axis_size("sec") == len(ORDER)
    for copy in copies:
        copy.wait()
    in_middle, in_last = jnp.int32(0), jnp.int32(0)
    for a in range(sectors):
        psi_copies[a].wait()
        op = jnp.where(most < dims_ref[a], left_ref[a].astype(jnp.float32), 0.0).astype(jnp.bfloat16)
        before = in_last
        for k in range(0, blocks, 2):
            both = jnp.concatenate([psi_ref[a, k], psi_ref[a, k + 1]], axis=1)
            part = jnp.dot(op, both, preferred_element_type=jnp.float32)
            for u in range(2):
                active = active_ref[a, k + u].astype(jnp.float32)
                half_ref[a, k + u] = (part[:, u * width:(u + 1) * width] * active).astype(jnp.bfloat16)
                item = a * blocks + k + u
                owner, slot = owner_ref[a, k + u], slot_ref[a, k + u]
                at = piece_at(owner ^ me, me) if by_swaps else owner
                second = slot >= pair_count
                at = at * pair_count + jnp.where(second, slot - pair_count, slot)
                is_early, is_last = at < held, at >= last
                at = (at - jnp.where(is_last, last, jnp.where(is_early, 0, held))) * 2 + second.astype(jnp.int32)
                list_ref[jnp.where(is_last, items + 1 + in_last, in_middle)] = at * items + item
                list_ref[2 * items + 2 + sectors + item] = jnp.where(is_early, at, 0)
                in_last = in_last + is_last.astype(jnp.int32)
                in_middle = in_middle + jnp.logical_not(is_early | is_last).astype(jnp.int32)
        list_ref[2 * items + 2 + a] = in_last - before
    list_ref[items] = in_middle
    list_ref[2 * items + 1] = in_last


def block_form(pair, second):
    tile, width = pair.shape
    lower = (lax.broadcasted_iota(jnp.int32, pair.shape, 1) < tile).astype(jnp.bfloat16)
    other = pltpu.roll(pair, tile, 1)
    top = jnp.where(second, other, pair) * lower
    low = jnp.where(second, pair, other) * (1 - lower)
    return jnp.concatenate([top, low], axis=0)


def two_products(halves, forms):
    zero = jnp.zeros_like(forms[0])
    top = jnp.concatenate([forms[0], zero], axis=1)
    low = jnp.concatenate([zero, forms[1]], axis=1)
    both = jnp.concatenate([top, low], axis=0)
    part = jnp.dot(jnp.concatenate(halves, axis=1), both, preferred_element_type=jnp.float32)
    width = part.shape[1] // 2
    return part[:, :width].astype(jnp.bfloat16), part[:, width:].astype(jnp.bfloat16)


def merge(piece_refs, pairs_ref):
    at = 0
    for piece in piece_refs:
        pairs_ref[at:at + piece.shape[0]] = piece[...]
        at += piece.shape[0]


def piece_at(r, me):
    at = jnp.int32(0)
    for parity in range(2):
        places = [ORDER.index(next(name for name in ORDER if name[parity] == i)) for i in range(len(ORDER))]
        for half in range(2):
            packed = sum(place << (4 * i) for i, place in enumerate(places[8 * half:8 * half + 7]))
            mine = jnp.where(r & 7 == 7, places[8 * half + 7], (packed >> (4 * (r & 7))) & 15)
            at = jnp.where((me & 1 == parity) & (r >> 3 == half), mine, at)
    return at


def early_kernel(list_ref, half_ref, *refs):
    piece_refs, (out_ref, pairs_ref) = refs[:-2], refs[-2:]
    sectors, blocks, tile, width = out_ref.shape
    first = 2 * sectors * blocks + 2 + sectors
    merge(piece_refs, pairs_ref)

    def one(a, carry):
        for k in range(0, blocks, 2):
            ats = [list_ref[first + a * blocks + k + u] for u in range(2)]
            forms = [block_form(pairs_ref[at // 2], at % 2 == 1) for at in ats]
            out_ref[a, k], out_ref[a, k + 1] = two_products([half_ref[a, k], half_ref[a, k + 1]], forms)
        return carry

    lax.fori_loop(0, sectors, one, 0, unroll=2)


def listed_products(group_size, first, list_ref, half_ref, pairs_ref, out_ref):
    sectors, blocks, tile, width = half_ref.shape
    items = sectors * blocks
    listed = list_ref[first + items]

    def group(g, carry):
        for u in range(0, group_size, 2):
            entries = [list_ref[first + jnp.minimum(g * group_size + u + n, listed - 1)] for n in range(2)]
            places, halves, forms = [], [], []
            for entry in entries:
                item, at = entry % items, entry // items
                places.append((item // blocks, item % blocks))
                halves.append(half_ref[places[-1]])
                forms.append(block_form(pairs_ref[at // 2], at % 2 == 1))
            out_ref[places[0]], out_ref[places[1]] = two_products(halves, forms)
        return carry

    lax.fori_loop(0, (listed + group_size - 1) // group_size, group, 0)


def middle_kernel(list_ref, early_ref, half_ref, *refs):
    piece_refs, (out_ref, pairs_ref) = refs[:-2], refs[-2:]
    out_ref[...] = early_ref[...]
    merge(piece_refs, pairs_ref)
    listed_products(16, 0, list_ref, half_ref, pairs_ref, out_ref)


def last_kernel(list_ref, middle_ref, half_ref, pairs_ref, out_hbm, out_ref, sems):
    sectors, blocks, tile, width = half_ref.shape
    items = sectors * blocks

    def store(a, ref):
        return pltpu.make_async_copy(ref.at[a], out_hbm.at[a], sems.at[a])

    for a in range(sectors):
        changed = list_ref[2 * items + 2 + a] > 0

        @pl.when(changed)
        def _():
            out_ref[a] = middle_ref[a]

        @pl.when(jnp.logical_not(changed))
        def _():
            store(a, middle_ref).start()

    listed_products(8, items + 1, list_ref, half_ref, pairs_ref, out_ref)
    for a in range(sectors):

        @pl.when(list_ref[2 * items + 2 + a] > 0)
        def _():
            store(a, out_ref).start()

    for a in range(sectors):
        store(a, out_ref).wait()


def swap(piece, even_bit, odd_bit):
    count = lax.axis_size("sec")
    return lax.ppermute(piece, "sec", [(i, i ^ (odd_bit if i & CORE else even_bit)) for i in range(count)])


def per_device(
    psi, left_ops, right_ops, dims_left, dims_right, right_owner, right_slot, term_active
):
    left_count, block_count, tile, width = psi.shape
    items = left_count * block_count
    pair_count = right_ops.shape[0] // 2
    count = lax.axis_size("sec")
    by_swaps = count == len(ORDER)
    flops = 2 * psi.size * tile
    smem = pl.BlockSpec(memory_space=pltpu.SMEM)
    vmem = pl.BlockSpec(memory_space=pltpu.VMEM)
    hbm = pl.BlockSpec(memory_space=pltpu.HBM)
    params = pltpu.CompilerParams(vmem_limit_bytes=VMEM_LIMIT)

    def in_hbm(*arrays):
        return [pltpu.with_memory_space_constraint(array, pltpu.HBM) for array in arrays]

    pairs = pl.pallas_call(
        pack_kernel,
        out_shape=jax.ShapeDtypeStruct((pair_count, tile, 2 * tile), jnp.bfloat16),
        in_specs=[hbm, hbm],
        out_specs=vmem,
        scratch_shapes=[
            pltpu.SMEM(dims_right.shape, jnp.int32),
            pltpu.VMEM(right_ops.shape, jnp.bfloat16),
            pltpu.SemaphoreType.DMA((2,)),
        ],
        compiler_params=params,
        cost_estimate=pl.CostEstimate(flops=0, bytes_accessed=2 * right_ops.size, transcendentals=0),
    )(*in_hbm(dims_right, right_ops))

    active = term_active.reshape(left_count, block_count)
    half, listed = pl.pallas_call(
        functools.partial(left_kernel, pair_count, len(EARLY if by_swaps else range(count)) * pair_count),
        out_shape=(
            jax.ShapeDtypeStruct(psi.shape, jnp.bfloat16),
            pltpu.SMEM((3 * items + 2 + left_count,), jnp.int32),
        ),
        in_specs=[hbm] * 6,
        out_specs=(vmem, smem),
        scratch_shapes=[
            pltpu.SMEM(dims_left.shape, jnp.int32),
            pltpu.SMEM(active.shape, jnp.int32),
            pltpu.SMEM(right_owner.shape, jnp.int32),
            pltpu.SMEM(right_slot.shape, jnp.int32),
            pltpu.VMEM(left_ops.shape, jnp.bfloat16),
            pltpu.VMEM(psi.shape, jnp.bfloat16),
            pltpu.SemaphoreType.DMA((5,)),
            pltpu.SemaphoreType.DMA((left_count,)),
        ],
        compiler_params=params,
        cost_estimate=pl.CostEstimate(flops=flops, bytes_accessed=2 * psi.size, transcendentals=0),
    )(*in_hbm(dims_left, active, right_owner, right_slot, left_ops, psi))
    listed = pltpu.with_memory_space_constraint(listed, pltpu.SMEM)

    if by_swaps:
        pieces = {OWN: pairs}

        def pass_on(*routes):
            for name, target in routes:
                pieces[target] = swap(pieces[name], name[0] ^ target[0], name[1] ^ target[1])

        def share(*names):
            for name in names:
                pieces[partner(name)] = swap(pieces[name], CORE, CORE)

        pass_on((OWN, BEYOND), (OWN, BESIDE), (OWN, SIDE))
        share(OWN)
        held = (BEYOND,)
        half, ends = lax.optimization_barrier((half, [pieces[name] for name in held]))
        pieces.update(zip(held, ends))
        pass_on((BEYOND, FIRST), (BESIDE, CORNER), (BEYOND, SECOND), (FIRST, END))
        share(BESIDE, SIDE, CORNER, FIRST, BEYOND)
        early = [pieces[name] for name in EARLY]
    else:
        early = [lax.all_gather(pairs, "sec", axis=0, tiled=True)]

    sigma = pl.pallas_call(
        early_kernel,
        out_shape=jax.ShapeDtypeStruct(psi.shape, jnp.bfloat16),
        in_specs=[smem] + [vmem] * (1 + len(early)),
        out_specs=vmem,
        scratch_shapes=[pltpu.VMEM((sum(piece.shape[0] for piece in early), tile, 2 * tile), jnp.bfloat16)],
        compiler_params=params,
        cost_estimate=pl.CostEstimate(flops=flops, bytes_accessed=2 * psi.size, transcendentals=0),
    )(listed, half, *early)
    if by_swaps:
        for name in (SECOND, END):
            pieces[name], _ = lax.optimization_barrier((pieces[name], sigma))
            share(name)
        sigma = pl.pallas_call(
            middle_kernel,
            out_shape=jax.ShapeDtypeStruct(psi.shape, jnp.bfloat16),
            in_specs=[smem] + [vmem] * (2 + len(MIDDLE)),
            out_specs=vmem,
            scratch_shapes=[pltpu.VMEM((len(MIDDLE) * pair_count, tile, 2 * tile), jnp.bfloat16)],
            compiler_params=params,
            cost_estimate=pl.CostEstimate(flops=flops // 4, bytes_accessed=psi.size // 2, transcendentals=0),
        )(listed, sigma, half, *[pieces[name] for name in MIDDLE])
        sigma = pl.pallas_call(
            last_kernel,
            out_shape=jax.ShapeDtypeStruct(psi.shape, jnp.bfloat16),
            in_specs=[smem] + [vmem] * 3,
            out_specs=hbm,
            scratch_shapes=[pltpu.VMEM(psi.shape, jnp.bfloat16), pltpu.SemaphoreType.DMA((left_count,))],
            compiler_params=params,
            cost_estimate=pl.CostEstimate(flops=flops // 16, bytes_accessed=2 * psi.size, transcendentals=0),
        )(listed, sigma, half, pieces[LAST[0]])
    if lax.axis_size("op") > 1:
        sigma = lax.psum_scatter(sigma, "op", scatter_dimension=3, tiled=True)
    return sigma


def solution(mesh):
    placed = (
        P(("grp", "sec"), None, None, None),
        P(("grp", "sec"), None, "op"),
        P(("grp", "sec"), None, "op"),
        P(("grp", "sec")),
        P(("grp", "sec")),
        P(("grp", "sec"), None),
        P(("grp", "sec"), None),
        P(("grp", "sec"), None, "op"),
    )
    return jax.shard_map(
        per_device,
        mesh=mesh,
        in_specs=placed,
        out_specs=P(("grp", "sec"), None, None, "op"),
        check_vma=False,
    )
```

```python
import functools

import jax
import jax.numpy as jnp
from jax import lax
from jax.experimental import pallas as pl
from jax.experimental.pallas import tpu as pltpu
from jax.sharding import PartitionSpec as P

VMEM_LIMIT = 48 * 1024 * 1024
FAR, NEAR, CROSS, CORE = 8, 4, 2, 1
OWN, SIDE, BESIDE, BEYOND, CORNER = (0, 0), (CROSS, CROSS), (NEAR, NEAR), (FAR, FAR), (NEAR | CROSS, NEAR | CROSS)
FIRST, SECOND = (FAR | NEAR, FAR | CROSS), (FAR | CROSS, FAR | NEAR)
END = (FAR | NEAR | CROSS, FAR | NEAR | CROSS)


def partner(name):
    return name[1] | CORE, name[0] | CORE


MIDDLE = (CORNER, SECOND, partner(CORNER), partner(BEYOND), partner(FIRST), END)
LAST = (partner(SECOND), partner(END))
EARLY = tuple(name for name in (
    OWN, SIDE, BESIDE, BEYOND, CORNER, FIRST, SECOND,
    partner(OWN), partner(SIDE), partner(BESIDE), partner(BEYOND), partner(CORNER), partner(FIRST), partner(SECOND),
) if name not in MIDDLE + LAST)
ORDER = EARLY + MIDDLE + LAST


def load_all(*copies):
    copies = [pltpu.make_async_copy(*copy) for copy in copies]
    for copy in copies:
        copy.start()
    return copies


def pack_kernel(dims_hbm, right_hbm, pairs_ref, dims_ref, right_ref, sems):
    count, tile, width = pairs_ref.shape
    copies = load_all((dims_hbm, dims_ref, sems.at[0]), (right_hbm, right_ref, sems.at[1]))
    rows = lax.broadcasted_iota(jnp.int32, (tile, tile), 0)
    cols = lax.broadcasted_iota(jnp.int32, (tile, tile), 1)
    most = jnp.maximum(rows, cols)
    for copy in copies:
        copy.wait()

    def kept(b):
        return jnp.where(most < dims_ref[b], right_ref[b].astype(jnp.float32), 0.0)

    for p in range(count):
        both = jnp.concatenate([kept(p), kept(p + count)], axis=0)
        pairs_ref[p] = both.T.astype(jnp.bfloat16)


def left_kernel(
    pair_count, held, dims_hbm, active_hbm, owner_hbm, slot_hbm, left_hbm, psi_hbm,
    half_ref, list_ref, dims_ref, active_ref, owner_ref, slot_ref, left_ref, psi_ref, sems, psi_sems,
):
    sectors, blocks, tile, width = psi_ref.shape
    items = sectors * blocks
    last = held + len(MIDDLE) * pair_count
    copies = load_all(
        (dims_hbm, dims_ref, sems.at[0]),
        (active_hbm, active_ref, sems.at[1]),
        (owner_hbm, owner_ref, sems.at[2]),
        (slot_hbm, slot_ref, sems.at[3]),
        (left_hbm, left_ref, sems.at[4]),
    )
    psi_copies = load_all(*[(psi_hbm.at[a], psi_ref.at[a], psi_sems.at[a]) for a in range(sectors)])
    rows = lax.broadcasted_iota(jnp.int32, (tile, tile), 0)
    cols = lax.broadcasted_iota(jnp.int32, (tile, tile), 1)
    most = jnp.maximum(rows, cols)
    me = lax.axis_index("sec")
    by_swaps = lax.axis_size("sec") == len(ORDER)
    for copy in copies:
        copy.wait()
    in_middle, in_last = jnp.int32(0), jnp.int32(0)
    for a in range(sectors):
        psi_copies[a].wait()
        op = jnp.where(most < dims_ref[a], left_ref[a].astype(jnp.float32), 0.0).astype(jnp.bfloat16)
        before = in_last
        for k in range(0, blocks, 2):
            both = jnp.concatenate([psi_ref[a, k], psi_ref[a, k + 1]], axis=1)
            part = jnp.dot(op, both, preferred_element_type=jnp.float32)
            for u in range(2):
                active = active_ref[a, k + u].astype(jnp.float32)
                half_ref[a, k + u] = (part[:, u * width:(u + 1) * width] * active).astype(jnp.bfloat16)
                item = a * blocks + k + u
                owner, slot = owner_ref[a, k + u], slot_ref[a, k + u]
                at = piece_at(owner ^ me, me) if by_swaps else owner
                second = slot >= pair_count
                at = at * pair_count + jnp.where(second, slot - pair_count, slot)
                is_early, is_last = at < held, at >= last
                at = (at - jnp.where(is_last, last, jnp.where(is_early, 0, held))) * 2 + second.astype(jnp.int32)
                list_ref[jnp.where(is_last, items + 1 + in_last, in_middle)] = at * items + item
                list_ref[2 * items + 2 + sectors + item] = jnp.where(is_early, at, 0)
                in_last = in_last + is_last.astype(jnp.int32)
                in_middle = in_middle + jnp.logical_not(is_early | is_last).astype(jnp.int32)
        list_ref[2 * items + 2 + a] = in_last - before
    list_ref[items] = in_middle
    list_ref[2 * items + 1] = in_last


def block_form(pair, second):
    tile, width = pair.shape
    lower = (lax.broadcasted_iota(jnp.int32, pair.shape, 1) < tile).astype(jnp.bfloat16)
    other = pltpu.roll(pair, tile, 1)
    top = jnp.where(second, other, pair) * lower
    low = jnp.where(second, pair, other) * (1 - lower)
    return jnp.concatenate([top, low], axis=0)


def two_products(halves, forms):
    zero = jnp.zeros_like(forms[0])
    top = jnp.concatenate([forms[0], zero], axis=1)
    low = jnp.concatenate([zero, forms[1]], axis=1)
    both = jnp.concatenate([top, low], axis=0)
    part = jnp.dot(jnp.concatenate(halves, axis=1), both, preferred_element_type=jnp.float32)
    width = part.shape[1] // 2
    return part[:, :width].astype(jnp.bfloat16), part[:, width:].astype(jnp.bfloat16)


def merge(piece_refs, pairs_ref):
    at = 0
    for piece in piece_refs:
        pairs_ref[at:at + piece.shape[0]] = piece[...]
        at += piece.shape[0]


def piece_at(r, me):
    at = jnp.int32(0)
    for parity in range(2):
        places = [ORDER.index(next(name for name in ORDER if name[parity] == i)) for i in range(len(ORDER))]
        for half in range(2):
            packed = sum(place << (4 * i) for i, place in enumerate(places[8 * half:8 * half + 7]))
            mine = jnp.where(r & 7 == 7, places[8 * half + 7], (packed >> (4 * (r & 7))) & 15)
            at = jnp.where((me & 1 == parity) & (r >> 3 == half), mine, at)
    return at


def early_kernel(list_ref, half_ref, *refs):
    piece_refs, (out_ref, pairs_ref) = refs[:-2], refs[-2:]
    sectors, blocks, tile, width = out_ref.shape
    first = 2 * sectors * blocks + 2 + sectors
    merge(piece_refs, pairs_ref)

    def one(a, carry):
        for k in range(0, blocks, 2):
            ats = [list_ref[first + a * blocks + k + u] for u in range(2)]
            forms = [block_form(pairs_ref[at // 2], at % 2 == 1) for at in ats]
            out_ref[a, k], out_ref[a, k + 1] = two_products([half_ref[a, k], half_ref[a, k + 1]], forms)
        return carry

    lax.fori_loop(0, sectors, one, 0, unroll=2)


def listed_products(group_size, first, list_ref, half_ref, pairs_ref, out_ref):
    sectors, blocks, tile, width = half_ref.shape
    items = sectors * blocks
    listed = list_ref[first + items]

    def group(g, carry):
        for u in range(0, group_size, 2):
            entries = [list_ref[first + jnp.minimum(g * group_size + u + n, listed - 1)] for n in range(2)]
            places, halves, forms = [], [], []
            for entry in entries:
                item, at = entry % items, entry // items
                places.append((item // blocks, item % blocks))
                halves.append(half_ref[places[-1]])
                forms.append(block_form(pairs_ref[at // 2], at % 2 == 1))
            out_ref[places[0]], out_ref[places[1]] = two_products(halves, forms)
        return carry

    lax.fori_loop(0, (listed + group_size - 1) // group_size, group, 0)


def middle_kernel(list_ref, early_ref, half_ref, *refs):
    piece_refs, (out_ref, pairs_ref) = refs[:-2], refs[-2:]
    out_ref[...] = early_ref[...]
    merge(piece_refs, pairs_ref)
    listed_products(16, 0, list_ref, half_ref, pairs_ref, out_ref)


def last_kernel(list_ref, middle_ref, half_ref, *refs):
    piece_refs, (out_hbm, pairs_ref, out_ref, sems) = refs[:-4], refs[-4:]
    sectors, blocks, tile, width = half_ref.shape
    items = sectors * blocks

    def store(a, ref):
        return pltpu.make_async_copy(ref.at[a], out_hbm.at[a], sems.at[a])

    for a in range(sectors):
        changed = list_ref[2 * items + 2 + a] > 0

        @pl.when(changed)
        def _():
            out_ref[a] = middle_ref[a]

        @pl.when(jnp.logical_not(changed))
        def _():
            store(a, middle_ref).start()

    merge(piece_refs, pairs_ref)
    listed_products(16, items + 1, list_ref, half_ref, pairs_ref, out_ref)
    for a in range(sectors):

        @pl.when(list_ref[2 * items + 2 + a] > 0)
        def _():
            store(a, out_ref).start()

    for a in range(sectors):
        store(a, out_ref).wait()


def swap(piece, even_bit, odd_bit):
    count = lax.axis_size("sec")
    return lax.ppermute(piece, "sec", [(i, i ^ (odd_bit if i & CORE else even_bit)) for i in range(count)])


def per_device(
    psi, left_ops, right_ops, dims_left, dims_right, right_owner, right_slot, term_active
):
    left_count, block_count, tile, width = psi.shape
    items = left_count * block_count
    pair_count = right_ops.shape[0] // 2
    count = lax.axis_size("sec")
    by_swaps = count == len(ORDER)
    flops = 2 * psi.size * tile
    smem = pl.BlockSpec(memory_space=pltpu.SMEM)
    vmem = pl.BlockSpec(memory_space=pltpu.VMEM)
    hbm = pl.BlockSpec(memory_space=pltpu.HBM)
    params = pltpu.CompilerParams(vmem_limit_bytes=VMEM_LIMIT)

    def in_hbm(*arrays):
        return [pltpu.with_memory_space_constraint(array, pltpu.HBM) for array in arrays]

    pairs = pl.pallas_call(
        pack_kernel,
        out_shape=jax.ShapeDtypeStruct((pair_count, tile, 2 * tile), jnp.bfloat16),
        in_specs=[hbm, hbm],
        out_specs=vmem,
        scratch_shapes=[
            pltpu.SMEM(dims_right.shape, jnp.int32),
            pltpu.VMEM(right_ops.shape, jnp.bfloat16),
            pltpu.SemaphoreType.DMA((2,)),
        ],
        compiler_params=params,
        cost_estimate=pl.CostEstimate(flops=0, bytes_accessed=2 * right_ops.size, transcendentals=0),
    )(*in_hbm(dims_right, right_ops))

    active = term_active.reshape(left_count, block_count)
    half, listed = pl.pallas_call(
        functools.partial(left_kernel, pair_count, len(EARLY if by_swaps else range(count)) * pair_count),
        out_shape=(
            jax.ShapeDtypeStruct(psi.shape, jnp.bfloat16),
            pltpu.SMEM((3 * items + 2 + left_count,), jnp.int32),
        ),
        in_specs=[hbm] * 6,
        out_specs=(vmem, smem),
        scratch_shapes=[
            pltpu.SMEM(dims_left.shape, jnp.int32),
            pltpu.SMEM(active.shape, jnp.int32),
            pltpu.SMEM(right_owner.shape, jnp.int32),
            pltpu.SMEM(right_slot.shape, jnp.int32),
            pltpu.VMEM(left_ops.shape, jnp.bfloat16),
            pltpu.VMEM(psi.shape, jnp.bfloat16),
            pltpu.SemaphoreType.DMA((5,)),
            pltpu.SemaphoreType.DMA((left_count,)),
        ],
        compiler_params=params,
        cost_estimate=pl.CostEstimate(flops=flops, bytes_accessed=2 * psi.size, transcendentals=0),
    )(*in_hbm(dims_left, active, right_owner, right_slot, left_ops, psi))
    listed = pltpu.with_memory_space_constraint(listed, pltpu.SMEM)

    if by_swaps:
        pieces = {OWN: pairs}

        def pass_on(*routes):
            for name, target in routes:
                pieces[target] = swap(pieces[name], name[0] ^ target[0], name[1] ^ target[1])

        def share(*names):
            for name in names:
                pieces[partner(name)] = swap(pieces[name], CORE, CORE)

        pass_on((OWN, BEYOND), (OWN, BESIDE), (OWN, SIDE))
        share(OWN)
        held = (BEYOND,)
        half, ends = lax.optimization_barrier((half, [pieces[name] for name in held]))
        pieces.update(zip(held, ends))
        pass_on((BEYOND, FIRST), (BESIDE, CORNER), (BEYOND, SECOND), (FIRST, END))
        share(BESIDE, SIDE, CORNER, FIRST, BEYOND)
        early = [pieces[name] for name in EARLY]
    else:
        early = [lax.all_gather(pairs, "sec", axis=0, tiled=True)]

    sigma = pl.pallas_call(
        early_kernel,
        out_shape=jax.ShapeDtypeStruct(psi.shape, jnp.bfloat16),
        in_specs=[smem] + [vmem] * (1 + len(early)),
        out_specs=vmem,
        scratch_shapes=[pltpu.VMEM((sum(piece.shape[0] for piece in early), tile, 2 * tile), jnp.bfloat16)],
        compiler_params=params,
        cost_estimate=pl.CostEstimate(flops=flops, bytes_accessed=2 * psi.size, transcendentals=0),
    )(listed, half, *early)
    if by_swaps:
        pieces[END], pieces[SECOND], sigma = lax.optimization_barrier((pieces[END], pieces[SECOND], sigma))
        share(END, SECOND)
        sigma = pl.pallas_call(
            middle_kernel,
            out_shape=jax.ShapeDtypeStruct(psi.shape, jnp.bfloat16),
            in_specs=[smem] + [vmem] * (2 + len(MIDDLE)),
            out_specs=vmem,
            scratch_shapes=[pltpu.VMEM((len(MIDDLE) * pair_count, tile, 2 * tile), jnp.bfloat16)],
            compiler_params=params,
            cost_estimate=pl.CostEstimate(flops=flops // 4, bytes_accessed=psi.size // 2, transcendentals=0),
        )(listed, sigma, half, *[pieces[name] for name in MIDDLE])
        sigma = pl.pallas_call(
            last_kernel,
            out_shape=jax.ShapeDtypeStruct(psi.shape, jnp.bfloat16),
            in_specs=[smem] + [vmem] * (2 + len(LAST)),
            out_specs=hbm,
            scratch_shapes=[
                pltpu.VMEM((len(LAST) * pair_count, tile, 2 * tile), jnp.bfloat16),
                pltpu.VMEM(psi.shape, jnp.bfloat16),
                pltpu.SemaphoreType.DMA((left_count,)),
            ],
            compiler_params=params,
            cost_estimate=pl.CostEstimate(flops=flops // 16, bytes_accessed=2 * psi.size, transcendentals=0),
        )(listed, sigma, half, *[pieces[name] for name in LAST])
    if lax.axis_size("op") > 1:
        sigma = lax.psum_scatter(sigma, "op", scatter_dimension=3, tiled=True)
    return sigma


def solution(mesh):
    placed = (
        P(("grp", "sec"), None, None, None),
        P(("grp", "sec"), None, "op"),
        P(("grp", "sec"), None, "op"),
        P(("grp", "sec")),
        P(("grp", "sec")),
        P(("grp", "sec"), None),
        P(("grp", "sec"), None),
        P(("grp", "sec"), None, "op"),
    )
    return jax.shard_map(
        per_device,
        mesh=mesh,
        in_specs=placed,
        out_specs=P(("grp", "sec"), None, None, "op"),
        check_vma=False,
    )
```

```python
import functools

import jax
import jax.numpy as jnp
from jax import lax
from jax.experimental import pallas as pl
from jax.experimental.pallas import tpu as pltpu
from jax.sharding import PartitionSpec as P

VMEM_LIMIT = 48 * 1024 * 1024
FAR, NEAR, CROSS, CORE = 8, 4, 2, 1
OWN, SIDE, BESIDE, BEYOND, CORNER = (0, 0), (CROSS, CROSS), (NEAR, NEAR), (FAR, FAR), (NEAR | CROSS, NEAR | CROSS)
FIRST, SECOND = (FAR | NEAR, FAR | CROSS), (FAR | CROSS, FAR | NEAR)
END = (FAR | NEAR | CROSS, FAR | NEAR | CROSS)


def partner(name):
    return name[1] | CORE, name[0] | CORE


MIDDLE = (CORNER, SECOND, partner(CORNER), partner(BEYOND), partner(FIRST), partner(SECOND), END)
LAST = (partner(END),)
EARLY = tuple(name for name in (
    OWN, SIDE, BESIDE, BEYOND, CORNER, FIRST, SECOND,
    partner(OWN), partner(SIDE), partner(BESIDE), partner(BEYOND), partner(CORNER), partner(FIRST), partner(SECOND),
) if name not in MIDDLE)
ORDER = EARLY + MIDDLE + LAST


def load_all(*copies):
    copies = [pltpu.make_async_copy(*copy) for copy in copies]
    for copy in copies:
        copy.start()
    return copies


def pack_kernel(dims_hbm, right_hbm, pairs_ref, dims_ref, right_ref, sems):
    count, tile, width = pairs_ref.shape
    copies = load_all((dims_hbm, dims_ref, sems.at[0]), (right_hbm, right_ref, sems.at[1]))
    rows = lax.broadcasted_iota(jnp.int32, (tile, tile), 0)
    cols = lax.broadcasted_iota(jnp.int32, (tile, tile), 1)
    most = jnp.maximum(rows, cols)
    for copy in copies:
        copy.wait()

    def kept(b):
        return jnp.where(most < dims_ref[b], right_ref[b].astype(jnp.float32), 0.0)

    for p in range(count):
        both = jnp.concatenate([kept(p), kept(p + count)], axis=0)
        pairs_ref[p] = both.T.astype(jnp.bfloat16)


def left_kernel(
    pair_count, held, dims_hbm, active_hbm, owner_hbm, slot_hbm, left_hbm, psi_hbm,
    half_ref, list_ref, dims_ref, active_ref, owner_ref, slot_ref, left_ref, psi_ref, sems, psi_sems,
):
    sectors, blocks, tile, width = psi_ref.shape
    items = sectors * blocks
    last = held + len(MIDDLE) * pair_count
    copies = load_all(
        (dims_hbm, dims_ref, sems.at[0]),
        (active_hbm, active_ref, sems.at[1]),
        (owner_hbm, owner_ref, sems.at[2]),
        (slot_hbm, slot_ref, sems.at[3]),
        (left_hbm, left_ref, sems.at[4]),
    )
    psi_copies = load_all(*[(psi_hbm.at[a], psi_ref.at[a], psi_sems.at[a]) for a in range(sectors)])
    rows = lax.broadcasted_iota(jnp.int32, (tile, tile), 0)
    cols = lax.broadcasted_iota(jnp.int32, (tile, tile), 1)
    most = jnp.maximum(rows, cols)
    me = lax.axis_index("sec")
    by_swaps = lax.axis_size("sec") == len(ORDER)
    for copy in copies:
        copy.wait()
    in_middle, in_last = jnp.int32(0), jnp.int32(0)
    for a in range(sectors):
        psi_copies[a].wait()
        op = jnp.where(most < dims_ref[a], left_ref[a].astype(jnp.float32), 0.0).astype(jnp.bfloat16)
        before = in_last
        for k in range(0, blocks, 2):
            both = jnp.concatenate([psi_ref[a, k], psi_ref[a, k + 1]], axis=1)
            part = jnp.dot(op, both, preferred_element_type=jnp.float32)
            for u in range(2):
                active = active_ref[a, k + u].astype(jnp.float32)
                half_ref[a, k + u] = (part[:, u * width:(u + 1) * width] * active).astype(jnp.bfloat16)
                item = a * blocks + k + u
                owner, slot = owner_ref[a, k + u], slot_ref[a, k + u]
                at = piece_at(owner ^ me, me) if by_swaps else owner
                second = slot >= pair_count
                at = at * pair_count + jnp.where(second, slot - pair_count, slot)
                is_early, is_last = at < held, at >= last
                at = (at - jnp.where(is_last, last, jnp.where(is_early, 0, held))) * 2 + second.astype(jnp.int32)
                list_ref[jnp.where(is_last, items + 1 + in_last, in_middle)] = at * items + item
                list_ref[2 * items + 2 + sectors + item] = jnp.where(is_early, at, 0)
                in_last = in_last + is_last.astype(jnp.int32)
                in_middle = in_middle + jnp.logical_not(is_early | is_last).astype(jnp.int32)
        list_ref[2 * items + 2 + a] = in_last - before
    list_ref[items] = in_middle
    list_ref[2 * items + 1] = in_last


def block_form(pair, second):
    tile, width = pair.shape
    lower = (lax.broadcasted_iota(jnp.int32, pair.shape, 1) < tile).astype(jnp.bfloat16)
    other = pltpu.roll(pair, tile, 1)
    top = jnp.where(second, other, pair) * lower
    low = jnp.where(second, pair, other) * (1 - lower)
    return jnp.concatenate([top, low], axis=0)


def two_products(halves, forms):
    zero = jnp.zeros_like(forms[0])
    top = jnp.concatenate([forms[0], zero], axis=1)
    low = jnp.concatenate([zero, forms[1]], axis=1)
    both = jnp.concatenate([top, low], axis=0)
    part = jnp.dot(jnp.concatenate(halves, axis=1), both, preferred_element_type=jnp.float32)
    width = part.shape[1] // 2
    return part[:, :width].astype(jnp.bfloat16), part[:, width:].astype(jnp.bfloat16)


def merge(piece_refs, pairs_ref):
    at = 0
    for piece in piece_refs:
        pairs_ref[at:at + piece.shape[0]] = piece[...]
        at += piece.shape[0]


def piece_at(r, me):
    at = jnp.int32(0)
    for parity in range(2):
        places = [ORDER.index(next(name for name in ORDER if name[parity] == i)) for i in range(len(ORDER))]
        for half in range(2):
            packed = sum(place << (4 * i) for i, place in enumerate(places[8 * half:8 * half + 7]))
            mine = jnp.where(r & 7 == 7, places[8 * half + 7], (packed >> (4 * (r & 7))) & 15)
            at = jnp.where((me & 1 == parity) & (r >> 3 == half), mine, at)
    return at


def early_kernel(list_ref, half_ref, *refs):
    piece_refs, (out_ref, pairs_ref) = refs[:-2], refs[-2:]
    sectors, blocks, tile, width = out_ref.shape
    first = 2 * sectors * blocks + 2 + sectors
    merge(piece_refs, pairs_ref)

    def one(a, carry):
        for k in range(0, blocks, 2):
            ats = [list_ref[first + a * blocks + k + u] for u in range(2)]
            forms = [block_form(pairs_ref[at // 2], at % 2 == 1) for at in ats]
            out_ref[a, k], out_ref[a, k + 1] = two_products([half_ref[a, k], half_ref[a, k + 1]], forms)
        return carry

    lax.fori_loop(0, sectors, one, 0, unroll=2)


def listed_products(group_size, first, list_ref, half_ref, pairs_ref, out_ref):
    sectors, blocks, tile, width = half_ref.shape
    items = sectors * blocks
    listed = list_ref[first + items]

    def group(g, carry):
        for u in range(0, group_size, 2):
            entries = [list_ref[first + jnp.minimum(g * group_size + u + n, listed - 1)] for n in range(2)]
            places, halves, forms = [], [], []
            for entry in entries:
                item, at = entry % items, entry // items
                places.append((item // blocks, item % blocks))
                halves.append(half_ref[places[-1]])
                forms.append(block_form(pairs_ref[at // 2], at % 2 == 1))
            out_ref[places[0]], out_ref[places[1]] = two_products(halves, forms)
        return carry

    lax.fori_loop(0, (listed + group_size - 1) // group_size, group, 0)


def middle_kernel(list_ref, early_ref, half_ref, *refs):
    piece_refs, (out_ref, pairs_ref) = refs[:-2], refs[-2:]
    out_ref[...] = early_ref[...]
    merge(piece_refs, pairs_ref)
    listed_products(16, 0, list_ref, half_ref, pairs_ref, out_ref)


def last_kernel(list_ref, middle_ref, half_ref, pairs_ref, out_hbm, out_ref, sems):
    sectors, blocks, tile, width = half_ref.shape
    items = sectors * blocks

    def store(a, ref):
        return pltpu.make_async_copy(ref.at[a], out_hbm.at[a], sems.at[a])

    for a in range(sectors):
        changed = list_ref[2 * items + 2 + a] > 0

        @pl.when(changed)
        def _():
            out_ref[a] = middle_ref[a]

        @pl.when(jnp.logical_not(changed))
        def _():
            store(a, middle_ref).start()

    listed_products(8, items + 1, list_ref, half_ref, pairs_ref, out_ref)
    for a in range(sectors):

        @pl.when(list_ref[2 * items + 2 + a] > 0)
        def _():
            store(a, out_ref).start()

    for a in range(sectors):
        store(a, out_ref).wait()


def swap(piece, even_bit, odd_bit):
    count = lax.axis_size("sec")
    return lax.ppermute(piece, "sec", [(i, i ^ (odd_bit if i & CORE else even_bit)) for i in range(count)])


def per_device(
    psi, left_ops, right_ops, dims_left, dims_right, right_owner, right_slot, term_active
):
    left_count, block_count, tile, width = psi.shape
    items = left_count * block_count
    pair_count = right_ops.shape[0] // 2
    count = lax.axis_size("sec")
    by_swaps = count == len(ORDER)
    flops = 2 * psi.size * tile
    smem = pl.BlockSpec(memory_space=pltpu.SMEM)
    vmem = pl.BlockSpec(memory_space=pltpu.VMEM)
    hbm = pl.BlockSpec(memory_space=pltpu.HBM)
    params = pltpu.CompilerParams(vmem_limit_bytes=VMEM_LIMIT)

    def in_hbm(*arrays):
        return [pltpu.with_memory_space_constraint(array, pltpu.HBM) for array in arrays]

    pairs = pl.pallas_call(
        pack_kernel,
        out_shape=jax.ShapeDtypeStruct((pair_count, tile, 2 * tile), jnp.bfloat16),
        in_specs=[hbm, hbm],
        out_specs=vmem,
        scratch_shapes=[
            pltpu.SMEM(dims_right.shape, jnp.int32),
            pltpu.VMEM(right_ops.shape, jnp.bfloat16),
            pltpu.SemaphoreType.DMA((2,)),
        ],
        compiler_params=params,
        cost_estimate=pl.CostEstimate(flops=0, bytes_accessed=2 * right_ops.size, transcendentals=0),
    )(*in_hbm(dims_right, right_ops))

    active = term_active.reshape(left_count, block_count)
    half, listed = pl.pallas_call(
        functools.partial(left_kernel, pair_count, len(EARLY if by_swaps else range(count)) * pair_count),
        out_shape=(
            jax.ShapeDtypeStruct(psi.shape, jnp.bfloat16),
            pltpu.SMEM((3 * items + 2 + left_count,), jnp.int32),
        ),
        in_specs=[hbm] * 6,
        out_specs=(vmem, smem),
        scratch_shapes=[
            pltpu.SMEM(dims_left.shape, jnp.int32),
            pltpu.SMEM(active.shape, jnp.int32),
            pltpu.SMEM(right_owner.shape, jnp.int32),
            pltpu.SMEM(right_slot.shape, jnp.int32),
            pltpu.VMEM(left_ops.shape, jnp.bfloat16),
            pltpu.VMEM(psi.shape, jnp.bfloat16),
            pltpu.SemaphoreType.DMA((5,)),
            pltpu.SemaphoreType.DMA((left_count,)),
        ],
        compiler_params=params,
        cost_estimate=pl.CostEstimate(flops=flops, bytes_accessed=2 * psi.size, transcendentals=0),
    )(*in_hbm(dims_left, active, right_owner, right_slot, left_ops, psi))
    listed = pltpu.with_memory_space_constraint(listed, pltpu.SMEM)

    if by_swaps:
        pieces = {OWN: pairs}

        def pass_on(*routes):
            for name, target in routes:
                pieces[target] = swap(pieces[name], name[0] ^ target[0], name[1] ^ target[1])

        def share(*names):
            for name in names:
                pieces[partner(name)] = swap(pieces[name], CORE, CORE)

        pass_on((OWN, BEYOND), (OWN, BESIDE), (OWN, SIDE))
        share(OWN)
        held = (BEYOND,)
        half, ends = lax.optimization_barrier((half, [pieces[name] for name in held]))
        pieces.update(zip(held, ends))
        pass_on((BEYOND, FIRST), (BESIDE, CORNER), (BEYOND, SECOND), (FIRST, END))
        share(BESIDE, SIDE, CORNER, FIRST, BEYOND)
        early = [pieces[name] for name in EARLY]
    else:
        early = [lax.all_gather(pairs, "sec", axis=0, tiled=True)]

    sigma = pl.pallas_call(
        early_kernel,
        out_shape=jax.ShapeDtypeStruct(psi.shape, jnp.bfloat16),
        in_specs=[smem] + [vmem] * (1 + len(early)),
        out_specs=vmem,
        scratch_shapes=[pltpu.VMEM((sum(piece.shape[0] for piece in early), tile, 2 * tile), jnp.bfloat16)],
        compiler_params=params,
        cost_estimate=pl.CostEstimate(flops=flops, bytes_accessed=2 * psi.size, transcendentals=0),
    )(listed, half, *early)
    if by_swaps:
        held = (partner(FIRST),)
        sigma, pieces[SECOND], ends = lax.optimization_barrier((sigma, pieces[SECOND], [pieces[name] for name in held]))
        pieces.update(zip(held, ends))
        share(SECOND)
        pieces[END], sigma = lax.optimization_barrier((pieces[END], sigma))
        share(END)
        sigma = pl.pallas_call(
            middle_kernel,
            out_shape=jax.ShapeDtypeStruct(psi.shape, jnp.bfloat16),
            in_specs=[smem] + [vmem] * (2 + len(MIDDLE)),
            out_specs=vmem,
            scratch_shapes=[pltpu.VMEM((len(MIDDLE) * pair_count, tile, 2 * tile), jnp.bfloat16)],
            compiler_params=params,
            cost_estimate=pl.CostEstimate(flops=flops // 4, bytes_accessed=psi.size // 2, transcendentals=0),
        )(listed, sigma, half, *[pieces[name] for name in MIDDLE])
        sigma = pl.pallas_call(
            last_kernel,
            out_shape=jax.ShapeDtypeStruct(psi.shape, jnp.bfloat16),
            in_specs=[smem] + [vmem] * 3,
            out_specs=hbm,
            scratch_shapes=[pltpu.VMEM(psi.shape, jnp.bfloat16), pltpu.SemaphoreType.DMA((left_count,))],
            compiler_params=params,
            cost_estimate=pl.CostEstimate(flops=flops // 16, bytes_accessed=2 * psi.size, transcendentals=0),
        )(listed, sigma, half, pieces[LAST[0]])
    if lax.axis_size("op") > 1:
        sigma = lax.psum_scatter(sigma, "op", scatter_dimension=3, tiled=True)
    return sigma


def solution(mesh):
    placed = (
        P(("grp", "sec"), None, None, None),
        P(("grp", "sec"), None, "op"),
        P(("grp", "sec"), None, "op"),
        P(("grp", "sec")),
        P(("grp", "sec")),
        P(("grp", "sec"), None),
        P(("grp", "sec"), None),
        P(("grp", "sec"), None, "op"),
    )
    return jax.shard_map(
        per_device,
        mesh=mesh,
        in_specs=placed,
        out_specs=P(("grp", "sec"), None, None, "op"),
        check_vma=False,
    )
```

```python
import functools

import jax
import jax.numpy as jnp
from jax import lax
from jax.experimental import pallas as pl
from jax.experimental.pallas import tpu as pltpu
from jax.sharding import PartitionSpec as P

VMEM_LIMIT = 48 * 1024 * 1024
FAR, NEAR, CROSS, CORE = 8, 4, 2, 1
OWN, SIDE, BESIDE, BEYOND, CORNER = (0, 0), (CROSS, CROSS), (NEAR, NEAR), (FAR, FAR), (NEAR | CROSS, NEAR | CROSS)
FIRST, SECOND = (FAR | NEAR, FAR | CROSS), (FAR | CROSS, FAR | NEAR)
END = (FAR | NEAR | CROSS, FAR | NEAR | CROSS)


def partner(name):
    return name[1] | CORE, name[0] | CORE


MIDDLE = (CORNER, SECOND, partner(CORNER), partner(BEYOND), partner(FIRST), END)
LAST = (partner(SECOND), partner(END))
EARLY = tuple(name for name in (
    OWN, SIDE, BESIDE, BEYOND, CORNER, FIRST, SECOND,
    partner(OWN), partner(SIDE), partner(BESIDE), partner(BEYOND), partner(CORNER), partner(FIRST), partner(SECOND),
) if name not in MIDDLE + LAST)
ORDER = EARLY + MIDDLE + LAST


def load_all(*copies):
    copies = [pltpu.make_async_copy(*copy) for copy in copies]
    for copy in copies:
        copy.start()
    return copies


def pack_kernel(dims_hbm, right_hbm, pairs_ref, dims_ref, right_ref, sems):
    count, tile, width = pairs_ref.shape
    parts = sems.shape[0] - 1
    step = count // parts
    copies = load_all(
        (dims_hbm, dims_ref, sems.at[parts, 0]),
        *[
            (right_hbm.at[pl.ds(half * count + part * step, step)],
             right_ref.at[pl.ds(half * count + part * step, step)], sems.at[part, half])
            for part in range(parts)
            for half in range(2)
        ],
    )
    rows = lax.broadcasted_iota(jnp.int32, (tile, tile), 0)
    cols = lax.broadcasted_iota(jnp.int32, (tile, tile), 1)
    most = jnp.maximum(rows, cols)

    def kept(b):
        return jnp.where(most < dims_ref[b], right_ref[b].astype(jnp.float32), 0.0)

    copies[0].wait()
    for part in range(parts):
        for copy in copies[1 + 2 * part:3 + 2 * part]:
            copy.wait()
        for p in range(part * step, (part + 1) * step):
            both = jnp.concatenate([kept(p), kept(p + count)], axis=0)
            pairs_ref[p] = both.T.astype(jnp.bfloat16)


def left_kernel(
    pair_count, held, dims_hbm, active_hbm, owner_hbm, slot_hbm, left_hbm, psi_hbm,
    half_ref, list_ref, dims_ref, active_ref, owner_ref, slot_ref, left_ref, psi_ref, sems, psi_sems,
):
    sectors, blocks, tile, width = psi_ref.shape
    items = sectors * blocks
    last = held + len(MIDDLE) * pair_count
    copies = load_all(
        (dims_hbm, dims_ref, sems.at[0]),
        (active_hbm, active_ref, sems.at[1]),
        (owner_hbm, owner_ref, sems.at[2]),
        (slot_hbm, slot_ref, sems.at[3]),
        (left_hbm, left_ref, sems.at[4]),
    )
    psi_copies = load_all(*[(psi_hbm.at[a], psi_ref.at[a], psi_sems.at[a]) for a in range(sectors)])
    rows = lax.broadcasted_iota(jnp.int32, (tile, tile), 0)
    cols = lax.broadcasted_iota(jnp.int32, (tile, tile), 1)
    most = jnp.maximum(rows, cols)
    me = lax.axis_index("sec")
    by_swaps = lax.axis_size("sec") == len(ORDER)
    for copy in copies:
        copy.wait()
    in_middle, in_last = jnp.int32(0), jnp.int32(0)
    for a in range(sectors):
        psi_copies[a].wait()
        op = jnp.where(most < dims_ref[a], left_ref[a].astype(jnp.float32), 0.0).astype(jnp.bfloat16)
        before = in_last
        for k in range(0, blocks, 2):
            both = jnp.concatenate([psi_ref[a, k], psi_ref[a, k + 1]], axis=1)
            part = jnp.dot(op, both, preferred_element_type=jnp.float32)
            for u in range(2):
                active = active_ref[a, k + u].astype(jnp.float32)
                half_ref[a, k + u] = (part[:, u * width:(u + 1) * width] * active).astype(jnp.bfloat16)
                item = a * blocks + k + u
                owner, slot = owner_ref[a, k + u], slot_ref[a, k + u]
                at = piece_at(owner ^ me, me) if by_swaps else owner
                second = slot >= pair_count
                at = at * pair_count + jnp.where(second, slot - pair_count, slot)
                is_early, is_last = at < held, at >= last
                at = (at - jnp.where(is_last, last, jnp.where(is_early, 0, held))) * 2 + second.astype(jnp.int32)
                list_ref[jnp.where(is_last, items + 1 + in_last, in_middle)] = at * items + item
                list_ref[2 * items + 2 + sectors + item] = jnp.where(is_early, at, 0)
                in_last = in_last + is_last.astype(jnp.int32)
                in_middle = in_middle + jnp.logical_not(is_early | is_last).astype(jnp.int32)
        list_ref[2 * items + 2 + a] = in_last - before
    list_ref[items] = in_middle
    list_ref[2 * items + 1] = in_last


def block_form(pair, second):
    tile, width = pair.shape
    lower = (lax.broadcasted_iota(jnp.int32, pair.shape, 1) < tile).astype(jnp.bfloat16)
    other = pltpu.roll(pair, tile, 1)
    top = jnp.where(second, other, pair) * lower
    low = jnp.where(second, pair, other) * (1 - lower)
    return jnp.concatenate([top, low], axis=0)


def two_products(halves, forms):
    zero = jnp.zeros_like(forms[0])
    top = jnp.concatenate([forms[0], zero], axis=1)
    low = jnp.concatenate([zero, forms[1]], axis=1)
    both = jnp.concatenate([top, low], axis=0)
    part = jnp.dot(jnp.concatenate(halves, axis=1), both, preferred_element_type=jnp.float32)
    width = part.shape[1] // 2
    return part[:, :width].astype(jnp.bfloat16), part[:, width:].astype(jnp.bfloat16)


def merge(piece_refs, pairs_ref):
    at = 0
    for piece in piece_refs:
        pairs_ref[at:at + piece.shape[0]] = piece[...]
        at += piece.shape[0]


def piece_at(r, me):
    at = jnp.int32(0)
    for parity in range(2):
        places = [ORDER.index(next(name for name in ORDER if name[parity] == i)) for i in range(len(ORDER))]
        for half in range(2):
            packed = sum(place << (4 * i) for i, place in enumerate(places[8 * half:8 * half + 7]))
            mine = jnp.where(r & 7 == 7, places[8 * half + 7], (packed >> (4 * (r & 7))) & 15)
            at = jnp.where((me & 1 == parity) & (r >> 3 == half), mine, at)
    return at


def early_kernel(list_ref, half_ref, *refs):
    piece_refs, (out_ref, pairs_ref) = refs[:-2], refs[-2:]
    sectors, blocks, tile, width = out_ref.shape
    first = 2 * sectors * blocks + 2 + sectors
    merge(piece_refs, pairs_ref)

    def one(a, carry):
        for k in range(0, blocks, 2):
            ats = [list_ref[first + a * blocks + k + u] for u in range(2)]
            forms = [block_form(pairs_ref[at // 2], at % 2 == 1) for at in ats]
            out_ref[a, k], out_ref[a, k + 1] = two_products([half_ref[a, k], half_ref[a, k + 1]], forms)
        return carry

    lax.fori_loop(0, sectors, one, 0, unroll=2)


def listed_products(group_size, first, list_ref, half_ref, pairs_ref, out_ref):
    sectors, blocks, tile, width = half_ref.shape
    items = sectors * blocks
    listed = list_ref[first + items]

    def group(g, carry):
        for u in range(0, group_size, 2):
            entries = [list_ref[first + jnp.minimum(g * group_size + u + n, listed - 1)] for n in range(2)]
            places, halves, forms = [], [], []
            for entry in entries:
                item, at = entry % items, entry // items
                places.append((item // blocks, item % blocks))
                halves.append(half_ref[places[-1]])
                forms.append(block_form(pairs_ref[at // 2], at % 2 == 1))
            out_ref[places[0]], out_ref[places[1]] = two_products(halves, forms)
        return carry

    lax.fori_loop(0, (listed + group_size - 1) // group_size, group, 0)


def middle_kernel(list_ref, early_ref, half_ref, *refs):
    piece_refs, (out_ref, pairs_ref) = refs[:-2], refs[-2:]
    out_ref[...] = early_ref[...]
    merge(piece_refs, pairs_ref)
    listed_products(16, 0, list_ref, half_ref, pairs_ref, out_ref)


def last_kernel(list_ref, middle_ref, half_ref, *refs):
    piece_refs, (out_hbm, pairs_ref, out_ref, sems) = refs[:-4], refs[-4:]
    sectors, blocks, tile, width = half_ref.shape
    items = sectors * blocks

    def store(a, ref):
        return pltpu.make_async_copy(ref.at[a], out_hbm.at[a], sems.at[a])

    for a in range(sectors):
        changed = list_ref[2 * items + 2 + a] > 0

        @pl.when(changed)
        def _():
            out_ref[a] = middle_ref[a]

        @pl.when(jnp.logical_not(changed))
        def _():
            store(a, middle_ref).start()

    merge(piece_refs, pairs_ref)
    listed_products(16, items + 1, list_ref, half_ref, pairs_ref, out_ref)
    for a in range(sectors):

        @pl.when(list_ref[2 * items + 2 + a] > 0)
        def _():
            store(a, out_ref).start()

    for a in range(sectors):
        store(a, out_ref).wait()


def swap(piece, even_bit, odd_bit):
    count = lax.axis_size("sec")
    return lax.ppermute(piece, "sec", [(i, i ^ (odd_bit if i & CORE else even_bit)) for i in range(count)])


def per_device(
    psi, left_ops, right_ops, dims_left, dims_right, right_owner, right_slot, term_active
):
    left_count, block_count, tile, width = psi.shape
    items = left_count * block_count
    pair_count = right_ops.shape[0] // 2
    count = lax.axis_size("sec")
    by_swaps = count == len(ORDER)
    flops = 2 * psi.size * tile
    smem = pl.BlockSpec(memory_space=pltpu.SMEM)
    vmem = pl.BlockSpec(memory_space=pltpu.VMEM)
    hbm = pl.BlockSpec(memory_space=pltpu.HBM)
    params = pltpu.CompilerParams(vmem_limit_bytes=VMEM_LIMIT)

    def in_hbm(*arrays):
        return [pltpu.with_memory_space_constraint(array, pltpu.HBM) for array in arrays]

    pairs = pl.pallas_call(
        pack_kernel,
        out_shape=jax.ShapeDtypeStruct((pair_count, tile, 2 * tile), jnp.bfloat16),
        in_specs=[hbm, hbm],
        out_specs=vmem,
        scratch_shapes=[
            pltpu.SMEM(dims_right.shape, jnp.int32),
            pltpu.VMEM(right_ops.shape, jnp.bfloat16),
            pltpu.SemaphoreType.DMA((5, 2)),
        ],
        compiler_params=params,
        cost_estimate=pl.CostEstimate(flops=0, bytes_accessed=2 * right_ops.size, transcendentals=0),
    )(*in_hbm(dims_right, right_ops))

    active = term_active.reshape(left_count, block_count)
    half, listed = pl.pallas_call(
        functools.partial(left_kernel, pair_count, len(EARLY if by_swaps else range(count)) * pair_count),
        out_shape=(
            jax.ShapeDtypeStruct(psi.shape, jnp.bfloat16),
            pltpu.SMEM((3 * items + 2 + left_count,), jnp.int32),
        ),
        in_specs=[hbm] * 6,
        out_specs=(vmem, smem),
        scratch_shapes=[
            pltpu.SMEM(dims_left.shape, jnp.int32),
            pltpu.SMEM(active.shape, jnp.int32),
            pltpu.SMEM(right_owner.shape, jnp.int32),
            pltpu.SMEM(right_slot.shape, jnp.int32),
            pltpu.VMEM(left_ops.shape, jnp.bfloat16),
            pltpu.VMEM(psi.shape, jnp.bfloat16),
            pltpu.SemaphoreType.DMA((5,)),
            pltpu.SemaphoreType.DMA((left_count,)),
        ],
        compiler_params=params,
        cost_estimate=pl.CostEstimate(flops=flops, bytes_accessed=2 * psi.size, transcendentals=0),
    )(*in_hbm(dims_left, active, right_owner, right_slot, left_ops, psi))
    listed = pltpu.with_memory_space_constraint(listed, pltpu.SMEM)

    if by_swaps:
        pieces = {OWN: pairs}

        def pass_on(*routes):
            for name, target in routes:
                pieces[target] = swap(pieces[name], name[0] ^ target[0], name[1] ^ target[1])

        def share(*names):
            for name in names:
                pieces[partner(name)] = swap(pieces[name], CORE, CORE)

        pass_on((OWN, BEYOND), (OWN, BESIDE), (OWN, SIDE))
        share(OWN)
        held = (BEYOND,)
        half, ends = lax.optimization_barrier((half, [pieces[name] for name in held]))
        pieces.update(zip(held, ends))
        pass_on((BEYOND, FIRST), (BESIDE, CORNER), (BEYOND, SECOND), (FIRST, END))
        share(BESIDE, SIDE, CORNER, FIRST, BEYOND)
        early = [pieces[name] for name in EARLY]
    else:
        early = [lax.all_gather(pairs, "sec", axis=0, tiled=True)]

    sigma = pl.pallas_call(
        early_kernel,
        out_shape=jax.ShapeDtypeStruct(psi.shape, jnp.bfloat16),
        in_specs=[smem] + [vmem] * (1 + len(early)),
        out_specs=vmem,
        scratch_shapes=[pltpu.VMEM((sum(piece.shape[0] for piece in early), tile, 2 * tile), jnp.bfloat16)],
        compiler_params=params,
        cost_estimate=pl.CostEstimate(flops=flops, bytes_accessed=2 * psi.size, transcendentals=0),
    )(listed, half, *early)
    if by_swaps:
        pieces[END], pieces[SECOND], sigma = lax.optimization_barrier((pieces[END], pieces[SECOND], sigma))
        share(END, SECOND)
        sigma = pl.pallas_call(
            middle_kernel,
            out_shape=jax.ShapeDtypeStruct(psi.shape, jnp.bfloat16),
            in_specs=[smem] + [vmem] * (2 + len(MIDDLE)),
            out_specs=vmem,
            scratch_shapes=[pltpu.VMEM((len(MIDDLE) * pair_count, tile, 2 * tile), jnp.bfloat16)],
            compiler_params=params,
            cost_estimate=pl.CostEstimate(flops=flops // 4, bytes_accessed=psi.size // 2, transcendentals=0),
        )(listed, sigma, half, *[pieces[name] for name in MIDDLE])
        sigma = pl.pallas_call(
            last_kernel,
            out_shape=jax.ShapeDtypeStruct(psi.shape, jnp.bfloat16),
            in_specs=[smem] + [vmem] * (2 + len(LAST)),
            out_specs=hbm,
            scratch_shapes=[
                pltpu.VMEM((len(LAST) * pair_count, tile, 2 * tile), jnp.bfloat16),
                pltpu.VMEM(psi.shape, jnp.bfloat16),
                pltpu.SemaphoreType.DMA((left_count,)),
            ],
            compiler_params=params,
            cost_estimate=pl.CostEstimate(flops=flops // 16, bytes_accessed=2 * psi.size, transcendentals=0),
        )(listed, sigma, half, *[pieces[name] for name in LAST])
    if lax.axis_size("op") > 1:
        sigma = lax.psum_scatter(sigma, "op", scatter_dimension=3, tiled=True)
    return sigma


def solution(mesh):
    placed = (
        P(("grp", "sec"), None, None, None),
        P(("grp", "sec"), None, "op"),
        P(("grp", "sec"), None, "op"),
        P(("grp", "sec")),
        P(("grp", "sec")),
        P(("grp", "sec"), None),
        P(("grp", "sec"), None),
        P(("grp", "sec"), None, "op"),
    )
    return jax.shard_map(
        per_device,
        mesh=mesh,
        in_specs=placed,
        out_specs=P(("grp", "sec"), None, None, "op"),
        check_vma=False,
    )
```

```python
import functools

import jax
import jax.numpy as jnp
from jax import lax
from jax.experimental import pallas as pl
from jax.experimental.pallas import tpu as pltpu
from jax.sharding import PartitionSpec as P

VMEM_LIMIT = 48 * 1024 * 1024
FAR, NEAR, CROSS, CORE = 8, 4, 2, 1
OWN, SIDE, BESIDE, BEYOND, CORNER = (0, 0), (CROSS, CROSS), (NEAR, NEAR), (FAR, FAR), (NEAR | CROSS, NEAR | CROSS)
FIRST, SECOND = (FAR | CROSS, FAR | NEAR), (FAR | NEAR, FAR | CROSS)
END = (FAR | NEAR | CROSS, FAR | NEAR | CROSS)


def partner(name):
    return name[1] | CORE, name[0] | CORE


MIDDLE = (CORNER, SECOND, partner(CORNER), partner(BEYOND), partner(FIRST), END)
LAST = (partner(SECOND), partner(END))
EARLY = tuple(name for name in (
    OWN, SIDE, BESIDE, BEYOND, CORNER, FIRST, SECOND,
    partner(OWN), partner(SIDE), partner(BESIDE), partner(BEYOND), partner(CORNER), partner(FIRST), partner(SECOND),
) if name not in MIDDLE + LAST)
ORDER = EARLY + MIDDLE + LAST


def load_all(*copies):
    copies = [pltpu.make_async_copy(*copy) for copy in copies]
    for copy in copies:
        copy.start()
    return copies


def pack_kernel(dims_hbm, right_hbm, pairs_ref, dims_ref, right_ref, sems):
    count, tile, width = pairs_ref.shape
    copies = load_all((dims_hbm, dims_ref, sems.at[0]), (right_hbm, right_ref, sems.at[1]))
    rows = lax.broadcasted_iota(jnp.int32, (tile, tile), 0)
    cols = lax.broadcasted_iota(jnp.int32, (tile, tile), 1)
    most = jnp.maximum(rows, cols)
    for copy in copies:
        copy.wait()

    def kept(b):
        return jnp.where(most < dims_ref[b], right_ref[b].astype(jnp.float32), 0.0)

    for p in range(count):
        both = jnp.concatenate([kept(p), kept(p + count)], axis=0)
        pairs_ref[p] = both.T.astype(jnp.bfloat16)


def left_kernel(
    pair_count, held, dims_hbm, active_hbm, owner_hbm, slot_hbm, left_hbm, psi_hbm,
    half_ref, list_ref, dims_ref, active_ref, owner_ref, slot_ref, left_ref, psi_ref, sems, psi_sems,
):
    sectors, blocks, tile, width = psi_ref.shape
    items = sectors * blocks
    last = held + len(MIDDLE) * pair_count
    copies = load_all(
        (dims_hbm, dims_ref, sems.at[0]),
        (active_hbm, active_ref, sems.at[1]),
        (owner_hbm, owner_ref, sems.at[2]),
        (slot_hbm, slot_ref, sems.at[3]),
        (left_hbm, left_ref, sems.at[4]),
    )
    psi_copies = load_all(*[(psi_hbm.at[a], psi_ref.at[a], psi_sems.at[a]) for a in range(sectors)])
    rows = lax.broadcasted_iota(jnp.int32, (tile, tile), 0)
    cols = lax.broadcasted_iota(jnp.int32, (tile, tile), 1)
    most = jnp.maximum(rows, cols)
    me = lax.axis_index("sec")
    by_swaps = lax.axis_size("sec") == len(ORDER)
    for copy in copies:
        copy.wait()
    in_middle, in_last = jnp.int32(0), jnp.int32(0)
    for a in range(sectors):
        psi_copies[a].wait()
        op = jnp.where(most < dims_ref[a], left_ref[a].astype(jnp.float32), 0.0).astype(jnp.bfloat16)
        before = in_last
        for k in range(0, blocks, 2):
            both = jnp.concatenate([psi_ref[a, k], psi_ref[a, k + 1]], axis=1)
            part = jnp.dot(op, both, preferred_element_type=jnp.float32)
            for u in range(2):
                active = active_ref[a, k + u].astype(jnp.float32)
                half_ref[a, k + u] = (part[:, u * width:(u + 1) * width] * active).astype(jnp.bfloat16)
                item = a * blocks + k + u
                owner, slot = owner_ref[a, k + u], slot_ref[a, k + u]
                at = piece_at(owner ^ me, me) if by_swaps else owner
                second = slot >= pair_count
                at = at * pair_count + jnp.where(second, slot - pair_count, slot)
                is_early, is_last = at < held, at >= last
                at = (at - jnp.where(is_last, last, jnp.where(is_early, 0, held))) * 2 + second.astype(jnp.int32)
                list_ref[jnp.where(is_last, items + 1 + in_last, in_middle)] = at * items + item
                list_ref[2 * items + 2 + sectors + item] = jnp.where(is_early, at, 0)
                in_last = in_last + is_last.astype(jnp.int32)
                in_middle = in_middle + jnp.logical_not(is_early | is_last).astype(jnp.int32)
        list_ref[2 * items + 2 + a] = in_last - before
    list_ref[items] = in_middle
    list_ref[2 * items + 1] = in_last


def block_form(pair, second):
    tile, width = pair.shape
    lower = (lax.broadcasted_iota(jnp.int32, pair.shape, 1) < tile).astype(jnp.bfloat16)
    other = pltpu.roll(pair, tile, 1)
    top = jnp.where(second, other, pair) * lower
    low = jnp.where(second, pair, other) * (1 - lower)
    return jnp.concatenate([top, low], axis=0)


def two_products(halves, forms):
    zero = jnp.zeros_like(forms[0])
    top = jnp.concatenate([forms[0], zero], axis=1)
    low = jnp.concatenate([zero, forms[1]], axis=1)
    both = jnp.concatenate([top, low], axis=0)
    part = jnp.dot(jnp.concatenate(halves, axis=1), both, preferred_element_type=jnp.float32)
    width = part.shape[1] // 2
    return part[:, :width].astype(jnp.bfloat16), part[:, width:].astype(jnp.bfloat16)


def merge(piece_refs, pairs_ref):
    at = 0
    for piece in piece_refs:
        pairs_ref[at:at + piece.shape[0]] = piece[...]
        at += piece.shape[0]


def piece_at(r, me):
    at = jnp.int32(0)
    for parity in range(2):
        places = [ORDER.index(next(name for name in ORDER if name[parity] == i)) for i in range(len(ORDER))]
        for half in range(2):
            packed = sum(place << (4 * i) for i, place in enumerate(places[8 * half:8 * half + 7]))
            mine = jnp.where(r & 7 == 7, places[8 * half + 7], (packed >> (4 * (r & 7))) & 15)
            at = jnp.where((me & 1 == parity) & (r >> 3 == half), mine, at)
    return at


def early_kernel(list_ref, half_ref, *refs):
    piece_refs, (out_ref, pairs_ref) = refs[:-2], refs[-2:]
    sectors, blocks, tile, width = out_ref.shape
    first = 2 * sectors * blocks + 2 + sectors
    merge(piece_refs, pairs_ref)

    def one(a, carry):
        for k in range(0, blocks, 2):
            ats = [list_ref[first + a * blocks + k + u] for u in range(2)]
            forms = [block_form(pairs_ref[at // 2], at % 2 == 1) for at in ats]
            out_ref[a, k], out_ref[a, k + 1] = two_products([half_ref[a, k], half_ref[a, k + 1]], forms)
        return carry

    lax.fori_loop(0, sectors, one, 0, unroll=2)


def listed_products(group_size, first, list_ref, half_ref, pairs_ref, out_ref):
    sectors, blocks, tile, width = half_ref.shape
    items = sectors * blocks
    listed = list_ref[first + items]

    def group(g, carry):
        for u in range(0, group_size, 2):
            entries = [list_ref[first + jnp.minimum(g * group_size + u + n, listed - 1)] for n in range(2)]
            places, halves, forms = [], [], []
            for entry in entries:
                item, at = entry % items, entry // items
                places.append((item // blocks, item % blocks))
                halves.append(half_ref[places[-1]])
                forms.append(block_form(pairs_ref[at // 2], at % 2 == 1))
            out_ref[places[0]], out_ref[places[1]] = two_products(halves, forms)
        return carry

    lax.fori_loop(0, (listed + group_size - 1) // group_size, group, 0)


def middle_kernel(list_ref, early_ref, half_ref, *refs):
    piece_refs, (out_ref, pairs_ref) = refs[:-2], refs[-2:]
    out_ref[...] = early_ref[...]
    merge(piece_refs, pairs_ref)
    listed_products(16, 0, list_ref, half_ref, pairs_ref, out_ref)


def last_kernel(list_ref, middle_ref, half_ref, *refs):
    piece_refs, (out_hbm, pairs_ref, out_ref, sems) = refs[:-4], refs[-4:]
    sectors, blocks, tile, width = half_ref.shape
    items = sectors * blocks

    def store(a, ref):
        return pltpu.make_async_copy(ref.at[a], out_hbm.at[a], sems.at[a])

    for a in range(sectors):
        changed = list_ref[2 * items + 2 + a] > 0

        @pl.when(changed)
        def _():
            out_ref[a] = middle_ref[a]

        @pl.when(jnp.logical_not(changed))
        def _():
            store(a, middle_ref).start()

    merge(piece_refs, pairs_ref)
    listed_products(16, items + 1, list_ref, half_ref, pairs_ref, out_ref)
    for a in range(sectors):

        @pl.when(list_ref[2 * items + 2 + a] > 0)
        def _():
            store(a, out_ref).start()

    for a in range(sectors):
        store(a, out_ref).wait()


def swap(piece, even_bit, odd_bit):
    count = lax.axis_size("sec")
    return lax.ppermute(piece, "sec", [(i, i ^ (odd_bit if i & CORE else even_bit)) for i in range(count)])


def per_device(
    psi, left_ops, right_ops, dims_left, dims_right, right_owner, right_slot, term_active
):
    left_count, block_count, tile, width = psi.shape
    items = left_count * block_count
    pair_count = right_ops.shape[0] // 2
    count = lax.axis_size("sec")
    by_swaps = count == len(ORDER)
    flops = 2 * psi.size * tile
    smem = pl.BlockSpec(memory_space=pltpu.SMEM)
    vmem = pl.BlockSpec(memory_space=pltpu.VMEM)
    hbm = pl.BlockSpec(memory_space=pltpu.HBM)
    params = pltpu.CompilerParams(vmem_limit_bytes=VMEM_LIMIT)

    def in_hbm(*arrays):
        return [pltpu.with_memory_space_constraint(array, pltpu.HBM) for array in arrays]

    pairs = pl.pallas_call(
        pack_kernel,
        out_shape=jax.ShapeDtypeStruct((pair_count, tile, 2 * tile), jnp.bfloat16),
        in_specs=[hbm, hbm],
        out_specs=vmem,
        scratch_shapes=[
            pltpu.SMEM(dims_right.shape, jnp.int32),
            pltpu.VMEM(right_ops.shape, jnp.bfloat16),
            pltpu.SemaphoreType.DMA((2,)),
        ],
        compiler_params=params,
        cost_estimate=pl.CostEstimate(flops=0, bytes_accessed=2 * right_ops.size, transcendentals=0),
    )(*in_hbm(dims_right, right_ops))

    active = term_active.reshape(left_count, block_count)
    half, listed = pl.pallas_call(
        functools.partial(left_kernel, pair_count, len(EARLY if by_swaps else range(count)) * pair_count),
        out_shape=(
            jax.ShapeDtypeStruct(psi.shape, jnp.bfloat16),
            pltpu.SMEM((3 * items + 2 + left_count,), jnp.int32),
        ),
        in_specs=[hbm] * 6,
        out_specs=(vmem, smem),
        scratch_shapes=[
            pltpu.SMEM(dims_left.shape, jnp.int32),
            pltpu.SMEM(active.shape, jnp.int32),
            pltpu.SMEM(right_owner.shape, jnp.int32),
            pltpu.SMEM(right_slot.shape, jnp.int32),
            pltpu.VMEM(left_ops.shape, jnp.bfloat16),
            pltpu.VMEM(psi.shape, jnp.bfloat16),
            pltpu.SemaphoreType.DMA((5,)),
            pltpu.SemaphoreType.DMA((left_count,)),
        ],
        compiler_params=params,
        cost_estimate=pl.CostEstimate(flops=flops, bytes_accessed=2 * psi.size, transcendentals=0),
    )(*in_hbm(dims_left, active, right_owner, right_slot, left_ops, psi))
    listed = pltpu.with_memory_space_constraint(listed, pltpu.SMEM)

    if by_swaps:
        pieces = {OWN: pairs}

        def pass_on(*routes):
            for name, target in routes:
                pieces[target] = swap(pieces[name], name[0] ^ target[0], name[1] ^ target[1])

        def share(*names):
            for name in names:
                pieces[partner(name)] = swap(pieces[name], CORE, CORE)

        pass_on((OWN, BEYOND), (OWN, BESIDE), (OWN, SIDE))
        share(OWN)
        held = (BEYOND,)
        half, ends = lax.optimization_barrier((half, [pieces[name] for name in held]))
        pieces.update(zip(held, ends))
        pass_on((BEYOND, FIRST), (BESIDE, CORNER), (BEYOND, SECOND), (FIRST, END))
        share(BESIDE, SIDE, CORNER, FIRST, BEYOND)
        early = [pieces[name] for name in EARLY]
    else:
        early = [lax.all_gather(pairs, "sec", axis=0, tiled=True)]

    sigma = pl.pallas_call(
        early_kernel,
        out_shape=jax.ShapeDtypeStruct(psi.shape, jnp.bfloat16),
        in_specs=[smem] + [vmem] * (1 + len(early)),
        out_specs=vmem,
        scratch_shapes=[pltpu.VMEM((sum(piece.shape[0] for piece in early), tile, 2 * tile), jnp.bfloat16)],
        compiler_params=params,
        cost_estimate=pl.CostEstimate(flops=flops, bytes_accessed=2 * psi.size, transcendentals=0),
    )(listed, half, *early)
    if by_swaps:
        pieces[END], pieces[SECOND], sigma = lax.optimization_barrier((pieces[END], pieces[SECOND], sigma))
        share(END, SECOND)
        sigma = pl.pallas_call(
            middle_kernel,
            out_shape=jax.ShapeDtypeStruct(psi.shape, jnp.bfloat16),
            in_specs=[smem] + [vmem] * (2 + len(MIDDLE)),
            out_specs=vmem,
            scratch_shapes=[pltpu.VMEM((len(MIDDLE) * pair_count, tile, 2 * tile), jnp.bfloat16)],
            compiler_params=params,
            cost_estimate=pl.CostEstimate(flops=flops // 4, bytes_accessed=psi.size // 2, transcendentals=0),
        )(listed, sigma, half, *[pieces[name] for name in MIDDLE])
        sigma = pl.pallas_call(
            last_kernel,
            out_shape=jax.ShapeDtypeStruct(psi.shape, jnp.bfloat16),
            in_specs=[smem] + [vmem] * (2 + len(LAST)),
            out_specs=hbm,
            scratch_shapes=[
                pltpu.VMEM((len(LAST) * pair_count, tile, 2 * tile), jnp.bfloat16),
                pltpu.VMEM(psi.shape, jnp.bfloat16),
                pltpu.SemaphoreType.DMA((left_count,)),
            ],
            compiler_params=params,
            cost_estimate=pl.CostEstimate(flops=flops // 16, bytes_accessed=2 * psi.size, transcendentals=0),
        )(listed, sigma, half, *[pieces[name] for name in LAST])
    if lax.axis_size("op") > 1:
        sigma = lax.psum_scatter(sigma, "op", scatter_dimension=3, tiled=True)
    return sigma


def solution(mesh):
    placed = (
        P(("grp", "sec"), None, None, None),
        P(("grp", "sec"), None, "op"),
        P(("grp", "sec"), None, "op"),
        P(("grp", "sec")),
        P(("grp", "sec")),
        P(("grp", "sec"), None),
        P(("grp", "sec"), None),
        P(("grp", "sec"), None, "op"),
    )
    return jax.shard_map(
        per_device,
        mesh=mesh,
        in_specs=placed,
        out_specs=P(("grp", "sec"), None, None, "op"),
        check_vma=False,
    )
```

```python
import functools

import jax
import jax.numpy as jnp
from jax import lax
from jax.experimental import pallas as pl
from jax.experimental.pallas import tpu as pltpu
from jax.sharding import PartitionSpec as P

VMEM_LIMIT = 48 * 1024 * 1024
FAR, NEAR, CROSS, CORE = 8, 4, 2, 1
OWN, SIDE, BESIDE, BEYOND, CORNER = (0, 0), (CROSS, NEAR), (NEAR, CROSS), (FAR, FAR), (NEAR | CROSS, NEAR | CROSS)
FIRST, SECOND = (FAR | NEAR, FAR | CROSS), (FAR | CROSS, FAR | NEAR)
END = (FAR | NEAR | CROSS, FAR | NEAR | CROSS)


def partner(name):
    return name[1] | CORE, name[0] | CORE


MIDDLE = (CORNER, SECOND, partner(CORNER), partner(BEYOND), partner(FIRST), END)
LAST = (partner(SECOND), partner(END))
EARLY = tuple(name for name in (
    OWN, SIDE, BESIDE, BEYOND, CORNER, FIRST, SECOND,
    partner(OWN), partner(SIDE), partner(BESIDE), partner(BEYOND), partner(CORNER), partner(FIRST), partner(SECOND),
) if name not in MIDDLE + LAST)
ORDER = EARLY + MIDDLE + LAST


def load_all(*copies):
    copies = [pltpu.make_async_copy(*copy) for copy in copies]
    for copy in copies:
        copy.start()
    return copies


def pack_kernel(dims_hbm, right_hbm, pairs_ref, dims_ref, right_ref, sems):
    count, tile, width = pairs_ref.shape
    copies = load_all((dims_hbm, dims_ref, sems.at[0]), (right_hbm, right_ref, sems.at[1]))
    rows = lax.broadcasted_iota(jnp.int32, (tile, tile), 0)
    cols = lax.broadcasted_iota(jnp.int32, (tile, tile), 1)
    most = jnp.maximum(rows, cols)
    for copy in copies:
        copy.wait()

    def kept(b):
        return jnp.where(most < dims_ref[b], right_ref[b].astype(jnp.float32), 0.0)

    for p in range(count):
        both = jnp.concatenate([kept(p), kept(p + count)], axis=0)
        pairs_ref[p] = both.T.astype(jnp.bfloat16)


def left_kernel(
    pair_count, held, dims_hbm, active_hbm, owner_hbm, slot_hbm, left_hbm, psi_hbm,
    half_ref, list_ref, dims_ref, active_ref, owner_ref, slot_ref, left_ref, psi_ref, sems, psi_sems,
):
    sectors, blocks, tile, width = psi_ref.shape
    items = sectors * blocks
    last = held + len(MIDDLE) * pair_count
    copies = load_all(
        (dims_hbm, dims_ref, sems.at[0]),
        (active_hbm, active_ref, sems.at[1]),
        (owner_hbm, owner_ref, sems.at[2]),
        (slot_hbm, slot_ref, sems.at[3]),
        (left_hbm, left_ref, sems.at[4]),
    )
    psi_copies = load_all(*[(psi_hbm.at[a], psi_ref.at[a], psi_sems.at[a]) for a in range(sectors)])
    rows = lax.broadcasted_iota(jnp.int32, (tile, tile), 0)
    cols = lax.broadcasted_iota(jnp.int32, (tile, tile), 1)
    most = jnp.maximum(rows, cols)
    me = lax.axis_index("sec")
    by_swaps = lax.axis_size("sec") == len(ORDER)
    for copy in copies:
        copy.wait()
    in_middle, in_last = jnp.int32(0), jnp.int32(0)
    for a in range(sectors):
        psi_copies[a].wait()
        op = jnp.where(most < dims_ref[a], left_ref[a].astype(jnp.float32), 0.0).astype(jnp.bfloat16)
        before = in_last
        for k in range(0, blocks, 2):
            both = jnp.concatenate([psi_ref[a, k], psi_ref[a, k + 1]], axis=1)
            part = jnp.dot(op, both, preferred_element_type=jnp.float32)
            for u in range(2):
                active = active_ref[a, k + u].astype(jnp.float32)
                half_ref[a, k + u] = (part[:, u * width:(u + 1) * width] * active).astype(jnp.bfloat16)
                item = a * blocks + k + u
                owner, slot = owner_ref[a, k + u], slot_ref[a, k + u]
                at = piece_at(owner ^ me, me) if by_swaps else owner
                second = slot >= pair_count
                at = at * pair_count + jnp.where(second, slot - pair_count, slot)
                is_early, is_last = at < held, at >= last
                at = (at - jnp.where(is_last, last, jnp.where(is_early, 0, held))) * 2 + second.astype(jnp.int32)
                list_ref[jnp.where(is_last, items + 1 + in_last, in_middle)] = at * items + item
                list_ref[2 * items + 2 + sectors + item] = jnp.where(is_early, at, 0)
                in_last = in_last + is_last.astype(jnp.int32)
                in_middle = in_middle + jnp.logical_not(is_early | is_last).astype(jnp.int32)
        list_ref[2 * items + 2 + a] = in_last - before
    list_ref[items] = in_middle
    list_ref[2 * items + 1] = in_last


def block_form(pair, second):
    tile, width = pair.shape
    lower = (lax.broadcasted_iota(jnp.int32, pair.shape, 1) < tile).astype(jnp.bfloat16)
    other = pltpu.roll(pair, tile, 1)
    top = jnp.where(second, other, pair) * lower
    low = jnp.where(second, pair, other) * (1 - lower)
    return jnp.concatenate([top, low], axis=0)


def two_products(halves, forms):
    zero = jnp.zeros_like(forms[0])
    top = jnp.concatenate([forms[0], zero], axis=1)
    low = jnp.concatenate([zero, forms[1]], axis=1)
    both = jnp.concatenate([top, low], axis=0)
    part = jnp.dot(jnp.concatenate(halves, axis=1), both, preferred_element_type=jnp.float32)
    width = part.shape[1] // 2
    return part[:, :width].astype(jnp.bfloat16), part[:, width:].astype(jnp.bfloat16)


def merge(piece_refs, pairs_ref):
    at = 0
    for piece in piece_refs:
        pairs_ref[at:at + piece.shape[0]] = piece[...]
        at += piece.shape[0]


def piece_at(r, me):
    at = jnp.int32(0)
    for parity in range(2):
        places = [ORDER.index(next(name for name in ORDER if name[parity] == i)) for i in range(len(ORDER))]
        for half in range(2):
            packed = sum(place << (4 * i) for i, place in enumerate(places[8 * half:8 * half + 7]))
            mine = jnp.where(r & 7 == 7, places[8 * half + 7], (packed >> (4 * (r & 7))) & 15)
            at = jnp.where((me & 1 == parity) & (r >> 3 == half), mine, at)
    return at


def early_kernel(list_ref, half_ref, *refs):
    piece_refs, (out_ref, pairs_ref) = refs[:-2], refs[-2:]
    sectors, blocks, tile, width = out_ref.shape
    first = 2 * sectors * blocks + 2 + sectors
    merge(piece_refs, pairs_ref)

    def one(a, carry):
        for k in range(0, blocks, 2):
            ats = [list_ref[first + a * blocks + k + u] for u in range(2)]
            forms = [block_form(pairs_ref[at // 2], at % 2 == 1) for at in ats]
            out_ref[a, k], out_ref[a, k + 1] = two_products([half_ref[a, k], half_ref[a, k + 1]], forms)
        return carry

    lax.fori_loop(0, sectors, one, 0, unroll=2)


def listed_products(group_size, first, list_ref, half_ref, pairs_ref, out_ref):
    sectors, blocks, tile, width = half_ref.shape
    items = sectors * blocks
    listed = list_ref[first + items]

    def group(g, carry):
        for u in range(0, group_size, 2):
            entries = [list_ref[first + jnp.minimum(g * group_size + u + n, listed - 1)] for n in range(2)]
            places, halves, forms = [], [], []
            for entry in entries:
                item, at = entry % items, entry // items
                places.append((item // blocks, item % blocks))
                halves.append(half_ref[places[-1]])
                forms.append(block_form(pairs_ref[at // 2], at % 2 == 1))
            out_ref[places[0]], out_ref[places[1]] = two_products(halves, forms)
        return carry

    lax.fori_loop(0, (listed + group_size - 1) // group_size, group, 0)


def middle_kernel(list_ref, early_ref, half_ref, *refs):
    piece_refs, (out_ref, pairs_ref) = refs[:-2], refs[-2:]
    out_ref[...] = early_ref[...]
    merge(piece_refs, pairs_ref)
    listed_products(16, 0, list_ref, half_ref, pairs_ref, out_ref)


def last_kernel(list_ref, middle_ref, half_ref, *refs):
    piece_refs, (out_hbm, pairs_ref, out_ref, sems) = refs[:-4], refs[-4:]
    sectors, blocks, tile, width = half_ref.shape
    items = sectors * blocks

    def store(a, ref):
        return pltpu.make_async_copy(ref.at[a], out_hbm.at[a], sems.at[a])

    for a in range(sectors):
        changed = list_ref[2 * items + 2 + a] > 0

        @pl.when(changed)
        def _():
            out_ref[a] = middle_ref[a]

        @pl.when(jnp.logical_not(changed))
        def _():
            store(a, middle_ref).start()

    merge(piece_refs, pairs_ref)
    listed_products(16, items + 1, list_ref, half_ref, pairs_ref, out_ref)
    for a in range(sectors):

        @pl.when(list_ref[2 * items + 2 + a] > 0)
        def _():
            store(a, out_ref).start()

    for a in range(sectors):
        store(a, out_ref).wait()


def swap(piece, even_bit, odd_bit):
    count = lax.axis_size("sec")
    return lax.ppermute(piece, "sec", [(i, i ^ (odd_bit if i & CORE else even_bit)) for i in range(count)])


def per_device(
    psi, left_ops, right_ops, dims_left, dims_right, right_owner, right_slot, term_active
):
    left_count, block_count, tile, width = psi.shape
    items = left_count * block_count
    pair_count = right_ops.shape[0] // 2
    count = lax.axis_size("sec")
    by_swaps = count == len(ORDER)
    flops = 2 * psi.size * tile
    smem = pl.BlockSpec(memory_space=pltpu.SMEM)
    vmem = pl.BlockSpec(memory_space=pltpu.VMEM)
    hbm = pl.BlockSpec(memory_space=pltpu.HBM)
    params = pltpu.CompilerParams(vmem_limit_bytes=VMEM_LIMIT)

    def in_hbm(*arrays):
        return [pltpu.with_memory_space_constraint(array, pltpu.HBM) for array in arrays]

    pairs = pl.pallas_call(
        pack_kernel,
        out_shape=jax.ShapeDtypeStruct((pair_count, tile, 2 * tile), jnp.bfloat16),
        in_specs=[hbm, hbm],
        out_specs=vmem,
        scratch_shapes=[
            pltpu.SMEM(dims_right.shape, jnp.int32),
            pltpu.VMEM(right_ops.shape, jnp.bfloat16),
            pltpu.SemaphoreType.DMA((2,)),
        ],
        compiler_params=params,
        cost_estimate=pl.CostEstimate(flops=0, bytes_accessed=2 * right_ops.size, transcendentals=0),
    )(*in_hbm(dims_right, right_ops))

    active = term_active.reshape(left_count, block_count)
    half, listed = pl.pallas_call(
        functools.partial(left_kernel, pair_count, len(EARLY if by_swaps else range(count)) * pair_count),
        out_shape=(
            jax.ShapeDtypeStruct(psi.shape, jnp.bfloat16),
            pltpu.SMEM((3 * items + 2 + left_count,), jnp.int32),
        ),
        in_specs=[hbm] * 6,
        out_specs=(vmem, smem),
        scratch_shapes=[
            pltpu.SMEM(dims_left.shape, jnp.int32),
            pltpu.SMEM(active.shape, jnp.int32),
            pltpu.SMEM(right_owner.shape, jnp.int32),
            pltpu.SMEM(right_slot.shape, jnp.int32),
            pltpu.VMEM(left_ops.shape, jnp.bfloat16),
            pltpu.VMEM(psi.shape, jnp.bfloat16),
            pltpu.SemaphoreType.DMA((5,)),
            pltpu.SemaphoreType.DMA((left_count,)),
        ],
        compiler_params=params,
        cost_estimate=pl.CostEstimate(flops=flops, bytes_accessed=2 * psi.size, transcendentals=0),
    )(*in_hbm(dims_left, active, right_owner, right_slot, left_ops, psi))
    listed = pltpu.with_memory_space_constraint(listed, pltpu.SMEM)

    if by_swaps:
        pieces = {OWN: pairs}

        def pass_on(*routes):
            for name, target in routes:
                pieces[target] = swap(pieces[name], name[0] ^ target[0], name[1] ^ target[1])

        def share(*names):
            for name in names:
                pieces[partner(name)] = swap(pieces[name], CORE, CORE)

        pass_on((OWN, BEYOND), (OWN, BESIDE), (OWN, SIDE))
        share(OWN)
        held = (BEYOND,)
        half, ends = lax.optimization_barrier((half, [pieces[name] for name in held]))
        pieces.update(zip(held, ends))
        pass_on((BEYOND, FIRST), (BESIDE, CORNER), (BEYOND, SECOND), (FIRST, END))
        share(BESIDE, SIDE, CORNER, FIRST, BEYOND)
        early = [pieces[name] for name in EARLY]
    else:
        early = [lax.all_gather(pairs, "sec", axis=0, tiled=True)]

    sigma = pl.pallas_call(
        early_kernel,
        out_shape=jax.ShapeDtypeStruct(psi.shape, jnp.bfloat16),
        in_specs=[smem] + [vmem] * (1 + len(early)),
        out_specs=vmem,
        scratch_shapes=[pltpu.VMEM((sum(piece.shape[0] for piece in early), tile, 2 * tile), jnp.bfloat16)],
        compiler_params=params,
        cost_estimate=pl.CostEstimate(flops=flops, bytes_accessed=2 * psi.size, transcendentals=0),
    )(listed, half, *early)
    if by_swaps:
        pieces[END], pieces[SECOND], sigma = lax.optimization_barrier((pieces[END], pieces[SECOND], sigma))
        share(END, SECOND)
        sigma = pl.pallas_call(
            middle_kernel,
            out_shape=jax.ShapeDtypeStruct(psi.shape, jnp.bfloat16),
            in_specs=[smem] + [vmem] * (2 + len(MIDDLE)),
            out_specs=vmem,
            scratch_shapes=[pltpu.VMEM((len(MIDDLE) * pair_count, tile, 2 * tile), jnp.bfloat16)],
            compiler_params=params,
            cost_estimate=pl.CostEstimate(flops=flops // 4, bytes_accessed=psi.size // 2, transcendentals=0),
        )(listed, sigma, half, *[pieces[name] for name in MIDDLE])
        sigma = pl.pallas_call(
            last_kernel,
            out_shape=jax.ShapeDtypeStruct(psi.shape, jnp.bfloat16),
            in_specs=[smem] + [vmem] * (2 + len(LAST)),
            out_specs=hbm,
            scratch_shapes=[
                pltpu.VMEM((len(LAST) * pair_count, tile, 2 * tile), jnp.bfloat16),
                pltpu.VMEM(psi.shape, jnp.bfloat16),
                pltpu.SemaphoreType.DMA((left_count,)),
            ],
            compiler_params=params,
            cost_estimate=pl.CostEstimate(flops=flops // 16, bytes_accessed=2 * psi.size, transcendentals=0),
        )(listed, sigma, half, *[pieces[name] for name in LAST])
    if lax.axis_size("op") > 1:
        sigma = lax.psum_scatter(sigma, "op", scatter_dimension=3, tiled=True)
    return sigma


def solution(mesh):
    placed = (
        P(("grp", "sec"), None, None, None),
        P(("grp", "sec"), None, "op"),
        P(("grp", "sec"), None, "op"),
        P(("grp", "sec")),
        P(("grp", "sec")),
        P(("grp", "sec"), None),
        P(("grp", "sec"), None),
        P(("grp", "sec"), None, "op"),
    )
    return jax.shard_map(
        per_device,
        mesh=mesh,
        in_specs=placed,
        out_specs=P(("grp", "sec"), None, None, "op"),
        check_vma=False,
    )
```

```python
import functools

import jax
import jax.numpy as jnp
from jax import lax
from jax.experimental import pallas as pl
from jax.experimental.pallas import tpu as pltpu
from jax.sharding import PartitionSpec as P

VMEM_LIMIT = 48 * 1024 * 1024
FAR, NEAR, CROSS, CORE = 8, 4, 2, 1
OWN, SIDE, BESIDE, BEYOND, CORNER = (0, 0), (CROSS, CROSS), (NEAR, NEAR), (FAR, FAR), (NEAR | CROSS, NEAR | CROSS)
FIRST, SECOND = (FAR | NEAR, FAR | CROSS), (FAR | CROSS, FAR | NEAR)
END = (FAR | NEAR | CROSS, FAR | NEAR | CROSS)


def partner(name):
    return name[1] | CORE, name[0] | CORE


MIDDLE = (CORNER, SECOND, partner(CORNER), partner(BEYOND), partner(FIRST), END)
LAST = (partner(SECOND), partner(END))
EARLY = tuple(name for name in (
    OWN, SIDE, BESIDE, BEYOND, CORNER, FIRST, SECOND,
    partner(OWN), partner(SIDE), partner(BESIDE), partner(BEYOND), partner(CORNER), partner(FIRST), partner(SECOND),
) if name not in MIDDLE + LAST)
ORDER = EARLY + MIDDLE + LAST


def load_all(*copies):
    copies = [pltpu.make_async_copy(*copy) for copy in copies]
    for copy in copies:
        copy.start()
    return copies


def pack_kernel(dims_hbm, right_hbm, pairs_ref, dims_ref, right_ref, sems):
    count, tile, width = pairs_ref.shape
    copies = load_all((dims_hbm, dims_ref, sems.at[0]), (right_hbm, right_ref, sems.at[1]))
    rows = lax.broadcasted_iota(jnp.int32, (tile, tile), 0)
    cols = lax.broadcasted_iota(jnp.int32, (tile, tile), 1)
    most = jnp.maximum(rows, cols)
    for copy in copies:
        copy.wait()

    def kept(b):
        return jnp.where(most < dims_ref[b], right_ref[b].astype(jnp.float32), 0.0)

    for p in range(count):
        both = jnp.concatenate([kept(p), kept(p + count)], axis=0)
        pairs_ref[p] = both.T.astype(jnp.bfloat16)


def left_kernel(
    pair_count, held, dims_hbm, active_hbm, owner_hbm, slot_hbm, left_hbm, psi_hbm,
    half_ref, list_ref, dims_ref, active_ref, owner_ref, slot_ref, left_ref, psi_ref, sems, psi_sems,
):
    sectors, blocks, tile, width = psi_ref.shape
    items = sectors * blocks
    last = held + len(MIDDLE) * pair_count
    copies = load_all(
        (dims_hbm, dims_ref, sems.at[0]),
        (active_hbm, active_ref, sems.at[1]),
        (owner_hbm, owner_ref, sems.at[2]),
        (slot_hbm, slot_ref, sems.at[3]),
        (left_hbm, left_ref, sems.at[4]),
    )
    psi_copies = load_all(*[(psi_hbm.at[a], psi_ref.at[a], psi_sems.at[a]) for a in range(sectors)])
    rows = lax.broadcasted_iota(jnp.int32, (tile, tile), 0)
    cols = lax.broadcasted_iota(jnp.int32, (tile, tile), 1)
    most = jnp.maximum(rows, cols)
    me = lax.axis_index("sec")
    by_swaps = lax.axis_size("sec") == len(ORDER)
    for copy in copies:
        copy.wait()
    in_middle, in_last = jnp.int32(0), jnp.int32(0)
    for a in range(sectors):
        psi_copies[a].wait()
        op = jnp.where(most < dims_ref[a], left_ref[a].astype(jnp.float32), 0.0).astype(jnp.bfloat16)
        before = in_last
        for k in range(0, blocks, 2):
            both = jnp.concatenate([psi_ref[a, k], psi_ref[a, k + 1]], axis=1)
            part = jnp.dot(op, both, preferred_element_type=jnp.float32)
            for u in range(2):
                active = active_ref[a, k + u].astype(jnp.float32)
                half_ref[a, k + u] = (part[:, u * width:(u + 1) * width] * active).astype(jnp.bfloat16)
                item = a * blocks + k + u
                owner, slot = owner_ref[a, k + u], slot_ref[a, k + u]
                at = piece_at(owner ^ me, me) if by_swaps else owner
                second = slot >= pair_count
                at = at * pair_count + jnp.where(second, slot - pair_count, slot)
                is_early, is_last = at < held, at >= last
                at = (at - jnp.where(is_last, last, jnp.where(is_early, 0, held))) * 2 + second.astype(jnp.int32)
                list_ref[jnp.where(is_last, items + 1 + in_last, in_middle)] = at * items + item
                list_ref[2 * items + 2 + sectors + item] = jnp.where(is_early, at, 0)
                in_last = in_last + is_last.astype(jnp.int32)
                in_middle = in_middle + jnp.logical_not(is_early | is_last).astype(jnp.int32)
        list_ref[2 * items + 2 + a] = in_last - before
    list_ref[items] = in_middle
    list_ref[2 * items + 1] = in_last


def block_form(pair, second):
    tile, width = pair.shape
    lower = (lax.broadcasted_iota(jnp.int32, pair.shape, 1) < tile).astype(jnp.bfloat16)
    other = pltpu.roll(pair, tile, 1)
    top = jnp.where(second, other, pair) * lower
    low = jnp.where(second, pair, other) * (1 - lower)
    return jnp.concatenate([top, low], axis=0)


def two_products(halves, forms):
    zero = jnp.zeros_like(forms[0])
    top = jnp.concatenate([forms[0], zero], axis=1)
    low = jnp.concatenate([zero, forms[1]], axis=1)
    both = jnp.concatenate([top, low], axis=0)
    part = jnp.dot(jnp.concatenate(halves, axis=1), both, preferred_element_type=jnp.float32)
    width = part.shape[1] // 2
    return part[:, :width].astype(jnp.bfloat16), part[:, width:].astype(jnp.bfloat16)


def merge(piece_refs, pairs_ref):
    at = 0
    for piece in piece_refs:
        pairs_ref[at:at + piece.shape[0]] = piece[...]
        at += piece.shape[0]


def piece_at(r, me):
    at = jnp.int32(0)
    for parity in range(2):
        places = [ORDER.index(next(name for name in ORDER if name[parity] == i)) for i in range(len(ORDER))]
        for half in range(2):
            packed = sum(place << (4 * i) for i, place in enumerate(places[8 * half:8 * half + 7]))
            mine = jnp.where(r & 7 == 7, places[8 * half + 7], (packed >> (4 * (r & 7))) & 15)
            at = jnp.where((me & 1 == parity) & (r >> 3 == half), mine, at)
    return at


def early_kernel(list_ref, half_ref, *refs):
    piece_refs, (out_ref, pairs_ref) = refs[:-2], refs[-2:]
    sectors, blocks, tile, width = out_ref.shape
    first = 2 * sectors * blocks + 2 + sectors
    merge(piece_refs, pairs_ref)

    def one(a, carry):
        for k in range(0, blocks, 2):
            ats = [list_ref[first + a * blocks + k + u] for u in range(2)]
            forms = [block_form(pairs_ref[at // 2], at % 2 == 1) for at in ats]
            out_ref[a, k], out_ref[a, k + 1] = two_products([half_ref[a, k], half_ref[a, k + 1]], forms)
        return carry

    lax.fori_loop(0, sectors, one, 0, unroll=2)


def listed_products(group_size, first, list_ref, half_ref, pairs_ref, out_ref):
    sectors, blocks, tile, width = half_ref.shape
    items = sectors * blocks
    listed = list_ref[first + items]

    def group(g, carry):
        for u in range(0, group_size, 2):
            entries = [list_ref[first + jnp.minimum(g * group_size + u + n, listed - 1)] for n in range(2)]
            places, halves, forms = [], [], []
            for entry in entries:
                item, at = entry % items, entry // items
                places.append((item // blocks, item % blocks))
                halves.append(half_ref[places[-1]])
                forms.append(block_form(pairs_ref[at // 2], at % 2 == 1))
            out_ref[places[0]], out_ref[places[1]] = two_products(halves, forms)
        return carry

    lax.fori_loop(0, (listed + group_size - 1) // group_size, group, 0)


def middle_kernel(list_ref, early_ref, half_ref, *refs):
    piece_refs, (out_ref, pairs_ref) = refs[:-2], refs[-2:]
    out_ref[...] = early_ref[...]
    merge(piece_refs, pairs_ref)
    listed_products(16, 0, list_ref, half_ref, pairs_ref, out_ref)


def last_kernel(list_ref, middle_ref, half_ref, *refs):
    piece_refs, (out_hbm, pairs_ref, out_ref, sems) = refs[:-4], refs[-4:]
    sectors, blocks, tile, width = half_ref.shape
    items = sectors * blocks

    def store(a, ref):
        return pltpu.make_async_copy(ref.at[a], out_hbm.at[a], sems.at[a])

    for a in range(sectors):
        changed = list_ref[2 * items + 2 + a] > 0

        @pl.when(changed)
        def _():
            out_ref[a] = middle_ref[a]

        @pl.when(jnp.logical_not(changed))
        def _():
            store(a, middle_ref).start()

    merge(piece_refs, pairs_ref)
    listed_products(8, items + 1, list_ref, half_ref, pairs_ref, out_ref)
    for a in range(sectors):

        @pl.when(list_ref[2 * items + 2 + a] > 0)
        def _():
            store(a, out_ref).start()

    for a in range(sectors):
        store(a, out_ref).wait()


def swap(piece, even_bit, odd_bit):
    count = lax.axis_size("sec")
    return lax.ppermute(piece, "sec", [(i, i ^ (odd_bit if i & CORE else even_bit)) for i in range(count)])


def per_device(
    psi, left_ops, right_ops, dims_left, dims_right, right_owner, right_slot, term_active
):
    left_count, block_count, tile, width = psi.shape
    items = left_count * block_count
    pair_count = right_ops.shape[0] // 2
    count = lax.axis_size("sec")
    by_swaps = count == len(ORDER)
    flops = 2 * psi.size * tile
    smem = pl.BlockSpec(memory_space=pltpu.SMEM)
    vmem = pl.BlockSpec(memory_space=pltpu.VMEM)
    hbm = pl.BlockSpec(memory_space=pltpu.HBM)
    params = pltpu.CompilerParams(vmem_limit_bytes=VMEM_LIMIT)

    def in_hbm(*arrays):
        return [pltpu.with_memory_space_constraint(array, pltpu.HBM) for array in arrays]

    pairs = pl.pallas_call(
        pack_kernel,
        out_shape=jax.ShapeDtypeStruct((pair_count, tile, 2 * tile), jnp.bfloat16),
        in_specs=[hbm, hbm],
        out_specs=vmem,
        scratch_shapes=[
            pltpu.SMEM(dims_right.shape, jnp.int32),
            pltpu.VMEM(right_ops.shape, jnp.bfloat16),
            pltpu.SemaphoreType.DMA((2,)),
        ],
        compiler_params=params,
        cost_estimate=pl.CostEstimate(flops=0, bytes_accessed=2 * right_ops.size, transcendentals=0),
    )(*in_hbm(dims_right, right_ops))

    active = term_active.reshape(left_count, block_count)
    half, listed = pl.pallas_call(
        functools.partial(left_kernel, pair_count, len(EARLY if by_swaps else range(count)) * pair_count),
        out_shape=(
            jax.ShapeDtypeStruct(psi.shape, jnp.bfloat16),
            pltpu.SMEM((3 * items + 2 + left_count,), jnp.int32),
        ),
        in_specs=[hbm] * 6,
        out_specs=(vmem, smem),
        scratch_shapes=[
            pltpu.SMEM(dims_left.shape, jnp.int32),
            pltpu.SMEM(active.shape, jnp.int32),
            pltpu.SMEM(right_owner.shape, jnp.int32),
            pltpu.SMEM(right_slot.shape, jnp.int32),
            pltpu.VMEM(left_ops.shape, jnp.bfloat16),
            pltpu.VMEM(psi.shape, jnp.bfloat16),
            pltpu.SemaphoreType.DMA((5,)),
            pltpu.SemaphoreType.DMA((left_count,)),
        ],
        compiler_params=params,
        cost_estimate=pl.CostEstimate(flops=flops, bytes_accessed=2 * psi.size, transcendentals=0),
    )(*in_hbm(dims_left, active, right_owner, right_slot, left_ops, psi))
    listed = pltpu.with_memory_space_constraint(listed, pltpu.SMEM)

    if by_swaps:
        pieces = {OWN: pairs}

        def pass_on(*routes):
            for name, target in routes:
                pieces[target] = swap(pieces[name], name[0] ^ target[0], name[1] ^ target[1])

        def share(*names):
            for name in names:
                pieces[partner(name)] = swap(pieces[name], CORE, CORE)

        pass_on((OWN, BEYOND), (OWN, BESIDE), (OWN, SIDE))
        share(OWN)
        held = (BEYOND,)
        half, ends = lax.optimization_barrier((half, [pieces[name] for name in held]))
        pieces.update(zip(held, ends))
        pass_on((BEYOND, FIRST), (BESIDE, CORNER), (BEYOND, SECOND), (FIRST, END))
        share(BESIDE, SIDE, CORNER, FIRST, BEYOND)
        early = [pieces[name] for name in EARLY]
    else:
        early = [lax.all_gather(pairs, "sec", axis=0, tiled=True)]

    sigma = pl.pallas_call(
        early_kernel,
        out_shape=jax.ShapeDtypeStruct(psi.shape, jnp.bfloat16),
        in_specs=[smem] + [vmem] * (1 + len(early)),
        out_specs=vmem,
        scratch_shapes=[pltpu.VMEM((sum(piece.shape[0] for piece in early), tile, 2 * tile), jnp.bfloat16)],
        compiler_params=params,
        cost_estimate=pl.CostEstimate(flops=flops, bytes_accessed=2 * psi.size, transcendentals=0),
    )(listed, half, *early)
    if by_swaps:
        pieces[END], pieces[SECOND], sigma = lax.optimization_barrier((pieces[END], pieces[SECOND], sigma))
        share(END, SECOND)
        sigma = pl.pallas_call(
            middle_kernel,
            out_shape=jax.ShapeDtypeStruct(psi.shape, jnp.bfloat16),
            in_specs=[smem] + [vmem] * (2 + len(MIDDLE)),
            out_specs=vmem,
            scratch_shapes=[pltpu.VMEM((len(MIDDLE) * pair_count, tile, 2 * tile), jnp.bfloat16)],
            compiler_params=params,
            cost_estimate=pl.CostEstimate(flops=flops // 4, bytes_accessed=psi.size // 2, transcendentals=0),
        )(listed, sigma, half, *[pieces[name] for name in MIDDLE])
        sigma = pl.pallas_call(
            last_kernel,
            out_shape=jax.ShapeDtypeStruct(psi.shape, jnp.bfloat16),
            in_specs=[smem] + [vmem] * (2 + len(LAST)),
            out_specs=hbm,
            scratch_shapes=[
                pltpu.VMEM((len(LAST) * pair_count, tile, 2 * tile), jnp.bfloat16),
                pltpu.VMEM(psi.shape, jnp.bfloat16),
                pltpu.SemaphoreType.DMA((left_count,)),
            ],
            compiler_params=params,
            cost_estimate=pl.CostEstimate(flops=flops // 16, bytes_accessed=2 * psi.size, transcendentals=0),
        )(listed, sigma, half, *[pieces[name] for name in LAST])
    if lax.axis_size("op") > 1:
        sigma = lax.psum_scatter(sigma, "op", scatter_dimension=3, tiled=True)
    return sigma


def solution(mesh):
    placed = (
        P(("grp", "sec"), None, None, None),
        P(("grp", "sec"), None, "op"),
        P(("grp", "sec"), None, "op"),
        P(("grp", "sec")),
        P(("grp", "sec")),
        P(("grp", "sec"), None),
        P(("grp", "sec"), None),
        P(("grp", "sec"), None, "op"),
    )
    return jax.shard_map(
        per_device,
        mesh=mesh,
        in_specs=placed,
        out_specs=P(("grp", "sec"), None, None, "op"),
        check_vma=False,
    )
```

```python
import functools

import jax
import jax.numpy as jnp
from jax import lax
from jax.experimental import pallas as pl
from jax.experimental.pallas import tpu as pltpu
from jax.sharding import PartitionSpec as P

VMEM_LIMIT = 48 * 1024 * 1024
FAR, NEAR, CROSS, CORE = 8, 4, 2, 1
OWN, SIDE, BESIDE, BEYOND, CORNER = (0, 0), (CROSS, CROSS), (NEAR, NEAR), (FAR, FAR), (NEAR | CROSS, NEAR | CROSS)
FIRST, SECOND = (FAR | NEAR, FAR | CROSS), (FAR | CROSS, FAR | NEAR)
END = (FAR | NEAR | CROSS, FAR | NEAR | CROSS)


def partner(name):
    return name[1] | CORE, name[0] | CORE


MIDDLE = (SECOND, partner(CORNER), partner(BEYOND), partner(FIRST), END)
LAST = (partner(SECOND), partner(END))
EARLY = tuple(name for name in (
    OWN, SIDE, BESIDE, BEYOND, CORNER, FIRST, SECOND,
    partner(OWN), partner(SIDE), partner(BESIDE), partner(BEYOND), partner(CORNER), partner(FIRST), partner(SECOND),
) if name not in MIDDLE + LAST)
ORDER = EARLY + MIDDLE + LAST


def load_all(*copies):
    copies = [pltpu.make_async_copy(*copy) for copy in copies]
    for copy in copies:
        copy.start()
    return copies


def pack_kernel(dims_hbm, right_hbm, pairs_ref, dims_ref, right_ref, sems):
    count, tile, width = pairs_ref.shape
    copies = load_all((dims_hbm, dims_ref, sems.at[0]), (right_hbm, right_ref, sems.at[1]))
    rows = lax.broadcasted_iota(jnp.int32, (tile, tile), 0)
    cols = lax.broadcasted_iota(jnp.int32, (tile, tile), 1)
    most = jnp.maximum(rows, cols)
    for copy in copies:
        copy.wait()

    def kept(b):
        return jnp.where(most < dims_ref[b], right_ref[b].astype(jnp.float32), 0.0)

    for p in range(count):
        both = jnp.concatenate([kept(p), kept(p + count)], axis=0)
        pairs_ref[p] = both.T.astype(jnp.bfloat16)


def left_kernel(
    pair_count, held, dims_hbm, active_hbm, owner_hbm, slot_hbm, left_hbm, psi_hbm,
    half_ref, list_ref, dims_ref, active_ref, owner_ref, slot_ref, left_ref, psi_ref, sems, psi_sems,
):
    sectors, blocks, tile, width = psi_ref.shape
    items = sectors * blocks
    last = held + len(MIDDLE) * pair_count
    copies = load_all(
        (dims_hbm, dims_ref, sems.at[0]),
        (active_hbm, active_ref, sems.at[1]),
        (owner_hbm, owner_ref, sems.at[2]),
        (slot_hbm, slot_ref, sems.at[3]),
        (left_hbm, left_ref, sems.at[4]),
    )
    psi_copies = load_all(*[(psi_hbm.at[a], psi_ref.at[a], psi_sems.at[a]) for a in range(sectors)])
    rows = lax.broadcasted_iota(jnp.int32, (tile, tile), 0)
    cols = lax.broadcasted_iota(jnp.int32, (tile, tile), 1)
    most = jnp.maximum(rows, cols)
    me = lax.axis_index("sec")
    by_swaps = lax.axis_size("sec") == len(ORDER)
    for copy in copies:
        copy.wait()
    in_middle, in_last = jnp.int32(0), jnp.int32(0)
    for a in range(sectors):
        psi_copies[a].wait()
        op = jnp.where(most < dims_ref[a], left_ref[a].astype(jnp.float32), 0.0).astype(jnp.bfloat16)
        before = in_last
        for k in range(0, blocks, 2):
            both = jnp.concatenate([psi_ref[a, k], psi_ref[a, k + 1]], axis=1)
            part = jnp.dot(op, both, preferred_element_type=jnp.float32)
            for u in range(2):
                active = active_ref[a, k + u].astype(jnp.float32)
                half_ref[a, k + u] = (part[:, u * width:(u + 1) * width] * active).astype(jnp.bfloat16)
                item = a * blocks + k + u
                owner, slot = owner_ref[a, k + u], slot_ref[a, k + u]
                at = piece_at(owner ^ me, me) if by_swaps else owner
                second = slot >= pair_count
                at = at * pair_count + jnp.where(second, slot - pair_count, slot)
                is_early, is_last = at < held, at >= last
                at = (at - jnp.where(is_last, last, jnp.where(is_early, 0, held))) * 2 + second.astype(jnp.int32)
                list_ref[jnp.where(is_last, items + 1 + in_last, in_middle)] = at * items + item
                list_ref[2 * items + 2 + sectors + item] = jnp.where(is_early, at, 0)
                in_last = in_last + is_last.astype(jnp.int32)
                in_middle = in_middle + jnp.logical_not(is_early | is_last).astype(jnp.int32)
        list_ref[2 * items + 2 + a] = in_last - before
    list_ref[items] = in_middle
    list_ref[2 * items + 1] = in_last


def block_form(pair, second):
    tile, width = pair.shape
    lower = (lax.broadcasted_iota(jnp.int32, pair.shape, 1) < tile).astype(jnp.bfloat16)
    other = pltpu.roll(pair, tile, 1)
    top = jnp.where(second, other, pair) * lower
    low = jnp.where(second, pair, other) * (1 - lower)
    return jnp.concatenate([top, low], axis=0)


def two_products(halves, forms):
    zero = jnp.zeros_like(forms[0])
    top = jnp.concatenate([forms[0], zero], axis=1)
    low = jnp.concatenate([zero, forms[1]], axis=1)
    both = jnp.concatenate([top, low], axis=0)
    part = jnp.dot(jnp.concatenate(halves, axis=1), both, preferred_element_type=jnp.float32)
    width = part.shape[1] // 2
    return part[:, :width].astype(jnp.bfloat16), part[:, width:].astype(jnp.bfloat16)


def merge(piece_refs, pairs_ref):
    at = 0
    for piece in piece_refs:
        pairs_ref[at:at + piece.shape[0]] = piece[...]
        at += piece.shape[0]


def piece_at(r, me):
    at = jnp.int32(0)
    for parity in range(2):
        places = [ORDER.index(next(name for name in ORDER if name[parity] == i)) for i in range(len(ORDER))]
        for half in range(2):
            packed = sum(place << (4 * i) for i, place in enumerate(places[8 * half:8 * half + 7]))
            mine = jnp.where(r & 7 == 7, places[8 * half + 7], (packed >> (4 * (r & 7))) & 15)
            at = jnp.where((me & 1 == parity) & (r >> 3 == half), mine, at)
    return at


def early_kernel(list_ref, half_ref, *refs):
    piece_refs, (out_ref, pairs_ref) = refs[:-2], refs[-2:]
    sectors, blocks, tile, width = out_ref.shape
    first = 2 * sectors * blocks + 2 + sectors
    merge(piece_refs, pairs_ref)

    def one(a, carry):
        for k in range(0, blocks, 2):
            ats = [list_ref[first + a * blocks + k + u] for u in range(2)]
            forms = [block_form(pairs_ref[at // 2], at % 2 == 1) for at in ats]
            out_ref[a, k], out_ref[a, k + 1] = two_products([half_ref[a, k], half_ref[a, k + 1]], forms)
        return carry

    lax.fori_loop(0, sectors, one, 0, unroll=2)


def listed_products(group_size, first, list_ref, half_ref, pairs_ref, out_ref):
    sectors, blocks, tile, width = half_ref.shape
    items = sectors * blocks
    listed = list_ref[first + items]

    def group(g, carry):
        for u in range(0, group_size, 2):
            entries = [list_ref[first + jnp.minimum(g * group_size + u + n, listed - 1)] for n in range(2)]
            places, halves, forms = [], [], []
            for entry in entries:
                item, at = entry % items, entry // items
                places.append((item // blocks, item % blocks))
                halves.append(half_ref[places[-1]])
                forms.append(block_form(pairs_ref[at // 2], at % 2 == 1))
            out_ref[places[0]], out_ref[places[1]] = two_products(halves, forms)
        return carry

    lax.fori_loop(0, (listed + group_size - 1) // group_size, group, 0)


def middle_kernel(list_ref, early_ref, half_ref, *refs):
    piece_refs, (out_ref, pairs_ref) = refs[:-2], refs[-2:]
    out_ref[...] = early_ref[...]
    merge(piece_refs, pairs_ref)
    listed_products(16, 0, list_ref, half_ref, pairs_ref, out_ref)


def last_kernel(list_ref, middle_ref, half_ref, *refs):
    piece_refs, (out_hbm, pairs_ref, out_ref, sems) = refs[:-4], refs[-4:]
    sectors, blocks, tile, width = half_ref.shape
    items = sectors * blocks

    def store(a, ref):
        return pltpu.make_async_copy(ref.at[a], out_hbm.at[a], sems.at[a])

    for a in range(sectors):
        changed = list_ref[2 * items + 2 + a] > 0

        @pl.when(changed)
        def _():
            out_ref[a] = middle_ref[a]

        @pl.when(jnp.logical_not(changed))
        def _():
            store(a, middle_ref).start()

    merge(piece_refs, pairs_ref)
    listed_products(8, items + 1, list_ref, half_ref, pairs_ref, out_ref)
    for a in range(sectors):

        @pl.when(list_ref[2 * items + 2 + a] > 0)
        def _():
            store(a, out_ref).start()

    for a in range(sectors):
        store(a, out_ref).wait()


def swap(piece, even_bit, odd_bit):
    count = lax.axis_size("sec")
    return lax.ppermute(piece, "sec", [(i, i ^ (odd_bit if i & CORE else even_bit)) for i in range(count)])


def per_device(
    psi, left_ops, right_ops, dims_left, dims_right, right_owner, right_slot, term_active
):
    left_count, block_count, tile, width = psi.shape
    items = left_count * block_count
    pair_count = right_ops.shape[0] // 2
    count = lax.axis_size("sec")
    by_swaps = count == len(ORDER)
    flops = 2 * psi.size * tile
    smem = pl.BlockSpec(memory_space=pltpu.SMEM)
    vmem = pl.BlockSpec(memory_space=pltpu.VMEM)
    hbm = pl.BlockSpec(memory_space=pltpu.HBM)
    params = pltpu.CompilerParams(vmem_limit_bytes=VMEM_LIMIT)

    def in_hbm(*arrays):
        return [pltpu.with_memory_space_constraint(array, pltpu.HBM) for array in arrays]

    pairs = pl.pallas_call(
        pack_kernel,
        out_shape=jax.ShapeDtypeStruct((pair_count, tile, 2 * tile), jnp.bfloat16),
        in_specs=[hbm, hbm],
        out_specs=vmem,
        scratch_shapes=[
            pltpu.SMEM(dims_right.shape, jnp.int32),
            pltpu.VMEM(right_ops.shape, jnp.bfloat16),
            pltpu.SemaphoreType.DMA((2,)),
        ],
        compiler_params=params,
        cost_estimate=pl.CostEstimate(flops=0, bytes_accessed=2 * right_ops.size, transcendentals=0),
    )(*in_hbm(dims_right, right_ops))

    active = term_active.reshape(left_count, block_count)
    half, listed = pl.pallas_call(
        functools.partial(left_kernel, pair_count, len(EARLY if by_swaps else range(count)) * pair_count),
        out_shape=(
            jax.ShapeDtypeStruct(psi.shape, jnp.bfloat16),
            pltpu.SMEM((3 * items + 2 + left_count,), jnp.int32),
        ),
        in_specs=[hbm] * 6,
        out_specs=(vmem, smem),
        scratch_shapes=[
            pltpu.SMEM(dims_left.shape, jnp.int32),
            pltpu.SMEM(active.shape, jnp.int32),
            pltpu.SMEM(right_owner.shape, jnp.int32),
            pltpu.SMEM(right_slot.shape, jnp.int32),
            pltpu.VMEM(left_ops.shape, jnp.bfloat16),
            pltpu.VMEM(psi.shape, jnp.bfloat16),
            pltpu.SemaphoreType.DMA((5,)),
            pltpu.SemaphoreType.DMA((left_count,)),
        ],
        compiler_params=params,
        cost_estimate=pl.CostEstimate(flops=flops, bytes_accessed=2 * psi.size, transcendentals=0),
    )(*in_hbm(dims_left, active, right_owner, right_slot, left_ops, psi))
    listed = pltpu.with_memory_space_constraint(listed, pltpu.SMEM)

    if by_swaps:
        pieces = {OWN: pairs}

        def pass_on(*routes):
            for name, target in routes:
                pieces[target] = swap(pieces[name], name[0] ^ target[0], name[1] ^ target[1])

        def share(*names):
            for name in names:
                pieces[partner(name)] = swap(pieces[name], CORE, CORE)

        pass_on((OWN, BEYOND), (OWN, BESIDE), (OWN, SIDE))
        share(OWN)
        held = (BEYOND,)
        half, ends = lax.optimization_barrier((half, [pieces[name] for name in held]))
        pieces.update(zip(held, ends))
        pass_on((BEYOND, FIRST), (BESIDE, CORNER), (BEYOND, SECOND), (FIRST, END))
        share(BESIDE, SIDE, CORNER, FIRST, BEYOND)
        early = [pieces[name] for name in EARLY]
    else:
        early = [lax.all_gather(pairs, "sec", axis=0, tiled=True)]

    sigma = pl.pallas_call(
        early_kernel,
        out_shape=jax.ShapeDtypeStruct(psi.shape, jnp.bfloat16),
        in_specs=[smem] + [vmem] * (1 + len(early)),
        out_specs=vmem,
        scratch_shapes=[pltpu.VMEM((sum(piece.shape[0] for piece in early), tile, 2 * tile), jnp.bfloat16)],
        compiler_params=params,
        cost_estimate=pl.CostEstimate(flops=flops, bytes_accessed=2 * psi.size, transcendentals=0),
    )(listed, half, *early)
    if by_swaps:
        pieces[END], pieces[SECOND], sigma = lax.optimization_barrier((pieces[END], pieces[SECOND], sigma))
        share(END, SECOND)
        sigma = pl.pallas_call(
            middle_kernel,
            out_shape=jax.ShapeDtypeStruct(psi.shape, jnp.bfloat16),
            in_specs=[smem] + [vmem] * (2 + len(MIDDLE)),
            out_specs=vmem,
            scratch_shapes=[pltpu.VMEM((len(MIDDLE) * pair_count, tile, 2 * tile), jnp.bfloat16)],
            compiler_params=params,
            cost_estimate=pl.CostEstimate(flops=flops // 4, bytes_accessed=psi.size // 2, transcendentals=0),
        )(listed, sigma, half, *[pieces[name] for name in MIDDLE])
        sigma = pl.pallas_call(
            last_kernel,
            out_shape=jax.ShapeDtypeStruct(psi.shape, jnp.bfloat16),
            in_specs=[smem] + [vmem] * (2 + len(LAST)),
            out_specs=hbm,
            scratch_shapes=[
                pltpu.VMEM((len(LAST) * pair_count, tile, 2 * tile), jnp.bfloat16),
                pltpu.VMEM(psi.shape, jnp.bfloat16),
                pltpu.SemaphoreType.DMA((left_count,)),
            ],
            compiler_params=params,
            cost_estimate=pl.CostEstimate(flops=flops // 16, bytes_accessed=2 * psi.size, transcendentals=0),
        )(listed, sigma, half, *[pieces[name] for name in LAST])
    if lax.axis_size("op") > 1:
        sigma = lax.psum_scatter(sigma, "op", scatter_dimension=3, tiled=True)
    return sigma


def solution(mesh):
    placed = (
        P(("grp", "sec"), None, None, None),
        P(("grp", "sec"), None, "op"),
        P(("grp", "sec"), None, "op"),
        P(("grp", "sec")),
        P(("grp", "sec")),
        P(("grp", "sec"), None),
        P(("grp", "sec"), None),
        P(("grp", "sec"), None, "op"),
    )
    return jax.shard_map(
        per_device,
        mesh=mesh,
        in_specs=placed,
        out_specs=P(("grp", "sec"), None, None, "op"),
        check_vma=False,
    )
```
